32 devices in a mesh: mp: 2 (over core), tile: 16 (over z, y, x).
Axes of the slice: x: 2, y: 2, z: 4, core: 2. Of those that a mesh axis runs over, the one named last changes fastest.
Arguments:
- tracers: float32 [2, 4, 64, 256, 512], P('mp', None, None, 'tile'), may hold values from -6 to 6
- diffusivity: float32 [2, 63, 256, 512], P('mp', None, 'tile'), may hold values from 0.05 to 60
- conductance: float32 [2, 256, 512], P('mp', 'tile'), may hold values from 0.2 to 4
- face_velocity: float32 [2, 64, 256, 512], P('mp', None, 'tile'), may hold values from -0.3 to 0.3
- partner: int32 [2, 2, 256, 512], P('mp', None, 'tile'), may hold values from 0 to 255, as said below
- weight: int32 [2, 2, 256, 512], P('mp', None, 'tile'), may hold values from 0 to 15, as said below
- sea_mask: int32 [256, 512], P('tile'), may hold values from 0 to 1, as said below
Outputs:
- tracers_out: float32 [2, 4, 64, 256, 512], P('mp', None, None, 'tile')
- surface_inflow: float32 [2, 4, 256, 512], P('mp', None, 'tile')
The draws below stay inside these ranges and needn't reach their ends.
Inputs may be any that keep to these rules, and one draw needn't show every extreme that they name: `partner`: entry [m, k, x, y] names a column of the other component in the same row y that intersects column (x, y) of component m, at most 9 cells from x along the periodic X direction; each intersection is listed on both sides with the same weight. `weight`: intersection area in units of 1 / 16 of a cell; 0 exactly where the ocean column of the intersection is land. `sea_mask`: 1 marks an ocean column, 0 land.
All inputs are finite; a program needn't handle non-finite values.
Results may differ from the reference program's by a relative error of at most 0.00002.
Values sent between devices are 32-bit elements; how exact they have to be, the bound alone decides.
No kernel may reach another device: no remote copies, remote signals or barrier semaphores. Data moves between devices by JAX's collectives and lax.ppermute only.
A program may use at most 192 MiB of HBM per device.

```python
import math
import jax
import jax.numpy as jnp
from jax import lax

CX = 16
NY = 512
LEV = 64
TRAC = 4
STEPS = 4
QUANT = 16
NXG = 256


def coastline(key):
    coarse = jax.random.randint(jax.random.fold_in(key, 31), (NXG // 4, NY // 4), 0, 10)
    sea_cells = (coarse >= 3).astype(jnp.int32)
    sea_cells = jnp.repeat(jnp.repeat(sea_cells, 4, axis=0), 4, axis=1)
    return sea_cells.at[:, 0].set(1)


def intersection_tables(key):
    sea_cells = coastline(key)
    shifts = jax.random.randint(jax.random.fold_in(key, 32), (NY,), -(CX // 2), CX // 2 + 1)
    shifts = shifts.at[0].set(CX // 2)
    fractions = jax.random.randint(jax.random.fold_in(key, 33), (NY,), 1, QUANT)
    fractions = fractions.at[0].set(1)
    column_ids = jnp.arange(NXG, dtype=jnp.int32)[:, None]
    ocean_first = jnp.mod(column_ids + shifts[None], NXG)
    ocean_second = jnp.mod(ocean_first + 1, NXG)
    ocean_partner = jnp.stack([ocean_first, ocean_second])
    ocean_weight = jnp.stack([(QUANT - fractions)[None] * sea_cells, fractions[None] * sea_cells])
    atmos_near = jnp.mod(column_ids - shifts[None], NXG)
    atmos_far = jnp.mod(atmos_near - 1, NXG)
    atmos_partner = jnp.stack([atmos_near, atmos_far])
    atmos_weight = jnp.stack([(QUANT - fractions)[None] * jnp.take_along_axis(sea_cells, atmos_near, axis=0), fractions[None] * jnp.take_along_axis(sea_cells, atmos_far, axis=0)])
    partner_table = jnp.stack([atmos_partner, ocean_partner]).astype(jnp.int32)
    weight_table = jnp.stack([atmos_weight, ocean_weight]).astype(jnp.int32)
    return (partner_table, weight_table, sea_cells.astype(jnp.int32))


def draw_partner(key, part):
    return intersection_tables(key)[0]


def draw_weight(key, part):
    return intersection_tables(key)[1]


def draw_sea_mask(key, part):
    return intersection_tables(key)[2]


def draw_diffusivity(key, part):
    key = jax.random.fold_in(key, 41)
    shape_all = (2, LEV - 1, NXG, NY)
    strong_low = 15.0
    share_of_four = 2
    background = jnp.exp(jax.random.uniform(jax.random.fold_in(key, 1), shape_all, jnp.float32, math.log(0.05), math.log(5.0)))
    strong = jnp.exp(jax.random.uniform(jax.random.fold_in(key, 2), shape_all, jnp.float32, math.log(strong_low), math.log(60.0)))
    flagged = jax.random.randint(jax.random.fold_in(key, 3), (2, NXG // 4, NY // 4), 0, 4) < share_of_four
    layer_depth = jax.random.randint(jax.random.fold_in(key, 4), (2, NXG // 4, NY // 4), LEV // 3, LEV)
    layer_depth = jnp.where(flagged, layer_depth, 0)
    layer_depth = jnp.repeat(jnp.repeat(layer_depth, 4, axis=1), 4, axis=2)
    levels = jnp.arange(LEV - 1, dtype=jnp.int32)[None, :, None, None]
    mixed = levels >= LEV - 1 - layer_depth[:, None]
    return jnp.where(mixed, strong, background).astype(jnp.float32)


def steps_of(key, extent, pieces, least, high):
    level = 1.0
    for axis_at, blocks in pieces:
        draws = jax.random.uniform(jax.random.fold_in(jax.random.fold_in(key, 6), axis_at), (blocks,), jnp.float32, least / len(pieces), high / len(pieces))
        level = level * jnp.repeat(jnp.exp(draws), extent[axis_at] // blocks).reshape((-1,) + (1,) * (len(extent) - 1 - axis_at))
    return level


def scatter_about(key, shape, deviation, limit, shards=(), kind=jnp.bfloat16):
    drawn = deviation * jax.random.normal(key, shape, jnp.float32)
    if shards:
        drawn = drawn * steps_of(key, shape, shards, -0.22, 0.18)
    return jnp.clip(drawn, -limit, limit).astype(kind)


def setup_inputs(seed: int = 0) -> dict:
    arg_keys = jax.random.split(jax.random.key(seed), 8)
    tracers = scatter_about(arg_keys[0], (2, TRAC, LEV, NXG, NY), 1.0, 6.0, ((0, 2), (3, 16)), jnp.float32)
    diffusivity = draw_diffusivity(jax.random.fold_in(arg_keys[7], 71), 0)
    conductance = jnp.clip(jnp.exp(math.log(4.0) - 2.9957323 * jax.random.uniform(arg_keys[2], (2, NXG, NY), jnp.float32) ** steps_of(arg_keys[2], (2, NXG, NY), ((0, 2), (1, 16)), -0.2, 0.2)), 0.2, 4.0)
    face_velocity = jnp.clip(jax.random.uniform(arg_keys[3], (2, LEV, NXG, NY), jnp.float32, -0.3, 0.3) * steps_of(arg_keys[3], (2, LEV, NXG, NY), ((0, 2), (2, 16)), -0.4, 0.0), -0.3, 0.3)
    partner = draw_partner(jax.random.fold_in(arg_keys[7], 71), 0)
    weight = draw_weight(jax.random.fold_in(arg_keys[7], 71), 0)
    sea_mask = draw_sea_mask(jax.random.fold_in(arg_keys[7], 71), 0)
    return {"tracers": tracers, "diffusivity": diffusivity, "conductance": conductance, "face_velocity": face_velocity, "partner": partner, "weight": weight, "sea_mask": sea_mask}


diffusion_nu = 0.12


def down_sweep(previous, coupling):
    zero_row = jnp.zeros_like(coupling[:, :1])
    lower_side = jnp.concatenate([zero_row, coupling], axis=1)
    upper_side = jnp.concatenate([coupling, zero_row], axis=1)

    def eliminate(state_in, inputs):
        ratio_prev, part_prev, pivot_prev = state_in
        source, low_side, high_side = inputs
        pivot_now = 1.0 + low_side + high_side - low_side * ratio_prev
        part_now = (source + low_side[:, None] * part_prev) / pivot_now[:, None]
        ratio_now = high_side / pivot_now
        return (ratio_now, part_now, pivot_now), (part_now, ratio_now)

    initial = (jnp.zeros_like(coupling[:, 0]), jnp.zeros_like(previous[:, :, 0]), jnp.ones_like(coupling[:, 0]))
    inputs = (jnp.moveaxis(previous, 2, 0), jnp.moveaxis(lower_side, 1, 0), jnp.moveaxis(upper_side, 1, 0))
    finals, (partials, ratios) = lax.scan(eliminate, initial, inputs, unroll=8)
    return partials, ratios, finals[2]


def up_sweep(partials, ratios, surface):
    def back_substitute(upper_value, inputs):
        part_now, ratio_now = inputs
        value_now = part_now + ratio_now[:, None] * upper_value
        return value_now, value_now

    _, lowers = lax.scan(back_substitute, surface, (partials[:-1], ratios[:-1]), reverse=True, unroll=8)
    column = jnp.concatenate([lowers, surface[None]], axis=0)
    return jnp.moveaxis(column, 0, 2)


def surface_flux(own_terms, peer_terms, weight):
    own_value = own_terms[:, :-2]
    own_slope = own_terms[:, -2]
    own_conduct = own_terms[:, -1]
    peer_value = peer_terms[:, :-2]
    peer_slope = peer_terms[:, -2]
    peer_conduct = peer_terms[:, -1]
    series = own_conduct[:, None] * peer_conduct / (own_conduct[:, None] + peer_conduct)
    denominator = 1.0 + series * (own_slope[:, None] + peer_slope)
    outflow = series[:, None] * (own_value[:, :, None] - peer_value) / denominator[:, None]
    return -jnp.sum(weight.astype(jnp.float32)[:, None] * outflow, axis=2) / QUANT


def advance(field_in, velocity, openness):
    open_east = (openness[:, :-1] * openness[:, 1:])[:, None, None]
    east_speed = velocity[:, None, :, :-1, :]
    left_side = field_in[..., :-1, :]
    right_side = field_in[..., 1:, :]
    east_flux = open_east * (jnp.maximum(east_speed, 0.0) * left_side + jnp.minimum(east_speed, 0.0) * right_side - diffusion_nu * (right_side - left_side))
    open_north = (openness[:, :, :-1] * openness[:, :, 1:])[:, None, None]
    north_flux = -diffusion_nu * open_north * (field_in[..., 1:] - field_in[..., :-1])
    north_padded = jnp.pad(north_flux, [(0, 0), (0, 0), (0, 0), (0, 0), (1, 1)])
    change_x = east_flux[..., 1:, :] - east_flux[..., :-1, :]
    change_y = north_padded[..., 1:] - north_padded[..., :-1]
    return field_in[..., 1:-1, :] - change_x - change_y[..., 1:-1, :]


def wrap_periodic(values):
    return jnp.concatenate([values[..., -1:, :], values, values[..., :1, :]], axis=-2)


def reference(tracers, diffusivity, conductance, face_velocity, partner, weight, sea_mask):
    partials, ratios, pivots = down_sweep(tracers, diffusivity)
    slopes = 1.0 / pivots
    own_terms = jnp.concatenate([partials[-1], slopes[:, None], conductance[:, None]], axis=1)
    other_terms = own_terms[::-1]
    shape_all = (2, TRAC + 2, 2, NXG, NY)
    peer_terms = jnp.take_along_axis(jnp.broadcast_to(other_terms[:, :, None], shape_all), jnp.broadcast_to(partner[:, None], shape_all), axis=3)
    inflow = surface_flux(own_terms, peer_terms, weight)
    surface = partials[-1] + slopes[:, None] * inflow
    columns = up_sweep(partials, ratios, surface)
    openness = jnp.stack([jnp.ones((NXG, NY), jnp.float32), sea_mask.astype(jnp.float32)])
    for section_index in range(STEPS):
        columns = advance(wrap_periodic(columns), wrap_periodic(face_velocity), wrap_periodic(openness))
    return columns, inflow
```

```python
import functools

import jax
import jax.numpy as jnp
from jax import lax
from jax.experimental import pallas as pl
from jax.experimental.pallas import tpu as pltpu
from jax.sharding import PartitionSpec as P

STEPS = 4
QUANT = 16
NU = 0.12
BLOCK = 8
CHUNKS = 4
F32 = jnp.float32


def params(mib, **more):
    return pltpu.CompilerParams(vmem_limit_bytes=mib * 2**20, **more)


def lane_parts(total, size=256):
    size = min(size, total)
    return [slice(start, start + size) for start in range(0, total, size)]


def eliminate(source, coupling, state, lanes, last):
    before, ratio, parts = state
    rows = []
    for at in range(BLOCK):
        now = coupling[at, :, lanes]
        if at == BLOCK - 1:
            now = jnp.where(last, 0.0, now)
        inverse = 1.0 / (1.0 + before + now - before * ratio)
        parts = [(source[t, at, :, lanes] + before * part) * inverse for t, part in enumerate(parts)]
        ratio = now * inverse
        before = now
        rows.append((parts, ratio, inverse))
    return (before, ratio, parts), rows


def down_kernel(reach, source, coupling, conduct, sea, terms, low, high, before_s, ratio_s, part_s, slope_s):
    step = pl.program_id(0)
    last = step == pl.num_programs(0) - 1
    tracers, width, rows = part_s.shape

    @pl.when(step == 0)
    def _():
        before_s[...] = jnp.zeros_like(before_s)
        ratio_s[...] = jnp.zeros_like(ratio_s)
        part_s[...] = jnp.zeros_like(part_s)

    for lanes in lane_parts(rows):
        state = (before_s[:, lanes], ratio_s[:, lanes], [part_s[t, :, lanes] for t in range(tracers)])
        (before, ratio, parts), levels = eliminate(source, coupling, state, lanes, last)
        before_s[:, lanes] = before
        ratio_s[:, lanes] = ratio
        slope_s[:, lanes] = levels[-1][2]
        for t in range(tracers):
            part_s[t, :, lanes] = parts[t]

    @pl.when(last)
    def _():
        fields = [part_s[t] for t in range(tracers)] + [slope_s[...], conduct[...]]
        for c, field in enumerate(fields):
            terms[c] = field
            low[c * reach : (c + 1) * reach, :] = field[width - reach :]
            high[c * reach : (c + 1) * reach, :] = field[:reach]
        mask = sea[...].astype(F32)
        at = len(fields) * reach
        low[at : at + 1, :] = mask[width - 1 :]
        high[at : at + 1, :] = mask[:1]


def down_to_surface(tracers, diffusivity, conductance, sea_mask, reach):
    count, levels, width, rows = tracers.shape
    packed = (count + 2) * reach + 1
    packed = -(-packed // 8) * 8
    whole = lambda *shape: pl.BlockSpec(shape, lambda i: (0,) * len(shape))
    return pl.pallas_call(
        functools.partial(down_kernel, reach),
        grid=(levels // BLOCK,),
        in_specs=[
            pl.BlockSpec((count, BLOCK, width, rows), lambda i: (0, i, 0, 0)),
            pl.BlockSpec((BLOCK, width, rows), lambda i: (i, 0, 0)),
            whole(width, rows),
            whole(width, rows),
        ],
        out_specs=[whole(count + 2, width, rows), whole(packed, rows), whole(packed, rows)],
        out_shape=[
            jax.ShapeDtypeStruct((count + 2, width, rows), F32),
            jax.ShapeDtypeStruct((packed, rows), F32),
            jax.ShapeDtypeStruct((packed, rows), F32),
        ],
        scratch_shapes=[
            pltpu.VMEM((width, rows), F32),
            pltpu.VMEM((width, rows), F32),
            pltpu.VMEM((count, width, rows), F32),
            pltpu.VMEM((width, rows), F32),
        ],
        compiler_params=params(24),
        cost_estimate=pl.CostEstimate(
            flops=20 * levels * width * rows, bytes_accessed=5 * levels * width * rows * 4, transcendentals=0
        ),
        name="down_to_surface",
    )(tracers, diffusivity, conductance, sea_mask)


def solve_kernel(
    blocks, source, coupling, fixed, scale, fixed_w, fixed_e, scale_w, scale_e, parts_s, ratios_s, before_s, fixed_s, scale_s
):
    step = pl.program_id(0)
    tracers, _, width, rows = source.shape

    @pl.when(step == 0)
    def _():
        before_s[...] = jnp.zeros_like(before_s)
        scale_s[...] = jnp.zeros_like(scale_s)
        fixed_s[...] = jnp.zeros_like(fixed_s)

    @pl.when(step < blocks)
    def _():
        last = step == blocks - 1
        base = step * BLOCK
        for lanes in lane_parts(rows):
            state = (before_s[:, lanes], scale_s[:, lanes], [fixed_s[t, :, lanes] for t in range(tracers)])
            (before, ratio, parts), levels = eliminate(source, coupling, state, lanes, last)
            for at, (part, ratio_at, _) in enumerate(levels):
                ratios_s[base + at, :, lanes] = ratio_at
                for t in range(tracers):
                    parts_s[t, base + at, :, lanes] = part[t]
            before_s[:, lanes] = before
            scale_s[:, lanes] = ratio
            for t in range(tracers):
                fixed_s[t, :, lanes] = parts[t]

    @pl.when(step >= blocks)
    def _():
        first = step == blocks
        base = (2 * blocks - 1 - step) * BLOCK
        for lanes in lane_parts(rows):
            scale_now = scale_s[:, lanes]
            fixed_now = [fixed_s[t, :, lanes] for t in range(tracers)]
            for at in reversed(range(BLOCK)):
                ratio = ratios_s[base + at, :, lanes]
                scale_now = ratio * scale_now
                fixed_now = [parts_s[t, base + at, :, lanes] + ratio * fixed_now[t] for t in range(tracers)]
                if at == BLOCK - 1:
                    scale_now = jnp.where(first, 1.0, scale_now)
                    fixed_now = [jnp.where(first, 0.0, f) for f in fixed_now]
                scale[at, :, lanes] = scale_now
                scale_w[at : at + 1, lanes] = scale_now[:1]
                scale_e[at : at + 1, lanes] = scale_now[width - 1 :]
                for t in range(tracers):
                    fixed[t, at, :, lanes] = fixed_now[t]
                    fixed_w[t, at : at + 1, lanes] = fixed_now[t][:1]
                    fixed_e[t, at : at + 1, lanes] = fixed_now[t][width - 1 :]
            scale_s[:, lanes] = scale_now
            for t in range(tracers):
                fixed_s[t, :, lanes] = fixed_now[t]


def solve_columns(tracers, diffusivity):
    count, levels, width, rows = tracers.shape
    blocks = levels // BLOCK
    down = lambda i: jnp.minimum(i, blocks - 1)
    up = lambda i: jnp.minimum(2 * blocks - 1 - i, blocks - 1)
    edge4 = pl.BlockSpec((count, BLOCK, rows), lambda i: (0, up(i), 0))
    edge1 = pl.BlockSpec((BLOCK, rows), lambda i: (up(i), 0))
    return pl.pallas_call(
        functools.partial(solve_kernel, blocks),
        grid=(2 * blocks,),
        in_specs=[
            pl.BlockSpec((count, BLOCK, width, rows), lambda i: (0, down(i), 0, 0)),
            pl.BlockSpec((BLOCK, width, rows), lambda i: (down(i), 0, 0)),
        ],
        out_specs=[
            pl.BlockSpec((count, BLOCK, width, rows), lambda i: (0, up(i), 0, 0)),
            pl.BlockSpec((BLOCK, width, rows), lambda i: (up(i), 0, 0)),
            edge4,
            edge4,
            edge1,
            edge1,
        ],
        out_shape=[
            jax.ShapeDtypeStruct((count, levels, width, rows), F32),
            jax.ShapeDtypeStruct((levels, width, rows), F32),
            jax.ShapeDtypeStruct((count, levels, rows), F32),
            jax.ShapeDtypeStruct((count, levels, rows), F32),
            jax.ShapeDtypeStruct((levels, rows), F32),
            jax.ShapeDtypeStruct((levels, rows), F32),
        ],
        scratch_shapes=[
            pltpu.VMEM((count, levels, width, rows), F32),
            pltpu.VMEM((levels, width, rows), F32),
            pltpu.VMEM((width, rows), F32),
            pltpu.VMEM((count, width, rows), F32),
            pltpu.VMEM((width, rows), F32),
        ],
        compiler_params=params(32),
        cost_estimate=pl.CostEstimate(
            flops=40 * levels * width * rows, bytes_accessed=10 * levels * width * rows * 4, transcendentals=0
        ),
        name="solve_columns",
    )(tracers, diffusivity)


def surface_kernel(
    reach, chunks, place, own, peer, low, high, partner, weight, sea,
    fixed_w, fixed_e, scale_w, scale_e,
    inflow, surface, open_e, open_w, coef_n, coef_s, *rest,
):
    edges_w, edges_e, wide = rest[:chunks], rest[chunks : 2 * chunks], rest[2 * chunks]
    channels, width, rows = own.shape
    tracers = channels - 2
    first = 2 * 8
    for c in range(channels):
        wide[c, first - reach : first, :] = low[c * reach : (c + 1) * reach, :]
        wide[c, first : first + width, :] = peer[c]
        wide[c, first + width : first + width + reach, :] = high[c * reach : (c + 1) * reach, :]

    start, total, ocean = place[0], place[1], place[2]
    for lanes in lane_parts(rows, 128):
        position = start + lax.broadcasted_iota(jnp.int32, (width, 128), 0)
        own_slope = own[tracers, :, lanes]
        own_conduct = own[tracers + 1, :, lanes]
        flow = [jnp.zeros((width, 128), F32) for _ in range(tracers)]
        for k in range(partner.shape[0]):
            apart = partner[k, :, lanes] - position
            apart = jnp.where(apart > reach, apart - total, apart)
            apart = jnp.where(apart < -reach, apart + total, apart)
            found = [jnp.zeros((width, 128), F32) for _ in range(channels)]
            for offset in range(-reach, reach + 1):
                hit = apart == offset
                window = slice(first + offset, first + offset + width)
                found = [jnp.where(hit, wide[c, window, lanes], f) for c, f in enumerate(found)]
            series = own_conduct * found[-1] / (own_conduct + found[-1])
            factor = weight[k, :, lanes].astype(F32) * series / (1.0 + series * (own_slope + found[-2]))
            flow = [flow[t] + factor * (own[t, :, lanes] - found[t]) for t in range(tracers)]
        for t in range(tracers):
            into = flow[t] * (-1.0 / QUANT)
            inflow[t, :, lanes] = into
            surface[t, :, lanes] = own[t, :, lanes] + own_slope * into

    free = jnp.broadcast_to(ocean, (width, rows)) == 0
    open_here = jnp.where(free, 1.0, sea[...].astype(F32))
    row = lax.broadcasted_iota(jnp.int32, (width, rows), 0)
    column = lax.broadcasted_iota(jnp.int32, (width, rows), 1)
    at = channels * reach
    from_west = jnp.where(free, 1.0, jnp.broadcast_to(low[at : at + 1, :], (width, rows)))
    from_east = jnp.where(free, 1.0, jnp.broadcast_to(high[at : at + 1, :], (width, rows)))
    open_e[...] = open_here * jnp.where(row == width - 1, from_east, pltpu.roll(open_here, width - 1, 0))
    open_w[...] = open_here * jnp.where(row == 0, from_west, pltpu.roll(open_here, 1, 0))
    north = open_here * jnp.where(column == rows - 1, 0.0, pltpu.roll(open_here, rows - 1, 1))
    south = open_here * jnp.where(column == 0, 0.0, pltpu.roll(open_here, 1, 1))
    coef_n[...] = NU * north
    coef_s[...] = NU * south

    levels = scale_w.shape[0]
    size = levels // chunks
    for t in range(tracers):
        top_w = surface[t, :1, :]
        top_e = surface[t, width - 1 :, :]
        for c in range(chunks):
            part = slice(c * size, (c + 1) * size)
            edges_w[c][t] = fixed_w[t, part, :] + scale_w[part, :] * top_w
            edges_e[c][t] = fixed_e[t, part, :] + scale_e[part, :] * top_e


def exchange_surface(place, own, peer, low, high, partner, weight, sea, fixed_w, fixed_e, scale_w, scale_e, reach):
    channels, width, rows = own.shape
    count, levels, _ = fixed_w.shape
    size = levels // CHUNKS
    plane = jax.ShapeDtypeStruct((width, rows), F32)
    edge = jax.ShapeDtypeStruct((count, size, rows), F32)
    vmem = pl.BlockSpec(memory_space=pltpu.VMEM)
    return pl.pallas_call(
        functools.partial(surface_kernel, reach, CHUNKS),
        in_specs=[pl.BlockSpec(memory_space=pltpu.SMEM)] + [vmem] * 11,
        out_specs=[vmem] * (6 + 2 * CHUNKS),
        out_shape=[
            jax.ShapeDtypeStruct((count, width, rows), F32),
            jax.ShapeDtypeStruct((count, width, rows), F32),
            plane,
            plane,
            plane,
            plane,
        ]
        + [edge] * (2 * CHUNKS),
        scratch_shapes=[pltpu.VMEM((channels, 16 + width + 16, rows), F32)],
        compiler_params=params(24),
        cost_estimate=pl.CostEstimate(flops=4000 * width * rows, bytes_accessed=4 * 2**20, transcendentals=0),
        name="exchange_surface",
    )(place, own, peer, low, high, partner, weight, sea, fixed_w, fixed_e, scale_w, scale_e)


def transport_kernel(opening, closing, *refs):
    refs = list(refs)
    field = refs.pop(0)
    if opening:
        scale, surface = refs.pop(0), refs.pop(0)
    speed, speed_w, halo_w, halo_e, open_e, open_w, coef_n, coef_s = refs[:8]
    rest = refs[8:]
    if closing:
        out = rest[-1]
    else:
        out, edge_w, edge_e = rest
    tracers, levels, width, rows = field.shape
    row = lax.broadcasted_iota(jnp.int32, (width, rows), 0)

    for at in range(levels):
        u = speed[at]
        here = slice(at, at + 1)
        u_west = jnp.where(row == 0, jnp.broadcast_to(speed_w[here, :], (width, rows)), pltpu.roll(u, 1, 0))
        east, west = open_e[...], open_w[...]
        north, south = coef_n[...], coef_s[...]
        leave_e = east * (jnp.maximum(u, 0.0) + NU)
        enter_e = east * (NU - jnp.minimum(u, 0.0))
        enter_w = west * (jnp.maximum(u_west, 0.0) + NU)
        leave_w = west * (NU - jnp.minimum(u_west, 0.0))
        stay = ((1.0 - leave_e) - leave_w) - (north + south)
        if opening:
            scale_at = scale[at]
        for t in range(tracers):
            q = field[t, at]
            if opening:
                q = q + scale_at * surface[t]
            q_east = jnp.where(
                row == width - 1, jnp.broadcast_to(halo_e[t, here, :], (width, rows)), pltpu.roll(q, width - 1, 0)
            )
            q_west = jnp.where(row == 0, jnp.broadcast_to(halo_w[t, here, :], (width, rows)), pltpu.roll(q, 1, 0))
            q_north = pltpu.roll(q, rows - 1, 1)
            q_south = pltpu.roll(q, 1, 1)
            new = (stay * q + enter_w * q_west) + (enter_e * q_east + (north * q_north + south * q_south))
            out[t, at] = new
            if not closing:
                edge_w[t, here, :] = new[:1]
                edge_e[t, here, :] = new[width - 1 :]


def transport(chunk, step, field, extra, speed, speed_w, halo_w, halo_e, planes, result):
    opening, closing = step == 0, step == STEPS - 1
    count, rows = field.shape[0], field.shape[3]
    width = field.shape[2]
    levels = speed.shape[0]
    size = levels // CHUNKS
    blocks = size // BLOCK
    base = chunk * blocks
    own = lambda i: i + base
    place = own if opening else (lambda i: i)
    block4 = lambda at: pl.BlockSpec((count, BLOCK, width, rows), lambda i: (0, at(i), 0, 0))
    plane = pl.BlockSpec((width, rows), lambda i: (0, 0))
    edge = pl.BlockSpec((count, BLOCK, rows), lambda i: (0, i, 0))
    args = [field]
    in_specs = [block4(place)]
    if opening:
        args += list(extra)
        in_specs += [
            pl.BlockSpec((BLOCK, width, rows), lambda i: (own(i), 0, 0)),
            pl.BlockSpec((count, width, rows), lambda i: (0, 0, 0)),
        ]
    args += [speed, speed_w, halo_w, halo_e, *planes]
    in_specs += [
        pl.BlockSpec((BLOCK, width, rows), lambda i: (own(i), 0, 0)),
        pl.BlockSpec((BLOCK, rows), lambda i: (own(i), 0)),
        edge,
        edge,
        plane,
        plane,
        plane,
        plane,
    ]
    aliases = {}
    if closing:
        out_specs = block4(own)
        out_shape = jax.ShapeDtypeStruct((count, levels, width, rows), F32)
        if result is not None:
            aliases = {len(args): 0}
            args.append(result)
            in_specs.append(pl.BlockSpec(memory_space=pl.ANY))
    else:
        out_specs = [block4(lambda i: i), edge, edge]
        out_shape = [
            jax.ShapeDtypeStruct((count, size, width, rows), F32),
            jax.ShapeDtypeStruct((count, size, rows), F32),
            jax.ShapeDtypeStruct((count, size, rows), F32),
        ]
    cells = size * width * rows
    return pl.pallas_call(
        functools.partial(transport_kernel, opening, closing),
        grid=(blocks,),
        in_specs=in_specs,
        out_specs=out_specs,
        out_shape=out_shape,
        input_output_aliases=aliases,
        compiler_params=params(24),
        cost_estimate=pl.CostEstimate(
            flops=18 * count * cells, bytes_accessed=(2 * count + 1) * cells * 4, transcendentals=0
        ),
        name="transport_" + ("first" if opening else "last" if closing else "middle"),
    )(*args)


def per_device(tracers, diffusivity, conductance, face_velocity, partner, weight, sea_mask):
    tiles = lax.axis_size("tile")
    tracers, diffusivity, conductance = tracers[0], diffusivity[0], conductance[0]
    speed, partner, weight = face_velocity[0], partner[0], weight[0]
    width = tracers.shape[2]
    reach = width // 2 + 1

    def move(value, shift, swap=False):
        pairs = []
        for m in range(2):
            for t in range(tiles):
                target = (1 - m if swap else m) * tiles + (t + shift) % tiles
                pairs.append((m * tiles + t, target))
        return lax.ppermute(value, ("mp", "tile"), pairs)

    own, low, high = down_to_surface(tracers, diffusivity, conductance, sea_mask, reach)
    peer = move(own, 0, swap=True)
    low = move(low, 1, swap=True)
    high = move(high, -1, swap=True)
    speed_w = move(speed[:, width - 1], 1)
    fixed, scale, fixed_w, fixed_e, scale_w, scale_e = solve_columns(tracers, diffusivity)

    place = jnp.stack([lax.axis_index("tile") * width, tiles * width, lax.axis_index("mp")]).astype(jnp.int32)
    inflow, surface, open_e, open_w, coef_n, coef_s, *edges = exchange_surface(
        place, own, peer, low, high, partner, weight, sea_mask, fixed_w, fixed_e, scale_w, scale_e, reach
    )
    planes = (open_e, open_w, coef_n, coef_s)
    edges_w, edges_e = edges[:CHUNKS], edges[CHUNKS:]
    fields = [fixed] * CHUNKS
    result = None
    for step in range(STEPS):
        for c in range(CHUNKS):
            halo_w = move(edges_e[c], 1)
            halo_e = move(edges_w[c], -1)
            out = transport(c, step, fields[c], (scale, surface), speed, speed_w, halo_w, halo_e, planes, result)
            if step == STEPS - 1:
                result = out
            else:
                fields[c], edges_w[c], edges_e[c] = out
    return result[None], inflow[None]


def solution(mesh):
    in_specs = (
        P("mp", None, None, "tile", None),
        P("mp", None, "tile", None),
        P("mp", "tile", None),
        P("mp", None, "tile", None),
        P("mp", None, "tile", None),
        P("mp", None, "tile", None),
        P("tile", None),
    )
    out_specs = (P("mp", None, None, "tile", None), P("mp", None, "tile", None))
    return jax.shard_map(
        per_device, mesh=mesh, in_specs=in_specs, out_specs=out_specs, check_vma=False
    )
```

```python
import functools

import jax
import jax.numpy as jnp
from jax import lax
from jax.experimental import pallas as pl
from jax.experimental.pallas import tpu as pltpu
from jax.sharding import PartitionSpec as P

STEPS = 4
QUANT = 16
NU = 0.12
BLOCK = 8
CHUNKS = 4
HALO = 2
F32 = jnp.float32


def params(mib, **more):
    return pltpu.CompilerParams(vmem_limit_bytes=mib * 2**20, **more)


def lane_parts(total, size=256):
    size = min(size, total)
    return [slice(start, start + size) for start in range(0, total, size)]


def eliminate(source, coupling, state, lanes, last):
    before, ratio, parts = state
    rows = []
    for at in range(BLOCK):
        now = coupling[at, :, lanes]
        if at == BLOCK - 1:
            now = jnp.where(last, 0.0, now)
        inverse = 1.0 / (1.0 + before + now - before * ratio)
        parts = [(source[t, at, :, lanes] + before * part) * inverse for t, part in enumerate(parts)]
        ratio = now * inverse
        before = now
        rows.append((parts, ratio, inverse))
    return (before, ratio, parts), rows


def down_kernel(reach, place, source, coupling, conduct, sea, terms, first_pair, second_pair, before_s, ratio_s, part_s, slope_s):
    step = pl.program_id(0)
    last = step == pl.num_programs(0) - 1
    tracers, width, rows = part_s.shape

    @pl.when(step == 0)
    def _():
        before_s[...] = jnp.zeros_like(before_s)
        ratio_s[...] = jnp.zeros_like(ratio_s)
        part_s[...] = jnp.zeros_like(part_s)

    for lanes in lane_parts(rows):
        state = (before_s[:, lanes], ratio_s[:, lanes], [part_s[t, :, lanes] for t in range(tracers)])
        (before, ratio, parts), levels = eliminate(source, coupling, state, lanes, last)
        before_s[:, lanes] = before
        ratio_s[:, lanes] = ratio
        slope_s[:, lanes] = levels[-1][2]
        for t in range(tracers):
            part_s[t, :, lanes] = parts[t]

    def pack(east, west):
        fields = [part_s[t] for t in range(tracers)] + [slope_s[...], conduct[...]]
        for c, field in enumerate(fields):
            terms[c] = field
            east[c * reach : (c + 1) * reach, :] = field[width - reach :]
            west[c * reach : (c + 1) * reach, :] = field[:reach]
        mask = sea[...].astype(F32)
        at = len(fields) * reach
        east[at : at + HALO, :] = mask[width - HALO :]
        west[at : at + HALO, :] = mask[:HALO]

    @pl.when(last & (place[3] == 1))
    def _():
        pack(first_pair, second_pair)

    @pl.when(last & (place[3] == 0))
    def _():
        pack(second_pair, first_pair)


def down_to_surface(place, tracers, diffusivity, conductance, sea_mask, reach):
    count, levels, width, rows = tracers.shape
    packed = (count + 2) * reach + HALO
    packed = -(-packed // 8) * 8
    whole = lambda *shape: pl.BlockSpec(shape, lambda i: (0,) * len(shape))
    return pl.pallas_call(
        functools.partial(down_kernel, reach),
        grid=(levels // BLOCK,),
        in_specs=[
            pl.BlockSpec(memory_space=pltpu.SMEM),
            pl.BlockSpec((count, BLOCK, width, rows), lambda i: (0, i, 0, 0)),
            pl.BlockSpec((BLOCK, width, rows), lambda i: (i, 0, 0)),
            whole(width, rows),
            whole(width, rows),
        ],
        out_specs=[whole(count + 2, width, rows), whole(packed, rows), whole(packed, rows)],
        out_shape=[
            jax.ShapeDtypeStruct((count + 2, width, rows), F32),
            jax.ShapeDtypeStruct((packed, rows), F32),
            jax.ShapeDtypeStruct((packed, rows), F32),
        ],
        scratch_shapes=[
            pltpu.VMEM((width, rows), F32),
            pltpu.VMEM((width, rows), F32),
            pltpu.VMEM((count, width, rows), F32),
            pltpu.VMEM((width, rows), F32),
        ],
        compiler_params=params(56),
        cost_estimate=pl.CostEstimate(
            flops=20 * levels * width * rows, bytes_accessed=5 * levels * width * rows * 4, transcendentals=0
        ),
        name="down_to_surface",
    )(place, tracers, diffusivity, conductance, sea_mask)


def speed_kernel(speed, to_east, to_west):
    width = speed.shape[1]
    for at in range(speed.shape[0]):
        to_east[HALO * at : HALO * (at + 1), :] = speed[at, width - HALO :, :]
        to_west[at : at + 1, :] = speed[at, :1, :]


def speed_edges(speed):
    levels, width, rows = speed.shape
    size = 16
    return pl.pallas_call(
        speed_kernel,
        grid=(levels // size,),
        in_specs=[pl.BlockSpec((size, width, rows), lambda i: (i, 0, 0))],
        out_specs=[
            pl.BlockSpec((HALO * size, rows), lambda i: (i, 0)),
            pl.BlockSpec((size, rows), lambda i: (i, 0)),
        ],
        out_shape=[
            jax.ShapeDtypeStruct((HALO * levels, rows), F32),
            jax.ShapeDtypeStruct((levels, rows), F32),
        ],
        compiler_params=params(56),
        cost_estimate=pl.CostEstimate(flops=0, bytes_accessed=levels * width * rows * 4, transcendentals=0),
        name="speed_edges",
    )(speed)


def solve_kernel(
    blocks, source, coupling, fixed, scale, fixed_w, fixed_e, scale_w, scale_e, parts_s, ratios_s, before_s, fixed_s, scale_s
):
    step = pl.program_id(0)
    tracers, _, width, rows = source.shape

    @pl.when(step == 0)
    def _():
        before_s[...] = jnp.zeros_like(before_s)
        scale_s[...] = jnp.zeros_like(scale_s)
        fixed_s[...] = jnp.zeros_like(fixed_s)

    @pl.when(step < blocks)
    def _():
        last = step == blocks - 1
        base = step * BLOCK
        for lanes in lane_parts(rows):
            state = (before_s[:, lanes], scale_s[:, lanes], [fixed_s[t, :, lanes] for t in range(tracers)])
            (before, ratio, parts), levels = eliminate(source, coupling, state, lanes, last)
            for at, (part, ratio_at, _) in enumerate(levels):
                ratios_s[base + at, :, lanes] = ratio_at
                for t in range(tracers):
                    parts_s[t, base + at, :, lanes] = part[t]
            before_s[:, lanes] = before
            scale_s[:, lanes] = ratio
            for t in range(tracers):
                fixed_s[t, :, lanes] = parts[t]

    @pl.when(step >= blocks)
    def _():
        first = step == blocks
        base = (2 * blocks - 1 - step) * BLOCK
        for lanes in lane_parts(rows):
            scale_now = scale_s[:, lanes]
            fixed_now = [fixed_s[t, :, lanes] for t in range(tracers)]
            for at in reversed(range(BLOCK)):
                ratio = ratios_s[base + at, :, lanes]
                scale_now = ratio * scale_now
                fixed_now = [parts_s[t, base + at, :, lanes] + ratio * fixed_now[t] for t in range(tracers)]
                if at == BLOCK - 1:
                    scale_now = jnp.where(first, 1.0, scale_now)
                    fixed_now = [jnp.where(first, 0.0, f) for f in fixed_now]
                edge = slice(HALO * at, HALO * (at + 1))
                scale[at, :, lanes] = scale_now
                scale_w[edge, lanes] = scale_now[:HALO]
                scale_e[edge, lanes] = scale_now[width - HALO :]
                for t in range(tracers):
                    fixed[t, at, :, lanes] = fixed_now[t]
                    fixed_w[t, edge, lanes] = fixed_now[t][:HALO]
                    fixed_e[t, edge, lanes] = fixed_now[t][width - HALO :]
            scale_s[:, lanes] = scale_now
            for t in range(tracers):
                fixed_s[t, :, lanes] = fixed_now[t]


def solve_columns(tracers, diffusivity):
    count, levels, width, rows = tracers.shape
    blocks = levels // BLOCK
    down = lambda i: jnp.minimum(i, blocks - 1)
    up = lambda i: jnp.minimum(2 * blocks - 1 - i, blocks - 1)
    edge4 = pl.BlockSpec((count, HALO * BLOCK, rows), lambda i: (0, up(i), 0))
    edge1 = pl.BlockSpec((HALO * BLOCK, rows), lambda i: (up(i), 0))
    return pl.pallas_call(
        functools.partial(solve_kernel, blocks),
        grid=(2 * blocks,),
        in_specs=[
            pl.BlockSpec((count, BLOCK, width, rows), lambda i: (0, down(i), 0, 0)),
            pl.BlockSpec((BLOCK, width, rows), lambda i: (down(i), 0, 0)),
        ],
        out_specs=[
            pl.BlockSpec((count, BLOCK, width, rows), lambda i: (0, up(i), 0, 0)),
            pl.BlockSpec((BLOCK, width, rows), lambda i: (up(i), 0, 0)),
            edge4,
            edge4,
            edge1,
            edge1,
        ],
        out_shape=[
            jax.ShapeDtypeStruct((count, levels, width, rows), F32),
            jax.ShapeDtypeStruct((levels, width, rows), F32),
            jax.ShapeDtypeStruct((count, HALO * levels, rows), F32),
            jax.ShapeDtypeStruct((count, HALO * levels, rows), F32),
            jax.ShapeDtypeStruct((HALO * levels, rows), F32),
            jax.ShapeDtypeStruct((HALO * levels, rows), F32),
        ],
        scratch_shapes=[
            pltpu.VMEM((count, levels, width, rows), F32),
            pltpu.VMEM((levels, width, rows), F32),
            pltpu.VMEM((width, rows), F32),
            pltpu.VMEM((count, width, rows), F32),
            pltpu.VMEM((width, rows), F32),
        ],
        compiler_params=params(56),
        cost_estimate=pl.CostEstimate(
            flops=40 * levels * width * rows, bytes_accessed=10 * levels * width * rows * 4, transcendentals=0
        ),
        name="solve_columns",
    )(tracers, diffusivity)


def surface_kernel(
    reach, place, own, peer, first_pair, second_pair, partner, weight, sea,
    fixed_w, fixed_e, scale_w, scale_e,
    inflow, surface, open_e, coef_n, coef_s, coef_0, *rest,
):
    chunks = (len(rest) - 2) // 2
    send_1, send_2, wide, opened = rest[:chunks], rest[chunks : 2 * chunks], rest[-2], rest[-1]
    channels, width, rows = own.shape
    tracers = channels - 2
    first = 2 * 8
    even = place[3] == 1

    for c in range(channels):
        wide[c, first : first + width, :] = peer[c]
    opened[:width, :] = sea[...].astype(F32)
    opened[width:, :] = jnp.zeros((8, rows), F32)

    def unpack(east, west):
        for c in range(channels):
            part = slice(c * reach, (c + 1) * reach)
            wide[c, first - reach : first, :] = west[part, :]
            wide[c, first + width : first + width + reach, :] = east[part, :]
        at = slice(channels * reach, channels * reach + HALO)
        opened[width : width + HALO, :] = east[at, :]
        opened[width + 8 - HALO :, :] = west[at, :]

    @pl.when(even)
    def _():
        unpack(first_pair, second_pair)

    @pl.when(jnp.logical_not(even))
    def _():
        unpack(second_pair, first_pair)

    start, total, ocean = place[0], place[1], place[2]
    for lanes in lane_parts(rows, 128):
        position = start + lax.broadcasted_iota(jnp.int32, (width, 128), 0)
        own_slope = own[tracers, :, lanes]
        own_conduct = own[tracers + 1, :, lanes]
        flow = [jnp.zeros((width, 128), F32) for _ in range(tracers)]
        for k in range(partner.shape[0]):
            apart = partner[k, :, lanes] - position
            apart = jnp.where(apart > reach, apart - total, apart)
            apart = jnp.where(apart < -reach, apart + total, apart)
            found = [jnp.zeros((width, 128), F32) for _ in range(channels)]
            for offset in range(-reach, reach + 1):
                hit = apart == offset
                window = slice(first + offset, first + offset + width)
                found = [jnp.where(hit, wide[c, window, lanes], f) for c, f in enumerate(found)]
            series = own_conduct * found[-1] / (own_conduct + found[-1])
            factor = weight[k, :, lanes].astype(F32) * series / (1.0 + series * (own_slope + found[-2]))
            flow = [flow[t] + factor * (own[t, :, lanes] - found[t]) for t in range(tracers)]
        for t in range(tracers):
            into = flow[t] * (-1.0 / QUANT)
            inflow[t, :, lanes] = into
            surface[t, :, lanes] = own[t, :, lanes] + own_slope * into

    size = scale_w.shape[0] // chunks
    for t in range(tracers):
        top_w = jnp.concatenate([surface[t, :HALO, :]] * (8 // HALO), axis=0)
        top_e = jnp.concatenate([surface[t, width - HALO :, :]] * (8 // HALO), axis=0)
        for c in range(chunks):
            for at in range(0, size, 8):
                part, to = slice(c * size + at, c * size + at + 8), slice(at, at + 8)
                value_w = fixed_w[t, part, :] + scale_w[part, :] * top_w
                value_e = fixed_e[t, part, :] + scale_e[part, :] * top_e
                send_1[c][t, to, :] = jnp.where(even, value_e, value_w)
                send_2[c][t, to, :] = jnp.where(even, value_w, value_e)

    wide_rows = width + 8
    free = jnp.broadcast_to(ocean, (wide_rows, rows)) == 0
    here = jnp.where(free, 1.0, opened[...])
    column = lax.broadcasted_iota(jnp.int32, (wide_rows, rows), 1)
    open_e[...] = here * pltpu.roll(here, wide_rows - 1, 0)
    north = NU * (here * jnp.where(column == rows - 1, 0.0, pltpu.roll(here, rows - 1, 1)))
    south = NU * (here * jnp.where(column == 0, 0.0, pltpu.roll(here, 1, 1)))
    coef_n[...] = north
    coef_s[...] = south
    coef_0[...] = 1.0 - (north + south)


def exchange_surface(place, own, peer, first_pair, second_pair, partner, weight, sea, edges, reach):
    channels, width, rows = own.shape
    count, rims, _ = edges[0].shape
    plane = jax.ShapeDtypeStruct((width, rows), F32)
    wide_plane = jax.ShapeDtypeStruct((width + 8, rows), F32)
    edge = jax.ShapeDtypeStruct((count, rims // CHUNKS, rows), F32)
    vmem = pl.BlockSpec(memory_space=pltpu.VMEM)
    return pl.pallas_call(
        functools.partial(surface_kernel, reach),
        in_specs=[pl.BlockSpec(memory_space=pltpu.SMEM)] + [vmem] * 11,
        out_specs=[vmem] * (6 + 2 * CHUNKS),
        out_shape=[
            jax.ShapeDtypeStruct((count, width, rows), F32),
            jax.ShapeDtypeStruct((count, width, rows), F32),
            wide_plane,
            wide_plane,
            wide_plane,
            wide_plane,
        ]
        + [edge] * (2 * CHUNKS),
        scratch_shapes=[pltpu.VMEM((channels, 16 + width + 16, rows), F32), pltpu.VMEM((width + 8, rows), F32)],
        compiler_params=params(24),
        cost_estimate=pl.CostEstimate(flops=4000 * width * rows, bytes_accessed=4 * 2**20, transcendentals=0),
        name="exchange_surface",
    )(place, own, peer, first_pair, second_pair, partner, weight, sea, *edges)


def transport_kernel(opening, closing, place, field, *refs):
    refs = list(refs)
    if opening:
        scale, surface = refs.pop(0), refs.pop(0)
    speed, speed_w, speed_e, first_pair, second_pair, open_e, coef_n, coef_s, coef_0 = refs[:9]
    refs = refs[9:]
    halo_s, speed_s = refs.pop(), refs.pop()
    if closing:
        out = refs[-1]
    else:
        out, send_1, send_2 = refs
    tracers, levels, width, rows = field.shape
    wide_rows = width + 8
    even = place[3] == 1

    def unpack(east, west):
        for at in range(levels):
            part = slice(HALO * at, HALO * (at + 1))
            for t in range(tracers):
                halo_s[t, at, :HALO, :] = east[t, part, :]
                halo_s[t, at, 8 - HALO :, :] = west[t, part, :]

    for at in range(levels):
        speed_s[at, :1, :] = speed_e[at : at + 1, :]
        speed_s[at, 8 - HALO :, :] = speed_w[HALO * at : HALO * (at + 1), :]

    @pl.when(even)
    def _():
        unpack(first_pair, second_pair)

    @pl.when(jnp.logical_not(even))
    def _():
        unpack(second_pair, first_pair)

    def level(at, _):
        u = jnp.concatenate([speed[at], speed_s[at]], axis=0)
        east = open_e[...]
        leave_e = east * (jnp.maximum(u, 0.0) + NU)
        enter_e = east * (NU - jnp.minimum(u, 0.0))
        enter_w = pltpu.roll(leave_e, 1, 0)
        leave_w = pltpu.roll(enter_e, 1, 0)
        stay = (coef_0[...] - leave_e) - leave_w
        if opening:
            scale_at = scale[at]
        for t in range(tracers):
            q = field[t, at]
            if opening:
                q = q + scale_at * surface[t]
            q = jnp.concatenate([q, halo_s[t, at]], axis=0)
            for kept in (wide_rows, width):
                q_west = pltpu.roll(q, 1, 0)[:kept]
                q_east = pltpu.roll(q, wide_rows - 1, 0)[:kept]
                own = q[:kept]
                q_north = pltpu.roll(own, rows - 1, 1)
                q_south = pltpu.roll(own, 1, 1)
                q = (stay[:kept] * own + enter_w[:kept] * q_west) + (
                    enter_e[:kept] * q_east + (coef_n[:kept, :] * q_north + coef_s[:kept, :] * q_south)
                )
            out[t, at] = q
        return 0

    lax.fori_loop(0, levels, level, 0)

    if not closing:

        def pack(east, west):
            for at in range(levels):
                part = slice(HALO * at, HALO * (at + 1))
                for t in range(tracers):
                    east[t, part, :] = out[t, at, width - HALO :, :]
                    west[t, part, :] = out[t, at, :HALO, :]

        @pl.when(even)
        def _():
            pack(send_1, send_2)

        @pl.when(jnp.logical_not(even))
        def _():
            pack(send_2, send_1)


def transport(place, chunk, part, field, extra, speed, speed_w, speed_e, first_pair, second_pair, planes, result):
    opening, closing = part == 0, part == STEPS // HALO - 1
    count, _, width, rows = field.shape
    levels = speed.shape[0]
    size = levels // CHUNKS
    blocks = size // BLOCK
    base = chunk * blocks
    own = lambda i: i + base
    at_field = own if opening else (lambda i: i)
    block4 = lambda at: pl.BlockSpec((count, BLOCK, width, rows), lambda i: (0, at(i), 0, 0))
    plane = pl.BlockSpec((width + 8, rows), lambda i: (0, 0))
    edge = pl.BlockSpec((count, HALO * BLOCK, rows), lambda i: (0, i, 0))
    args = [place, field]
    in_specs = [pl.BlockSpec(memory_space=pltpu.SMEM), block4(at_field)]
    if opening:
        args += list(extra)
        in_specs += [
            pl.BlockSpec((BLOCK, width, rows), lambda i: (own(i), 0, 0)),
            pl.BlockSpec((count, width, rows), lambda i: (0, 0, 0)),
        ]
    args += [speed, speed_w, speed_e, first_pair, second_pair, *planes]
    in_specs += [
        pl.BlockSpec((BLOCK, width, rows), lambda i: (own(i), 0, 0)),
        pl.BlockSpec((HALO * BLOCK, rows), lambda i: (own(i), 0)),
        pl.BlockSpec((BLOCK, rows), lambda i: (own(i), 0)),
        edge,
        edge,
    ] + [plane] * len(planes)
    aliases = {}
    if closing:
        out_specs = block4(own)
        out_shape = jax.ShapeDtypeStruct((count, levels, width, rows), F32)
        if result is not None:
            aliases = {len(args): 0}
            args.append(result)
            in_specs.append(pl.BlockSpec(memory_space=pl.ANY))
    else:
        out_specs = [block4(lambda i: i), edge, edge]
        out_shape = [
            jax.ShapeDtypeStruct((count, size, width, rows), F32),
            jax.ShapeDtypeStruct((count, HALO * size, rows), F32),
            jax.ShapeDtypeStruct((count, HALO * size, rows), F32),
        ]
    cells = size * width * rows
    return pl.pallas_call(
        functools.partial(transport_kernel, opening, closing),
        grid=(blocks,),
        in_specs=in_specs,
        out_specs=out_specs,
        out_shape=out_shape,
        scratch_shapes=[pltpu.VMEM((BLOCK, 8, rows), F32), pltpu.VMEM((count, BLOCK, 8, rows), F32)],
        input_output_aliases=aliases,
        compiler_params=params(56),
        cost_estimate=pl.CostEstimate(
            flops=40 * count * cells, bytes_accessed=(2 * count + 1) * cells * 4, transcendentals=0
        ),
        name="transport_" + ("first" if opening else "last"),
    )(*args)


def per_device(tracers, diffusivity, conductance, face_velocity, partner, weight, sea_mask):
    tiles = lax.axis_size("tile")
    tracers, diffusivity, conductance = tracers[0], diffusivity[0], conductance[0]
    speed, partner, weight = face_velocity[0], partner[0], weight[0]
    width = tracers.shape[2]
    reach = width // 2 + 1

    def move(value, target_of, swap=False):
        pairs = []
        for m in range(2):
            for t in range(tiles):
                target = (1 - m if swap else m) * tiles + target_of(t) % tiles
                pairs.append((m * tiles + t, target))
        return lax.ppermute(value, ("mp", "tile"), pairs)

    one = lambda t: t + 1 - 2 * (t % 2)
    two = lambda t: t - 1 + 2 * (t % 2)

    tile = lax.axis_index("tile")
    place = jnp.stack([tile * width, tiles * width, lax.axis_index("mp"), 1 - tile % 2]).astype(jnp.int32)

    own, terms_1, terms_2 = down_to_surface(place, tracers, diffusivity, conductance, sea_mask, reach)
    peer = move(own, lambda t: t, swap=True)
    terms_1 = move(terms_1, one, swap=True)
    terms_2 = move(terms_2, two, swap=True)
    to_east, to_west = speed_edges(speed)
    speed_w = move(to_east, lambda t: t + 1)
    speed_e = move(to_west, lambda t: t - 1)
    fixed, scale, *edges = solve_columns(tracers, diffusivity)

    inflow, surface, *rest = exchange_surface(
        place, own, peer, terms_1, terms_2, partner, weight, sea_mask, edges, reach
    )
    planes, sends = rest[:4], rest[4:]
    sends_1, sends_2 = sends[:CHUNKS], sends[CHUNKS:]
    fields = [fixed] * CHUNKS
    result = None
    for part in range(STEPS // HALO):
        for c in range(CHUNKS):
            first_pair = move(sends_1[c], one)
            second_pair = move(sends_2[c], two)
            out = transport(
                place, c, part, fields[c], (scale, surface), speed, speed_w, speed_e, first_pair, second_pair, planes, result
            )
            if part == STEPS // HALO - 1:
                result = out
            else:
                fields[c], sends_1[c], sends_2[c] = out
    return result[None], inflow[None]


def solution(mesh):
    in_specs = (
        P("mp", None, None, "tile", None),
        P("mp", None, "tile", None),
        P("mp", "tile", None),
        P("mp", None, "tile", None),
        P("mp", None, "tile", None),
        P("mp", None, "tile", None),
        P("tile", None),
    )
    out_specs = (P("mp", None, None, "tile", None), P("mp", None, "tile", None))
    return jax.shard_map(
        per_device, mesh=mesh, in_specs=in_specs, out_specs=out_specs, check_vma=False
    )
```

```python
import functools

import jax
import jax.numpy as jnp
from jax import lax
from jax.experimental import pallas as pl
from jax.experimental.pallas import tpu as pltpu
from jax.sharding import PartitionSpec as P

STEPS = 4
QUANT = 16
NU = 0.12
ROWS8 = 8
CHUNKS = 4
HALO = 2
F32 = jnp.float32
VMEM = pl.BlockSpec(memory_space=pltpu.VMEM)
HBM = pl.BlockSpec(memory_space=pltpu.HBM)


def shape_of(*shape):
    return jax.ShapeDtypeStruct(shape, F32)


def params(mib):
    return pltpu.CompilerParams(vmem_limit_bytes=mib * 2**20)


def is_even():
    return lax.rem(lax.axis_index("tile"), 2) == 0


def either(even, call, first, second):
    @pl.when(even)
    def _():
        call(first, second)

    @pl.when(jnp.logical_not(even))
    def _():
        call(second, first)


def lane_parts(total, size=256):
    size = min(size, total)
    return [slice(start, start + size) for start in range(0, total, size)]


def down_kernel(reach, source, coupling, conduct, sea, parts, ratios, terms, mask, first_pair, second_pair, sea_s, sems):
    tracers, levels, width, rows = source.shape
    blocks = levels // ROWS8
    small = [
        pltpu.make_async_copy(conduct, terms.at[tracers + 1], sems.at[2, 0]),
        pltpu.make_async_copy(sea, sea_s, sems.at[2, 1]),
    ]
    copies = []
    for b in range(blocks):
        part = pl.ds(b * ROWS8, ROWS8)
        pair = [pltpu.make_async_copy(source.at[:, part], parts.at[:, part], sems.at[0, b])]
        part = pl.ds(b * ROWS8, min(ROWS8, levels - 1 - b * ROWS8))
        pair.append(pltpu.make_async_copy(coupling.at[part], ratios.at[part], sems.at[1, b]))
        copies.append(pair)
    for pair in copies:
        for copy in pair:
            copy.start()
    for copy in small:
        copy.start()

    lanes_all = lane_parts(rows)
    zero = jnp.zeros((width, rows // len(lanes_all)), F32)
    states = [(zero, zero, [zero] * tracers, zero)] * len(lanes_all)
    for b in range(blocks):
        for copy in copies[b]:
            copy.wait()
        for p, lanes in enumerate(lanes_all):
            before, ratio, part, inverse = states[p]
            for l in range(b * ROWS8, (b + 1) * ROWS8):
                now = ratios[l, :, lanes] if l < levels - 1 else zero
                inverse = 1.0 / (1.0 + before + now - before * ratio)
                part = [(parts[t, l, :, lanes] + before * part[t]) * inverse for t in range(tracers)]
                ratio = now * inverse
                before = now
                ratios[l, :, lanes] = ratio
                for t in range(tracers):
                    parts[t, l, :, lanes] = part[t]
            states[p] = (before, ratio, part, inverse)
    for lanes, state in zip(lanes_all, states):
        for t in range(tracers):
            terms[t, :, lanes] = state[2][t]
        terms[tracers, :, lanes] = state[3]
    for copy in small:
        copy.wait()
    mask[...] = sea_s[...].astype(F32)

    def pack(east, west):
        for c in range(tracers + 2):
            east[c * reach : (c + 1) * reach, :] = terms[c, width - reach :, :]
            west[c * reach : (c + 1) * reach, :] = terms[c, :reach, :]
        at = (tracers + 2) * reach
        east[at : at + HALO, :] = mask[width - HALO :, :]
        west[at : at + HALO, :] = mask[:HALO, :]

    either(is_even(), pack, first_pair, second_pair)


def down_to_surface(tracers, diffusivity, conductance, sea_mask, reach):
    count, levels, width, rows = tracers.shape
    packed = (count + 2) * reach + HALO
    packed = -(-packed // 8) * 8
    return pl.pallas_call(
        functools.partial(down_kernel, reach),
        in_specs=[HBM] * 4,
        out_specs=[VMEM] * 6,
        out_shape=[
            shape_of(count, levels, width, rows),
            shape_of(levels, width, rows),
            shape_of(count + 2, width, rows),
            shape_of(width, rows),
            shape_of(packed, rows),
            shape_of(packed, rows),
        ],
        scratch_shapes=[pltpu.VMEM((width, rows), jnp.int32), pltpu.SemaphoreType.DMA((3, levels // ROWS8))],
        compiler_params=params(41),
        cost_estimate=pl.CostEstimate(
            flops=20 * levels * width * rows, bytes_accessed=10 * levels * width * rows * 4, transcendentals=0
        ),
        name="down_to_surface",
    )(tracers, diffusivity, conductance, sea_mask)


def up_kernel(rim, parts, ratios, speed_in, fixed, scale, speed, rims, rim_scale, to_east, to_west, sem):
    tracers, levels, width, rows = parts.shape
    copy = pltpu.make_async_copy(speed_in, speed, sem)
    copy.start()
    for lanes in lane_parts(rows):
        lane_count = lanes.stop - lanes.start
        scale_now = jnp.ones((width, lane_count), F32)
        fixed_now = [jnp.zeros((width, lane_count), F32)] * tracers
        for l in reversed(range(levels)):
            if l < levels - 1:
                ratio = ratios[l, :, lanes]
                scale_now = ratio * scale_now
                fixed_now = [parts[t, l, :, lanes] + ratio * fixed_now[t] for t in range(tracers)]
            scale[l, :, lanes] = scale_now
            for t in range(tracers):
                fixed[t, l, :, lanes] = fixed_now[t]
            for c, x in enumerate(rim):
                rim_scale[c, l : l + 1, lanes] = scale_now[x : x + 1]
                for t in range(tracers):
                    rims[t, c, l : l + 1, lanes] = fixed_now[t][x : x + 1]
    copy.wait()
    for l in range(levels):
        to_west[l : l + 1, :] = speed[l, :1, :]
        for c in range(HALO):
            x = width - HALO + c
            to_east[c, l : l + 1, :] = speed[l, x : x + 1, :]


def up_from_surface(parts, ratios, speed, rim):
    count, levels, width, rows = parts.shape
    return pl.pallas_call(
        functools.partial(up_kernel, rim),
        in_specs=[VMEM, VMEM, HBM],
        out_specs=[VMEM] * 7,
        out_shape=[
            shape_of(count, levels, width, rows),
            shape_of(levels, width, rows),
            shape_of(levels, width, rows),
            shape_of(count, len(rim), levels, rows),
            shape_of(len(rim), levels, rows),
            shape_of(HALO, levels, rows),
            shape_of(levels, rows),
        ],
        input_output_aliases={0: 0, 1: 1},
        scratch_shapes=[pltpu.SemaphoreType.DMA],
        compiler_params=params(30),
        cost_estimate=pl.CostEstimate(
            flops=10 * levels * width * rows, bytes_accessed=10 * levels * width * rows * 4, transcendentals=0
        ),
        name="up_from_surface",
    )(parts, ratios, speed)


def surface_kernel(
    reach, own, peer, first_pair, second_pair, partner, weight, mask, rims, rim_scale,
    inflow, surface, open_e, coef_n, coef_s, coef_0, *rest,
):
    chunks = (len(rest) - 2) // 2
    send_1, send_2, wide, opened = rest[:chunks], rest[chunks : 2 * chunks], rest[-2], rest[-1]
    channels, width, rows = own.shape
    tracers = channels - 2
    first = 2 * 8
    even = is_even()

    for c in range(channels):
        wide[c, first : first + width, :] = peer[c]
    opened[:width, :] = mask[...]
    opened[width:, :] = jnp.zeros((ROWS8, rows), F32)

    def unpack(east, west):
        for c in range(channels):
            part = slice(c * reach, (c + 1) * reach)
            wide[c, first - reach : first, :] = west[part, :]
            wide[c, first + width : first + width + reach, :] = east[part, :]
        at = slice(channels * reach, channels * reach + HALO)
        opened[width : width + HALO, :] = east[at, :]
        opened[width + ROWS8 - HALO :, :] = west[at, :]

    either(even, unpack, first_pair, second_pair)

    start = lax.axis_index("tile") * width
    total = lax.axis_size("tile") * width
    for lanes in lane_parts(rows, 128):
        position = start + lax.broadcasted_iota(jnp.int32, (width, 128), 0)
        own_slope = own[tracers, :, lanes]
        own_conduct = own[tracers + 1, :, lanes]
        flow = [jnp.zeros((width, 128), F32) for _ in range(tracers)]
        for k in range(partner.shape[0]):
            apart = partner[k, :, lanes] - position
            apart = jnp.where(apart > reach, apart - total, apart)
            apart = jnp.where(apart < -reach, apart + total, apart)
            found = [jnp.zeros((width, 128), F32) for _ in range(channels)]
            for offset in range(-reach, reach + 1):
                hit = apart == offset
                window = slice(first + offset, first + offset + width)
                found = [jnp.where(hit, wide[c, window, lanes], f) for c, f in enumerate(found)]
            series = own_conduct * found[-1] / (own_conduct + found[-1])
            factor = weight[k, :, lanes].astype(F32) * series / (1.0 + series * (own_slope + found[-2]))
            flow = [flow[t] + factor * (own[t, :, lanes] - found[t]) for t in range(tracers)]
        for t in range(tracers):
            into = flow[t] * (-1.0 / QUANT)
            inflow[t, :, lanes] = into
            surface[t, :, lanes] = own[t, :, lanes] + own_slope * into

    size = rim_scale.shape[1] // chunks
    for c in range(chunks):
        part = slice(c * size, (c + 1) * size)
        for t in range(tracers):
            for x in range(HALO):
                e = width - HALO + x
                west = rims[t, x, part, :] + rim_scale[x, part, :] * surface[t, x : x + 1, :]
                east = rims[t, HALO + x, part, :] + rim_scale[HALO + x, part, :] * surface[t, e : e + 1, :]
                send_1[c][t, x] = jnp.where(even, east, west)
                send_2[c][t, x] = jnp.where(even, west, east)

    wide_rows = width + ROWS8
    free = jnp.broadcast_to(lax.axis_index("mp"), (wide_rows, rows)) == 0
    here = jnp.where(free, 1.0, opened[...])
    column = lax.broadcasted_iota(jnp.int32, (wide_rows, rows), 1)
    open_e[...] = here * pltpu.roll(here, wide_rows - 1, 0)
    north = NU * (here * jnp.where(column == rows - 1, 0.0, pltpu.roll(here, rows - 1, 1)))
    south = NU * (here * jnp.where(column == 0, 0.0, pltpu.roll(here, 1, 1)))
    coef_n[...] = north
    coef_s[...] = south
    coef_0[...] = 1.0 - (north + south)


def exchange_surface(own, peer, first_pair, second_pair, partner, weight, mask, rims, rim_scale, reach):
    channels, width, rows = own.shape
    count, _, levels, _ = rims.shape
    plane = shape_of(width + ROWS8, rows)
    edge = shape_of(count, HALO, levels // CHUNKS, rows)
    return pl.pallas_call(
        functools.partial(surface_kernel, reach),
        in_specs=[VMEM] * 9,
        out_specs=[VMEM] * (6 + 2 * CHUNKS),
        out_shape=[shape_of(count, width, rows)] * 2 + [plane] * 4 + [edge] * (2 * CHUNKS),
        scratch_shapes=[pltpu.VMEM((channels, 16 + width + 16, rows), F32), pltpu.VMEM((width + ROWS8, rows), F32)],
        compiler_params=params(20),
        cost_estimate=pl.CostEstimate(flops=4000 * width * rows, bytes_accessed=4 * 2**20, transcendentals=0),
        name="exchange_surface",
    )(own, peer, first_pair, second_pair, partner, weight, mask, rims, rim_scale)


def leaving(u, opening):
    return opening * (jnp.maximum(u, 0.0) + NU), opening * (NU - jnp.minimum(u, 0.0))


def stencil(q, q_west, q_east, coefs):
    stay, enter_w, enter_e, north, south = coefs
    rows = q.shape[-1]
    q_north, q_south = pltpu.roll(q, rows - 1, 1), pltpu.roll(q, 1, 1)
    return (stay * q + enter_w * q_west) + (enter_e * q_east + (north * q_north + south * q_south))


def from_west(tiles, row):
    at = lax.broadcasted_iota(jnp.int32, tiles[0].shape, 0) == 0
    rolled = [pltpu.roll(tile, 1, 0) for tile in tiles]
    before = [jnp.broadcast_to(row, tiles[0].shape)] + rolled[:-1]
    return [jnp.where(at, b, r) for b, r in zip(before, rolled)]


def from_east(tiles, row):
    at = lax.broadcasted_iota(jnp.int32, tiles[0].shape, 0) == ROWS8 - 1
    rolled = [pltpu.roll(tile, ROWS8 - 1, 0) for tile in tiles]
    after = rolled[1:] + [jnp.broadcast_to(row, tiles[0].shape)]
    return [jnp.where(at, a, r) for a, r in zip(after, rolled)]


def transport_kernel(
    chunk, size, closing, scale, surface, speed, speed_w, speed_e, speed_own,
    own_1, own_2, halo_1, halo_2, open_e, coef_n, coef_s, coef_0, field, *refs,
):
    halo_w, halo_e, coef_w = refs[-3:]
    if closing:
        out, stage, sems = refs[-6], refs[-5], refs[-4]
    else:
        out, send_1, send_2, rim_w, rim_e = refs[-8:-3]
    tracers, levels, width, rows = field.shape
    blocks = size // ROWS8
    even = is_even()

    part = slice(chunk * size, (chunk + 1) * size)
    last = width + ROWS8 - 1
    spread = lambda ref, x: jnp.broadcast_to(ref[x : x + 1, :], (size, rows))
    split = lambda value: value.reshape(blocks, ROWS8, rows)

    leave_e, enter_e = leaving(speed_w[1, part, :], spread(open_e, last))
    enter_w, leave_w = leaving(speed_w[0, part, :], spread(open_e, last - 1))
    stay = (spread(coef_0, last) - leave_e) - leave_w
    coef_w[0] = split(leave_e)
    coef_w[1] = split(enter_e)
    coefs_w = (stay, enter_w, enter_e, spread(coef_n, last), spread(coef_s, last))
    leave_e, enter_e = leaving(speed_e[part, :], spread(open_e, width))
    enter_w, leave_w = leaving(speed_own[1, part, :], spread(open_e, width - 1))
    stay = (spread(coef_0, width) - leave_e) - leave_w
    coefs_e = (stay, enter_w, enter_e, spread(coef_n, width), spread(coef_s, width))
    for t in range(tracers):
        own_w = jnp.where(even, own_2[t, 0], own_1[t, 0])
        own_e = jnp.where(even, own_1[t, 1], own_2[t, 1])
        far_w, near_w = [jnp.where(even, halo_2[t, x], halo_1[t, x]) for x in range(HALO)]
        near_e, far_e = [jnp.where(even, halo_1[t, x], halo_2[t, x]) for x in range(HALO)]
        halo_w[0, t] = split(near_w)
        halo_e[0, t] = split(near_e)
        halo_w[1, t] = split(stencil(near_w, far_w, own_w, coefs_w))
        halo_e[1, t] = split(stencil(near_e, own_e, far_e, coefs_e))

    def block(b, _):
        for at in range(ROWS8):
            l = chunk * size + b * ROWS8 + at
            here = slice(at, at + 1)
            tiles = [slice(x, x + ROWS8) for x in range(0, width, ROWS8)]
            pairs = [leaving(speed[l, x, :], open_e[x, :]) for x in tiles]
            leave_e, enter_e = [p[0] for p in pairs], [p[1] for p in pairs]
            enter_w = from_west(leave_e, coef_w[0, b, here, :])
            leave_w = from_west(enter_e, coef_w[1, b, here, :])
            stay = [(coef_0[x, :] - e) - w for x, e, w in zip(tiles, leave_e, leave_w)]
            coefs = [
                (s, w, e, coef_n[x, :], coef_s[x, :]) for x, s, w, e in zip(tiles, stay, enter_w, enter_e)
            ]
            for t in range(tracers):
                q = [field[t, l, x, :] for x in tiles]
                if not closing:
                    q = [v + scale[l, x, :] * surface[t, x, :] for x, v in zip(tiles, q)]
                for step in range(HALO):
                    q_west = from_west(q, halo_w[step, t, b, here, :])
                    q_east = from_east(q, halo_e[step, t, b, here, :])
                    q = [stencil(*args) for args in zip(q, q_west, q_east, coefs)]
                for x, v in zip(tiles, q):
                    if closing:
                        stage[t, b * ROWS8 + at, x, :] = v
                    else:
                        out[t, l, x, :] = v
                if not closing:
                    for x in range(HALO):
                        e = ROWS8 - HALO + x
                        rim_w[t, x, b, here, :] = q[0][x : x + 1]
                        rim_e[t, x, b, here, :] = q[-1][e : e + 1]
        return 0

    if closing:
        copies = []
        for b in range(blocks):
            block(b, 0)
            to = pl.ds(chunk * size + b * ROWS8, ROWS8)
            copy = pltpu.make_async_copy(stage.at[:, pl.ds(b * ROWS8, ROWS8)], out.at[:, to], sems.at[b])
            copy.start()
            copies.append(copy)
        for copy in copies:
            copy.wait()
    else:
        lax.fori_loop(0, blocks, block, 0)
        for t in range(tracers):
            for x in range(HALO):
                west, east = rim_w[t, x].reshape(size, rows), rim_e[t, x].reshape(size, rows)
                send_1[t, x] = jnp.where(even, east, west)
                send_2[t, x] = jnp.where(even, west, east)


def transport(chunk, closing, field, scale, surface, speeds, own, halos, planes, result):
    count, levels, width, rows = field.shape
    size = levels // CHUNKS
    blocks = size // ROWS8
    args = [scale, surface, *speeds, *own, *halos, *planes, field]
    in_specs = [VMEM] * len(args)
    halo = pltpu.VMEM((HALO, count, blocks, ROWS8, rows), F32)
    scratch = [halo, halo, pltpu.VMEM((2, blocks, ROWS8, rows), F32)]
    edge = shape_of(count, HALO, size, rows)
    if closing:
        out_shape = [shape_of(count, levels, width, rows)]
        out_specs = [HBM]
        aliases = {}
        if result is not None:
            aliases = {len(args): 0}
            args.append(result)
            in_specs.append(HBM)
        scratch = [pltpu.VMEM((count, size, width, rows), F32), pltpu.SemaphoreType.DMA((blocks,))] + scratch
    else:
        out_shape = [shape_of(count, levels, width, rows), edge, edge]
        out_specs = [VMEM] * 3
        aliases = {len(args) - 1: 0}
        rim = pltpu.VMEM((count, HALO, blocks, ROWS8, rows), F32)
        scratch = [rim, rim] + scratch
    cells = size * width * rows
    return pl.pallas_call(
        functools.partial(transport_kernel, chunk, size, closing),
        in_specs=in_specs,
        out_specs=out_specs,
        out_shape=out_shape,
        scratch_shapes=scratch,
        input_output_aliases=aliases,
        compiler_params=params(20),
        cost_estimate=pl.CostEstimate(
            flops=36 * count * cells, bytes_accessed=(2 * count + 1) * cells * 4, transcendentals=0
        ),
        name="transport_" + ("last" if closing else "first"),
    )(*args)


def per_device(tracers, diffusivity, conductance, face_velocity, partner, weight, sea_mask):
    tiles = lax.axis_size("tile")
    tracers, diffusivity, conductance = tracers[0], diffusivity[0], conductance[0]
    speed, partner, weight = face_velocity[0], partner[0], weight[0]
    width = tracers.shape[2]
    reach = width // 2 + 1

    def move(value, target_of, swap=False):
        pairs = []
        for m in range(2):
            for t in range(tiles):
                target = (1 - m if swap else m) * tiles + target_of(t) % tiles
                pairs.append((m * tiles + t, target))
        return lax.ppermute(value, ("mp", "tile"), pairs)

    one = lambda t: t + 1 - 2 * (t % 2)
    two = lambda t: t - 1 + 2 * (t % 2)

    parts, ratios, own, mask, terms_1, terms_2 = down_to_surface(tracers, diffusivity, conductance, sea_mask, reach)
    terms_1 = move(terms_1, one, swap=True)
    terms_2 = move(terms_2, two, swap=True)
    peer = move(own, lambda t: t, swap=True)
    rim = tuple(range(HALO)) + tuple(range(width - HALO, width))
    field, scale, speed, rims, rim_scale, speed_own, to_west = up_from_surface(parts, ratios, speed, rim)
    speed_w = move(speed_own, lambda t: t + 1)
    speed_e = move(to_west, lambda t: t - 1)
    speeds = (speed, speed_w, speed_e, speed_own)

    inflow, surface, *rest = exchange_surface(own, peer, terms_1, terms_2, partner, weight, mask, rims, rim_scale, reach)
    planes, sends = rest[:4], rest[4:]
    sends = list(zip(sends[:CHUNKS], sends[CHUNKS:]))
    result = None
    for closing in (False, True):
        for c in range(CHUNKS):
            halos = (move(sends[c][0], one), move(sends[c][1], two))
            out = transport(c, closing, field, scale, surface, speeds, sends[c], halos, planes, result)
            if closing:
                result = out[0]
            else:
                field, sends[c] = out[0], out[1:]
    return result[None], inflow[None]


def solution(mesh):
    in_specs = (
        P("mp", None, None, "tile", None),
        P("mp", None, "tile", None),
        P("mp", "tile", None),
        P("mp", None, "tile", None),
        P("mp", None, "tile", None),
        P("mp", None, "tile", None),
        P("tile", None),
    )
    out_specs = (P("mp", None, None, "tile", None), P("mp", None, "tile", None))
    return jax.shard_map(
        per_device, mesh=mesh, in_specs=in_specs, out_specs=out_specs, check_vma=False
    )
```

```python
import functools

import jax
import jax.numpy as jnp
from jax import lax
from jax.experimental import pallas as pl
from jax.experimental.pallas import tpu as pltpu
from jax.sharding import PartitionSpec as P

STEPS = 4
QUANT = 16
NU = 0.12
ROWS8 = 8
CHUNKS = 4
HALO = 2
F32 = jnp.float32
VMEM = pl.BlockSpec(memory_space=pltpu.VMEM)
HBM = pl.BlockSpec(memory_space=pltpu.HBM)


def shape_of(*shape):
    return jax.ShapeDtypeStruct(shape, F32)


def params(mib):
    return pltpu.CompilerParams(vmem_limit_bytes=mib * 2**20)


def is_even():
    return lax.rem(lax.axis_index("tile"), 2) == 0


def either(even, call, first, second):
    @pl.when(even)
    def _():
        call(first, second)

    @pl.when(jnp.logical_not(even))
    def _():
        call(second, first)


def lane_parts(total, size=256):
    size = min(size, total)
    return [slice(start, start + size) for start in range(0, total, size)]


def down_kernel(reach, source, coupling, conduct, sea, parts, ratios, terms, mask, first_pair, second_pair, sea_s, sems):
    tracers, levels, width, rows = source.shape
    blocks = levels // ROWS8
    small = [
        pltpu.make_async_copy(conduct, terms.at[tracers + 1], sems.at[2, 0]),
        pltpu.make_async_copy(sea, sea_s, sems.at[2, 1]),
    ]
    copies = []
    for b in range(blocks):
        part = pl.ds(b * ROWS8, ROWS8)
        pair = [pltpu.make_async_copy(source.at[:, part], parts.at[:, part], sems.at[0, b])]
        part = pl.ds(b * ROWS8, min(ROWS8, levels - 1 - b * ROWS8))
        pair.append(pltpu.make_async_copy(coupling.at[part], ratios.at[part], sems.at[1, b]))
        copies.append(pair)
    for pair in copies:
        for copy in pair:
            copy.start()
    for copy in small:
        copy.start()

    lanes_all = lane_parts(rows)
    zero = jnp.zeros((width, rows // len(lanes_all)), F32)
    states = [(zero, zero, [zero] * tracers, zero)] * len(lanes_all)
    for b in range(blocks):
        for copy in copies[b]:
            copy.wait()
        for p, lanes in enumerate(lanes_all):
            before, ratio, part, inverse = states[p]
            for l in range(b * ROWS8, (b + 1) * ROWS8):
                now = ratios[l, :, lanes] if l < levels - 1 else zero
                inverse = 1.0 / (1.0 + before + now - before * ratio)
                part = [(parts[t, l, :, lanes] + before * part[t]) * inverse for t in range(tracers)]
                ratio = now * inverse
                before = now
                ratios[l, :, lanes] = ratio
                for t in range(tracers):
                    parts[t, l, :, lanes] = part[t]
            states[p] = (before, ratio, part, inverse)
    for lanes, state in zip(lanes_all, states):
        for t in range(tracers):
            terms[t, :, lanes] = state[2][t]
        terms[tracers, :, lanes] = state[3]
    for copy in small:
        copy.wait()
    mask[...] = sea_s[...].astype(F32)

    def pack(east, west):
        for c in range(tracers + 2):
            east[c * reach : (c + 1) * reach, :] = terms[c, width - reach :, :]
            west[c * reach : (c + 1) * reach, :] = terms[c, :reach, :]
        at = (tracers + 2) * reach
        east[at : at + HALO, :] = mask[width - HALO :, :]
        west[at : at + HALO, :] = mask[:HALO, :]

    either(is_even(), pack, first_pair, second_pair)


def down_to_surface(tracers, diffusivity, conductance, sea_mask, reach):
    count, levels, width, rows = tracers.shape
    packed = (count + 2) * reach + HALO
    packed = -(-packed // 8) * 8
    return pl.pallas_call(
        functools.partial(down_kernel, reach),
        in_specs=[HBM] * 4,
        out_specs=[VMEM] * 6,
        out_shape=[
            shape_of(count, levels, width, rows),
            shape_of(levels, width, rows),
            shape_of(count + 2, width, rows),
            shape_of(width, rows),
            shape_of(packed, rows),
            shape_of(packed, rows),
        ],
        scratch_shapes=[pltpu.VMEM((width, rows), jnp.int32), pltpu.SemaphoreType.DMA((3, levels // ROWS8))],
        compiler_params=params(41),
        cost_estimate=pl.CostEstimate(
            flops=20 * levels * width * rows, bytes_accessed=10 * levels * width * rows * 4, transcendentals=0
        ),
        name="down_to_surface",
    )(tracers, diffusivity, conductance, sea_mask)


def up_kernel(rim, parts, ratios, speed_in, fixed, scale, speed, rims, rim_scale, to_east, to_west, sem):
    tracers, levels, width, rows = parts.shape
    copy = pltpu.make_async_copy(speed_in, speed, sem)
    copy.start()
    for lanes in lane_parts(rows):
        lane_count = lanes.stop - lanes.start
        scale_now = jnp.ones((width, lane_count), F32)
        fixed_now = [jnp.zeros((width, lane_count), F32)] * tracers
        for l in reversed(range(levels)):
            if l < levels - 1:
                ratio = ratios[l, :, lanes]
                scale_now = ratio * scale_now
                fixed_now = [parts[t, l, :, lanes] + ratio * fixed_now[t] for t in range(tracers)]
            scale[l, :, lanes] = scale_now
            for t in range(tracers):
                fixed[t, l, :, lanes] = fixed_now[t]
            for c, x in enumerate(rim):
                rim_scale[c, l : l + 1, lanes] = scale_now[x : x + 1]
                for t in range(tracers):
                    rims[t, c, l : l + 1, lanes] = fixed_now[t][x : x + 1]
    copy.wait()
    for l in range(levels):
        to_west[l : l + 1, :] = speed[l, :1, :]
        for c in range(HALO):
            x = width - HALO + c
            to_east[c, l : l + 1, :] = speed[l, x : x + 1, :]


def up_from_surface(parts, ratios, speed, rim):
    count, levels, width, rows = parts.shape
    return pl.pallas_call(
        functools.partial(up_kernel, rim),
        in_specs=[VMEM, VMEM, HBM],
        out_specs=[VMEM] * 7,
        out_shape=[
            shape_of(count, levels, width, rows),
            shape_of(levels, width, rows),
            shape_of(levels, width, rows),
            shape_of(count, len(rim), levels, rows),
            shape_of(len(rim), levels, rows),
            shape_of(HALO, levels, rows),
            shape_of(levels, rows),
        ],
        input_output_aliases={0: 0, 1: 1},
        scratch_shapes=[pltpu.SemaphoreType.DMA],
        compiler_params=params(30),
        cost_estimate=pl.CostEstimate(
            flops=10 * levels * width * rows, bytes_accessed=10 * levels * width * rows * 4, transcendentals=0
        ),
        name="up_from_surface",
    )(parts, ratios, speed)


def surface_kernel(
    reach, own, peer, first_pair, second_pair, partner, weight, mask, rims, rim_scale,
    inflow, surface, open_e, coef_n, *rest,
):
    chunks = (len(rest) - 2) // 2
    send_1, send_2, wide, opened = rest[:chunks], rest[chunks : 2 * chunks], rest[-2], rest[-1]
    channels, width, rows = own.shape
    tracers = channels - 2
    first = 2 * 8
    even = is_even()

    for c in range(channels):
        wide[c, first : first + width, :] = peer[c]
    opened[:width, :] = mask[...]
    opened[width:, :] = jnp.zeros((ROWS8, rows), F32)

    def unpack(east, west):
        for c in range(channels):
            part = slice(c * reach, (c + 1) * reach)
            wide[c, first - reach : first, :] = west[part, :]
            wide[c, first + width : first + width + reach, :] = east[part, :]
        at = slice(channels * reach, channels * reach + HALO)
        opened[width : width + HALO, :] = east[at, :]
        opened[width + ROWS8 - HALO :, :] = west[at, :]

    either(even, unpack, first_pair, second_pair)

    start = lax.axis_index("tile") * width
    total = lax.axis_size("tile") * width
    for lanes in lane_parts(rows, 128):
        position = start + lax.broadcasted_iota(jnp.int32, (width, 128), 0)
        own_slope = own[tracers, :, lanes]
        own_conduct = own[tracers + 1, :, lanes]
        flow = [jnp.zeros((width, 128), F32) for _ in range(tracers)]
        for k in range(partner.shape[0]):
            apart = partner[k, :, lanes] - position
            apart = jnp.where(apart > reach, apart - total, apart)
            apart = jnp.where(apart < -reach, apart + total, apart)
            found = [jnp.zeros((width, 128), F32) for _ in range(channels)]
            for offset in range(-reach, reach + 1):
                hit = apart == offset
                window = slice(first + offset, first + offset + width)
                found = [jnp.where(hit, wide[c, window, lanes], f) for c, f in enumerate(found)]
            series = own_conduct * found[-1] / (own_conduct + found[-1])
            factor = weight[k, :, lanes].astype(F32) * series / (1.0 + series * (own_slope + found[-2]))
            flow = [flow[t] + factor * (own[t, :, lanes] - found[t]) for t in range(tracers)]
        for t in range(tracers):
            into = flow[t] * (-1.0 / QUANT)
            inflow[t, :, lanes] = into
            surface[t, :, lanes] = own[t, :, lanes] + own_slope * into

    size = rim_scale.shape[1] // chunks
    for c in range(chunks):
        part = slice(c * size, (c + 1) * size)
        for t in range(tracers):
            for x in range(HALO):
                e = width - HALO + x
                west = rims[t, x, part, :] + rim_scale[x, part, :] * surface[t, x : x + 1, :]
                east = rims[t, HALO + x, part, :] + rim_scale[HALO + x, part, :] * surface[t, e : e + 1, :]
                send_1[c][t, x] = jnp.where(even, east, west)
                send_2[c][t, x] = jnp.where(even, west, east)

    wide_rows = width + ROWS8
    free = jnp.broadcast_to(lax.axis_index("mp"), (wide_rows, rows)) == 0
    here = jnp.where(free, 1.0, opened[...])
    column = lax.broadcasted_iota(jnp.int32, (wide_rows, rows), 1)
    open_e[...] = here * pltpu.roll(here, wide_rows - 1, 0)
    coef_n[...] = NU * (here * jnp.where(column == rows - 1, 0.0, pltpu.roll(here, rows - 1, 1)))


def exchange_surface(own, peer, first_pair, second_pair, partner, weight, mask, rims, rim_scale, reach):
    channels, width, rows = own.shape
    count, _, levels, _ = rims.shape
    plane = shape_of(width + ROWS8, rows)
    edge = shape_of(count, HALO, levels // CHUNKS, rows)
    return pl.pallas_call(
        functools.partial(surface_kernel, reach),
        in_specs=[VMEM] * 9,
        out_specs=[VMEM] * (4 + 2 * CHUNKS),
        out_shape=[shape_of(count, width, rows)] * 2 + [plane] * 2 + [edge] * (2 * CHUNKS),
        scratch_shapes=[pltpu.VMEM((channels, 16 + width + 16, rows), F32), pltpu.VMEM((width + ROWS8, rows), F32)],
        compiler_params=params(20),
        cost_estimate=pl.CostEstimate(flops=4000 * width * rows, bytes_accessed=4 * 2**20, transcendentals=0),
        name="exchange_surface",
    )(own, peer, first_pair, second_pair, partner, weight, mask, rims, rim_scale)


def stepped(q, a, b, north, first, last):
    rows = q[first].shape[-1]
    flux_w = a(first - 1) * q[first - 1] + b(first - 1) * q[first]
    new = {}
    for x in range(first, last):
        flux_e = a(x) * q[x] + b(x) * q[x + 1]
        flux_n = north(x) * (pltpu.roll(q[x], rows - 1, 1) - q[x])
        new[x] = (q[x] - (flux_e - flux_w)) + (flux_n - pltpu.roll(flux_n, 1, 1))
        flux_w = flux_e
    return new


def two_steps(q, a, b, north, width):
    for step in range(HALO):
        rim = HALO - 1 - step
        q = stepped(q, a, b, north, -rim, width + rim)
    return q


def ring(x, width):
    return x if x >= 0 else width + ROWS8 + x


def spread_north(coef_n, north_s, width):
    for x in range(1 - HALO, width + HALO - 1):
        row = ring(x, width)
        north_s[x + HALO] = jnp.broadcast_to(coef_n[row : row + 1, :], north_s.shape[1:])


def halo_columns(even, halo_1, halo_2, t, part, width):
    q = {}
    for c in range(HALO):
        q[c - HALO] = jnp.where(even, halo_2[t, c, part, :], halo_1[t, c, part, :])
        q[c + width] = jnp.where(even, halo_1[t, c, part, :], halo_2[t, c, part, :])
    return q


def first_kernel(
    chunk, size, fixed, scale, surface, speed, speed_w, speed_e, halo_1, halo_2, open_e, coef_n,
    field, coefs, send_1, send_2, coef_n_out, north_s,
):
    tracers, levels, width, rows = fixed.shape
    even = is_even()
    spread_north(coef_n, north_s, width)
    north = lambda x: north_s[x + HALO]

    def block(i, _):
        start = pl.multiple_of(i * ROWS8, ROWS8)
        part, whole = pl.ds(start, ROWS8), pl.ds(chunk * size + start, ROWS8)
        u = dict(enumerate(jnp.swapaxes(speed[whole], 0, 1)))
        for c in range(HALO):
            u[c - HALO] = speed_w[c, whole, :]
        u[width] = speed_e[whole, :]
        for x in range(-HALO, width + HALO - 1):
            row = ring(x, width)
            opening = jnp.broadcast_to(open_e[row : row + 1, :], (ROWS8, rows))
            coefs[0, x + HALO, part, :] = opening * (jnp.maximum(u[x], 0.0) + NU)
            coefs[1, x + HALO, part, :] = opening * (jnp.minimum(u[x], 0.0) - NU)

        a = lambda x: coefs[0, x + HALO, part, :]
        b = lambda x: coefs[1, x + HALO, part, :]

        def tracer(t, _):
            value = fixed[t, whole] + scale[whole] * surface[t][None]
            q = dict(enumerate(jnp.swapaxes(value, 0, 1)))
            q.update(halo_columns(even, halo_1, halo_2, t, part, width))
            q = two_steps(q, a, b, north, width)
            for x in range(width):
                field[t, x, part, :] = q[x]
            for c in range(HALO):
                west, east = q[c], q[width - HALO + c]
                send_1[t, c, part, :] = jnp.where(even, east, west)
                send_2[t, c, part, :] = jnp.where(even, west, east)
            return 0

        lax.fori_loop(0, tracers, tracer, 0)
        return 0

    lax.fori_loop(0, size // ROWS8, block, 0)


def last_kernel(chunk, size, field, coefs, halo_1, halo_2, coef_n, *refs):
    out, coef_n_out, stage, north_s, sems = refs[-5:]
    tracers, width, _, rows = field.shape
    even = is_even()
    spread_north(coef_n, north_s, width)
    north = lambda x: north_s[x + HALO]
    copies = []
    for i in range(size // ROWS8):
        part = pl.ds(i * ROWS8, ROWS8)
        a = lambda x: coefs[0, x + HALO, part, :]
        b = lambda x: coefs[1, x + HALO, part, :]

        def tracer(t, _):
            q = {x: field[t, x, part, :] for x in range(width)}
            q.update(halo_columns(even, halo_1, halo_2, t, part, width))
            q = two_steps(q, a, b, north, width)
            stage[t, part] = jnp.swapaxes(jnp.stack([q[x] for x in range(width)]), 0, 1)
            return 0

        lax.fori_loop(0, tracers, tracer, 0)
        to = pl.ds(chunk * size + i * ROWS8, ROWS8)
        copy = pltpu.make_async_copy(stage.at[:, part], out.at[:, to], sems.at[i])
        copy.start()
        copies.append(copy)
    for copy in copies:
        copy.wait()


def transport_first(chunk, fixed, scale, surface, speeds, halos, planes):
    count, levels, width, rows = fixed.shape
    size = levels // CHUNKS
    args = [fixed, scale, surface, *speeds, *halos, *planes]
    cells = size * width * rows
    field, coefs, send_1, send_2, coef_n = pl.pallas_call(
        functools.partial(first_kernel, chunk, size),
        in_specs=[VMEM] * len(args),
        out_specs=[VMEM] * 5,
        out_shape=[
            shape_of(count, width, size, rows),
            shape_of(2, width + 2 * HALO - 1, size, rows),
            shape_of(count, HALO, size, rows),
            shape_of(count, HALO, size, rows),
            shape_of(*planes[1].shape),
        ],
        scratch_shapes=[pltpu.VMEM((width + 2 * HALO, ROWS8, rows), F32)],
        input_output_aliases={len(args) - 1: 4},
        compiler_params=params(20),
        cost_estimate=pl.CostEstimate(
            flops=36 * count * cells, bytes_accessed=(2 * count + 1) * cells * 4, transcendentals=0
        ),
        name="transport_first",
    )(*args)
    return field, coefs, (send_1, send_2), (planes[0], coef_n)


def transport_last(chunk, levels, field, coefs, halos, planes, result):
    count, width, size, rows = field.shape
    args = [field, coefs, *halos, planes[1]]
    in_specs = [VMEM] * len(args)
    aliases = {len(args) - 1: 1}
    if result is not None:
        aliases[len(args)] = 0
        args.append(result)
        in_specs.append(HBM)
    cells = size * width * rows
    result, coef_n = pl.pallas_call(
        functools.partial(last_kernel, chunk, size),
        in_specs=in_specs,
        out_specs=[HBM, VMEM],
        out_shape=[shape_of(count, levels, width, rows), shape_of(*planes[1].shape)],
        scratch_shapes=[
            pltpu.VMEM((count, size, width, rows), F32),
            pltpu.VMEM((width + 2 * HALO, ROWS8, rows), F32),
            pltpu.SemaphoreType.DMA((size // ROWS8,)),
        ],
        input_output_aliases=aliases,
        compiler_params=params(20),
        cost_estimate=pl.CostEstimate(
            flops=36 * count * cells, bytes_accessed=(2 * count + 1) * cells * 4, transcendentals=0
        ),
        name="transport_last",
    )(*args)
    return result, (planes[0], coef_n)


def per_device(tracers, diffusivity, conductance, face_velocity, partner, weight, sea_mask):
    tiles = lax.axis_size("tile")
    tracers, diffusivity, conductance = tracers[0], diffusivity[0], conductance[0]
    speed, partner, weight = face_velocity[0], partner[0], weight[0]
    width = tracers.shape[2]
    reach = width // 2 + 1

    def move(value, target_of, swap=False):
        pairs = []
        for m in range(2):
            for t in range(tiles):
                target = (1 - m if swap else m) * tiles + target_of(t) % tiles
                pairs.append((m * tiles + t, target))
        return lax.ppermute(value, ("mp", "tile"), pairs)

    one = lambda t: t + 1 - 2 * (t % 2)
    two = lambda t: t - 1 + 2 * (t % 2)

    parts, ratios, own, mask, terms_1, terms_2 = down_to_surface(tracers, diffusivity, conductance, sea_mask, reach)
    terms_1 = move(terms_1, one, swap=True)
    terms_2 = move(terms_2, two, swap=True)
    peer = move(own, lambda t: t, swap=True)
    rim = tuple(range(HALO)) + tuple(range(width - HALO, width))
    fixed, scale, speed, rims, rim_scale, to_east, to_west = up_from_surface(parts, ratios, speed, rim)
    speed_w = move(to_east, lambda t: t + 1)
    speed_e = move(to_west, lambda t: t - 1)
    speeds = (speed, speed_w, speed_e)

    inflow, surface, open_e, coef_n, *sends = exchange_surface(
        own, peer, terms_1, terms_2, partner, weight, mask, rims, rim_scale, reach
    )
    planes = (open_e, coef_n)
    sends = list(zip(sends[:CHUNKS], sends[CHUNKS:]))
    fields, coefs, result = [None] * CHUNKS, [None] * CHUNKS, None
    for c in range(CHUNKS):
        halos = (move(sends[c][0], one), move(sends[c][1], two))
        fields[c], coefs[c], sends[c], planes = transport_first(c, fixed, scale, surface, speeds, halos, planes)
    for c in range(CHUNKS):
        halos = (move(sends[c][0], one), move(sends[c][1], two))
        result, planes = transport_last(c, fixed.shape[1], fields[c], coefs[c], halos, planes, result)
    return result[None], inflow[None]


def solution(mesh):
    in_specs = (
        P("mp", None, None, "tile", None),
        P("mp", None, "tile", None),
        P("mp", "tile", None),
        P("mp", None, "tile", None),
        P("mp", None, "tile", None),
        P("mp", None, "tile", None),
        P("tile", None),
    )
    out_specs = (P("mp", None, None, "tile", None), P("mp", None, "tile", None))
    return jax.shard_map(
        per_device, mesh=mesh, in_specs=in_specs, out_specs=out_specs, check_vma=False
    )
```

```python
import functools

import jax
import jax.numpy as jnp
from jax import lax
from jax.experimental import pallas as pl
from jax.experimental.pallas import tpu as pltpu
from jax.sharding import PartitionSpec as P

STEPS = 4
QUANT = 16
NU = 0.12
ROWS8 = 8
CHUNKS = 4
HALO = 2
F32 = jnp.float32
VMEM = pl.BlockSpec(memory_space=pltpu.VMEM)
HBM = pl.BlockSpec(memory_space=pltpu.HBM)


def shape_of(*shape):
    return jax.ShapeDtypeStruct(shape, F32)


def params(mib):
    return pltpu.CompilerParams(vmem_limit_bytes=mib * 2**20)


def is_even():
    return lax.rem(lax.axis_index("tile"), 2) == 0


def either(even, call, first, second):
    @pl.when(even)
    def _():
        call(first, second)

    @pl.when(jnp.logical_not(even))
    def _():
        call(second, first)


def lane_parts(total, size=256):
    size = min(size, total)
    return [slice(start, start + size) for start in range(0, total, size)]


def down_kernel(reach, source, coupling, conduct, sea, parts, ratios, terms, mask, first_pair, second_pair, sea_s, sems):
    tracers, levels, width, rows = source.shape
    blocks = levels // ROWS8
    small = [
        pltpu.make_async_copy(conduct, terms.at[tracers + 1], sems.at[2, 0]),
        pltpu.make_async_copy(sea, sea_s, sems.at[2, 1]),
    ]
    copies = []
    for b in range(blocks):
        part = pl.ds(b * ROWS8, ROWS8)
        pair = [pltpu.make_async_copy(source.at[:, part], parts.at[:, part], sems.at[0, b])]
        part = pl.ds(b * ROWS8, min(ROWS8, levels - 1 - b * ROWS8))
        pair.append(pltpu.make_async_copy(coupling.at[part], ratios.at[part], sems.at[1, b]))
        copies.append(pair)
    for pair in copies:
        for copy in pair:
            copy.start()
    for copy in small:
        copy.start()

    lanes_all = lane_parts(rows)
    zero = jnp.zeros((width, rows // len(lanes_all)), F32)
    states = [(zero, zero, [zero] * tracers, zero)] * len(lanes_all)
    for b in range(blocks):
        for copy in copies[b]:
            copy.wait()
        for p, lanes in enumerate(lanes_all):
            before, ratio, part, inverse = states[p]
            for l in range(b * ROWS8, (b + 1) * ROWS8):
                now = ratios[l, :, lanes] if l < levels - 1 else zero
                inverse = 1.0 / (1.0 + before + now - before * ratio)
                part = [(parts[t, l, :, lanes] + before * part[t]) * inverse for t in range(tracers)]
                ratio = now * inverse
                before = now
                ratios[l, :, lanes] = ratio
                for t in range(tracers):
                    parts[t, l, :, lanes] = part[t]
            states[p] = (before, ratio, part, inverse)
    for lanes, state in zip(lanes_all, states):
        for t in range(tracers):
            terms[t, :, lanes] = state[2][t]
        terms[tracers, :, lanes] = state[3]
    for copy in small:
        copy.wait()
    mask[...] = sea_s[...].astype(F32)

    def pack(east, west):
        for c in range(tracers + 2):
            east[c * reach : (c + 1) * reach, :] = terms[c, width - reach :, :]
            west[c * reach : (c + 1) * reach, :] = terms[c, :reach, :]
        at = (tracers + 2) * reach
        east[at : at + HALO, :] = mask[width - HALO :, :]
        west[at : at + HALO, :] = mask[:HALO, :]

    either(is_even(), pack, first_pair, second_pair)


def down_to_surface(tracers, diffusivity, conductance, sea_mask, reach):
    count, levels, width, rows = tracers.shape
    packed = (count + 2) * reach + HALO
    packed = -(-packed // 8) * 8
    return pl.pallas_call(
        functools.partial(down_kernel, reach),
        in_specs=[HBM] * 4,
        out_specs=[VMEM] * 6,
        out_shape=[
            shape_of(count, levels, width, rows),
            shape_of(levels, width, rows),
            shape_of(count + 2, width, rows),
            shape_of(width, rows),
            shape_of(packed, rows),
            shape_of(packed, rows),
        ],
        scratch_shapes=[pltpu.VMEM((width, rows), jnp.int32), pltpu.SemaphoreType.DMA((3, levels // ROWS8))],
        compiler_params=params(41),
        cost_estimate=pl.CostEstimate(
            flops=20 * levels * width * rows, bytes_accessed=10 * levels * width * rows * 4, transcendentals=0
        ),
        name="down_to_surface",
    )(tracers, diffusivity, conductance, sea_mask)


def up_kernel(rim, parts, ratios, speed_in, fixed, scale, speed, rims, rim_scale, to_east, to_west, sem):
    tracers, levels, width, rows = parts.shape
    copy = pltpu.make_async_copy(speed_in, speed, sem)
    copy.start()
    for lanes in lane_parts(rows):
        lane_count = lanes.stop - lanes.start
        scale_now = jnp.ones((width, lane_count), F32)
        fixed_now = [jnp.zeros((width, lane_count), F32)] * tracers
        for l in reversed(range(levels)):
            if l < levels - 1:
                ratio = ratios[l, :, lanes]
                scale_now = ratio * scale_now
                fixed_now = [parts[t, l, :, lanes] + ratio * fixed_now[t] for t in range(tracers)]
            scale[l, :, lanes] = scale_now
            for t in range(tracers):
                fixed[t, l, :, lanes] = fixed_now[t]
            for c, x in enumerate(rim):
                rim_scale[c, l : l + 1, lanes] = scale_now[x : x + 1]
                for t in range(tracers):
                    rims[t, c, l : l + 1, lanes] = fixed_now[t][x : x + 1]
    copy.wait()
    for l in range(levels):
        to_west[l : l + 1, :] = speed[l, :1, :]
        for c in range(HALO):
            x = width - HALO + c
            to_east[c, l : l + 1, :] = speed[l, x : x + 1, :]


def up_from_surface(parts, ratios, speed, rim):
    count, levels, width, rows = parts.shape
    return pl.pallas_call(
        functools.partial(up_kernel, rim),
        in_specs=[VMEM, VMEM, HBM],
        out_specs=[VMEM] * 7,
        out_shape=[
            shape_of(count, levels, width, rows),
            shape_of(levels, width, rows),
            shape_of(levels, width, rows),
            shape_of(count, len(rim), levels, rows),
            shape_of(len(rim), levels, rows),
            shape_of(HALO, levels, rows),
            shape_of(levels, rows),
        ],
        input_output_aliases={0: 0, 1: 1},
        scratch_shapes=[pltpu.SemaphoreType.DMA],
        compiler_params=params(30),
        cost_estimate=pl.CostEstimate(
            flops=10 * levels * width * rows, bytes_accessed=10 * levels * width * rows * 4, transcendentals=0
        ),
        name="up_from_surface",
    )(parts, ratios, speed)


def surface_kernel(
    reach, own, peer, first_pair, second_pair, partner, weight, mask, rims, rim_scale,
    inflow, surface, open_e, coef_n, *rest,
):
    chunks = (len(rest) - 2) // 2
    send_1, send_2, wide, opened = rest[:chunks], rest[chunks : 2 * chunks], rest[-2], rest[-1]
    channels, width, rows = own.shape
    tracers = channels - 2
    first = 2 * 8
    even = is_even()

    for c in range(channels):
        wide[c, first : first + width, :] = peer[c]
    opened[:width, :] = mask[...]
    opened[width:, :] = jnp.zeros((ROWS8, rows), F32)

    def unpack(east, west):
        for c in range(channels):
            part = slice(c * reach, (c + 1) * reach)
            wide[c, first - reach : first, :] = west[part, :]
            wide[c, first + width : first + width + reach, :] = east[part, :]
        at = slice(channels * reach, channels * reach + HALO)
        opened[width : width + HALO, :] = east[at, :]
        opened[width + ROWS8 - HALO :, :] = west[at, :]

    either(even, unpack, first_pair, second_pair)

    start = lax.axis_index("tile") * width
    total = lax.axis_size("tile") * width
    for lanes in lane_parts(rows, 128):
        position = start + lax.broadcasted_iota(jnp.int32, (width, 128), 0)
        own_slope = own[tracers, :, lanes]
        own_conduct = own[tracers + 1, :, lanes]
        flow = [jnp.zeros((width, 128), F32) for _ in range(tracers)]
        for k in range(partner.shape[0]):
            apart = partner[k, :, lanes] - position
            apart = jnp.where(apart > reach, apart - total, apart)
            apart = jnp.where(apart < -reach, apart + total, apart)
            found = [jnp.zeros((width, 128), F32) for _ in range(channels)]
            for offset in range(-reach, reach + 1):
                hit = apart == offset
                window = slice(first + offset, first + offset + width)
                found = [jnp.where(hit, wide[c, window, lanes], f) for c, f in enumerate(found)]
            series = own_conduct * found[-1] / (own_conduct + found[-1])
            factor = weight[k, :, lanes].astype(F32) * series / (1.0 + series * (own_slope + found[-2]))
            flow = [flow[t] + factor * (own[t, :, lanes] - found[t]) for t in range(tracers)]
        for t in range(tracers):
            into = flow[t] * (-1.0 / QUANT)
            inflow[t, :, lanes] = into
            surface[t, :, lanes] = own[t, :, lanes] + own_slope * into

    size = rim_scale.shape[1] // chunks
    for c in range(chunks):
        part = slice(c * size, (c + 1) * size)
        for t in range(tracers):
            for x in range(HALO):
                e = width - HALO + x
                west = rims[t, x, part, :] + rim_scale[x, part, :] * surface[t, x : x + 1, :]
                east = rims[t, HALO + x, part, :] + rim_scale[HALO + x, part, :] * surface[t, e : e + 1, :]
                send_1[c][t, x] = jnp.where(even, east, west)
                send_2[c][t, x] = jnp.where(even, west, east)

    wide_rows = width + ROWS8
    free = jnp.broadcast_to(lax.axis_index("mp"), (wide_rows, rows)) == 0
    here = jnp.where(free, 1.0, opened[...])
    column = lax.broadcasted_iota(jnp.int32, (wide_rows, rows), 1)
    open_e[...] = here * pltpu.roll(here, wide_rows - 1, 0)
    coef_n[...] = NU * (here * jnp.where(column == rows - 1, 0.0, pltpu.roll(here, rows - 1, 1)))


def exchange_surface(own, peer, first_pair, second_pair, partner, weight, mask, rims, rim_scale, reach):
    channels, width, rows = own.shape
    count, _, levels, _ = rims.shape
    plane = shape_of(width + ROWS8, rows)
    edge = shape_of(count, HALO, levels // CHUNKS, rows)
    return pl.pallas_call(
        functools.partial(surface_kernel, reach),
        in_specs=[VMEM] * 9,
        out_specs=[VMEM] * (4 + 2 * CHUNKS),
        out_shape=[shape_of(count, width, rows)] * 2 + [plane] * 2 + [edge] * (2 * CHUNKS),
        scratch_shapes=[pltpu.VMEM((channels, 16 + width + 16, rows), F32), pltpu.VMEM((width + ROWS8, rows), F32)],
        compiler_params=params(20),
        cost_estimate=pl.CostEstimate(flops=4000 * width * rows, bytes_accessed=4 * 2**20, transcendentals=0),
        name="exchange_surface",
    )(own, peer, first_pair, second_pair, partner, weight, mask, rims, rim_scale)


def two_steps(q, a, b, north, width, put):
    def along_y(x, value):
        flux = north(x) * (pltpu.roll(value, value.shape[-1] - 1, 1) - value)
        return flux - pltpu.roll(flux, 1, 1)

    here = q(-1)
    flux = a(-2) * q(-2) + b(-2) * here
    once_before, flux_before = None, None
    for x in range(-1, width + 1):
        east = q(x + 1)
        flux_e = a(x) * here + b(x) * east
        once = (here - (flux_e - flux)) + along_y(x, here)
        if once_before is not None:
            flux_once = a(x - 1) * once_before + b(x - 1) * once
            if flux_before is not None:
                put(x - 1, (once_before - (flux_once - flux_before)) + along_y(x - 1, once_before))
            flux_before = flux_once
        here, flux, once_before = east, flux_e, once


def tiles_in(turn, value):
    levels, width, _ = value.shape
    for j in range(turn.shape[0]):
        turn[j] = value[:, :, 128 * j : 128 * (j + 1)].reshape(levels * width, 128)


def column(turn, x, width):
    parts = [turn[j, pl.ds(x, ROWS8, stride=width), :] for j in range(turn.shape[0])]
    return jnp.concatenate(parts, axis=1)


def put_column(turn, x, width, value):
    for j in range(turn.shape[0]):
        turn[j, pl.ds(x, ROWS8, stride=width), :] = value[:, 128 * j : 128 * (j + 1)]


def ring(x, width):
    return x if x >= 0 else width + ROWS8 + x


def spread_north(coef_n, north_s, width):
    for x in range(1 - HALO, width + HALO - 1):
        row = ring(x, width)
        north_s[x + HALO] = jnp.broadcast_to(coef_n[row : row + 1, :], north_s.shape[1:])


def halo_column(even, halo_1, halo_2, t, part, x, width):
    west, c = x < 0, (x + HALO if x < 0 else x - width)
    first, second = halo_1[t, c, part, :], halo_2[t, c, part, :]
    return jnp.where(even, second, first) if west else jnp.where(even, first, second)


def first_kernel(
    chunk, size, fixed, scale, surface, speed, speed_w, speed_e, halo_1, halo_2, open_e, coef_n,
    field, coefs, send_1, send_2, coef_n_out, north_s, turn, turn_speed,
):
    tracers, levels, width, rows = fixed.shape
    even = is_even()
    spread_north(coef_n, north_s, width)
    north = lambda x: north_s[x + HALO]

    def block(i, _):
        start = pl.multiple_of(i * ROWS8, ROWS8)
        part, whole = pl.ds(start, ROWS8), pl.ds(chunk * size + start, ROWS8)
        tiles_in(turn_speed, speed[whole])
        for x in range(-HALO, width + HALO - 1):
            if x < 0:
                u = speed_w[x + HALO, whole, :]
            elif x == width:
                u = speed_e[whole, :]
            else:
                u = column(turn_speed, x, width)
            row = ring(x, width)
            opening = jnp.broadcast_to(open_e[row : row + 1, :], (ROWS8, rows))
            coefs[0, x + HALO, part, :] = opening * (jnp.maximum(u, 0.0) + NU)
            coefs[1, x + HALO, part, :] = opening * (jnp.minimum(u, 0.0) - NU)

        a = lambda x: coefs[0, x + HALO, part, :]
        b = lambda x: coefs[1, x + HALO, part, :]

        def tracer(t, _):
            tiles_in(turn, fixed[t, whole] + scale[whole] * surface[t][None])

            def q(x):
                if 0 <= x < width:
                    return column(turn, x, width)
                return halo_column(even, halo_1, halo_2, t, part, x, width)

            edge = {}

            def put(x, value):
                field[t, x, part, :] = value
                if x < HALO:
                    edge[x] = value
                elif x >= width - HALO:
                    c = x - (width - HALO)
                    send_1[t, c, part, :] = jnp.where(even, value, edge[c])
                    send_2[t, c, part, :] = jnp.where(even, edge[c], value)

            two_steps(q, a, b, north, width, put)
            return 0

        lax.fori_loop(0, tracers, tracer, 0)
        return 0

    lax.fori_loop(0, size // ROWS8, block, 0)


def last_kernel(chunk, size, field, coefs, halo_1, halo_2, coef_n, *refs):
    out, coef_n_out, stage, north_s, turn, sems = refs[-6:]
    tracers, width, _, rows = field.shape
    even = is_even()
    spread_north(coef_n, north_s, width)
    north = lambda x: north_s[x + HALO]
    copies = []
    for i in range(size // ROWS8):
        part = pl.ds(i * ROWS8, ROWS8)
        a = lambda x: coefs[0, x + HALO, part, :]
        b = lambda x: coefs[1, x + HALO, part, :]

        def tracer(t, _):
            def q(x):
                if 0 <= x < width:
                    return field[t, x, part, :]
                return halo_column(even, halo_1, halo_2, t, part, x, width)

            two_steps(q, a, b, north, width, lambda x, value: put_column(turn, x, width, value))
            for j in range(turn.shape[0]):
                stage[t, part, :, 128 * j : 128 * (j + 1)] = turn[j].reshape(ROWS8, width, 128)
            return 0

        lax.fori_loop(0, tracers, tracer, 0)
        to = pl.ds(chunk * size + i * ROWS8, ROWS8)
        copy = pltpu.make_async_copy(stage.at[:, part], out.at[:, to], sems.at[i])
        copy.start()
        copies.append(copy)
    for copy in copies:
        copy.wait()


def transport_first(chunk, fixed, scale, surface, speeds, halos, planes):
    count, levels, width, rows = fixed.shape
    size = levels // CHUNKS
    args = [fixed, scale, surface, *speeds, *halos, *planes]
    cells = size * width * rows
    field, coefs, send_1, send_2, coef_n = pl.pallas_call(
        functools.partial(first_kernel, chunk, size),
        in_specs=[VMEM] * len(args),
        out_specs=[VMEM] * 5,
        out_shape=[
            shape_of(count, width, size, rows),
            shape_of(2, width + 2 * HALO - 1, size, rows),
            shape_of(count, HALO, size, rows),
            shape_of(count, HALO, size, rows),
            shape_of(*planes[1].shape),
        ],
        scratch_shapes=[
            pltpu.VMEM((width + 2 * HALO, ROWS8, rows), F32),
            pltpu.VMEM((rows // 128, ROWS8 * width, 128), F32),
            pltpu.VMEM((rows // 128, ROWS8 * width, 128), F32),
        ],
        input_output_aliases={len(args) - 1: 4},
        compiler_params=params(20),
        cost_estimate=pl.CostEstimate(
            flops=36 * count * cells, bytes_accessed=(2 * count + 1) * cells * 4, transcendentals=0
        ),
        name="transport_first",
    )(*args)
    return field, coefs, (send_1, send_2), (planes[0], coef_n)


def transport_last(chunk, levels, field, coefs, halos, planes, result):
    count, width, size, rows = field.shape
    args = [field, coefs, *halos, planes[1]]
    in_specs = [VMEM] * len(args)
    aliases = {len(args) - 1: 1}
    if result is not None:
        aliases[len(args)] = 0
        args.append(result)
        in_specs.append(HBM)
    cells = size * width * rows
    result, coef_n = pl.pallas_call(
        functools.partial(last_kernel, chunk, size),
        in_specs=in_specs,
        out_specs=[HBM, VMEM],
        out_shape=[shape_of(count, levels, width, rows), shape_of(*planes[1].shape)],
        scratch_shapes=[
            pltpu.VMEM((count, size, width, rows), F32),
            pltpu.VMEM((width + 2 * HALO, ROWS8, rows), F32),
            pltpu.VMEM((rows // 128, ROWS8 * width, 128), F32),
            pltpu.SemaphoreType.DMA((size // ROWS8,)),
        ],
        input_output_aliases=aliases,
        compiler_params=params(20),
        cost_estimate=pl.CostEstimate(
            flops=36 * count * cells, bytes_accessed=(2 * count + 1) * cells * 4, transcendentals=0
        ),
        name="transport_last",
    )(*args)
    return result, (planes[0], coef_n)


def per_device(tracers, diffusivity, conductance, face_velocity, partner, weight, sea_mask):
    tiles = lax.axis_size("tile")
    tracers, diffusivity, conductance = tracers[0], diffusivity[0], conductance[0]
    speed, partner, weight = face_velocity[0], partner[0], weight[0]
    width = tracers.shape[2]
    reach = width // 2 + 1

    def move(value, target_of, swap=False):
        pairs = []
        for m in range(2):
            for t in range(tiles):
                target = (1 - m if swap else m) * tiles + target_of(t) % tiles
                pairs.append((m * tiles + t, target))
        return lax.ppermute(value, ("mp", "tile"), pairs)

    one = lambda t: t + 1 - 2 * (t % 2)
    two = lambda t: t - 1 + 2 * (t % 2)

    parts, ratios, own, mask, terms_1, terms_2 = down_to_surface(tracers, diffusivity, conductance, sea_mask, reach)
    terms_1 = move(terms_1, one, swap=True)
    terms_2 = move(terms_2, two, swap=True)
    peer = move(own, lambda t: t, swap=True)
    rim = tuple(range(HALO)) + tuple(range(width - HALO, width))
    fixed, scale, speed, rims, rim_scale, to_east, to_west = up_from_surface(parts, ratios, speed, rim)
    speed_w = move(to_east, lambda t: t + 1)
    speed_e = move(to_west, lambda t: t - 1)
    speeds = (speed, speed_w, speed_e)

    inflow, surface, open_e, coef_n, *sends = exchange_surface(
        own, peer, terms_1, terms_2, partner, weight, mask, rims, rim_scale, reach
    )
    planes = (open_e, coef_n)
    sends = list(zip(sends[:CHUNKS], sends[CHUNKS:]))
    fields, coefs, result = [None] * CHUNKS, [None] * CHUNKS, None
    for c in range(CHUNKS):
        halos = (move(sends[c][0], one), move(sends[c][1], two))
        fields[c], coefs[c], sends[c], planes = transport_first(c, fixed, scale, surface, speeds, halos, planes)
    for c in range(CHUNKS):
        halos = (move(sends[c][0], one), move(sends[c][1], two))
        result, planes = transport_last(c, fixed.shape[1], fields[c], coefs[c], halos, planes, result)
    return result[None], inflow[None]


def solution(mesh):
    in_specs = (
        P("mp", None, None, "tile", None),
        P("mp", None, "tile", None),
        P("mp", "tile", None),
        P("mp", None, "tile", None),
        P("mp", None, "tile", None),
        P("mp", None, "tile", None),
        P("tile", None),
    )
    out_specs = (P("mp", None, None, "tile", None), P("mp", None, "tile", None))
    return jax.shard_map(
        per_device, mesh=mesh, in_specs=in_specs, out_specs=out_specs, check_vma=False
    )
```

```python
import functools

import jax
import jax.numpy as jnp
from jax import lax
from jax.experimental import pallas as pl
from jax.experimental.pallas import tpu as pltpu
from jax.sharding import PartitionSpec as P

STEPS = 4
QUANT = 16
NU = 0.12
ROWS8 = 8
CHUNKS = 4
HALO = 2
F32 = jnp.float32
VMEM = pl.BlockSpec(memory_space=pltpu.VMEM)
HBM = pl.BlockSpec(memory_space=pltpu.HBM)


def shape_of(*shape):
    return jax.ShapeDtypeStruct(shape, F32)


def params(mib):
    return pltpu.CompilerParams(vmem_limit_bytes=mib * 2**20)


def is_even():
    return lax.rem(lax.axis_index("tile"), 2) == 0


def either(even, call, first, second):
    @pl.when(even)
    def _():
        call(first, second)

    @pl.when(jnp.logical_not(even))
    def _():
        call(second, first)


def lane_parts(total, size=256):
    size = min(size, total)
    return [slice(start, start + size) for start in range(0, total, size)]


def down_kernel(reach, source, coupling, conduct, sea, order, parts, ratios, terms, mask, first_pair, second_pair, sea_s, sems):
    tracers, levels, width, rows = source.shape
    blocks = levels // ROWS8
    small = [
        pltpu.make_async_copy(conduct, terms.at[tracers + 1], sems.at[2, 0]),
        pltpu.make_async_copy(sea, sea_s, sems.at[2, 1]),
    ]
    copies = []
    for b in range(blocks):
        part = pl.ds(b * ROWS8, ROWS8)
        pair = [pltpu.make_async_copy(source.at[:, part], parts.at[:, part], sems.at[0, b])]
        part = pl.ds(b * ROWS8, min(ROWS8, levels - 1 - b * ROWS8))
        pair.append(pltpu.make_async_copy(coupling.at[part], ratios.at[part], sems.at[1, b]))
        copies.append(pair)
    for pair in copies:
        for copy in pair:
            copy.start()
    for copy in small:
        copy.start()

    lanes_all = lane_parts(rows)
    zero = jnp.zeros((width, rows // len(lanes_all)), F32)
    states = [(zero, zero, [zero] * tracers, zero)] * len(lanes_all)
    for b in range(blocks):
        for copy in copies[b]:
            copy.wait()
        for p, lanes in enumerate(lanes_all):
            before, ratio, part, inverse = states[p]
            for l in range(b * ROWS8, (b + 1) * ROWS8):
                now = ratios[l, :, lanes] if l < levels - 1 else zero
                inverse = 1.0 / (1.0 + before + now - before * ratio)
                part = [(parts[t, l, :, lanes] + before * part[t]) * inverse for t in range(tracers)]
                ratio = now * inverse
                before = now
                ratios[l, :, lanes] = ratio
                for t in range(tracers):
                    parts[t, l, :, lanes] = part[t]
            states[p] = (before, ratio, part, inverse)
    for lanes, state in zip(lanes_all, states):
        for t in range(tracers):
            terms[t, :, lanes] = state[2][t]
        terms[tracers, :, lanes] = state[3]
    for copy in small:
        copy.wait()
    mask[...] = sea_s[...].astype(F32)

    def pack(east, west):
        for c in range(tracers + 2):
            east[c * reach : (c + 1) * reach, :] = terms[c, width - reach :, :]
            west[c * reach : (c + 1) * reach, :] = terms[c, :reach, :]
        at = (tracers + 2) * reach
        east[at : at + HALO, :] = mask[width - HALO :, :]
        west[at : at + HALO, :] = mask[:HALO, :]

    either(is_even(), pack, first_pair, second_pair)


def down_to_surface(tracers, diffusivity, conductance, sea_mask, order, reach):
    count, levels, width, rows = tracers.shape
    packed = (count + 2) * reach + HALO
    packed = -(-packed // 8) * 8
    return pl.pallas_call(
        functools.partial(down_kernel, reach),
        in_specs=[HBM] * 4 + [VMEM],
        out_specs=[VMEM] * 6,
        out_shape=[
            shape_of(count, levels, width, rows),
            shape_of(levels, width, rows),
            shape_of(count + 2, width, rows),
            shape_of(width, rows),
            shape_of(packed, rows),
            shape_of(packed, rows),
        ],
        scratch_shapes=[pltpu.VMEM((width, rows), jnp.int32), pltpu.SemaphoreType.DMA((3, levels // ROWS8))],
        compiler_params=params(41),
        cost_estimate=pl.CostEstimate(
            flops=20 * levels * width * rows, bytes_accessed=10 * levels * width * rows * 4, transcendentals=0
        ),
        name="down_to_surface",
    )(tracers, diffusivity, conductance, sea_mask, order)


def up_kernel(rim, parts, ratios, speed_w, fixed, scale, rims, rim_scale):
    tracers, levels, width, rows = parts.shape
    for lanes in lane_parts(rows):
        lane_count = lanes.stop - lanes.start
        scale_now = jnp.ones((width, lane_count), F32)
        fixed_now = [jnp.zeros((width, lane_count), F32)] * tracers
        for l in reversed(range(levels)):
            if l < levels - 1:
                ratio = ratios[l, :, lanes]
                scale_now = ratio * scale_now
                fixed_now = [parts[t, l, :, lanes] + ratio * fixed_now[t] for t in range(tracers)]
            scale[l, :, lanes] = scale_now
            for t in range(tracers):
                fixed[t, l, :, lanes] = fixed_now[t]
            for c, x in enumerate(rim):
                rim_scale[c, l : l + 1, lanes] = scale_now[x : x + 1]
                for t in range(tracers):
                    rims[t, c, l : l + 1, lanes] = fixed_now[t][x : x + 1]


def speed_kernel(speed, to_east, to_west, order):
    order[...] = jnp.zeros_like(order)
    levels, width, _ = speed.shape
    for l in range(levels):
        to_west[l : l + 1, :] = speed[l, :1, :]
        for c in range(HALO):
            x = width - HALO + c
            to_east[c, l : l + 1, :] = speed[l, x : x + 1, :]


def speed_edges(speed):
    levels, width, rows = speed.shape
    return pl.pallas_call(
        speed_kernel,
        in_specs=[VMEM],
        out_specs=[VMEM] * 3,
        out_shape=[shape_of(HALO, levels, rows), shape_of(levels, rows), shape_of(ROWS8, 128)],
        compiler_params=params(20),
        cost_estimate=pl.CostEstimate(flops=0, bytes_accessed=levels * width * rows * 4, transcendentals=0),
        name="speed_edges",
    )(speed)


def up_from_surface(parts, ratios, arrived, rim):
    count, levels, width, rows = parts.shape
    return pl.pallas_call(
        functools.partial(up_kernel, rim),
        in_specs=[VMEM] * 3,
        out_specs=[VMEM] * 4,
        out_shape=[
            shape_of(count, levels, width, rows),
            shape_of(levels, width, rows),
            shape_of(count, len(rim), levels, rows),
            shape_of(len(rim), levels, rows),
        ],
        input_output_aliases={0: 0, 1: 1},
        compiler_params=params(20),
        cost_estimate=pl.CostEstimate(
            flops=10 * levels * width * rows, bytes_accessed=10 * levels * width * rows * 4, transcendentals=0
        ),
        name="up_from_surface",
    )(parts, ratios, arrived)


def surface_kernel(
    reach, own, peer, first_pair, second_pair, partner, weight, mask, rims, rim_scale, speed_e,
    inflow, surface, open_e, coef_n, *rest,
):
    chunks = (len(rest) - 2) // 2
    send_1, send_2, wide, opened = rest[:chunks], rest[chunks : 2 * chunks], rest[-2], rest[-1]
    channels, width, rows = own.shape
    tracers = channels - 2
    first = 2 * 8
    even = is_even()

    for c in range(channels):
        wide[c, first : first + width, :] = peer[c]
    opened[:width, :] = mask[...]
    opened[width:, :] = jnp.zeros((ROWS8, rows), F32)

    def unpack(east, west):
        for c in range(channels):
            part = slice(c * reach, (c + 1) * reach)
            wide[c, first - reach : first, :] = west[part, :]
            wide[c, first + width : first + width + reach, :] = east[part, :]
        at = slice(channels * reach, channels * reach + HALO)
        opened[width : width + HALO, :] = east[at, :]
        opened[width + ROWS8 - HALO :, :] = west[at, :]

    either(even, unpack, first_pair, second_pair)

    start = lax.axis_index("tile") * width
    total = lax.axis_size("tile") * width
    for lanes in lane_parts(rows, 128):
        position = start + lax.broadcasted_iota(jnp.int32, (width, 128), 0)
        own_slope = own[tracers, :, lanes]
        own_conduct = own[tracers + 1, :, lanes]
        flow = [jnp.zeros((width, 128), F32) for _ in range(tracers)]
        for k in range(partner.shape[0]):
            apart = partner[k, :, lanes] - position
            apart = jnp.where(apart > reach, apart - total, apart)
            apart = jnp.where(apart < -reach, apart + total, apart)
            found = [jnp.zeros((width, 128), F32) for _ in range(channels)]
            for offset in range(-reach, reach + 1):
                hit = apart == offset
                window = slice(first + offset, first + offset + width)
                found = [jnp.where(hit, wide[c, window, lanes], f) for c, f in enumerate(found)]
            series = own_conduct * found[-1] / (own_conduct + found[-1])
            factor = weight[k, :, lanes].astype(F32) * series / (1.0 + series * (own_slope + found[-2]))
            flow = [flow[t] + factor * (own[t, :, lanes] - found[t]) for t in range(tracers)]
        for t in range(tracers):
            into = flow[t] * (-1.0 / QUANT)
            inflow[t, :, lanes] = into
            surface[t, :, lanes] = own[t, :, lanes] + own_slope * into

    size = rim_scale.shape[1] // chunks
    for c in range(chunks):
        part = slice(c * size, (c + 1) * size)
        for t in range(tracers):
            for x in range(HALO):
                e = width - HALO + x
                west = rims[t, x, part, :] + rim_scale[x, part, :] * surface[t, x : x + 1, :]
                east = rims[t, HALO + x, part, :] + rim_scale[HALO + x, part, :] * surface[t, e : e + 1, :]
                send_1[c][t, x] = jnp.where(even, east, west)
                send_2[c][t, x] = jnp.where(even, west, east)

    wide_rows = width + ROWS8
    free = jnp.broadcast_to(lax.axis_index("mp"), (wide_rows, rows)) == 0
    here = jnp.where(free, 1.0, opened[...])
    column = lax.broadcasted_iota(jnp.int32, (wide_rows, rows), 1)
    open_e[...] = here * pltpu.roll(here, wide_rows - 1, 0)
    coef_n[...] = NU * (here * jnp.where(column == rows - 1, 0.0, pltpu.roll(here, rows - 1, 1)))


def exchange_surface(own, peer, first_pair, second_pair, partner, weight, mask, rims, rim_scale, arrived, reach):
    channels, width, rows = own.shape
    count, _, levels, _ = rims.shape
    plane = shape_of(width + ROWS8, rows)
    edge = shape_of(count, HALO, levels // CHUNKS, rows)
    return pl.pallas_call(
        functools.partial(surface_kernel, reach),
        in_specs=[VMEM] * 10,
        out_specs=[VMEM] * (4 + 2 * CHUNKS),
        out_shape=[shape_of(count, width, rows)] * 2 + [plane] * 2 + [edge] * (2 * CHUNKS),
        scratch_shapes=[pltpu.VMEM((channels, 16 + width + 16, rows), F32), pltpu.VMEM((width + ROWS8, rows), F32)],
        compiler_params=params(20),
        cost_estimate=pl.CostEstimate(flops=4000 * width * rows, bytes_accessed=4 * 2**20, transcendentals=0),
        name="exchange_surface",
    )(own, peer, first_pair, second_pair, partner, weight, mask, rims, rim_scale, arrived)


def two_steps(q, a, b, north, width, put):
    def along_y(x, value):
        flux = north(x) * (pltpu.roll(value, value.shape[-1] - 1, 1) - value)
        return flux - pltpu.roll(flux, 1, 1)

    here = q(-1)
    flux = a(-2) * q(-2) + b(-2) * here
    once_before, flux_before = None, None
    for x in range(-1, width + 1):
        east = q(x + 1)
        flux_e = a(x) * here + b(x) * east
        once = (here - (flux_e - flux)) + along_y(x, here)
        if once_before is not None:
            flux_once = a(x - 1) * once_before + b(x - 1) * once
            if flux_before is not None:
                put(x - 1, (once_before - (flux_once - flux_before)) + along_y(x - 1, once_before))
            flux_before = flux_once
        here, flux, once_before = east, flux_e, once


def tiles_in(turn, value):
    levels, width, _ = value.shape
    for j in range(turn.shape[0]):
        turn[j] = value[:, :, 128 * j : 128 * (j + 1)].reshape(levels * width, 128)


def column(turn, x, width):
    parts = [turn[j, pl.ds(x, ROWS8, stride=width), :] for j in range(turn.shape[0])]
    return jnp.concatenate(parts, axis=1)


def put_column(turn, x, width, value):
    for j in range(turn.shape[0]):
        turn[j, pl.ds(x, ROWS8, stride=width), :] = value[:, 128 * j : 128 * (j + 1)]


def ring(x, width):
    return x if x >= 0 else width + ROWS8 + x


def spread_north(coef_n, north_s, width):
    for x in range(1 - HALO, width + HALO - 1):
        row = ring(x, width)
        north_s[x + HALO] = jnp.broadcast_to(coef_n[row : row + 1, :], north_s.shape[1:])


def halo_column(even, halo_1, halo_2, t, part, x, width):
    west, c = x < 0, (x + HALO if x < 0 else x - width)
    first, second = halo_1[t, c, part, :], halo_2[t, c, part, :]
    return jnp.where(even, second, first) if west else jnp.where(even, first, second)


def first_kernel(
    chunk, size, fixed, scale, surface, speed, speed_w, speed_e, halo_1, halo_2, open_e, coef_n,
    field, coefs, send_1, send_2, coef_n_out, north_s, turn, turn_speed,
):
    tracers, levels, width, rows = fixed.shape
    even = is_even()
    spread_north(coef_n, north_s, width)
    north = lambda x: north_s[x + HALO]

    def block(i, _):
        start = pl.multiple_of(i * ROWS8, ROWS8)
        part, whole = pl.ds(start, ROWS8), pl.ds(chunk * size + start, ROWS8)
        tiles_in(turn_speed, speed[whole])
        for x in range(-HALO, width + HALO - 1):
            if x < 0:
                u = speed_w[x + HALO, whole, :]
            elif x == width:
                u = speed_e[whole, :]
            else:
                u = column(turn_speed, x, width)
            row = ring(x, width)
            opening = jnp.broadcast_to(open_e[row : row + 1, :], (ROWS8, rows))
            coefs[0, x + HALO, part, :] = opening * (jnp.maximum(u, 0.0) + NU)
            coefs[1, x + HALO, part, :] = opening * (jnp.minimum(u, 0.0) - NU)

        a = lambda x: coefs[0, x + HALO, part, :]
        b = lambda x: coefs[1, x + HALO, part, :]

        def tracer(t, _):
            tiles_in(turn, fixed[t, whole] + scale[whole] * surface[t][None])

            def q(x):
                if 0 <= x < width:
                    return column(turn, x, width)
                return halo_column(even, halo_1, halo_2, t, part, x, width)

            edge = {}

            def put(x, value):
                field[t, x, part, :] = value
                if x < HALO:
                    edge[x] = value
                elif x >= width - HALO:
                    c = x - (width - HALO)
                    send_1[t, c, part, :] = jnp.where(even, value, edge[c])
                    send_2[t, c, part, :] = jnp.where(even, edge[c], value)

            two_steps(q, a, b, north, width, put)
            return 0

        lax.fori_loop(0, tracers, tracer, 0)
        return 0

    lax.fori_loop(0, size // ROWS8, block, 0)


def last_kernel(chunk, size, field, coefs, halo_1, halo_2, coef_n, *refs):
    out, coef_n_out, stage, north_s, turn, sems = refs[-6:]
    tracers, width, _, rows = field.shape
    even = is_even()
    spread_north(coef_n, north_s, width)
    north = lambda x: north_s[x + HALO]
    copies = []
    for i in range(size // ROWS8):
        part = pl.ds(i * ROWS8, ROWS8)
        a = lambda x: coefs[0, x + HALO, part, :]
        b = lambda x: coefs[1, x + HALO, part, :]

        def tracer(t, _):
            def q(x):
                if 0 <= x < width:
                    return field[t, x, part, :]
                return halo_column(even, halo_1, halo_2, t, part, x, width)

            two_steps(q, a, b, north, width, lambda x, value: put_column(turn, x, width, value))
            for j in range(turn.shape[0]):
                stage[t, part, :, 128 * j : 128 * (j + 1)] = turn[j].reshape(ROWS8, width, 128)
            return 0

        lax.fori_loop(0, tracers, tracer, 0)
        to = pl.ds(chunk * size + i * ROWS8, ROWS8)
        copy = pltpu.make_async_copy(stage.at[:, part], out.at[:, to], sems.at[i])
        copy.start()
        copies.append(copy)
    for copy in copies:
        copy.wait()


def transport_first(chunk, fixed, scale, surface, speeds, halos, planes):
    count, levels, width, rows = fixed.shape
    size = levels // CHUNKS
    args = [fixed, scale, surface, *speeds, *halos, *planes]
    cells = size * width * rows
    field, coefs, send_1, send_2, coef_n = pl.pallas_call(
        functools.partial(first_kernel, chunk, size),
        in_specs=[VMEM] * len(args),
        out_specs=[VMEM] * 5,
        out_shape=[
            shape_of(count, width, size, rows),
            shape_of(2, width + 2 * HALO - 1, size, rows),
            shape_of(count, HALO, size, rows),
            shape_of(count, HALO, size, rows),
            shape_of(*planes[1].shape),
        ],
        scratch_shapes=[
            pltpu.VMEM((width + 2 * HALO, ROWS8, rows), F32),
            pltpu.VMEM((rows // 128, ROWS8 * width, 128), F32),
            pltpu.VMEM((rows // 128, ROWS8 * width, 128), F32),
        ],
        input_output_aliases={len(args) - 1: 4},
        compiler_params=params(20),
        cost_estimate=pl.CostEstimate(
            flops=36 * count * cells, bytes_accessed=(2 * count + 1) * cells * 4, transcendentals=0
        ),
        name="transport_first",
    )(*args)
    return field, coefs, (send_1, send_2), (planes[0], coef_n)


def transport_last(chunk, levels, field, coefs, halos, planes, result):
    count, width, size, rows = field.shape
    args = [field, coefs, *halos, planes[1]]
    in_specs = [VMEM] * len(args)
    aliases = {len(args) - 1: 1}
    if result is not None:
        aliases[len(args)] = 0
        args.append(result)
        in_specs.append(HBM)
    cells = size * width * rows
    result, coef_n = pl.pallas_call(
        functools.partial(last_kernel, chunk, size),
        in_specs=in_specs,
        out_specs=[HBM, VMEM],
        out_shape=[shape_of(count, levels, width, rows), shape_of(*planes[1].shape)],
        scratch_shapes=[
            pltpu.VMEM((count, size, width, rows), F32),
            pltpu.VMEM((width + 2 * HALO, ROWS8, rows), F32),
            pltpu.VMEM((rows // 128, ROWS8 * width, 128), F32),
            pltpu.SemaphoreType.DMA((size // ROWS8,)),
        ],
        input_output_aliases=aliases,
        compiler_params=params(20),
        cost_estimate=pl.CostEstimate(
            flops=36 * count * cells, bytes_accessed=(2 * count + 1) * cells * 4, transcendentals=0
        ),
        name="transport_last",
    )(*args)
    return result, (planes[0], coef_n)


def per_device(tracers, diffusivity, conductance, face_velocity, partner, weight, sea_mask):
    tiles = lax.axis_size("tile")
    tracers, diffusivity, conductance = tracers[0], diffusivity[0], conductance[0]
    speed, partner, weight = face_velocity[0], partner[0], weight[0]
    width = tracers.shape[2]
    reach = width // 2 + 1

    def move(value, target_of, swap=False):
        pairs = []
        for m in range(2):
            for t in range(tiles):
                target = (1 - m if swap else m) * tiles + target_of(t) % tiles
                pairs.append((m * tiles + t, target))
        return lax.ppermute(value, ("mp", "tile"), pairs)

    one = lambda t: t + 1 - 2 * (t % 2)
    two = lambda t: t - 1 + 2 * (t % 2)

    to_east, to_west, order = speed_edges(speed)
    speed_w = move(to_east, lambda t: t + 1)
    speed_e = move(to_west, lambda t: t - 1)
    speeds = (speed, speed_w, speed_e)

    parts, ratios, own, mask, terms_1, terms_2 = down_to_surface(
        tracers, diffusivity, conductance, sea_mask, order, reach
    )
    terms_1 = move(terms_1, one, swap=True)
    terms_2 = move(terms_2, two, swap=True)
    peer = move(own, lambda t: t, swap=True)
    rim = tuple(range(HALO)) + tuple(range(width - HALO, width))
    fixed, scale, rims, rim_scale = up_from_surface(parts, ratios, speed_w, rim)

    inflow, surface, open_e, coef_n, *sends = exchange_surface(
        own, peer, terms_1, terms_2, partner, weight, mask, rims, rim_scale, speed_e, reach
    )
    planes = (open_e, coef_n)
    sends = list(zip(sends[:CHUNKS], sends[CHUNKS:]))
    fields, coefs, result = [None] * CHUNKS, [None] * CHUNKS, None
    for c in range(CHUNKS):
        halos = (move(sends[c][0], one), move(sends[c][1], two))
        fields[c], coefs[c], sends[c], planes = transport_first(c, fixed, scale, surface, speeds, halos, planes)
    for c in range(CHUNKS):
        halos = (move(sends[c][0], one), move(sends[c][1], two))
        result, planes = transport_last(c, fixed.shape[1], fields[c], coefs[c], halos, planes, result)
    return result[None], inflow[None]


def solution(mesh):
    in_specs = (
        P("mp", None, None, "tile", None),
        P("mp", None, "tile", None),
        P("mp", "tile", None),
        P("mp", None, "tile", None),
        P("mp", None, "tile", None),
        P("mp", None, "tile", None),
        P("tile", None),
    )
    out_specs = (P("mp", None, None, "tile", None), P("mp", None, "tile", None))
    return jax.shard_map(
        per_device, mesh=mesh, in_specs=in_specs, out_specs=out_specs, check_vma=False
    )
```

```python
import functools

import jax
import jax.numpy as jnp
from jax import lax
from jax.experimental import pallas as pl
from jax.experimental.pallas import tpu as pltpu
from jax.sharding import PartitionSpec as P

STEPS = 4
QUANT = 16
NU = 0.12
ROWS8 = 8
CHUNKS = 2
HALO = 2
F32 = jnp.float32
VMEM = pl.BlockSpec(memory_space=pltpu.VMEM)
HBM = pl.BlockSpec(memory_space=pltpu.HBM)


def shape_of(*shape):
    return jax.ShapeDtypeStruct(shape, F32)


def params(mib):
    return pltpu.CompilerParams(vmem_limit_bytes=mib * 2**20)


def is_even():
    return lax.rem(lax.axis_index("tile"), 2) == 0


def either(even, call, first, second):
    @pl.when(even)
    def _():
        call(first, second)

    @pl.when(jnp.logical_not(even))
    def _():
        call(second, first)


def lane_parts(total, size=256):
    size = min(size, total)
    return [slice(start, start + size) for start in range(0, total, size)]


def down_kernel(reach, source, coupling, conduct, sea, order, parts, ratios, terms, mask, first_pair, second_pair, sea_s, sems):
    tracers, levels, width, rows = source.shape
    blocks = levels // ROWS8
    small = [
        pltpu.make_async_copy(conduct, terms.at[tracers + 1], sems.at[2, 0]),
        pltpu.make_async_copy(sea, sea_s, sems.at[2, 1]),
    ]
    copies = []
    for b in range(blocks):
        part = pl.ds(b * ROWS8, ROWS8)
        pair = [pltpu.make_async_copy(source.at[:, part], parts.at[:, part], sems.at[0, b])]
        part = pl.ds(b * ROWS8, min(ROWS8, levels - 1 - b * ROWS8))
        pair.append(pltpu.make_async_copy(coupling.at[part], ratios.at[part], sems.at[1, b]))
        copies.append(pair)
    for pair in copies:
        for copy in pair:
            copy.start()
    for copy in small:
        copy.start()

    lanes_all = lane_parts(rows)
    zero = jnp.zeros((width, rows // len(lanes_all)), F32)
    states = [(zero, zero, [zero] * tracers, zero)] * len(lanes_all)
    for b in range(blocks):
        for copy in copies[b]:
            copy.wait()
        for p, lanes in enumerate(lanes_all):
            before, ratio, part, inverse = states[p]
            for l in range(b * ROWS8, (b + 1) * ROWS8):
                now = ratios[l, :, lanes] if l < levels - 1 else zero
                inverse = 1.0 / (1.0 + before + now - before * ratio)
                part = [(parts[t, l, :, lanes] + before * part[t]) * inverse for t in range(tracers)]
                ratio = now * inverse
                before = now
                ratios[l, :, lanes] = ratio
                for t in range(tracers):
                    parts[t, l, :, lanes] = part[t]
            states[p] = (before, ratio, part, inverse)
    for lanes, state in zip(lanes_all, states):
        for t in range(tracers):
            terms[t, :, lanes] = state[2][t]
        terms[tracers, :, lanes] = state[3]
    for copy in small:
        copy.wait()
    mask[...] = sea_s[...].astype(F32)

    def pack(east, west):
        for c in range(tracers + 2):
            east[c * reach : (c + 1) * reach, :] = terms[c, width - reach :, :]
            west[c * reach : (c + 1) * reach, :] = terms[c, :reach, :]
        at = (tracers + 2) * reach
        east[at : at + HALO, :] = mask[width - HALO :, :]
        west[at : at + HALO, :] = mask[:HALO, :]

    either(is_even(), pack, first_pair, second_pair)


def down_to_surface(tracers, diffusivity, conductance, sea_mask, order, reach):
    count, levels, width, rows = tracers.shape
    packed = (count + 2) * reach + HALO
    packed = -(-packed // 8) * 8
    return pl.pallas_call(
        functools.partial(down_kernel, reach),
        in_specs=[HBM] * 4 + [VMEM],
        out_specs=[VMEM] * 6,
        out_shape=[
            shape_of(count, levels, width, rows),
            shape_of(levels, width, rows),
            shape_of(count + 2, width, rows),
            shape_of(width, rows),
            shape_of(packed, rows),
            shape_of(packed, rows),
        ],
        scratch_shapes=[pltpu.VMEM((width, rows), jnp.int32), pltpu.SemaphoreType.DMA((3, levels // ROWS8))],
        compiler_params=params(41),
        cost_estimate=pl.CostEstimate(
            flops=20 * levels * width * rows, bytes_accessed=10 * levels * width * rows * 4, transcendentals=0
        ),
        name="down_to_surface",
    )(tracers, diffusivity, conductance, sea_mask, order)


def up_kernel(rim, parts, ratios, speed_w, fixed, scale, rims, rim_scale):
    tracers, levels, width, rows = parts.shape
    for lanes in lane_parts(rows):
        lane_count = lanes.stop - lanes.start
        scale_now = jnp.ones((width, lane_count), F32)
        fixed_now = [jnp.zeros((width, lane_count), F32)] * tracers
        for l in reversed(range(levels)):
            if l < levels - 1:
                ratio = ratios[l, :, lanes]
                scale_now = ratio * scale_now
                fixed_now = [parts[t, l, :, lanes] + ratio * fixed_now[t] for t in range(tracers)]
            scale[l, :, lanes] = scale_now
            for t in range(tracers):
                fixed[t, l, :, lanes] = fixed_now[t]
            for c, x in enumerate(rim):
                rim_scale[c, l : l + 1, lanes] = scale_now[x : x + 1]
                for t in range(tracers):
                    rims[t, c, l : l + 1, lanes] = fixed_now[t][x : x + 1]


def speed_kernel(speed, to_east, to_west, order):
    order[...] = jnp.zeros_like(order)
    levels, width, _ = speed.shape
    for l in range(levels):
        to_west[l : l + 1, :] = speed[l, :1, :]
        for c in range(HALO):
            x = width - HALO + c
            to_east[c, l : l + 1, :] = speed[l, x : x + 1, :]


def speed_edges(speed):
    levels, width, rows = speed.shape
    return pl.pallas_call(
        speed_kernel,
        in_specs=[VMEM],
        out_specs=[VMEM] * 3,
        out_shape=[shape_of(HALO, levels, rows), shape_of(levels, rows), shape_of(ROWS8, 128)],
        compiler_params=params(20),
        cost_estimate=pl.CostEstimate(flops=0, bytes_accessed=levels * width * rows * 4, transcendentals=0),
        name="speed_edges",
    )(speed)


def up_from_surface(parts, ratios, arrived, rim):
    count, levels, width, rows = parts.shape
    return pl.pallas_call(
        functools.partial(up_kernel, rim),
        in_specs=[VMEM] * 3,
        out_specs=[VMEM] * 4,
        out_shape=[
            shape_of(count, levels, width, rows),
            shape_of(levels, width, rows),
            shape_of(count, len(rim), levels, rows),
            shape_of(len(rim), levels, rows),
        ],
        input_output_aliases={0: 0, 1: 1},
        compiler_params=params(20),
        cost_estimate=pl.CostEstimate(
            flops=10 * levels * width * rows, bytes_accessed=10 * levels * width * rows * 4, transcendentals=0
        ),
        name="up_from_surface",
    )(parts, ratios, arrived)


def surface_kernel(
    reach, own, peer, first_pair, second_pair, partner, weight, mask, rims, rim_scale, speed_e,
    inflow, surface, open_e, coef_n, *rest,
):
    chunks = (len(rest) - 2) // 2
    send_1, send_2, wide, opened = rest[:chunks], rest[chunks : 2 * chunks], rest[-2], rest[-1]
    channels, width, rows = own.shape
    tracers = channels - 2
    first = 2 * 8
    even = is_even()

    for c in range(channels):
        wide[c, first : first + width, :] = peer[c]
    opened[:width, :] = mask[...]
    opened[width:, :] = jnp.zeros((ROWS8, rows), F32)

    def unpack(east, west):
        for c in range(channels):
            part = slice(c * reach, (c + 1) * reach)
            wide[c, first - reach : first, :] = west[part, :]
            wide[c, first + width : first + width + reach, :] = east[part, :]
        at = slice(channels * reach, channels * reach + HALO)
        opened[width : width + HALO, :] = east[at, :]
        opened[width + ROWS8 - HALO :, :] = west[at, :]

    either(even, unpack, first_pair, second_pair)

    start = lax.axis_index("tile") * width
    total = lax.axis_size("tile") * width
    for lanes in lane_parts(rows, 128):
        position = start + lax.broadcasted_iota(jnp.int32, (width, 128), 0)
        own_slope = own[tracers, :, lanes]
        own_conduct = own[tracers + 1, :, lanes]
        flow = [jnp.zeros((width, 128), F32) for _ in range(tracers)]
        for k in range(partner.shape[0]):
            apart = partner[k, :, lanes] - position
            apart = jnp.where(apart > reach, apart - total, apart)
            apart = jnp.where(apart < -reach, apart + total, apart)
            found = [jnp.zeros((width, 128), F32) for _ in range(channels)]
            for offset in range(-reach, reach + 1):
                hit = apart == offset
                window = slice(first + offset, first + offset + width)
                found = [jnp.where(hit, wide[c, window, lanes], f) for c, f in enumerate(found)]
            series = own_conduct * found[-1] / (own_conduct + found[-1])
            factor = weight[k, :, lanes].astype(F32) * series / (1.0 + series * (own_slope + found[-2]))
            flow = [flow[t] + factor * (own[t, :, lanes] - found[t]) for t in range(tracers)]
        for t in range(tracers):
            into = flow[t] * (-1.0 / QUANT)
            inflow[t, :, lanes] = into
            surface[t, :, lanes] = own[t, :, lanes] + own_slope * into

    size = rim_scale.shape[1] // chunks
    for c in range(chunks):
        part = slice(c * size, (c + 1) * size)
        for t in range(tracers):
            for x in range(HALO):
                e = width - HALO + x
                west = rims[t, x, part, :] + rim_scale[x, part, :] * surface[t, x : x + 1, :]
                east = rims[t, HALO + x, part, :] + rim_scale[HALO + x, part, :] * surface[t, e : e + 1, :]
                send_1[c][t, x] = jnp.where(even, east, west)
                send_2[c][t, x] = jnp.where(even, west, east)

    wide_rows = width + ROWS8
    free = jnp.broadcast_to(lax.axis_index("mp"), (wide_rows, rows)) == 0
    here = jnp.where(free, 1.0, opened[...])
    column = lax.broadcasted_iota(jnp.int32, (wide_rows, rows), 1)
    open_e[...] = here * pltpu.roll(here, wide_rows - 1, 0)
    coef_n[...] = NU * (here * jnp.where(column == rows - 1, 0.0, pltpu.roll(here, rows - 1, 1)))


def exchange_surface(own, peer, first_pair, second_pair, partner, weight, mask, rims, rim_scale, arrived, reach):
    channels, width, rows = own.shape
    count, _, levels, _ = rims.shape
    plane = shape_of(width + ROWS8, rows)
    edge = shape_of(count, HALO, levels // CHUNKS, rows)
    return pl.pallas_call(
        functools.partial(surface_kernel, reach),
        in_specs=[VMEM] * 10,
        out_specs=[VMEM] * (4 + 2 * CHUNKS),
        out_shape=[shape_of(count, width, rows)] * 2 + [plane] * 2 + [edge] * (2 * CHUNKS),
        scratch_shapes=[pltpu.VMEM((channels, 16 + width + 16, rows), F32), pltpu.VMEM((width + ROWS8, rows), F32)],
        compiler_params=params(20),
        cost_estimate=pl.CostEstimate(flops=4000 * width * rows, bytes_accessed=4 * 2**20, transcendentals=0),
        name="exchange_surface",
    )(own, peer, first_pair, second_pair, partner, weight, mask, rims, rim_scale, arrived)


def two_steps(q, a, b, north, first, last, put):
    def along_y(x, value):
        flux = north(x) * (pltpu.roll(value, value.shape[-1] - 1, 1) - value)
        return flux - pltpu.roll(flux, 1, 1)

    here = q(first - 1)
    flux = a(first - 2) * q(first - 2) + b(first - 2) * here
    once_before, flux_before = None, None
    for x in range(first - 1, last + 1):
        east = q(x + 1)
        flux_e = a(x) * here + b(x) * east
        once = (here - (flux_e - flux)) + along_y(x, here)
        if once_before is not None:
            flux_once = a(x - 1) * once_before + b(x - 1) * once
            if flux_before is not None:
                put(x - 1, (once_before - (flux_once - flux_before)) + along_y(x - 1, once_before))
            flux_before = flux_once
        here, flux, once_before = east, flux_e, once


def tiles_in(turn, value):
    levels, width, _ = value.shape
    for j in range(turn.shape[0]):
        turn[j] = value[:, :, 128 * j : 128 * (j + 1)].reshape(levels * width, 128)


def column(turn, x, width):
    parts = [turn[j, pl.ds(x, ROWS8, stride=width), :] for j in range(turn.shape[0])]
    return jnp.concatenate(parts, axis=1)


def put_column(stage, t, start, x, value):
    parts, tracers, levels, width, lanes = stage.shape
    rows = stage.reshape(parts, tracers, levels * width, lanes)
    for j in range(parts):
        at = pl.ds(start * width + x, ROWS8, stride=width)
        rows[j, t, at, :] = value[:, lanes * j : lanes * (j + 1)]


def ring(x, width):
    return x if x >= 0 else width + ROWS8 + x


def spread_north(coef_n, north_s, width):
    for x in range(1 - HALO, width + HALO - 1):
        row = ring(x, width)
        north_s[x + HALO] = jnp.broadcast_to(coef_n[row : row + 1, :], north_s.shape[1:])


def halo_column(even, halo_1, halo_2, t, part, x, width):
    west, c = x < 0, (x + HALO if x < 0 else x - width)
    first, second = halo_1[t, c, part, :], halo_2[t, c, part, :]
    return jnp.where(even, second, first) if west else jnp.where(even, first, second)


def blocks_of(size):
    return [pl.ds(start, ROWS8) for start in range(0, size, ROWS8)]


def faces(coefs, part):
    return [lambda x, i=i: coefs[i, x + HALO, part, :] for i in range(2)]


def first_inner_kernel(
    chunk, fixed, scale, surface, speed, speed_w, speed_e, open_e, coef_n,
    field, rims, coefs, coef_n_out, north_s, turn, turn_speed,
):
    tracers, levels, width, rows = fixed.shape
    size = field.shape[2]
    spread_north(coef_n, north_s, width)
    north = lambda x: north_s[x + HALO]

    def block(i, _):
        start = pl.multiple_of(i * ROWS8, ROWS8)
        part, whole = pl.ds(start, ROWS8), pl.ds(chunk * size + start, ROWS8)
        tiles_in(turn_speed, speed[whole])
        for x in range(-HALO, width + HALO - 1):
            if x < 0:
                u = speed_w[x + HALO, whole, :]
            elif x == width:
                u = speed_e[whole, :]
            else:
                u = column(turn_speed, x, width)
            row = ring(x, width)
            opening = jnp.broadcast_to(open_e[row : row + 1, :], (ROWS8, rows))
            coefs[0, x + HALO, part, :] = opening * (jnp.maximum(u, 0.0) + NU)
            coefs[1, x + HALO, part, :] = opening * (jnp.minimum(u, 0.0) - NU)

        def tracer(t, _):
            tiles_in(turn, fixed[t, whole] + scale[whole] * surface[t][None])

            def q(x):
                value = column(turn, x, width)
                if rim_place(x, width) is not None:
                    rims[t, rim_place(x, width), part, :] = value
                return value

            def put(x, value):
                field[t, x, part, :] = value

            two_steps(q, *faces(coefs, part), north, HALO, width - HALO, put)
            return 0

        lax.fori_loop(0, tracers, tracer, 0)
        return 0

    lax.fori_loop(0, size // ROWS8, block, 0)


def rim_place(x, width):
    if x < 2 * HALO:
        return x
    return x - (width - 4 * HALO) if x >= width - 2 * HALO else None


def halo_column(even, halo_1, halo_2, t, part, x, width):
    west, c = x < 0, (x + HALO if x < 0 else x - width)
    first, second = halo_1[t, c, part, :], halo_2[t, c, part, :]
    return jnp.where(even, second, first) if west else jnp.where(even, first, second)


def first_rim_kernel(rims, coefs, halo_1, halo_2, coef_n, field_in, field, send_1, send_2, coef_n_out, north_s):
    tracers, width, size, rows = field.shape
    even = is_even()
    spread_north(coef_n, north_s, width)
    north = lambda x: north_s[x + HALO]

    def block(i, _):
        part = pl.ds(pl.multiple_of(i * ROWS8, ROWS8), ROWS8)

        def tracer(t, _):
            def q(x):
                if 0 <= x < width:
                    return rims[t, rim_place(x, width), part, :]
                return halo_column(even, halo_1, halo_2, t, part, x, width)

            edge = {}

            def put(x, value):
                field[t, x, part, :] = value
                edge[x] = value

            two_steps(q, *faces(coefs, part), north, 0, HALO, put)
            two_steps(q, *faces(coefs, part), north, width - HALO, width, put)
            for c in range(HALO):
                west, east = edge[c], edge[width - HALO + c]
                send_1[t, c, part, :] = jnp.where(even, east, west)
                send_2[t, c, part, :] = jnp.where(even, west, east)
            return 0

        lax.fori_loop(0, tracers, tracer, 0)
        return 0

    lax.fori_loop(0, size // ROWS8, block, 0)


def last_inner_kernel(field, coefs, coef_n, stage, coef_n_out, north_s):
    tracers, width, size, rows = field.shape
    spread_north(coef_n, north_s, width)
    north = lambda x: north_s[x + HALO]

    def block(i, _):
        start = pl.multiple_of(i * ROWS8, ROWS8)
        part = pl.ds(start, ROWS8)

        def tracer(t, _):
            q = lambda x: field[t, x, part, :]
            put = lambda x, value: put_column(stage, t, start, x, value)
            two_steps(q, *faces(coefs, part), north, HALO, width - HALO, put)
            return 0

        lax.fori_loop(0, tracers, tracer, 0)
        return 0

    lax.fori_loop(0, size // ROWS8, block, 0)


def last_rim_kernel(chunk, field, coefs, halo_1, halo_2, coef_n, stage_in, *refs):
    out, stage, coef_n_out, north_s, sems = refs[-5:]
    tracers, width, size, rows = field.shape
    even = is_even()
    spread_north(coef_n, north_s, width)
    north = lambda x: north_s[x + HALO]
    copies = []
    for i, part in enumerate(blocks_of(size)):

        def tracer(t, _):
            def q(x):
                if 0 <= x < width:
                    return field[t, x, part, :]
                return halo_column(even, halo_1, halo_2, t, part, x, width)

            put = lambda x, value: put_column(stage, t, i * ROWS8, x, value)
            two_steps(q, *faces(coefs, part), north, 0, HALO, put)
            two_steps(q, *faces(coefs, part), north, width - HALO, width, put)
            return 0

        lax.fori_loop(0, tracers, tracer, 0)
        to = pl.ds(chunk * size + i * ROWS8, ROWS8)
        for j in range(stage.shape[0]):
            lanes = pl.ds(128 * j, 128)
            copy = pltpu.make_async_copy(stage.at[j, :, part], out.at[:, to, :, lanes], sems.at[i, j])
            copy.start()
            copies.append(copy)
    for copy in copies:
        copy.wait()


def transport_call(kernel, name, args, out_shape, aliases, scratch, cells, hbm=(), out_hbm=()):
    return pl.pallas_call(
        kernel,
        in_specs=[HBM if i in hbm else VMEM for i in range(len(args))],
        out_specs=[HBM if i in out_hbm else VMEM for i in range(len(out_shape))],
        out_shape=out_shape,
        scratch_shapes=scratch,
        input_output_aliases=aliases,
        compiler_params=params(16),
        cost_estimate=pl.CostEstimate(flops=36 * cells, bytes_accessed=8 * cells, transcendentals=0),
        name=name,
    )(*args)


def north_scratch(width, rows):
    return pltpu.VMEM((width + 2 * HALO, ROWS8, rows), F32)


def first_inner(chunk, fixed, scale, surface, speeds, open_e, coef_n):
    count, levels, width, rows = fixed.shape
    size = levels // CHUNKS
    args = [fixed, scale, surface, *speeds, open_e, coef_n]
    out_shape = [
        shape_of(count, width, size, rows),
        shape_of(count, 4 * HALO, size, rows),
        shape_of(2, width + 2 * HALO - 1, size, rows),
        shape_of(*coef_n.shape),
    ]
    turn = pltpu.VMEM((rows // 128, ROWS8 * width, 128), F32)
    return transport_call(
        functools.partial(first_inner_kernel, chunk), "first_inner", args, out_shape, {len(args) - 1: 3},
        [north_scratch(width, rows), turn, turn], count * size * width * rows,
    )


def first_rim(field, rims, coefs, halos, coef_n):
    count, width, size, rows = field.shape
    args = [rims, coefs, *halos, coef_n, field]
    edge = shape_of(count, HALO, size, rows)
    out_shape = [shape_of(*field.shape), edge, edge, shape_of(*coef_n.shape)]
    field, send_1, send_2, coef_n = transport_call(
        first_rim_kernel, "first_rim", args, out_shape, {5: 0, 4: 3},
        [north_scratch(width, rows)], count * size * 4 * rows,
    )
    return field, (send_1, send_2), coef_n


def last_inner(field, coefs, coef_n):
    count, width, size, rows = field.shape
    out_shape = [shape_of(rows // 128, count, size, width, 128), shape_of(*coef_n.shape)]
    return transport_call(
        last_inner_kernel, "last_inner", [field, coefs, coef_n], out_shape, {2: 1},
        [north_scratch(width, rows)], count * size * width * rows,
    )


def last_rim(chunk, levels, field, coefs, halos, stage, coef_n, result):
    count, width, size, rows = field.shape
    args = [field, coefs, *halos, coef_n, stage]
    aliases = {4: 2, 5: 1}
    if result is not None:
        aliases[6] = 0
        args.append(result)
    out_shape = [shape_of(count, levels, width, rows), shape_of(*stage.shape), shape_of(*coef_n.shape)]
    result, _, coef_n = transport_call(
        functools.partial(last_rim_kernel, chunk), "last_rim", args, out_shape, aliases,
        [north_scratch(width, rows), pltpu.SemaphoreType.DMA((size // ROWS8, rows // 128))],
        count * size * 4 * rows, hbm=(6,), out_hbm=(0,),
    )
    return result, coef_n


def per_device(tracers, diffusivity, conductance, face_velocity, partner, weight, sea_mask):
    tiles = lax.axis_size("tile")
    tracers, diffusivity, conductance = tracers[0], diffusivity[0], conductance[0]
    speed, partner, weight = face_velocity[0], partner[0], weight[0]
    width = tracers.shape[2]
    reach = width // 2 + 1

    def move(value, target_of, swap=False):
        pairs = []
        for m in range(2):
            for t in range(tiles):
                target = (1 - m if swap else m) * tiles + target_of(t) % tiles
                pairs.append((m * tiles + t, target))
        return lax.ppermute(value, ("mp", "tile"), pairs)

    one = lambda t: t + 1 - 2 * (t % 2)
    two = lambda t: t - 1 + 2 * (t % 2)

    to_east, to_west, order = speed_edges(speed)
    speed_w = move(to_east, lambda t: t + 1)
    speed_e = move(to_west, lambda t: t - 1)
    speeds = (speed, speed_w, speed_e)

    parts, ratios, own, mask, terms_1, terms_2 = down_to_surface(
        tracers, diffusivity, conductance, sea_mask, order, reach
    )
    terms_1 = move(terms_1, one, swap=True)
    terms_2 = move(terms_2, two, swap=True)
    peer = move(own, lambda t: t, swap=True)
    rim = tuple(range(HALO)) + tuple(range(width - HALO, width))
    fixed, scale, rims, rim_scale = up_from_surface(parts, ratios, speed_w, rim)

    inflow, surface, open_e, coef_n, *sends = exchange_surface(
        own, peer, terms_1, terms_2, partner, weight, mask, rims, rim_scale, speed_e, reach
    )
    chunks = range(CHUNKS)
    sends = list(zip(sends[:CHUNKS], sends[CHUNKS:]))
    exchange = lambda pair: (move(pair[0], one), move(pair[1], two))

    halos = [exchange(sends[c]) for c in chunks]
    fields, rims, coefs, stages = [None] * CHUNKS, [None] * CHUNKS, [None] * CHUNKS, [None] * CHUNKS
    for c in chunks:
        fields[c], rims[c], coefs[c], coef_n = first_inner(c, fixed, scale, surface, speeds, open_e, coef_n)
    for c in chunks:
        fields[c], sends[c], coef_n = first_rim(fields[c], rims[c], coefs[c], halos[c], coef_n)
        halos[c] = exchange(sends[c])
    for c in chunks:
        stages[c], coef_n = last_inner(fields[c], coefs[c], coef_n)
    result = None
    for c in chunks:
        result, coef_n = last_rim(c, fixed.shape[1], fields[c], coefs[c], halos[c], stages[c], coef_n, result)
    return result[None], inflow[None]


def solution(mesh):
    in_specs = (
        P("mp", None, None, "tile", None),
        P("mp", None, "tile", None),
        P("mp", "tile", None),
        P("mp", None, "tile", None),
        P("mp", None, "tile", None),
        P("mp", None, "tile", None),
        P("tile", None),
    )
    out_specs = (P("mp", None, None, "tile", None), P("mp", None, "tile", None))
    return jax.shard_map(
        per_device, mesh=mesh, in_specs=in_specs, out_specs=out_specs, check_vma=False
    )
```

```python
import functools

import jax
import jax.numpy as jnp
from jax import lax
from jax.experimental import pallas as pl
from jax.experimental.pallas import tpu as pltpu
from jax.sharding import PartitionSpec as P

STEPS = 4
QUANT = 16
NU = 0.12
ROWS8 = 8
CHUNKS = 2
HALO = 2
F32 = jnp.float32
VMEM = pl.BlockSpec(memory_space=pltpu.VMEM)
HBM = pl.BlockSpec(memory_space=pltpu.HBM)


def shape_of(*shape):
    return jax.ShapeDtypeStruct(shape, F32)


def params(mib):
    return pltpu.CompilerParams(vmem_limit_bytes=mib * 2**20)


def is_even():
    return lax.rem(lax.axis_index("tile"), 2) == 0


def either(even, call, first, second):
    @pl.when(even)
    def _():
        call(first, second)

    @pl.when(jnp.logical_not(even))
    def _():
        call(second, first)


def lane_parts(total, size=256):
    size = min(size, total)
    return [slice(start, start + size) for start in range(0, total, size)]


def down_kernel(reach, source, coupling, signed, order, parts, ratios, terms, first_pair, second_pair, sems):
    tracers, levels, width, rows = source.shape
    blocks = levels // ROWS8
    copies = []
    for b in range(blocks):
        part = pl.ds(b * ROWS8, ROWS8)
        pair = [pltpu.make_async_copy(source.at[:, part], parts.at[:, part], sems.at[0, b])]
        part = pl.ds(b * ROWS8, min(ROWS8, levels - 1 - b * ROWS8))
        pair.append(pltpu.make_async_copy(coupling.at[part], ratios.at[part], sems.at[1, b]))
        copies.append(pair)
    for pair in copies:
        for copy in pair:
            copy.start()

    lanes_all = lane_parts(rows)
    zero = jnp.zeros((width, rows // len(lanes_all)), F32)
    states = [(zero, zero, [zero] * tracers, zero)] * len(lanes_all)
    for b in range(blocks):
        for copy in copies[b]:
            copy.wait()
        for p, lanes in enumerate(lanes_all):
            before, ratio, part, inverse = states[p]
            for l in range(b * ROWS8, (b + 1) * ROWS8):
                now = ratios[l, :, lanes] if l < levels - 1 else zero
                inverse = 1.0 / (1.0 + before + now - before * ratio)
                part = [(parts[t, l, :, lanes] + before * part[t]) * inverse for t in range(tracers)]
                ratio = now * inverse
                before = now
                ratios[l, :, lanes] = ratio
                for t in range(tracers):
                    parts[t, l, :, lanes] = part[t]
            states[p] = (before, ratio, part, inverse)
    for lanes, state in zip(lanes_all, states):
        for t in range(tracers):
            terms[t, :, lanes] = state[2][t]
        terms[tracers, :, lanes] = state[3]
    terms[tracers + 1] = jnp.abs(signed[...])
    mask = jnp.where(signed[...] > 0.0, 1.0, 0.0)

    def pack(east, west):
        for c in range(tracers + 2):
            east[c * reach : (c + 1) * reach, :] = terms[c, width - reach :, :]
            west[c * reach : (c + 1) * reach, :] = terms[c, :reach, :]
        at = (tracers + 2) * reach
        east[at : at + HALO, :] = mask[width - HALO :]
        west[at : at + HALO, :] = mask[:HALO]

    either(is_even(), pack, first_pair, second_pair)


def down_to_surface(tracers, diffusivity, signed, order, reach):
    count, levels, width, rows = tracers.shape
    packed = (count + 2) * reach + HALO
    packed = -(-packed // 8) * 8
    return pl.pallas_call(
        functools.partial(down_kernel, reach),
        in_specs=[HBM, HBM, VMEM, VMEM],
        out_specs=[VMEM] * 5,
        out_shape=[
            shape_of(count, levels, width, rows),
            shape_of(levels, width, rows),
            shape_of(count + 2, width, rows),
            shape_of(packed, rows),
            shape_of(packed, rows),
        ],
        scratch_shapes=[pltpu.SemaphoreType.DMA((2, levels // ROWS8))],
        compiler_params=params(41),
        cost_estimate=pl.CostEstimate(
            flops=20 * levels * width * rows, bytes_accessed=10 * levels * width * rows * 4, transcendentals=0
        ),
        name="down_to_surface",
    )(tracers, diffusivity, signed, order)


def up_kernel(rim, parts, ratios, to_west, arrived, fixed, scale, to_west_out, rims, rim_scale):
    tracers, levels, width, rows = parts.shape
    for lanes in lane_parts(rows):
        lane_count = lanes.stop - lanes.start
        scale_now = jnp.ones((width, lane_count), F32)
        fixed_now = [jnp.zeros((width, lane_count), F32)] * tracers
        for l in reversed(range(levels)):
            if l < levels - 1:
                ratio = ratios[l, :, lanes]
                scale_now = ratio * scale_now
                fixed_now = [parts[t, l, :, lanes] + ratio * fixed_now[t] for t in range(tracers)]
            scale[l, :, lanes] = scale_now
            for t in range(tracers):
                fixed[t, l, :, lanes] = fixed_now[t]
            for c, x in enumerate(rim):
                rim_scale[c, l : l + 1, lanes] = scale_now[x : x + 1]
                for t in range(tracers):
                    rims[t, c, l : l + 1, lanes] = fixed_now[t][x : x + 1]


def speed_kernel(speed, to_east, to_west, order):
    order[...] = jnp.zeros_like(order)
    levels, width, _ = speed.shape
    for l in range(levels):
        to_west[l : l + 1, :] = speed[l, :1, :]
        for c in range(HALO):
            x = width - HALO + c
            to_east[c, l : l + 1, :] = speed[l, x : x + 1, :]


def speed_edges(speed):
    levels, width, rows = speed.shape
    return pl.pallas_call(
        speed_kernel,
        in_specs=[VMEM],
        out_specs=[VMEM] * 3,
        out_shape=[shape_of(HALO, levels, rows), shape_of(levels, rows), shape_of(ROWS8, 128)],
        compiler_params=params(20),
        cost_estimate=pl.CostEstimate(flops=0, bytes_accessed=levels * width * rows * 4, transcendentals=0),
        name="speed_edges",
    )(speed)


def up_from_surface(parts, ratios, to_west, arrived, rim):
    count, levels, width, rows = parts.shape
    return pl.pallas_call(
        functools.partial(up_kernel, rim),
        in_specs=[VMEM] * 4,
        out_specs=[VMEM] * 5,
        out_shape=[
            shape_of(count, levels, width, rows),
            shape_of(levels, width, rows),
            shape_of(*to_west.shape),
            shape_of(count, len(rim), levels, rows),
            shape_of(len(rim), levels, rows),
        ],
        input_output_aliases={0: 0, 1: 1, 2: 2},
        compiler_params=params(20),
        cost_estimate=pl.CostEstimate(
            flops=10 * levels * width * rows, bytes_accessed=10 * levels * width * rows * 4, transcendentals=0
        ),
        name="up_from_surface",
    )(parts, ratios, to_west, arrived)


def surface_kernel(
    reach, own, peer, first_pair, second_pair, partner, weight, signed, rims, rim_scale,
    inflow, surface, open_e, coef_n, *rest,
):
    chunks = (len(rest) - 2) // 2
    send_1, send_2, wide, opened = rest[:chunks], rest[chunks : 2 * chunks], rest[-2], rest[-1]
    channels, width, rows = own.shape
    tracers = channels - 2
    first = 2 * 8
    even = is_even()

    for c in range(channels):
        wide[c, first : first + width, :] = peer[c]
    opened[:width, :] = jnp.where(signed[...] > 0.0, 1.0, 0.0)
    opened[width:, :] = jnp.zeros((ROWS8, rows), F32)

    def unpack(east, west):
        for c in range(channels):
            part = slice(c * reach, (c + 1) * reach)
            wide[c, first - reach : first, :] = west[part, :]
            wide[c, first + width : first + width + reach, :] = east[part, :]
        at = slice(channels * reach, channels * reach + HALO)
        opened[width : width + HALO, :] = east[at, :]
        opened[width + ROWS8 - HALO :, :] = west[at, :]

    either(even, unpack, first_pair, second_pair)

    start = lax.axis_index("tile") * width
    total = lax.axis_size("tile") * width
    for lanes in lane_parts(rows, 128):
        position = start + lax.broadcasted_iota(jnp.int32, (width, 128), 0)
        own_slope = own[tracers, :, lanes]
        own_conduct = own[tracers + 1, :, lanes]
        flow = [jnp.zeros((width, 128), F32) for _ in range(tracers)]
        for k in range(partner.shape[0]):
            apart = partner[k, :, lanes] - position
            apart = jnp.where(apart > reach, apart - total, apart)
            apart = jnp.where(apart < -reach, apart + total, apart)
            found = [jnp.zeros((width, 128), F32) for _ in range(channels)]
            for offset in range(-reach, reach + 1):
                hit = apart == offset
                window = slice(first + offset, first + offset + width)
                found = [jnp.where(hit, wide[c, window, lanes], f) for c, f in enumerate(found)]
            series = own_conduct * found[-1] / (own_conduct + found[-1])
            factor = weight[k, :, lanes].astype(F32) * series / (1.0 + series * (own_slope + found[-2]))
            flow = [flow[t] + factor * (own[t, :, lanes] - found[t]) for t in range(tracers)]
        for t in range(tracers):
            into = flow[t] * (-1.0 / QUANT)
            inflow[t, :, lanes] = into
            surface[t, :, lanes] = own[t, :, lanes] + own_slope * into

    size = rim_scale.shape[1] // chunks
    for c in range(chunks):
        part = slice(c * size, (c + 1) * size)
        for t in range(tracers):
            for x in range(HALO):
                e = width - HALO + x
                west = rims[t, x, part, :] + rim_scale[x, part, :] * surface[t, x : x + 1, :]
                east = rims[t, HALO + x, part, :] + rim_scale[HALO + x, part, :] * surface[t, e : e + 1, :]
                send_1[c][t, x] = jnp.where(even, east, west)
                send_2[c][t, x] = jnp.where(even, west, east)

    wide_rows = width + ROWS8
    free = jnp.broadcast_to(lax.axis_index("mp"), (wide_rows, rows)) == 0
    here = jnp.where(free, 1.0, opened[...])
    column = lax.broadcasted_iota(jnp.int32, (wide_rows, rows), 1)
    open_e[...] = here * pltpu.roll(here, wide_rows - 1, 0)
    coef_n[...] = NU * (here * jnp.where(column == rows - 1, 0.0, pltpu.roll(here, rows - 1, 1)))


def exchange_surface(own, peer, first_pair, second_pair, partner, weight, signed, rims, rim_scale, reach):
    channels, width, rows = own.shape
    count, _, levels, _ = rims.shape
    plane = shape_of(width + ROWS8, rows)
    edge = shape_of(count, HALO, levels // CHUNKS, rows)
    return pl.pallas_call(
        functools.partial(surface_kernel, reach),
        in_specs=[VMEM] * 9,
        out_specs=[VMEM] * (4 + 2 * CHUNKS),
        out_shape=[shape_of(count, width, rows)] * 2 + [plane] * 2 + [edge] * (2 * CHUNKS),
        scratch_shapes=[pltpu.VMEM((channels, 16 + width + 16, rows), F32), pltpu.VMEM((width + ROWS8, rows), F32)],
        compiler_params=params(20),
        cost_estimate=pl.CostEstimate(flops=4000 * width * rows, bytes_accessed=4 * 2**20, transcendentals=0),
        name="exchange_surface",
    )(own, peer, first_pair, second_pair, partner, weight, signed, rims, rim_scale)


def two_steps(q, a, b, north, first, last, put):
    def along_y(x, value):
        flux = north(x) * (pltpu.roll(value, value.shape[-1] - 1, 1) - value)
        return flux - pltpu.roll(flux, 1, 1)

    here = q(first - 1)
    flux = a(first - 2) * q(first - 2) + b(first - 2) * here
    once_before, flux_before = None, None
    for x in range(first - 1, last + 1):
        east = q(x + 1)
        flux_e = a(x) * here + b(x) * east
        once = (here - (flux_e - flux)) + along_y(x, here)
        if once_before is not None:
            flux_once = a(x - 1) * once_before + b(x - 1) * once
            if flux_before is not None:
                put(x - 1, (once_before - (flux_once - flux_before)) + along_y(x - 1, once_before))
            flux_before = flux_once
        here, flux, once_before = east, flux_e, once


def tiles_in(turn, value):
    levels, width, _ = value.shape
    for j in range(turn.shape[0]):
        turn[j] = value[:, :, 128 * j : 128 * (j + 1)].reshape(levels * width, 128)


def column(turn, x, width):
    parts = [turn[j, pl.ds(x, ROWS8, stride=width), :] for j in range(turn.shape[0])]
    return jnp.concatenate(parts, axis=1)


def put_column(stage, t, start, x, value):
    parts, tracers, levels, width, lanes = stage.shape
    rows = stage.reshape(parts, tracers, levels * width, lanes)
    for j in range(parts):
        at = pl.ds(start * width + x, ROWS8, stride=width)
        rows[j, t, at, :] = value[:, lanes * j : lanes * (j + 1)]


def ring(x, width):
    return x if x >= 0 else width + ROWS8 + x


def spread_north(coef_n, north_s, width):
    for x in range(1 - HALO, width + HALO - 1):
        row = ring(x, width)
        north_s[x + HALO] = jnp.broadcast_to(coef_n[row : row + 1, :], north_s.shape[1:])


def halo_column(even, halo_1, halo_2, t, part, x, width):
    west, c = x < 0, (x + HALO if x < 0 else x - width)
    first, second = halo_1[t, c, part, :], halo_2[t, c, part, :]
    return jnp.where(even, second, first) if west else jnp.where(even, first, second)


def blocks_of(size):
    return [pl.ds(start, ROWS8) for start in range(0, size, ROWS8)]


def face(coefs, part, x, u, open_e, width):
    row = ring(x, width)
    opening = jnp.broadcast_to(open_e[row : row + 1, :], u.shape)
    coefs[0, x + HALO, part, :] = opening * (jnp.maximum(u, 0.0) + NU)
    coefs[1, x + HALO, part, :] = opening * (jnp.minimum(u, 0.0) - NU)


def faces(coefs, part):
    return [lambda x, i=i: coefs[i, x + HALO, part, :] for i in range(2)]


def first_inner_kernel(
    chunk, fixed, scale, surface, speed, open_e, coef_n,
    field, rims, coefs, coef_n_out, north_s, turn, turn_speed,
):
    tracers, levels, width, rows = fixed.shape
    size = field.shape[2]
    spread_north(coef_n, north_s, width)
    north = lambda x: north_s[x + HALO]

    def block(i, _):
        start = pl.multiple_of(i * ROWS8, ROWS8)
        part, whole = pl.ds(start, ROWS8), pl.ds(chunk * size + start, ROWS8)
        tiles_in(turn_speed, speed[whole])
        for x in range(width):
            face(coefs, part, x, column(turn_speed, x, width), open_e, width)

        def tracer(t, _):
            tiles_in(turn, fixed[t, whole] + scale[whole] * surface[t][None])

            def q(x):
                value = column(turn, x, width)
                if rim_place(x, width) is not None:
                    rims[t, rim_place(x, width), part, :] = value
                return value

            def put(x, value):
                field[t, x, part, :] = value

            two_steps(q, *faces(coefs, part), north, HALO, width - HALO, put)
            return 0

        lax.fori_loop(0, tracers, tracer, 0)
        return 0

    lax.fori_loop(0, size // ROWS8, block, 0)


def rim_place(x, width):
    if x < 2 * HALO:
        return x
    return x - (width - 4 * HALO) if x >= width - 2 * HALO else None


def halo_column(even, halo_1, halo_2, t, part, x, width):
    west, c = x < 0, (x + HALO if x < 0 else x - width)
    first, second = halo_1[t, c, part, :], halo_2[t, c, part, :]
    return jnp.where(even, second, first) if west else jnp.where(even, first, second)


def first_rim_kernel(
    chunk, rims, speed_w, speed_e, open_e, halo_1, halo_2, coef_n, field_in, coefs_in,
    field, coefs, send_1, send_2, coef_n_out, north_s,
):
    tracers, width, size, rows = field.shape
    even = is_even()
    spread_north(coef_n, north_s, width)
    north = lambda x: north_s[x + HALO]

    def block(i, _):
        start = pl.multiple_of(i * ROWS8, ROWS8)
        part, whole = pl.ds(start, ROWS8), pl.ds(chunk * size + start, ROWS8)
        for x in range(-HALO, 0):
            face(coefs, part, x, speed_w[x + HALO, whole, :], open_e, width)
        face(coefs, part, width, speed_e[whole, :], open_e, width)

        def tracer(t):
            def q(x):
                if 0 <= x < width:
                    return rims[t, rim_place(x, width), part, :]
                return halo_column(even, halo_1, halo_2, t, part, x, width)

            edge = {}

            def put(x, value):
                field[t, x, part, :] = value
                edge[x] = value

            two_steps(q, *faces(coefs, part), north, 0, HALO, put)
            two_steps(q, *faces(coefs, part), north, width - HALO, width, put)
            for c in range(HALO):
                west, east = edge[c], edge[width - HALO + c]
                send_1[t, c, part, :] = jnp.where(even, east, west)
                send_2[t, c, part, :] = jnp.where(even, west, east)

        for t in range(tracers):
            tracer(t)
        return 0

    lax.fori_loop(0, size // ROWS8, block, 0)


def last_inner_kernel(field, coefs, coef_n, stage, coef_n_out, north_s):
    tracers, width, size, rows = field.shape
    spread_north(coef_n, north_s, width)
    north = lambda x: north_s[x + HALO]

    def block(i, _):
        start = pl.multiple_of(i * ROWS8, ROWS8)
        part = pl.ds(start, ROWS8)

        def tracer(t, _):
            q = lambda x: field[t, x, part, :]
            put = lambda x, value: put_column(stage, t, start, x, value)
            two_steps(q, *faces(coefs, part), north, HALO, width - HALO, put)
            return 0

        lax.fori_loop(0, tracers, tracer, 0)
        return 0

    lax.fori_loop(0, size // ROWS8, block, 0)


def last_rim_kernel(chunk, field, coefs, halo_1, halo_2, coef_n, stage_in, *refs):
    out, stage, coef_n_out, north_s, sems = refs[-5:]
    tracers, width, size, rows = field.shape
    even = is_even()
    spread_north(coef_n, north_s, width)
    north = lambda x: north_s[x + HALO]
    copies = []
    for i, part in enumerate(blocks_of(size)):

        def tracer(t):
            def q(x):
                if 0 <= x < width:
                    return field[t, x, part, :]
                return halo_column(even, halo_1, halo_2, t, part, x, width)

            put = lambda x, value: put_column(stage, t, i * ROWS8, x, value)
            two_steps(q, *faces(coefs, part), north, 0, HALO, put)
            two_steps(q, *faces(coefs, part), north, width - HALO, width, put)

        for t in range(tracers):
            tracer(t)
        to = pl.ds(chunk * size + i * ROWS8, ROWS8)
        for j in range(stage.shape[0]):
            lanes = pl.ds(128 * j, 128)
            copy = pltpu.make_async_copy(stage.at[j, :, part], out.at[:, to, :, lanes], sems.at[i, j])
            copy.start()
            copies.append(copy)
    for copy in copies:
        copy.wait()


def transport_call(kernel, name, args, out_shape, aliases, scratch, cells, hbm=(), out_hbm=()):
    return pl.pallas_call(
        kernel,
        in_specs=[HBM if i in hbm else VMEM for i in range(len(args))],
        out_specs=[HBM if i in out_hbm else VMEM for i in range(len(out_shape))],
        out_shape=out_shape,
        scratch_shapes=scratch,
        input_output_aliases=aliases,
        compiler_params=params(16),
        cost_estimate=pl.CostEstimate(flops=36 * cells, bytes_accessed=8 * cells, transcendentals=0),
        name=name,
    )(*args)


def north_scratch(width, rows):
    return pltpu.VMEM((width + 2 * HALO, ROWS8, rows), F32)


def first_inner(chunk, fixed, scale, surface, speed, open_e, coef_n):
    count, levels, width, rows = fixed.shape
    size = levels // CHUNKS
    args = [fixed, scale, surface, speed, open_e, coef_n]
    out_shape = [
        shape_of(count, width, size, rows),
        shape_of(count, 4 * HALO, size, rows),
        shape_of(2, width + 2 * HALO - 1, size, rows),
        shape_of(*coef_n.shape),
    ]
    turn = pltpu.VMEM((rows // 128, ROWS8 * width, 128), F32)
    return transport_call(
        functools.partial(first_inner_kernel, chunk), "first_inner", args, out_shape, {len(args) - 1: 3},
        [north_scratch(width, rows), turn, turn], count * size * width * rows,
    )


def first_rim(chunk, field, rims, coefs, speed_w, speed_e, open_e, halos, coef_n):
    count, width, size, rows = field.shape
    args = [rims, speed_w, speed_e, open_e, *halos, coef_n, field, coefs]
    edge = shape_of(count, HALO, size, rows)
    out_shape = [shape_of(*field.shape), shape_of(*coefs.shape), edge, edge, shape_of(*coef_n.shape)]
    field, coefs, send_1, send_2, coef_n = transport_call(
        functools.partial(first_rim_kernel, chunk), "first_rim", args, out_shape, {6: 4, 7: 0, 8: 1},
        [north_scratch(width, rows)], count * size * 4 * rows,
    )
    return field, coefs, (send_1, send_2), coef_n


def last_inner(field, coefs, coef_n):
    count, width, size, rows = field.shape
    out_shape = [shape_of(rows // 128, count, size, width, 128), shape_of(*coef_n.shape)]
    return transport_call(
        last_inner_kernel, "last_inner", [field, coefs, coef_n], out_shape, {2: 1},
        [north_scratch(width, rows)], count * size * width * rows,
    )


def last_rim(chunk, levels, field, coefs, halos, stage, coef_n, result):
    count, width, size, rows = field.shape
    args = [field, coefs, *halos, coef_n, stage]
    aliases = {4: 2, 5: 1}
    if result is not None:
        aliases[6] = 0
        args.append(result)
    out_shape = [shape_of(count, levels, width, rows), shape_of(*stage.shape), shape_of(*coef_n.shape)]
    result, _, coef_n = transport_call(
        functools.partial(last_rim_kernel, chunk), "last_rim", args, out_shape, aliases,
        [north_scratch(width, rows), pltpu.SemaphoreType.DMA((size // ROWS8, rows // 128))],
        count * size * 4 * rows, hbm=(6,), out_hbm=(0,),
    )
    return result, coef_n


def per_device(tracers, diffusivity, conductance, face_velocity, partner, weight, sea_mask):
    tiles = lax.axis_size("tile")
    tracers, diffusivity, conductance = tracers[0], diffusivity[0], conductance[0]
    speed, partner, weight = face_velocity[0], partner[0], weight[0]
    width = tracers.shape[2]
    reach = width // 2 + 1

    def move(value, target_of, swap=False):
        pairs = []
        for m in range(2):
            for t in range(tiles):
                target = (1 - m if swap else m) * tiles + target_of(t) % tiles
                pairs.append((m * tiles + t, target))
        return lax.ppermute(value, ("mp", "tile"), pairs)

    one = lambda t: t + 1 - 2 * (t % 2)
    two = lambda t: t - 1 + 2 * (t % 2)

    to_east, to_west, order = speed_edges(speed)
    speed_w = move(to_east, lambda t: t + 1)
    signed = jnp.where(sea_mask > 0, conductance, -conductance)
    parts, ratios, own, terms_1, terms_2 = down_to_surface(tracers, diffusivity, signed, order, reach)
    terms_1 = move(terms_1, one, swap=True)
    terms_2 = move(terms_2, two, swap=True)
    peer = move(own, lambda t: t, swap=True)
    rim = tuple(range(HALO)) + tuple(range(width - HALO, width))
    fixed, scale, to_west, rims, rim_scale = up_from_surface(parts, ratios, to_west, speed_w, rim)
    speed_e = move(to_west, lambda t: t - 1)

    inflow, surface, open_e, coef_n, *sends = exchange_surface(
        own, peer, terms_1, terms_2, partner, weight, signed, rims, rim_scale, reach
    )
    chunks = range(CHUNKS)
    sends = list(zip(sends[:CHUNKS], sends[CHUNKS:]))
    exchange = lambda pair: (move(pair[0], one), move(pair[1], two))

    halos = [exchange(sends[c]) for c in chunks]
    fields, rims, coefs, stages = [None] * CHUNKS, [None] * CHUNKS, [None] * CHUNKS, [None] * CHUNKS
    for c in chunks:
        fields[c], rims[c], coefs[c], coef_n = first_inner(c, fixed, scale, surface, speed, open_e, coef_n)
    for c in chunks:
        fields[c], coefs[c], sends[c], coef_n = first_rim(
            c, fields[c], rims[c], coefs[c], speed_w, speed_e, open_e, halos[c], coef_n
        )
        halos[c] = exchange(sends[c])
    for c in chunks:
        stages[c], coef_n = last_inner(fields[c], coefs[c], coef_n)
    result = None
    for c in chunks:
        result, coef_n = last_rim(c, fixed.shape[1], fields[c], coefs[c], halos[c], stages[c], coef_n, result)
    return result[None], inflow[None]


def solution(mesh):
    in_specs = (
        P("mp", None, None, "tile", None),
        P("mp", None, "tile", None),
        P("mp", "tile", None),
        P("mp", None, "tile", None),
        P("mp", None, "tile", None),
        P("mp", None, "tile", None),
        P("tile", None),
    )
    out_specs = (P("mp", None, None, "tile", None), P("mp", None, "tile", None))
    return jax.shard_map(
        per_device, mesh=mesh, in_specs=in_specs, out_specs=out_specs, check_vma=False
    )
```

```python
import functools

import jax
import jax.numpy as jnp
from jax import lax
from jax.experimental import pallas as pl
from jax.experimental.pallas import tpu as pltpu
from jax.sharding import PartitionSpec as P

STEPS = 4
QUANT = 16
NU = 0.12
ROWS8 = 8
PARTS = (3, 5)
HALO = 2
F32 = jnp.float32
VMEM = pl.BlockSpec(memory_space=pltpu.VMEM)
HBM = pl.BlockSpec(memory_space=pltpu.HBM)


def shape_of(*shape):
    return jax.ShapeDtypeStruct(shape, F32)


def params(mib):
    return pltpu.CompilerParams(vmem_limit_bytes=mib * 2**20)


def is_even():
    return lax.rem(lax.axis_index("tile"), 2) == 0


def either(even, call, first, second):
    @pl.when(even)
    def _():
        call(first, second)

    @pl.when(jnp.logical_not(even))
    def _():
        call(second, first)


def chunks_of(levels):
    sizes = [part * levels // sum(PARTS) for part in PARTS]
    return [(sum(sizes[:c]), size) for c, size in enumerate(sizes)]


def lane_parts(total, size=256):
    size = min(size, total)
    return [slice(start, start + size) for start in range(0, total, size)]


def down_kernel(reach, source, coupling, signed, order, parts, ratios, terms, first_pair, second_pair, state, part_s, sems):
    tracers, levels, width, rows = source.shape
    blocks = levels // ROWS8

    def copy_of(b):
        part = pl.ds(b * ROWS8, ROWS8)
        return pltpu.make_async_copy(source.at[:, part], parts.at[:, part], sems.at[b])

    couplings = pltpu.make_async_copy(coupling, ratios.at[pl.ds(0, levels - 1)], sems.at[blocks])
    couplings.start()
    for b in range(blocks):
        copy_of(b).start()
    state[...] = jnp.zeros_like(state)
    part_s[...] = jnp.zeros_like(part_s)
    couplings.wait()

    def block(b, _):
        copy_of(b).wait()
        for lanes in lane_parts(rows):
            before, ratio, inverse = [state[i, :, lanes] for i in range(3)]
            part = [part_s[t, :, lanes] for t in range(tracers)]
            for at in range(ROWS8):
                l = b * ROWS8 + at
                now = ratios[l, :, lanes]
                if at == ROWS8 - 1:
                    now = jnp.where(b == blocks - 1, 0.0, now)
                inverse = 1.0 / (1.0 + before + now - before * ratio)
                part = [(parts[t, l, :, lanes] + before * part[t]) * inverse for t in range(tracers)]
                ratio = now * inverse
                before = now
                ratios[l, :, lanes] = ratio
                for t in range(tracers):
                    parts[t, l, :, lanes] = part[t]
            for i, value in enumerate((before, ratio, inverse)):
                state[i, :, lanes] = value
            for t in range(tracers):
                part_s[t, :, lanes] = part[t]
        return 0

    lax.fori_loop(0, blocks, block, 0)
    for t in range(tracers):
        terms[t] = part_s[t]
    terms[tracers] = state[2]
    terms[tracers + 1] = jnp.abs(signed[...])
    mask = jnp.where(signed[...] > 0.0, 1.0, 0.0)

    def pack(east, west):
        for c in range(tracers + 2):
            east[c * reach : (c + 1) * reach, :] = terms[c, width - reach :, :]
            west[c * reach : (c + 1) * reach, :] = terms[c, :reach, :]
        at = (tracers + 2) * reach
        east[at : at + HALO, :] = mask[width - HALO :]
        west[at : at + HALO, :] = mask[:HALO]

    either(is_even(), pack, first_pair, second_pair)


def down_to_surface(tracers, diffusivity, signed, order, reach):
    count, levels, width, rows = tracers.shape
    packed = (count + 2) * reach + HALO
    packed = -(-packed // 8) * 8
    return pl.pallas_call(
        functools.partial(down_kernel, reach),
        in_specs=[HBM, HBM, VMEM, VMEM],
        out_specs=[VMEM] * 5,
        out_shape=[
            shape_of(count, levels, width, rows),
            shape_of(levels, width, rows),
            shape_of(count + 2, width, rows),
            shape_of(packed, rows),
            shape_of(packed, rows),
        ],
        scratch_shapes=[
            pltpu.VMEM((3, width, rows), F32),
            pltpu.VMEM((count, width, rows), F32),
            pltpu.SemaphoreType.DMA((levels // ROWS8 + 1,)),
        ],
        compiler_params=params(41),
        cost_estimate=pl.CostEstimate(
            flops=20 * levels * width * rows, bytes_accessed=10 * levels * width * rows * 4, transcendentals=0
        ),
        name="down_to_surface",
    )(tracers, diffusivity, signed, order)


def up_kernel(rim, parts, ratios, arrived, fixed, scale, rims, rim_scale):
    tracers, levels, width, rows = parts.shape
    blocks = levels // ROWS8
    for lanes in lane_parts(rows):

        def block(i, state):
            b = blocks - 1 - i
            start = pl.multiple_of(b * ROWS8, ROWS8)
            scale_now, fixed_now = state[0], list(state[1:])
            for at in reversed(range(ROWS8)):
                l = start + at
                ratio = ratios[l, :, lanes]
                scale_now = ratio * scale_now
                fixed_now = [parts[t, l, :, lanes] + ratio * fixed_now[t] for t in range(tracers)]
                if at == ROWS8 - 1:
                    scale_now = jnp.where(i == 0, 1.0, scale_now)
                    fixed_now = [jnp.where(i == 0, 0.0, value) for value in fixed_now]
                scale[l, :, lanes] = scale_now
                for t in range(tracers):
                    fixed[t, l, :, lanes] = fixed_now[t]
                for c, x in enumerate(rim):
                    rim_scale[c, b, at : at + 1, lanes] = scale_now[x : x + 1]
                    for t in range(tracers):
                        rims[t, c, b, at : at + 1, lanes] = fixed_now[t][x : x + 1]
            return scale_now, *fixed_now

        zero = jnp.zeros((width, lanes.stop - lanes.start), F32)
        lax.fori_loop(0, blocks, block, (zero,) * (1 + tracers))


def speed_kernel(speed, to_east, to_west, order):
    order[...] = jnp.zeros_like(order)
    levels, width, _ = speed.shape
    for l in range(levels):
        to_west[l : l + 1, :] = speed[l, :1, :]
        for c in range(HALO):
            x = width - HALO + c
            to_east[c, l : l + 1, :] = speed[l, x : x + 1, :]


def speed_edges(speed):
    levels, width, rows = speed.shape
    return pl.pallas_call(
        speed_kernel,
        in_specs=[VMEM],
        out_specs=[VMEM] * 3,
        out_shape=[shape_of(HALO, levels, rows), shape_of(levels, rows), shape_of(ROWS8, 128)],
        compiler_params=params(20),
        cost_estimate=pl.CostEstimate(flops=0, bytes_accessed=levels * width * rows * 4, transcendentals=0),
        name="speed_edges",
    )(speed)


def up_from_surface(parts, ratios, arrived, rim):
    count, levels, width, rows = parts.shape
    fixed, scale, rims, rim_scale = pl.pallas_call(
        functools.partial(up_kernel, rim),
        in_specs=[VMEM] * 3,
        out_specs=[VMEM] * 4,
        out_shape=[
            shape_of(count, levels, width, rows),
            shape_of(levels, width, rows),
            shape_of(count, len(rim), levels // ROWS8, ROWS8, rows),
            shape_of(len(rim), levels // ROWS8, ROWS8, rows),
        ],
        input_output_aliases={0: 0, 1: 1},
        compiler_params=params(20),
        cost_estimate=pl.CostEstimate(
            flops=10 * levels * width * rows, bytes_accessed=10 * levels * width * rows * 4, transcendentals=0
        ),
        name="up_from_surface",
    )(parts, ratios, arrived)
    rims, rim_scale = rims.reshape(count, len(rim), levels, rows), rim_scale.reshape(len(rim), levels, rows)
    return fixed, scale, rims, rim_scale


def surface_kernel(
    reach, own, peer, first_pair, second_pair, partner, weight, signed, rims, rim_scale, arrived,
    inflow, surface, open_e, coef_n, *rest,
):
    chunks = chunks_of(rims.shape[2])
    send_1, send_2, wide, opened = rest[: len(chunks)], rest[len(chunks) : 2 * len(chunks)], rest[-2], rest[-1]
    channels, width, rows = own.shape
    tracers = channels - 2
    first = 2 * 8
    even = is_even()

    for c in range(channels):
        wide[c, first : first + width, :] = peer[c]
    opened[:width, :] = jnp.where(signed[...] > 0.0, 1.0, 0.0)
    opened[width:, :] = jnp.zeros((ROWS8, rows), F32)

    def unpack(east, west):
        for c in range(channels):
            part = slice(c * reach, (c + 1) * reach)
            wide[c, first - reach : first, :] = west[part, :]
            wide[c, first + width : first + width + reach, :] = east[part, :]
        at = slice(channels * reach, channels * reach + HALO)
        opened[width : width + HALO, :] = east[at, :]
        opened[width + ROWS8 - HALO :, :] = west[at, :]

    either(even, unpack, first_pair, second_pair)

    start = lax.axis_index("tile") * width
    total = lax.axis_size("tile") * width
    for lanes in lane_parts(rows, 128):
        position = start + lax.broadcasted_iota(jnp.int32, (width, 128), 0)
        own_slope = own[tracers, :, lanes]
        own_conduct = own[tracers + 1, :, lanes]
        flow = [jnp.zeros((width, 128), F32) for _ in range(tracers)]
        for k in range(partner.shape[0]):
            apart = partner[k, :, lanes] - position
            apart = jnp.where(apart > reach, apart - total, apart)
            apart = jnp.where(apart < -reach, apart + total, apart)
            found = [jnp.zeros((width, 128), F32) for _ in range(channels)]
            for offset in range(-reach, reach + 1):
                hit = apart == offset
                window = slice(first + offset, first + offset + width)
                found = [jnp.where(hit, wide[c, window, lanes], f) for c, f in enumerate(found)]
            series = own_conduct * found[-1] / (own_conduct + found[-1])
            factor = weight[k, :, lanes].astype(F32) * series / (1.0 + series * (own_slope + found[-2]))
            flow = [flow[t] + factor * (own[t, :, lanes] - found[t]) for t in range(tracers)]
        for t in range(tracers):
            into = flow[t] * (-1.0 / QUANT)
            inflow[t, :, lanes] = into
            surface[t, :, lanes] = own[t, :, lanes] + own_slope * into

    for c, (begin, size) in enumerate(chunks):
        part = slice(begin, begin + size)
        for t in range(tracers):
            for x in range(HALO):
                e = width - HALO + x
                west = rims[t, x, part, :] + rim_scale[x, part, :] * surface[t, x : x + 1, :]
                east = rims[t, HALO + x, part, :] + rim_scale[HALO + x, part, :] * surface[t, e : e + 1, :]
                send_1[c][t, x] = jnp.where(even, east, west)
                send_2[c][t, x] = jnp.where(even, west, east)

    wide_rows = width + ROWS8
    free = jnp.broadcast_to(lax.axis_index("mp"), (wide_rows, rows)) == 0
    here = jnp.where(free, 1.0, opened[...])
    column = lax.broadcasted_iota(jnp.int32, (wide_rows, rows), 1)
    open_e[...] = here * pltpu.roll(here, wide_rows - 1, 0)
    coef_n[...] = NU * (here * jnp.where(column == rows - 1, 0.0, pltpu.roll(here, rows - 1, 1)))


def exchange_surface(own, peer, first_pair, second_pair, partner, weight, signed, rims, rim_scale, arrived, reach):
    channels, width, rows = own.shape
    count, _, levels, _ = rims.shape
    plane = shape_of(width + ROWS8, rows)
    edges = [shape_of(count, HALO, size, rows) for _, size in chunks_of(levels)]
    return pl.pallas_call(
        functools.partial(surface_kernel, reach),
        in_specs=[VMEM] * 10,
        out_specs=[VMEM] * (4 + 2 * len(edges)),
        out_shape=[shape_of(count, width, rows)] * 2 + [plane] * 2 + edges * 2,
        scratch_shapes=[pltpu.VMEM((channels, 16 + width + 16, rows), F32), pltpu.VMEM((width + ROWS8, rows), F32)],
        compiler_params=params(20),
        cost_estimate=pl.CostEstimate(flops=4000 * width * rows, bytes_accessed=4 * 2**20, transcendentals=0),
        name="exchange_surface",
    )(own, peer, first_pair, second_pair, partner, weight, signed, rims, rim_scale, arrived)


def two_steps(q, a, b, north, first, last, put):
    def along_y(x, value):
        flux = north(x) * (pltpu.roll(value, value.shape[-1] - 1, 1) - value)
        return flux - pltpu.roll(flux, 1, 1)

    here = q(first - 1)
    flux = a(first - 2) * q(first - 2) + b(first - 2) * here
    once_before, flux_before = None, None
    for x in range(first - 1, last + 1):
        east = q(x + 1)
        flux_e = a(x) * here + b(x) * east
        once = (here - (flux_e - flux)) + along_y(x, here)
        if once_before is not None:
            flux_once = a(x - 1) * once_before + b(x - 1) * once
            if flux_before is not None:
                put(x - 1, (once_before - (flux_once - flux_before)) + along_y(x - 1, once_before))
            flux_before = flux_once
        here, flux, once_before = east, flux_e, once


def tiles_in(turn, value):
    levels, width, _ = value.shape
    for j in range(turn.shape[0]):
        turn[j] = value[:, :, 128 * j : 128 * (j + 1)].reshape(levels * width, 128)


def column(turn, x, width):
    parts = [turn[j, pl.ds(x, ROWS8, stride=width), :] for j in range(turn.shape[0])]
    return jnp.concatenate(parts, axis=1)


def put_column(stage, t, start, x, value):
    parts, tracers, levels, width, lanes = stage.shape
    rows = stage.reshape(parts, tracers, levels * width, lanes)
    for j in range(parts):
        at = pl.ds(start * width + x, ROWS8, stride=width)
        rows[j, t, at, :] = value[:, lanes * j : lanes * (j + 1)]


def ring(x, width):
    return x if x >= 0 else width + ROWS8 + x


def spread_north(coef_n, north_s, width):
    for x in range(1 - HALO, width + HALO - 1):
        row = ring(x, width)
        north_s[x + HALO] = jnp.broadcast_to(coef_n[row : row + 1, :], north_s.shape[1:])


def halo_column(even, halo_1, halo_2, t, part, x, width):
    west, c = x < 0, (x + HALO if x < 0 else x - width)
    first, second = halo_1[t, c, part, :], halo_2[t, c, part, :]
    return jnp.where(even, second, first) if west else jnp.where(even, first, second)


def face(coefs, part, x, u, open_e, width):
    row = ring(x, width)
    opening = jnp.broadcast_to(open_e[row : row + 1, :], u.shape)
    coefs[0, x + HALO, part, :] = opening * (jnp.maximum(u, 0.0) + NU)
    coefs[1, x + HALO, part, :] = opening * (jnp.minimum(u, 0.0) - NU)


def faces(coefs, part):
    return [lambda x, i=i: coefs[i, x + HALO, part, :] for i in range(2)]


def first_inner_kernel(
    begin, fixed, scale, surface, speed, open_e, coef_n,
    field, rims, coefs, coef_n_out, north_s, turn, turn_speed,
):
    tracers, levels, width, rows = fixed.shape
    size = field.shape[2]
    spread_north(coef_n, north_s, width)
    north = lambda x: north_s[x + HALO]

    def block(i, _):
        start = pl.multiple_of(i * ROWS8, ROWS8)
        part, whole = pl.ds(start, ROWS8), pl.ds(begin + start, ROWS8)
        tiles_in(turn_speed, speed[whole])
        for x in range(width):
            face(coefs, part, x, column(turn_speed, x, width), open_e, width)

        def tracer(t, _):
            tiles_in(turn, fixed[t, whole] + scale[whole] * surface[t][None])

            def q(x):
                value = column(turn, x, width)
                if rim_place(x, width) is not None:
                    rims[t, rim_place(x, width), part, :] = value
                return value

            def put(x, value):
                field[t, x, part, :] = value

            two_steps(q, *faces(coefs, part), north, HALO, width - HALO, put)
            return 0

        lax.fori_loop(0, tracers, tracer, 0)
        return 0

    lax.fori_loop(0, size // ROWS8, block, 0)


def rim_place(x, width):
    if x < 2 * HALO:
        return x
    return x - (width - 4 * HALO) if x >= width - 2 * HALO else None


def halo_column(even, halo_1, halo_2, t, part, x, width):
    west, c = x < 0, (x + HALO if x < 0 else x - width)
    first, second = halo_1[t, c, part, :], halo_2[t, c, part, :]
    return jnp.where(even, second, first) if west else jnp.where(even, first, second)


def first_rim_kernel(
    begin, rims, speed_w, speed_e, open_e, halo_1, halo_2, coef_n, field_in, coefs_in,
    field, coefs, send_1, send_2, coef_n_out, north_s,
):
    tracers, width, size, rows = field.shape
    even = is_even()
    spread_north(coef_n, north_s, width)
    north = lambda x: north_s[x + HALO]

    def block(i, _):
        start = pl.multiple_of(i * ROWS8, ROWS8)
        part, whole = pl.ds(start, ROWS8), pl.ds(begin + start, ROWS8)
        for x in range(-HALO, 0):
            face(coefs, part, x, speed_w[x + HALO, whole, :], open_e, width)
        face(coefs, part, width, speed_e[whole, :], open_e, width)

        def tracer(t, _):
            def q(x):
                if 0 <= x < width:
                    return rims[t, rim_place(x, width), part, :]
                return halo_column(even, halo_1, halo_2, t, part, x, width)

            edge = {}

            def put(x, value):
                field[t, x, part, :] = value
                edge[x] = value

            two_steps(q, *faces(coefs, part), north, 0, HALO, put)
            two_steps(q, *faces(coefs, part), north, width - HALO, width, put)
            for c in range(HALO):
                west, east = edge[c], edge[width - HALO + c]
                send_1[t, c, part, :] = jnp.where(even, east, west)
                send_2[t, c, part, :] = jnp.where(even, west, east)
            return 0

        lax.fori_loop(0, tracers, tracer, 0)
        return 0

    lax.fori_loop(0, size // ROWS8, block, 0)


def last_inner_kernel(field, coefs, coef_n, stage, coef_n_out, north_s):
    tracers, width, size, rows = field.shape
    spread_north(coef_n, north_s, width)
    north = lambda x: north_s[x + HALO]

    def block(i, _):
        start = pl.multiple_of(i * ROWS8, ROWS8)
        part = pl.ds(start, ROWS8)

        def tracer(t, _):
            q = lambda x: field[t, x, part, :]
            put = lambda x, value: put_column(stage, t, start, x, value)
            two_steps(q, *faces(coefs, part), north, HALO, width - HALO, put)
            return 0

        lax.fori_loop(0, tracers, tracer, 0)
        return 0

    lax.fori_loop(0, size // ROWS8, block, 0)


def last_rim_kernel(begin, field, coefs, halo_1, halo_2, coef_n, stage_in, *refs):
    out, stage, coef_n_out, north_s, sems = refs[-5:]
    tracers, width, size, rows = field.shape
    even = is_even()
    spread_north(coef_n, north_s, width)
    north = lambda x: north_s[x + HALO]

    def copies_of(i):
        start = pl.multiple_of(i * ROWS8, ROWS8)
        part, to = pl.ds(start, ROWS8), pl.ds(begin + start, ROWS8)
        return [
            pltpu.make_async_copy(stage.at[j, :, part], out.at[:, to, :, pl.ds(128 * j, 128)], sems.at[i, j])
            for j in range(stage.shape[0])
        ]

    def block(i, _):
        start = pl.multiple_of(i * ROWS8, ROWS8)
        part = pl.ds(start, ROWS8)

        def tracer(t, _):
            def q(x):
                if 0 <= x < width:
                    return field[t, x, part, :]
                return halo_column(even, halo_1, halo_2, t, part, x, width)

            put = lambda x, value: put_column(stage, t, start, x, value)
            two_steps(q, *faces(coefs, part), north, 0, HALO, put)
            two_steps(q, *faces(coefs, part), north, width - HALO, width, put)
            return 0

        lax.fori_loop(0, tracers, tracer, 0)
        for copy in copies_of(i):
            copy.start()
        return 0

    def finish(i, _):
        for copy in copies_of(i):
            copy.wait()
        return 0

    lax.fori_loop(0, size // ROWS8, block, 0)
    lax.fori_loop(0, size // ROWS8, finish, 0)


def transport_call(kernel, name, args, out_shape, aliases, scratch, cells, hbm=(), out_hbm=()):
    return pl.pallas_call(
        kernel,
        in_specs=[HBM if i in hbm else VMEM for i in range(len(args))],
        out_specs=[HBM if i in out_hbm else VMEM for i in range(len(out_shape))],
        out_shape=out_shape,
        scratch_shapes=scratch,
        input_output_aliases=aliases,
        compiler_params=params(16),
        cost_estimate=pl.CostEstimate(flops=36 * cells, bytes_accessed=8 * cells, transcendentals=0),
        name=name,
    )(*args)


def north_scratch(width, rows):
    return pltpu.VMEM((width + 2 * HALO, ROWS8, rows), F32)


def first_inner(chunk, fixed, scale, surface, speed, open_e, coef_n):
    count, levels, width, rows = fixed.shape
    begin, size = chunk
    args = [fixed, scale, surface, speed, open_e, coef_n]
    out_shape = [
        shape_of(count, width, size, rows),
        shape_of(count, 4 * HALO, size, rows),
        shape_of(2, width + 2 * HALO - 1, size, rows),
        shape_of(*coef_n.shape),
    ]
    turn = pltpu.VMEM((rows // 128, ROWS8 * width, 128), F32)
    return transport_call(
        functools.partial(first_inner_kernel, begin), "first_inner", args, out_shape, {len(args) - 1: 3},
        [north_scratch(width, rows), turn, turn], count * size * width * rows,
    )


def first_rim(chunk, field, rims, coefs, speed_w, speed_e, open_e, halos, coef_n):
    count, width, size, rows = field.shape
    args = [rims, speed_w, speed_e, open_e, *halos, coef_n, field, coefs]
    edge = shape_of(count, HALO, size, rows)
    out_shape = [shape_of(*field.shape), shape_of(*coefs.shape), edge, edge, shape_of(*coef_n.shape)]
    field, coefs, send_1, send_2, coef_n = transport_call(
        functools.partial(first_rim_kernel, chunk[0]), "first_rim", args, out_shape, {6: 4, 7: 0, 8: 1},
        [north_scratch(width, rows)], count * size * 4 * rows,
    )
    return field, coefs, (send_1, send_2), coef_n


def last_inner(field, coefs, coef_n):
    count, width, size, rows = field.shape
    out_shape = [shape_of(rows // 128, count, size, width, 128), shape_of(*coef_n.shape)]
    return transport_call(
        last_inner_kernel, "last_inner", [field, coefs, coef_n], out_shape, {2: 1},
        [north_scratch(width, rows)], count * size * width * rows,
    )


def last_rim(chunk, levels, field, coefs, halos, stage, coef_n, result):
    count, width, size, rows = field.shape
    args = [field, coefs, *halos, coef_n, stage]
    aliases = {4: 2, 5: 1}
    if result is not None:
        aliases[6] = 0
        args.append(result)
    out_shape = [shape_of(count, levels, width, rows), shape_of(*stage.shape), shape_of(*coef_n.shape)]
    result, _, coef_n = transport_call(
        functools.partial(last_rim_kernel, chunk[0]), "last_rim", args, out_shape, aliases,
        [north_scratch(width, rows), pltpu.SemaphoreType.DMA((size // ROWS8, rows // 128))],
        count * size * 4 * rows, hbm=(6,), out_hbm=(0,),
    )
    return result, coef_n


def per_device(tracers, diffusivity, conductance, face_velocity, partner, weight, sea_mask):
    tiles = lax.axis_size("tile")
    tracers, diffusivity, conductance = tracers[0], diffusivity[0], conductance[0]
    speed, partner, weight = face_velocity[0], partner[0], weight[0]
    width = tracers.shape[2]
    reach = width // 2 + 1

    def move(value, target_of, swap=False):
        pairs = []
        for m in range(2):
            for t in range(tiles):
                target = (1 - m if swap else m) * tiles + target_of(t) % tiles
                pairs.append((m * tiles + t, target))
        return lax.ppermute(value, ("mp", "tile"), pairs)

    one = lambda t: t + 1 - 2 * (t % 2)
    two = lambda t: t - 1 + 2 * (t % 2)

    to_east, to_west, order = speed_edges(speed)
    speed_w = move(to_east, lambda t: t + 1)
    signed = jnp.where(sea_mask > 0, conductance, -conductance)
    parts, ratios, own, terms_1, terms_2 = down_to_surface(tracers, diffusivity, signed, order, reach)
    terms_1 = move(terms_1, one, swap=True)
    terms_2 = move(terms_2, two, swap=True)
    peer = move(own, lambda t: t, swap=True)
    rim = tuple(range(HALO)) + tuple(range(width - HALO, width))
    speed_e = move(to_west, lambda t: t - 1)
    fixed, scale, rims, rim_scale = up_from_surface(parts, ratios, speed_w, rim)

    inflow, surface, open_e, coef_n, *sends = exchange_surface(
        own, peer, terms_1, terms_2, partner, weight, signed, rims, rim_scale, speed_e, reach
    )
    levels = fixed.shape[1]
    chunks = chunks_of(levels)
    every = range(len(chunks))
    exchange = lambda pair: (move(pair[0], one), move(pair[1], two))
    halos = [exchange((sends[c], sends[len(chunks) + c])) for c in every]
    fields, rims, coefs, stages = [[None] * len(chunks) for _ in range(4)]
    for c in every:
        fields[c], rims[c], coefs[c], coef_n = first_inner(chunks[c], fixed, scale, surface, speed, open_e, coef_n)
    for c in every:
        fields[c], coefs[c], pair, coef_n = first_rim(
            chunks[c], fields[c], rims[c], coefs[c], speed_w, speed_e, open_e, halos[c], coef_n
        )
        halos[c] = exchange(pair)
    for c in every:
        stages[c], coef_n = last_inner(fields[c], coefs[c], coef_n)
    result = None
    for c in every:
        result, coef_n = last_rim(chunks[c], levels, fields[c], coefs[c], halos[c], stages[c], coef_n, result)
    return result[None], inflow[None]


def solution(mesh):
    in_specs = (
        P("mp", None, None, "tile", None),
        P("mp", None, "tile", None),
        P("mp", "tile", None),
        P("mp", None, "tile", None),
        P("mp", None, "tile", None),
        P("mp", None, "tile", None),
        P("tile", None),
    )
    out_specs = (P("mp", None, None, "tile", None), P("mp", None, "tile", None))
    return jax.shard_map(
        per_device, mesh=mesh, in_specs=in_specs, out_specs=out_specs, check_vma=False
    )
```

```python
import functools

import jax
import jax.numpy as jnp
from jax import lax
from jax.experimental import pallas as pl
from jax.experimental.pallas import tpu as pltpu
from jax.sharding import PartitionSpec as P

STEPS = 4
QUANT = 16
NU = 0.12
ROWS8 = 8
PARTS = (1, 1)
HALO = 2
F32 = jnp.float32
LITTLE = pl.CostEstimate(flops=1, bytes_accessed=1024, transcendentals=0)
VMEM = pl.BlockSpec(memory_space=pltpu.VMEM)
HBM = pl.BlockSpec(memory_space=pltpu.HBM)


def shape_of(*shape):
    return jax.ShapeDtypeStruct(shape, F32)


def params(mib):
    return pltpu.CompilerParams(vmem_limit_bytes=mib * 2**20)


def is_even():
    return lax.rem(lax.axis_index("tile"), 2) == 0


def either(even, call, first, second):
    @pl.when(even)
    def _():
        call(first, second)

    @pl.when(jnp.logical_not(even))
    def _():
        call(second, first)


def chunks_of(levels):
    sizes = [part * levels // sum(PARTS) for part in PARTS]
    return [(sum(sizes[:c]), size) for c, size in enumerate(sizes)]


def lane_parts(total, size=256):
    size = min(size, total)
    return [slice(start, start + size) for start in range(0, total, size)]


def down_kernel(reach, source, coupling, signed, parts, ratios, terms, first_pair, second_pair, state, part_s, sems):
    tracers, levels, width, rows = source.shape
    blocks = levels // ROWS8

    def copy_of(b):
        part = pl.ds(b * ROWS8, ROWS8)
        return pltpu.make_async_copy(source.at[:, part], parts.at[:, part], sems.at[b])

    couplings = pltpu.make_async_copy(coupling, ratios.at[pl.ds(0, levels - 1)], sems.at[blocks])
    couplings.start()
    for b in range(blocks):
        copy_of(b).start()
    state[...] = jnp.zeros_like(state)
    part_s[...] = jnp.zeros_like(part_s)
    couplings.wait()

    def block(b, _):
        copy_of(b).wait()
        for lanes in lane_parts(rows):
            before, ratio, inverse = [state[i, :, lanes] for i in range(3)]
            part = [part_s[t, :, lanes] for t in range(tracers)]
            for at in range(ROWS8):
                l = b * ROWS8 + at
                now = ratios[l, :, lanes]
                if at == ROWS8 - 1:
                    now = jnp.where(b == blocks - 1, 0.0, now)
                inverse = 1.0 / (1.0 + before + now - before * ratio)
                part = [(parts[t, l, :, lanes] + before * part[t]) * inverse for t in range(tracers)]
                ratio = now * inverse
                before = now
                ratios[l, :, lanes] = ratio
                for t in range(tracers):
                    parts[t, l, :, lanes] = part[t]
            for i, value in enumerate((before, ratio, inverse)):
                state[i, :, lanes] = value
            for t in range(tracers):
                part_s[t, :, lanes] = part[t]
        return 0

    lax.fori_loop(0, blocks, block, 0)
    for t in range(tracers):
        terms[t] = part_s[t]
    terms[tracers] = state[2]
    terms[tracers + 1] = jnp.abs(signed[...])
    mask = jnp.where(signed[...] > 0.0, 1.0, 0.0)

    def pack(east, west):
        for c in range(tracers + 2):
            east[c * reach : (c + 1) * reach, :] = terms[c, width - reach :, :]
            west[c * reach : (c + 1) * reach, :] = terms[c, :reach, :]
        at = (tracers + 2) * reach
        east[at : at + HALO, :] = mask[width - HALO :]
        west[at : at + HALO, :] = mask[:HALO]

    either(is_even(), pack, first_pair, second_pair)


def down_to_surface(tracers, diffusivity, signed, reach):
    count, levels, width, rows = tracers.shape
    packed = (count + 2) * reach + HALO
    packed = -(-packed // 8) * 8
    return pl.pallas_call(
        functools.partial(down_kernel, reach),
        in_specs=[HBM, HBM, VMEM],
        out_specs=[VMEM] * 5,
        out_shape=[
            shape_of(count, levels, width, rows),
            shape_of(levels, width, rows),
            shape_of(count + 2, width, rows),
            shape_of(packed, rows),
            shape_of(packed, rows),
        ],
        scratch_shapes=[
            pltpu.VMEM((3, width, rows), F32),
            pltpu.VMEM((count, width, rows), F32),
            pltpu.SemaphoreType.DMA((levels // ROWS8 + 1,)),
        ],
        compiler_params=params(41),
        cost_estimate=LITTLE,
        name="down_to_surface",
    )(tracers, diffusivity, signed)


def up_kernel(rim, parts, ratios, fixed, scale, rims, rim_scale):
    tracers, levels, width, rows = parts.shape
    blocks = levels // ROWS8
    for lanes in lane_parts(rows):

        def block(i, state):
            b = blocks - 1 - i
            start = pl.multiple_of(b * ROWS8, ROWS8)
            scale_now, fixed_now = state[0], list(state[1:])
            for at in reversed(range(ROWS8)):
                l = start + at
                ratio = ratios[l, :, lanes]
                scale_now = ratio * scale_now
                fixed_now = [parts[t, l, :, lanes] + ratio * fixed_now[t] for t in range(tracers)]
                if at == ROWS8 - 1:
                    scale_now = jnp.where(i == 0, 1.0, scale_now)
                    fixed_now = [jnp.where(i == 0, 0.0, value) for value in fixed_now]
                scale[l, :, lanes] = scale_now
                for t in range(tracers):
                    fixed[t, l, :, lanes] = fixed_now[t]
                for c, x in enumerate(rim):
                    rim_scale[c, b, at : at + 1, lanes] = scale_now[x : x + 1]
                    for t in range(tracers):
                        rims[t, c, b, at : at + 1, lanes] = fixed_now[t][x : x + 1]
            return scale_now, *fixed_now

        zero = jnp.zeros((width, lanes.stop - lanes.start), F32)
        lax.fori_loop(0, blocks, block, (zero,) * (1 + tracers))


def speed_kernel(columns, speed, after, *out):
    for l in range(speed.shape[0]):
        for ref, x in zip(out, columns):
            ref[l : l + 1, :] = speed[l, x : x + 1, :]


def speed_columns(speed, columns, after):
    levels, width, rows = speed.shape
    return pl.pallas_call(
        functools.partial(speed_kernel, columns),
        in_specs=[VMEM] * 2,
        out_specs=[VMEM] * len(columns),
        out_shape=[shape_of(levels, rows)] * len(columns),
        compiler_params=params(20),
        cost_estimate=LITTLE,
        name="speed_columns",
    )(speed, after)


def up_from_surface(parts, ratios, rim):
    count, levels, width, rows = parts.shape
    fixed, scale, rims, rim_scale = pl.pallas_call(
        functools.partial(up_kernel, rim),
        in_specs=[VMEM] * 2,
        out_specs=[VMEM] * 4,
        out_shape=[
            shape_of(count, levels, width, rows),
            shape_of(levels, width, rows),
            shape_of(count, len(rim), levels // ROWS8, ROWS8, rows),
            shape_of(len(rim), levels // ROWS8, ROWS8, rows),
        ],
        input_output_aliases={0: 0, 1: 1},
        compiler_params=params(20),
        cost_estimate=LITTLE,
        name="up_from_surface",
    )(parts, ratios)
    rims, rim_scale = rims.reshape(count, len(rim), levels, rows), rim_scale.reshape(len(rim), levels, rows)
    return fixed, scale, rims, rim_scale


def leaving(u, opening):
    return opening * (jnp.maximum(u, 0.0) + NU), opening * (jnp.minimum(u, 0.0) - NU)


def surface_kernel(
    reach, own, peer, first_pair, second_pair, partner, weight, signed, rims, rim_scale, speed_0, speed_1, arrived,
    inflow, surface, open_e, coef_n, *rest,
):
    chunks = chunks_of(rims.shape[2])
    send_1, send_2, wide, opened = rest[: len(chunks)], rest[len(chunks) : 2 * len(chunks)], rest[-2], rest[-1]
    channels, width, rows = own.shape
    tracers = channels - 2
    first = 2 * 8
    even = is_even()

    for c in range(channels):
        wide[c, first : first + width, :] = peer[c]
    opened[:width, :] = jnp.where(signed[...] > 0.0, 1.0, 0.0)
    opened[width:, :] = jnp.zeros((ROWS8, rows), F32)

    def unpack(east, west):
        for c in range(channels):
            part = slice(c * reach, (c + 1) * reach)
            wide[c, first - reach : first, :] = west[part, :]
            wide[c, first + width : first + width + reach, :] = east[part, :]
        at = slice(channels * reach, channels * reach + HALO)
        opened[width : width + HALO, :] = east[at, :]
        opened[width + ROWS8 - HALO :, :] = west[at, :]

    either(even, unpack, first_pair, second_pair)

    start = lax.axis_index("tile") * width
    total = lax.axis_size("tile") * width
    for lanes in lane_parts(rows, 128):
        position = start + lax.broadcasted_iota(jnp.int32, (width, 128), 0)
        own_slope = own[tracers, :, lanes]
        own_conduct = own[tracers + 1, :, lanes]
        flow = [jnp.zeros((width, 128), F32) for _ in range(tracers)]
        for k in range(partner.shape[0]):
            apart = partner[k, :, lanes] - position
            apart = jnp.where(apart > reach, apart - total, apart)
            apart = jnp.where(apart < -reach, apart + total, apart)
            found = [jnp.zeros((width, 128), F32) for _ in range(channels)]
            for offset in range(-reach, reach + 1):
                hit = apart == offset
                window = slice(first + offset, first + offset + width)
                found = [jnp.where(hit, wide[c, window, lanes], f) for c, f in enumerate(found)]
            series = own_conduct * found[-1] / (own_conduct + found[-1])
            factor = weight[k, :, lanes].astype(F32) * series / (1.0 + series * (own_slope + found[-2]))
            flow = [flow[t] + factor * (own[t, :, lanes] - found[t]) for t in range(tracers)]
        for t in range(tracers):
            into = flow[t] * (-1.0 / QUANT)
            inflow[t, :, lanes] = into
            surface[t, :, lanes] = own[t, :, lanes] + own_slope * into

    wide_rows = width + ROWS8
    free = jnp.broadcast_to(lax.axis_index("mp"), (wide_rows, rows)) == 0
    here = jnp.where(free, 1.0, opened[...])
    column = lax.broadcasted_iota(jnp.int32, (wide_rows, rows), 1)
    open_e[...] = here * pltpu.roll(here, wide_rows - 1, 0)
    coef_n[...] = NU * (here * jnp.where(column == rows - 1, 0.0, pltpu.roll(here, rows - 1, 1)))

    for c, (begin, size) in enumerate(chunks):
        part = slice(begin, begin + size)
        faces_w = leaving(speed_0[part, :], open_e[:1, :])
        faces_e = leaving(speed_1[part, :], open_e[width - 2 : width - 1, :])
        for t in range(tracers):
            columns = []
            for i, x in enumerate((0, 1, width - 2, width - 1)):
                columns.append(rims[t, i, part, :] + rim_scale[i, part, :] * surface[t, x : x + 1, :])
            west = columns[0], faces_w[0] * columns[0] + faces_w[1] * columns[1]
            east = columns[3], faces_e[0] * columns[2] + faces_e[1] * columns[3]
            for i in range(2):
                send_1[c][t, i] = jnp.where(even, east[i], west[i])
                send_2[c][t, i] = jnp.where(even, west[i], east[i])


def exchange_surface(
    own, peer, first_pair, second_pair, partner, weight, signed, rims, rim_scale, speeds, arrived, reach
):
    channels, width, rows = own.shape
    count, _, levels, _ = rims.shape
    plane = shape_of(width + ROWS8, rows)
    edges = [shape_of(count, 2, size, rows) for _, size in chunks_of(levels)]
    return pl.pallas_call(
        functools.partial(surface_kernel, reach),
        in_specs=[VMEM] * 12,
        out_specs=[VMEM] * (4 + 2 * len(edges)),
        out_shape=[shape_of(count, width, rows)] * 2 + [plane] * 2 + edges * 2,
        scratch_shapes=[pltpu.VMEM((channels, 16 + width + 16, rows), F32), pltpu.VMEM((width + ROWS8, rows), F32)],
        compiler_params=params(20),
        cost_estimate=LITTLE,
        name="exchange_surface",
    )(own, peer, first_pair, second_pair, partner, weight, signed, rims, rim_scale, *speeds, arrived)


def two_steps(q, a, b, north, first, last, put, flux_first=None, flux_last=None):
    def along_y(x, value):
        flux = north(x) * (pltpu.roll(value, value.shape[-1] - 1, 1) - value)
        return flux - pltpu.roll(flux, 1, 1)

    here = q(first - 1)
    flux = flux_first
    if flux is None:
        flux = a(first - 2) * q(first - 2) + b(first - 2) * here
    once_before, flux_before = None, None
    for x in range(first - 1, last + 1):
        if x == last and flux_last is not None:
            east, flux_e = None, flux_last
        else:
            east = q(x + 1)
            flux_e = a(x) * here + b(x) * east
        once = (here - (flux_e - flux)) + along_y(x, here)
        if once_before is not None:
            flux_once = a(x - 1) * once_before + b(x - 1) * once
            if flux_before is not None:
                put(x - 1, (once_before - (flux_once - flux_before)) + along_y(x - 1, once_before))
            flux_before = flux_once
        here, flux, once_before = east, flux_e, once


def tiles_in(turn, value):
    levels, width, _ = value.shape
    for j in range(turn.shape[0]):
        turn[j] = value[:, :, 128 * j : 128 * (j + 1)].reshape(levels * width, 128)


def column(turn, x, width):
    parts = [turn[j, pl.ds(x, ROWS8, stride=width), :] for j in range(turn.shape[0])]
    return jnp.concatenate(parts, axis=1)


def put_column(stage, t, start, x, value):
    parts, tracers, levels, width, lanes = stage.shape
    rows = stage.reshape(parts, tracers, levels * width, lanes)
    for j in range(parts):
        at = pl.ds(start * width + x, ROWS8, stride=width)
        rows[j, t, at, :] = value[:, lanes * j : lanes * (j + 1)]


def ring(x, width):
    return x if x >= 0 else width + ROWS8 + x


def spread_north(coef_n, north_s, width):
    for x in range(1 - HALO, width + HALO - 1):
        row = ring(x, width)
        north_s[x + HALO] = jnp.broadcast_to(coef_n[row : row + 1, :], north_s.shape[1:])


def face(coefs, part, x, u, open_e, width):
    row = ring(x, width)
    coefs[0, x + 1, part, :], coefs[1, x + 1, part, :] = leaving(u, open_e[row : row + 1, :])


def faces(coefs, part):
    return [lambda x, i=i: coefs[i, x + 1, part, :] for i in range(2)]


def first_inner_kernel(
    begin, fixed, scale, surface, speed, open_e, coef_n,
    field, rims, coefs, coef_n_out, north_s, turn, turn_speed,
):
    tracers, levels, width, rows = fixed.shape
    size = field.shape[2]
    spread_north(coef_n, north_s, width)
    north = lambda x: north_s[x + HALO]

    def block(i, _):
        start = pl.multiple_of(i * ROWS8, ROWS8)
        part, whole = pl.ds(start, ROWS8), pl.ds(begin + start, ROWS8)
        tiles_in(turn_speed, speed[whole])
        for x in range(width):
            face(coefs, part, x, column(turn_speed, x, width), open_e, width)

        def tracer(t, _):
            tiles_in(turn, fixed[t, whole] + scale[whole] * surface[t][None])

            def q(x):
                value = column(turn, x, width)
                if rim_place(x, width) is not None:
                    rims[t, rim_place(x, width), part, :] = value
                return value

            def put(x, value):
                field[t, x, part, :] = value

            two_steps(q, *faces(coefs, part), north, HALO, width - HALO, put)
            return 0

        lax.fori_loop(0, tracers, tracer, 0)
        return 0

    lax.fori_loop(0, size // ROWS8, block, 0)


def rim_place(x, width):
    if x < 2 * HALO:
        return x
    return x - (width - 4 * HALO) if x >= width - 2 * HALO else None


def both_rims(even, halo_1, halo_2, t, part, own, coefs, north, width, put):
    west = [jnp.where(even, halo_2[t, i, part, :], halo_1[t, i, part, :]) for i in range(2)]
    q = lambda x: west[0] if x < 0 else own(x)
    two_steps(q, *faces(coefs, part), north, 0, HALO, put, flux_first=west[1])
    east = [jnp.where(even, halo_1[t, i, part, :], halo_2[t, i, part, :]) for i in range(2)]
    q = lambda x: east[0] if x == width else own(x)
    two_steps(q, *faces(coefs, part), north, width - HALO, width, put, flux_last=east[1])


def first_rim_kernel(
    begin, rims, speed_w, open_e, halo_1, halo_2, coef_n, field_in, coefs_in,
    field, coefs, send_1, send_2, coef_n_out, north_s,
):
    tracers, width, size, rows = field.shape
    even = is_even()
    spread_north(coef_n, north_s, width)
    north = lambda x: north_s[x + HALO]

    def block(i, _):
        start = pl.multiple_of(i * ROWS8, ROWS8)
        part, whole = pl.ds(start, ROWS8), pl.ds(begin + start, ROWS8)
        face(coefs, part, -1, speed_w[whole, :], open_e, width)
        a, b = faces(coefs, part)

        def tracer(t, _):
            edge = {}

            def put(x, value):
                field[t, x, part, :] = value
                edge[x] = value

            own = lambda x: rims[t, rim_place(x, width), part, :]
            both_rims(even, halo_1, halo_2, t, part, own, coefs, north, width, put)
            end = width - 1
            west = edge[0], a(0) * edge[0] + b(0) * edge[1]
            east = edge[end], a(end - 1) * edge[end - 1] + b(end - 1) * edge[end]
            for i in range(2):
                send_1[t, i, part, :] = jnp.where(even, east[i], west[i])
                send_2[t, i, part, :] = jnp.where(even, west[i], east[i])
            return 0

        lax.fori_loop(0, tracers, tracer, 0)
        return 0

    lax.fori_loop(0, size // ROWS8, block, 0)


def last_inner_kernel(field, coefs, coef_n, stage, coef_n_out, north_s):
    tracers, width, size, rows = field.shape
    spread_north(coef_n, north_s, width)
    north = lambda x: north_s[x + HALO]

    def block(i, _):
        start = pl.multiple_of(i * ROWS8, ROWS8)
        part = pl.ds(start, ROWS8)

        def tracer(t, _):
            q = lambda x: field[t, x, part, :]
            put = lambda x, value: put_column(stage, t, start, x, value)
            two_steps(q, *faces(coefs, part), north, HALO, width - HALO, put)
            return 0

        lax.fori_loop(0, tracers, tracer, 0)
        return 0

    lax.fori_loop(0, size // ROWS8, block, 0)


def last_rim_kernel(begin, field, coefs, halo_1, halo_2, coef_n, stage_in, *refs):
    out, stage, coef_n_out, north_s, sems = refs[-5:]
    tracers, width, size, rows = field.shape
    even = is_even()
    spread_north(coef_n, north_s, width)
    north = lambda x: north_s[x + HALO]

    def copies_of(i):
        start = pl.multiple_of(i * ROWS8, ROWS8)
        part, to = pl.ds(start, ROWS8), pl.ds(begin + start, ROWS8)
        return [
            pltpu.make_async_copy(stage.at[j, :, part], out.at[:, to, :, pl.ds(128 * j, 128)], sems.at[i, j])
            for j in range(stage.shape[0])
        ]

    def block(i, _):
        start = pl.multiple_of(i * ROWS8, ROWS8)
        part = pl.ds(start, ROWS8)

        def tracer(t, _):
            own = lambda x: field[t, x, part, :]
            put = lambda x, value: put_column(stage, t, start, x, value)
            both_rims(even, halo_1, halo_2, t, part, own, coefs, north, width, put)
            return 0

        lax.fori_loop(0, tracers, tracer, 0)
        for copy in copies_of(i):
            copy.start()
        return 0

    def finish(i, _):
        for copy in copies_of(i):
            copy.wait()
        return 0

    lax.fori_loop(0, size // ROWS8, block, 0)
    lax.fori_loop(0, size // ROWS8, finish, 0)


def transport_call(kernel, name, args, out_shape, aliases, scratch, cells, hbm=(), out_hbm=()):
    return pl.pallas_call(
        kernel,
        in_specs=[HBM if i in hbm else VMEM for i in range(len(args))],
        out_specs=[HBM if i in out_hbm else VMEM for i in range(len(out_shape))],
        out_shape=out_shape,
        scratch_shapes=scratch,
        input_output_aliases=aliases,
        compiler_params=params(16),
        cost_estimate=LITTLE,
        name=name,
    )(*args)


def north_scratch(width, rows):
    return pltpu.VMEM((width + 2 * HALO, ROWS8, rows), F32)


def first_inner(chunk, fixed, scale, surface, speed, open_e, coef_n):
    count, levels, width, rows = fixed.shape
    begin, size = chunk
    args = [fixed, scale, surface, speed, open_e, coef_n]
    out_shape = [
        shape_of(count, width, size, rows),
        shape_of(count, 4 * HALO, size, rows),
        shape_of(2, width + 1, size, rows),
        shape_of(*coef_n.shape),
    ]
    turn = pltpu.VMEM((rows // 128, ROWS8 * width, 128), F32)
    return transport_call(
        functools.partial(first_inner_kernel, begin), "first_inner", args, out_shape, {len(args) - 1: 3},
        [north_scratch(width, rows), turn, turn], count * size * width * rows,
    )


def first_rim(chunk, field, rims, coefs, speed_w, open_e, halos, coef_n):
    count, width, size, rows = field.shape
    args = [rims, speed_w, open_e, *halos, coef_n, field, coefs]
    edge = shape_of(count, 2, size, rows)
    out_shape = [shape_of(*field.shape), shape_of(*coefs.shape), edge, edge, shape_of(*coef_n.shape)]
    field, coefs, send_1, send_2, coef_n = transport_call(
        functools.partial(first_rim_kernel, chunk[0]), "first_rim", args, out_shape, {5: 4, 6: 0, 7: 1},
        [north_scratch(width, rows)], count * size * 4 * rows,
    )
    return field, coefs, (send_1, send_2), coef_n


def last_inner(field, coefs, coef_n):
    count, width, size, rows = field.shape
    out_shape = [shape_of(rows // 128, count, size, width, 128), shape_of(*coef_n.shape)]
    return transport_call(
        last_inner_kernel, "last_inner", [field, coefs, coef_n], out_shape, {2: 1},
        [north_scratch(width, rows)], count * size * width * rows,
    )


def last_rim(chunk, levels, field, coefs, halos, stage, coef_n, result):
    count, width, size, rows = field.shape
    args = [field, coefs, *halos, coef_n, stage]
    aliases = {4: 2, 5: 1}
    if result is not None:
        aliases[6] = 0
        args.append(result)
    out_shape = [shape_of(count, levels, width, rows), shape_of(*stage.shape), shape_of(*coef_n.shape)]
    result, _, coef_n = transport_call(
        functools.partial(last_rim_kernel, chunk[0]), "last_rim", args, out_shape, aliases,
        [north_scratch(width, rows), pltpu.SemaphoreType.DMA((size // ROWS8, rows // 128))],
        count * size * 4 * rows, hbm=(6,), out_hbm=(0,),
    )
    return result, coef_n


def per_device(tracers, diffusivity, conductance, face_velocity, partner, weight, sea_mask):
    tiles = lax.axis_size("tile")
    tracers, diffusivity, conductance = tracers[0], diffusivity[0], conductance[0]
    speed, partner, weight = face_velocity[0], partner[0], weight[0]
    width = tracers.shape[2]
    reach = width // 2 + 1

    def move(value, target_of, swap=False):
        pairs = []
        for m in range(2):
            for t in range(tiles):
                target = (1 - m if swap else m) * tiles + target_of(t) % tiles
                pairs.append((m * tiles + t, target))
        return lax.ppermute(value, ("mp", "tile"), pairs)

    one = lambda t: t + 1 - 2 * (t % 2)
    two = lambda t: t - 1 + 2 * (t % 2)

    signed = jnp.where(sea_mask > 0, conductance, -conductance)
    parts, ratios, own, terms_1, terms_2 = down_to_surface(tracers, diffusivity, signed, reach)
    terms_1 = move(terms_1, one, swap=True)
    terms_2 = move(terms_2, two, swap=True)
    peer = move(own, lambda t: t, swap=True)
    *speeds, to_east = speed_columns(speed, (0, width - 2, width - 1), own)
    speed_w = move(to_east, lambda t: t + 1)
    rim = (0, 1, width - 2, width - 1)
    fixed, scale, rims, rim_scale = up_from_surface(parts, ratios, rim)

    inflow, surface, open_e, coef_n, *sends = exchange_surface(
        own, peer, terms_1, terms_2, partner, weight, signed, rims, rim_scale, speeds, speed_w, reach
    )
    levels = fixed.shape[1]
    chunks = chunks_of(levels)
    every = range(len(chunks))
    exchange = lambda pair: (move(pair[0], one), move(pair[1], two))
    halos = [exchange((sends[c], sends[len(chunks) + c])) for c in every]
    fields, rims, coefs, stages = [[None] * len(chunks) for _ in range(4)]
    for c in every:
        fields[c], rims[c], coefs[c], coef_n = first_inner(chunks[c], fixed, scale, surface, speed, open_e, coef_n)
    for c in every:
        fields[c], coefs[c], pair, coef_n = first_rim(
            chunks[c], fields[c], rims[c], coefs[c], speed_w, open_e, halos[c], coef_n
        )
        halos[c] = exchange(pair)
    for c in every:
        stages[c], coef_n = last_inner(fields[c], coefs[c], coef_n)
    result = None
    for c in every:
        result, coef_n = last_rim(chunks[c], levels, fields[c], coefs[c], halos[c], stages[c], coef_n, result)
    return result[None], inflow[None]


def solution(mesh):
    in_specs = (
        P("mp", None, None, "tile", None),
        P("mp", None, "tile", None),
        P("mp", "tile", None),
        P("mp", None, "tile", None),
        P("mp", None, "tile", None),
        P("mp", None, "tile", None),
        P("tile", None),
    )
    out_specs = (P("mp", None, None, "tile", None), P("mp", None, "tile", None))
    return jax.shard_map(
        per_device, mesh=mesh, in_specs=in_specs, out_specs=out_specs, check_vma=False
    )
```

```python
import functools

import jax
import jax.numpy as jnp
from jax import lax
from jax.experimental import pallas as pl
from jax.experimental.pallas import tpu as pltpu
from jax.sharding import PartitionSpec as P

STEPS = 4
QUANT = 16
NU = 0.12
ROWS8 = 8
PARTS = (1, 1)
HALO = 2
F32 = jnp.float32
LITTLE = pl.CostEstimate(flops=1, bytes_accessed=1024, transcendentals=0)
VMEM = pl.BlockSpec(memory_space=pltpu.VMEM)
HBM = pl.BlockSpec(memory_space=pltpu.HBM)


def shape_of(*shape):
    return jax.ShapeDtypeStruct(shape, F32)


def params(mib):
    return pltpu.CompilerParams(vmem_limit_bytes=mib * 2**20)


def is_even():
    return lax.rem(lax.axis_index("tile"), 2) == 0


def either(even, call, first, second):
    @pl.when(even)
    def _():
        call(first, second)

    @pl.when(jnp.logical_not(even))
    def _():
        call(second, first)


def chunks_of(levels):
    sizes = [part * levels // sum(PARTS) for part in PARTS]
    return [(sum(sizes[:c]), size) for c, size in enumerate(sizes)]


def lane_parts(total, size=256):
    size = min(size, total)
    return [slice(start, start + size) for start in range(0, total, size)]


def down_kernel(reach, source, coupling, signed, order, parts, ratios, slope, terms, first_pair, second_pair, state, part_s, sems):
    tracers, levels, width, rows = source.shape
    blocks = levels // ROWS8

    def copy_of(b):
        part = pl.ds(b * ROWS8, ROWS8)
        return pltpu.make_async_copy(source.at[:, part], parts.at[:, part], sems.at[b])

    couplings = pltpu.make_async_copy(coupling, ratios.at[pl.ds(0, levels - 1)], sems.at[blocks])
    couplings.start()
    for b in range(blocks):
        copy_of(b).start()
    state[...] = jnp.zeros_like(state)
    part_s[...] = jnp.zeros_like(part_s)
    couplings.wait()

    def block(b, _):
        copy_of(b).wait()
        for lanes in lane_parts(rows):
            before, ratio, inverse = [state[i, :, lanes] for i in range(3)]
            part = [part_s[t, :, lanes] for t in range(tracers)]
            for at in range(ROWS8):
                l = b * ROWS8 + at
                now = ratios[l, :, lanes]
                if at == ROWS8 - 1:
                    now = jnp.where(b == blocks - 1, 0.0, now)
                inverse = 1.0 / (1.0 + before + now - before * ratio)
                part = [(parts[t, l, :, lanes] + before * part[t]) * inverse for t in range(tracers)]
                ratio = now * inverse
                before = now
                ratios[l, :, lanes] = ratio
                for t in range(tracers):
                    parts[t, l, :, lanes] = part[t]
            for i, value in enumerate((before, ratio, inverse)):
                state[i, :, lanes] = value
            for t in range(tracers):
                part_s[t, :, lanes] = part[t]
        return 0

    lax.fori_loop(0, blocks, block, 0)
    for t in range(tracers):
        terms[t] = part_s[t]
    slope[...] = state[2]
    terms[tracers] = 1.0 / jnp.abs(signed[...]) + state[2]
    mask = jnp.where(signed[...] > 0.0, 1.0, 0.0)

    def pack(east, west):
        for c in range(tracers + 1):
            east[c * reach : (c + 1) * reach, :] = terms[c, width - reach :, :]
            west[c * reach : (c + 1) * reach, :] = terms[c, :reach, :]
        at = (tracers + 1) * reach
        east[at : at + HALO, :] = mask[width - HALO :]
        west[at : at + HALO, :] = mask[:HALO]

    either(is_even(), pack, first_pair, second_pair)


def down_to_surface(tracers, diffusivity, signed, order, reach):
    count, levels, width, rows = tracers.shape
    packed = (count + 1) * reach + HALO
    packed = -(-packed // 8) * 8
    return pl.pallas_call(
        functools.partial(down_kernel, reach),
        in_specs=[HBM, HBM, VMEM, VMEM],
        out_specs=[VMEM] * 6,
        out_shape=[
            shape_of(count, levels, width, rows),
            shape_of(levels, width, rows),
            shape_of(width, rows),
            shape_of(count + 1, width, rows),
            shape_of(packed, rows),
            shape_of(packed, rows),
        ],
        scratch_shapes=[
            pltpu.VMEM((3, width, rows), F32),
            pltpu.VMEM((count, width, rows), F32),
            pltpu.SemaphoreType.DMA((levels // ROWS8 + 1,)),
        ],
        compiler_params=params(41),
        cost_estimate=LITTLE,
        name="down_to_surface",
    )(tracers, diffusivity, signed, order)


def up_kernel(rim, parts, ratios, arrived, fixed, scale, rims, rim_scale):
    tracers, levels, width, rows = parts.shape
    blocks = levels // ROWS8
    for lanes in lane_parts(rows):

        def block(i, state):
            b = blocks - 1 - i
            start = pl.multiple_of(b * ROWS8, ROWS8)
            scale_now, fixed_now = state[0], list(state[1:])
            for at in reversed(range(ROWS8)):
                l = start + at
                ratio = ratios[l, :, lanes]
                scale_now = ratio * scale_now
                fixed_now = [parts[t, l, :, lanes] + ratio * fixed_now[t] for t in range(tracers)]
                if at == ROWS8 - 1:
                    scale_now = jnp.where(i == 0, 1.0, scale_now)
                    fixed_now = [jnp.where(i == 0, 0.0, value) for value in fixed_now]
                scale[l, :, lanes] = scale_now
                for t in range(tracers):
                    fixed[t, l, :, lanes] = fixed_now[t]
                for c, x in enumerate(rim):
                    rim_scale[c, b, at : at + 1, lanes] = scale_now[x : x + 1]
                    for t in range(tracers):
                        rims[t, c, b, at : at + 1, lanes] = fixed_now[t][x : x + 1]
            return scale_now, *fixed_now

        zero = jnp.zeros((width, lanes.stop - lanes.start), F32)
        lax.fori_loop(0, blocks, block, (zero,) * (1 + tracers))


def speed_kernel(columns, speed, *out):
    out[-1][...] = jnp.zeros_like(out[-1])
    out[-2][speed.shape[0] :, :] = jnp.zeros((out[-2].shape[0] - speed.shape[0], out[-2].shape[1]), F32)
    for l in range(speed.shape[0]):
        for ref, x in zip(out, columns):
            ref[l : l + 1, :] = speed[l, x : x + 1, :]


def speed_columns(speed, columns):
    levels, width, rows = speed.shape
    return pl.pallas_call(
        functools.partial(speed_kernel, columns),
        in_specs=[VMEM],
        out_specs=[VMEM] * (len(columns) + 1),
        out_shape=[shape_of(levels, rows)] * (len(columns) - 1)
        + [shape_of(levels + levels // 2, rows), shape_of(ROWS8, 128)],
        compiler_params=params(20),
        cost_estimate=LITTLE,
        name="speed_columns",
    )(speed)


def up_from_surface(parts, ratios, arrived, rim):
    count, levels, width, rows = parts.shape
    fixed, scale, rims, rim_scale = pl.pallas_call(
        functools.partial(up_kernel, rim),
        in_specs=[VMEM] * 3,
        out_specs=[VMEM] * 4,
        out_shape=[
            shape_of(count, levels, width, rows),
            shape_of(levels, width, rows),
            shape_of(count, len(rim), levels // ROWS8, ROWS8, rows),
            shape_of(len(rim), levels // ROWS8, ROWS8, rows),
        ],
        input_output_aliases={0: 0, 1: 1},
        compiler_params=params(20),
        cost_estimate=LITTLE,
        name="up_from_surface",
    )(parts, ratios, arrived)
    rims, rim_scale = rims.reshape(count, len(rim), levels, rows), rim_scale.reshape(len(rim), levels, rows)
    return fixed, scale, rims, rim_scale


def leaving(u, opening):
    return opening * (jnp.maximum(u, 0.0) + NU), opening * (jnp.minimum(u, 0.0) - NU)


def surface_kernel(
    reach, own, slope, peer, first_pair, second_pair, partner, weight, signed, rims, rim_scale, speed_0, speed_1,
    inflow, surface, open_e, coef_n, *rest,
):
    chunks = chunks_of(rims.shape[2])
    send_1, send_2, wide, opened = rest[: len(chunks)], rest[len(chunks) : 2 * len(chunks)], rest[-2], rest[-1]
    channels, width, rows = own.shape
    tracers = channels - 1
    first = 2 * 8
    even = is_even()

    for c in range(channels):
        wide[c, first : first + width, :] = peer[c]
    opened[:width, :] = jnp.where(signed[...] > 0.0, 1.0, 0.0)
    opened[width:, :] = jnp.zeros((ROWS8, rows), F32)

    def unpack(east, west):
        for c in range(channels):
            part = slice(c * reach, (c + 1) * reach)
            wide[c, first - reach : first, :] = west[part, :]
            wide[c, first + width : first + width + reach, :] = east[part, :]
        at = slice(channels * reach, channels * reach + HALO)
        opened[width : width + HALO, :] = east[at, :]
        opened[width + ROWS8 - HALO :, :] = west[at, :]

    either(even, unpack, first_pair, second_pair)

    start = lax.axis_index("tile") * width
    total = lax.axis_size("tile") * width
    for lanes in lane_parts(rows, 128):
        position = start + lax.broadcasted_iota(jnp.int32, (width, 128), 0)
        own_rest = own[tracers, :, lanes]
        flow = [jnp.zeros((width, 128), F32) for _ in range(tracers)]
        for k in range(partner.shape[0]):
            apart = partner[k, :, lanes] - position
            apart = jnp.where(apart > reach, apart - total, apart)
            apart = jnp.where(apart < -reach, apart + total, apart)
            found = [jnp.zeros((width, 128), F32) for _ in range(channels)]
            for offset in range(-reach, reach + 1):
                hit = apart == offset
                window = slice(first + offset, first + offset + width)
                found = [jnp.where(hit, wide[c, window, lanes], f) for c, f in enumerate(found)]
            factor = weight[k, :, lanes].astype(F32) / (own_rest + found[-1])
            flow = [flow[t] + factor * (own[t, :, lanes] - found[t]) for t in range(tracers)]
        for t in range(tracers):
            into = flow[t] * (-1.0 / QUANT)
            inflow[t, :, lanes] = into
            surface[t, :, lanes] = own[t, :, lanes] + slope[:, lanes] * into

    wide_rows = width + ROWS8
    free = jnp.broadcast_to(lax.axis_index("mp"), (wide_rows, rows)) == 0
    here = jnp.where(free, 1.0, opened[...])
    column = lax.broadcasted_iota(jnp.int32, (wide_rows, rows), 1)
    open_e[...] = here * pltpu.roll(here, wide_rows - 1, 0)
    coef_n[...] = NU * (here * jnp.where(column == rows - 1, 0.0, pltpu.roll(here, rows - 1, 1)))

    for c, (begin, size) in enumerate(chunks):
        part = slice(begin, begin + size)
        faces_w = leaving(speed_0[part, :], open_e[:1, :])
        faces_e = leaving(speed_1[part, :], open_e[width - 2 : width - 1, :])
        for t in range(tracers):
            columns = []
            for i, x in enumerate((0, 1, width - 2, width - 1)):
                columns.append(rims[t, i, part, :] + rim_scale[i, part, :] * surface[t, x : x + 1, :])
            west = columns[0], faces_w[0] * columns[0] + faces_w[1] * columns[1]
            east = columns[3], faces_e[0] * columns[2] + faces_e[1] * columns[3]
            for i in range(2):
                send_1[c][t, i] = jnp.where(even, east[i], west[i])
                send_2[c][t, i] = jnp.where(even, west[i], east[i])


def exchange_surface(
    own, slope, peer, first_pair, second_pair, partner, weight, signed, rims, rim_scale, speeds, reach
):
    channels, width, rows = own.shape
    count, _, levels, _ = rims.shape
    plane = shape_of(width + ROWS8, rows)
    edges = [shape_of(count, 2, size, rows) for _, size in chunks_of(levels)]
    return pl.pallas_call(
        functools.partial(surface_kernel, reach),
        in_specs=[VMEM] * 12,
        out_specs=[VMEM] * (4 + 2 * len(edges)),
        out_shape=[shape_of(count, width, rows)] * 2 + [plane] * 2 + edges * 2,
        scratch_shapes=[pltpu.VMEM((channels, 16 + width + 16, rows), F32), pltpu.VMEM((width + ROWS8, rows), F32)],
        compiler_params=params(20),
        cost_estimate=LITTLE,
        name="exchange_surface",
    )(own, slope, peer, first_pair, second_pair, partner, weight, signed, rims, rim_scale, *speeds)


def two_steps(q, a, b, north, first, last, put, flux_first=None, flux_last=None):
    def along_y(x, value):
        flux = north(x) * (pltpu.roll(value, value.shape[-1] - 1, 1) - value)
        return flux - pltpu.roll(flux, 1, 1)

    here = q(first - 1)
    flux = flux_first
    if flux is None:
        flux = a(first - 2) * q(first - 2) + b(first - 2) * here
    once_before, flux_before = None, None
    for x in range(first - 1, last + 1):
        if x == last and flux_last is not None:
            east, flux_e = None, flux_last
        else:
            east = q(x + 1)
            flux_e = a(x) * here + b(x) * east
        once = (here - (flux_e - flux)) + along_y(x, here)
        if once_before is not None:
            flux_once = a(x - 1) * once_before + b(x - 1) * once
            if flux_before is not None:
                put(x - 1, (once_before - (flux_once - flux_before)) + along_y(x - 1, once_before))
            flux_before = flux_once
        here, flux, once_before = east, flux_e, once


def tiles_in(turn, value):
    levels, width, _ = value.shape
    for j in range(turn.shape[0]):
        turn[j] = value[:, :, 128 * j : 128 * (j + 1)].reshape(levels * width, 128)


def column(turn, x, width):
    parts = [turn[j, pl.ds(x, ROWS8, stride=width), :] for j in range(turn.shape[0])]
    return jnp.concatenate(parts, axis=1)


def put_column(stage, t, start, x, value):
    parts, tracers, levels, width, lanes = stage.shape
    rows = stage.reshape(parts, tracers, levels * width, lanes)
    for j in range(parts):
        at = pl.ds(start * width + x, ROWS8, stride=width)
        rows[j, t, at, :] = value[:, lanes * j : lanes * (j + 1)]


def ring(x, width):
    return x if x >= 0 else width + ROWS8 + x


def spread_north(coef_n, north_s, width):
    for x in range(1 - HALO, width + HALO - 1):
        row = ring(x, width)
        north_s[x + HALO] = jnp.broadcast_to(coef_n[row : row + 1, :], north_s.shape[1:])


def face(coefs, part, x, u, open_e, width):
    row = ring(x, width)
    coefs[0, x + 1, part, :], coefs[1, x + 1, part, :] = leaving(u, open_e[row : row + 1, :])


def faces(coefs, part):
    return [lambda x, i=i: coefs[i, x + 1, part, :] for i in range(2)]


def first_inner_kernel(
    begin, fixed, scale, surface, speed, open_e, coef_n,
    field, rims, coefs, coef_n_out, north_s, turn, turn_speed,
):
    tracers, levels, width, rows = fixed.shape
    size = field.shape[2]
    spread_north(coef_n, north_s, width)
    north = lambda x: north_s[x + HALO]

    def block(i, _):
        start = pl.multiple_of(i * ROWS8, ROWS8)
        part, whole = pl.ds(start, ROWS8), pl.ds(begin + start, ROWS8)
        tiles_in(turn_speed, speed[whole])
        for x in range(width):
            face(coefs, part, x, column(turn_speed, x, width), open_e, width)

        def tracer(t, _):
            tiles_in(turn, fixed[t, whole] + scale[whole] * surface[t][None])

            def q(x):
                value = column(turn, x, width)
                if rim_place(x, width) is not None:
                    rims[t, rim_place(x, width), part, :] = value
                return value

            def put(x, value):
                field[t, x, part, :] = value

            two_steps(q, *faces(coefs, part), north, HALO, width - HALO, put)
            return 0

        lax.fori_loop(0, tracers, tracer, 0)
        return 0

    lax.fori_loop(0, size // ROWS8, block, 0)


def rim_place(x, width):
    if x < 2 * HALO:
        return x
    return x - (width - 4 * HALO) if x >= width - 2 * HALO else None


def both_rims(even, halo_1, halo_2, t, part, own, coefs, north, width, put):
    west = [jnp.where(even, halo_2[t, i, part, :], halo_1[t, i, part, :]) for i in range(2)]
    q = lambda x: west[0] if x < 0 else own(x)
    two_steps(q, *faces(coefs, part), north, 0, HALO, put, flux_first=west[1])
    east = [jnp.where(even, halo_1[t, i, part, :], halo_2[t, i, part, :]) for i in range(2)]
    q = lambda x: east[0] if x == width else own(x)
    two_steps(q, *faces(coefs, part), north, width - HALO, width, put, flux_last=east[1])


def first_rim_kernel(
    begin, rims, speed_w, open_e, halo_1, halo_2, coef_n, field_in, coefs_in,
    field, coefs, send_1, send_2, coef_n_out, north_s,
):
    tracers, width, size, rows = field.shape
    even = is_even()
    spread_north(coef_n, north_s, width)
    north = lambda x: north_s[x + HALO]

    def block(i, _):
        start = pl.multiple_of(i * ROWS8, ROWS8)
        part, whole = pl.ds(start, ROWS8), pl.ds(begin + start, ROWS8)
        face(coefs, part, -1, speed_w[whole, :], open_e, width)
        a, b = faces(coefs, part)

        def tracer(t, _):
            edge = {}

            def put(x, value):
                field[t, x, part, :] = value
                edge[x] = value

            own = lambda x: rims[t, rim_place(x, width), part, :]
            both_rims(even, halo_1, halo_2, t, part, own, coefs, north, width, put)
            end = width - 1
            west = edge[0], a(0) * edge[0] + b(0) * edge[1]
            east = edge[end], a(end - 1) * edge[end - 1] + b(end - 1) * edge[end]
            for i in range(2):
                send_1[t, i, part, :] = jnp.where(even, east[i], west[i])
                send_2[t, i, part, :] = jnp.where(even, west[i], east[i])
            return 0

        lax.fori_loop(0, tracers, tracer, 0)
        return 0

    lax.fori_loop(0, size // ROWS8, block, 0)


def last_inner_kernel(field, coefs, coef_n, stage, coef_n_out, north_s):
    tracers, width, size, rows = field.shape
    spread_north(coef_n, north_s, width)
    north = lambda x: north_s[x + HALO]

    def block(i, _):
        start = pl.multiple_of(i * ROWS8, ROWS8)
        part = pl.ds(start, ROWS8)

        def tracer(t, _):
            q = lambda x: field[t, x, part, :]
            put = lambda x, value: put_column(stage, t, start, x, value)
            two_steps(q, *faces(coefs, part), north, HALO, width - HALO, put)
            return 0

        lax.fori_loop(0, tracers, tracer, 0)
        return 0

    lax.fori_loop(0, size // ROWS8, block, 0)


def last_rim_kernel(begin, field, coefs, halo_1, halo_2, coef_n, stage_in, *refs):
    out, stage, coef_n_out, north_s, sems = refs[-5:]
    tracers, width, size, rows = field.shape
    even = is_even()
    spread_north(coef_n, north_s, width)
    north = lambda x: north_s[x + HALO]

    def copies_of(i):
        start = pl.multiple_of(i * ROWS8, ROWS8)
        part, to = pl.ds(start, ROWS8), pl.ds(begin + start, ROWS8)
        return [
            pltpu.make_async_copy(stage.at[j, :, part], out.at[:, to, :, pl.ds(128 * j, 128)], sems.at[i, j])
            for j in range(stage.shape[0])
        ]

    def block(i, _):
        start = pl.multiple_of(i * ROWS8, ROWS8)
        part = pl.ds(start, ROWS8)

        def tracer(t, _):
            own = lambda x: field[t, x, part, :]
            put = lambda x, value: put_column(stage, t, start, x, value)
            both_rims(even, halo_1, halo_2, t, part, own, coefs, north, width, put)
            return 0

        lax.fori_loop(0, tracers, tracer, 0)
        for copy in copies_of(i):
            copy.start()
        return 0

    def finish(i, _):
        for copy in copies_of(i):
            copy.wait()
        return 0

    lax.fori_loop(0, size // ROWS8, block, 0)
    lax.fori_loop(0, size // ROWS8, finish, 0)


def transport_call(kernel, name, args, out_shape, aliases, scratch, cells, hbm=(), out_hbm=()):
    return pl.pallas_call(
        kernel,
        in_specs=[HBM if i in hbm else VMEM for i in range(len(args))],
        out_specs=[HBM if i in out_hbm else VMEM for i in range(len(out_shape))],
        out_shape=out_shape,
        scratch_shapes=scratch,
        input_output_aliases=aliases,
        compiler_params=params(16),
        cost_estimate=LITTLE,
        name=name,
    )(*args)


def north_scratch(width, rows):
    return pltpu.VMEM((width + 2 * HALO, ROWS8, rows), F32)


def first_inner(chunk, fixed, scale, surface, speed, open_e, coef_n):
    count, levels, width, rows = fixed.shape
    begin, size = chunk
    args = [fixed, scale, surface, speed, open_e, coef_n]
    out_shape = [
        shape_of(count, width, size, rows),
        shape_of(count, 4 * HALO, size, rows),
        shape_of(2, width + 1, size, rows),
        shape_of(*coef_n.shape),
    ]
    turn = pltpu.VMEM((rows // 128, ROWS8 * width, 128), F32)
    return transport_call(
        functools.partial(first_inner_kernel, begin), "first_inner", args, out_shape, {len(args) - 1: 3},
        [north_scratch(width, rows), turn, turn], count * size * width * rows,
    )


def first_rim(chunk, field, rims, coefs, speed_w, open_e, halos, coef_n):
    count, width, size, rows = field.shape
    args = [rims, speed_w, open_e, *halos, coef_n, field, coefs]
    edge = shape_of(count, 2, size, rows)
    out_shape = [shape_of(*field.shape), shape_of(*coefs.shape), edge, edge, shape_of(*coef_n.shape)]
    field, coefs, send_1, send_2, coef_n = transport_call(
        functools.partial(first_rim_kernel, chunk[0]), "first_rim", args, out_shape, {5: 4, 6: 0, 7: 1},
        [north_scratch(width, rows)], count * size * 4 * rows,
    )
    return field, coefs, (send_1, send_2), coef_n


def last_inner(field, coefs, coef_n):
    count, width, size, rows = field.shape
    out_shape = [shape_of(rows // 128, count, size, width, 128), shape_of(*coef_n.shape)]
    return transport_call(
        last_inner_kernel, "last_inner", [field, coefs, coef_n], out_shape, {2: 1},
        [north_scratch(width, rows)], count * size * width * rows,
    )


def last_rim(chunk, levels, field, coefs, halos, stage, coef_n, result):
    count, width, size, rows = field.shape
    args = [field, coefs, *halos, coef_n, stage]
    aliases = {4: 2, 5: 1}
    if result is not None:
        aliases[6] = 0
        args.append(result)
    out_shape = [shape_of(count, levels, width, rows), shape_of(*stage.shape), shape_of(*coef_n.shape)]
    result, _, coef_n = transport_call(
        functools.partial(last_rim_kernel, chunk[0]), "last_rim", args, out_shape, aliases,
        [north_scratch(width, rows), pltpu.SemaphoreType.DMA((size // ROWS8, rows // 128))],
        count * size * 4 * rows, hbm=(6,), out_hbm=(0,),
    )
    return result, coef_n


def per_device(tracers, diffusivity, conductance, face_velocity, partner, weight, sea_mask):
    tiles = lax.axis_size("tile")
    tracers, diffusivity, conductance = tracers[0], diffusivity[0], conductance[0]
    speed, partner, weight = face_velocity[0], partner[0], weight[0]
    width = tracers.shape[2]
    reach = width // 2 + 1

    def move(value, target_of, swap=False):
        pairs = []
        for m in range(2):
            for t in range(tiles):
                target = (1 - m if swap else m) * tiles + target_of(t) % tiles
                pairs.append((m * tiles + t, target))
        return lax.ppermute(value, ("mp", "tile"), pairs)

    one = lambda t: t + 1 - 2 * (t % 2)
    two = lambda t: t - 1 + 2 * (t % 2)

    *speeds, to_east, order = speed_columns(speed, (0, width - 2, width - 1))
    speed_w = move(to_east, lambda t: t + 1)
    signed = jnp.where(sea_mask > 0, conductance, -conductance)
    parts, ratios, slope, own, terms_1, terms_2 = down_to_surface(tracers, diffusivity, signed, order, reach)
    terms_1 = move(terms_1, one, swap=True)
    terms_2 = move(terms_2, two, swap=True)
    peer = move(own, lambda t: t, swap=True)
    rim = (0, 1, width - 2, width - 1)
    fixed, scale, rims, rim_scale = up_from_surface(parts, ratios, speed_w, rim)

    inflow, surface, open_e, coef_n, *sends = exchange_surface(
        own, slope, peer, terms_1, terms_2, partner, weight, signed, rims, rim_scale, speeds, reach
    )
    levels = fixed.shape[1]
    chunks = chunks_of(levels)
    every = range(len(chunks))
    exchange = lambda pair: (move(pair[0], one), move(pair[1], two))
    halos = [exchange((sends[c], sends[len(chunks) + c])) for c in every]
    fields, rims, coefs, stages = [[None] * len(chunks) for _ in range(4)]
    for c in every:
        fields[c], rims[c], coefs[c], coef_n = first_inner(chunks[c], fixed, scale, surface, speed, open_e, coef_n)
    for c in every:
        fields[c], coefs[c], pair, coef_n = first_rim(
            chunks[c], fields[c], rims[c], coefs[c], speed_w, open_e, halos[c], coef_n
        )
        halos[c] = exchange(pair)
    for c in every:
        stages[c], coef_n = last_inner(fields[c], coefs[c], coef_n)
    result = None
    for c in every:
        result, coef_n = last_rim(chunks[c], levels, fields[c], coefs[c], halos[c], stages[c], coef_n, result)
    return result[None], inflow[None]


def solution(mesh):
    in_specs = (
        P("mp", None, None, "tile", None),
        P("mp", None, "tile", None),
        P("mp", "tile", None),
        P("mp", None, "tile", None),
        P("mp", None, "tile", None),
        P("mp", None, "tile", None),
        P("tile", None),
    )
    out_specs = (P("mp", None, None, "tile", None), P("mp", None, "tile", None))
    return jax.shard_map(
        per_device, mesh=mesh, in_specs=in_specs, out_specs=out_specs, check_vma=False
    )
```

```python
import functools

import jax
import jax.numpy as jnp
from jax import lax
from jax.experimental import pallas as pl
from jax.experimental.pallas import tpu as pltpu
from jax.sharding import PartitionSpec as P

STEPS = 4
QUANT = 16
NU = 0.12
ROWS8 = 8
PARTS = (1, 1)
HALO = 2
F32 = jnp.float32
LITTLE = pl.CostEstimate(flops=1, bytes_accessed=1024, transcendentals=0)
VMEM = pl.BlockSpec(memory_space=pltpu.VMEM)
HBM = pl.BlockSpec(memory_space=pltpu.HBM)


def shape_of(*shape):
    return jax.ShapeDtypeStruct(shape, F32)


def params(mib):
    return pltpu.CompilerParams(vmem_limit_bytes=mib * 2**20)


def is_even():
    return lax.rem(lax.axis_index("tile"), 2) == 0


def either(even, call, first, second):
    @pl.when(even)
    def _():
        call(first, second)

    @pl.when(jnp.logical_not(even))
    def _():
        call(second, first)


def chunks_of(levels):
    sizes = [part * levels // sum(PARTS) for part in PARTS]
    return [(sum(sizes[:c]), size) for c, size in enumerate(sizes)]


def lane_parts(total, size=256):
    size = min(size, total)
    return [slice(start, start + size) for start in range(0, total, size)]


def down_kernel(reach, source, coupling, signed, order, parts, ratios, slope, terms, first_pair, second_pair, state, part_s, sems):
    tracers, levels, width, rows = source.shape
    blocks = levels // ROWS8

    def copy_of(b):
        part = pl.ds(b * ROWS8, ROWS8)
        return pltpu.make_async_copy(source.at[:, part], parts.at[:, part], sems.at[b])

    couplings = pltpu.make_async_copy(coupling, ratios.at[pl.ds(0, levels - 1)], sems.at[blocks])
    couplings.start()
    for b in range(blocks):
        copy_of(b).start()
    state[...] = jnp.zeros_like(state)
    part_s[...] = jnp.zeros_like(part_s)
    couplings.wait()

    def block(b, _):
        copy_of(b).wait()
        for lanes in lane_parts(rows):
            before, ratio, inverse = [state[i, :, lanes] for i in range(3)]
            part = [part_s[t, :, lanes] for t in range(tracers)]
            for at in range(ROWS8):
                l = b * ROWS8 + at
                now = ratios[l, :, lanes]
                if at == ROWS8 - 1:
                    now = jnp.where(b == blocks - 1, 0.0, now)
                inverse = 1.0 / (1.0 + before + now - before * ratio)
                part = [(parts[t, l, :, lanes] + before * part[t]) * inverse for t in range(tracers)]
                ratio = now * inverse
                before = now
                ratios[l, :, lanes] = ratio
                for t in range(tracers):
                    parts[t, l, :, lanes] = part[t]
            for i, value in enumerate((before, ratio, inverse)):
                state[i, :, lanes] = value
            for t in range(tracers):
                part_s[t, :, lanes] = part[t]
        return 0

    lax.fori_loop(0, blocks, block, 0)
    for t in range(tracers):
        terms[t] = part_s[t]
    slope[...] = state[2]
    terms[tracers] = 1.0 / jnp.abs(signed[...]) + state[2]
    mask = jnp.where(signed[...] > 0.0, 1.0, 0.0)

    def pack(east, west):
        for c in range(tracers + 1):
            east[c * reach : (c + 1) * reach, :] = terms[c, width - reach :, :]
            west[c * reach : (c + 1) * reach, :] = terms[c, :reach, :]
        at = (tracers + 1) * reach
        east[at : at + HALO, :] = mask[width - HALO :]
        west[at : at + HALO, :] = mask[:HALO]

    either(is_even(), pack, first_pair, second_pair)


def down_to_surface(tracers, diffusivity, signed, order, reach):
    count, levels, width, rows = tracers.shape
    packed = (count + 1) * reach + HALO
    packed = -(-packed // 8) * 8
    return pl.pallas_call(
        functools.partial(down_kernel, reach),
        in_specs=[HBM, HBM, VMEM, VMEM],
        out_specs=[VMEM] * 6,
        out_shape=[
            shape_of(count, levels, width, rows),
            shape_of(levels, width, rows),
            shape_of(width, rows),
            shape_of(count + 1, width, rows),
            shape_of(packed, rows),
            shape_of(packed, rows),
        ],
        scratch_shapes=[
            pltpu.VMEM((3, width, rows), F32),
            pltpu.VMEM((count, width, rows), F32),
            pltpu.SemaphoreType.DMA((levels // ROWS8 + 1,)),
        ],
        compiler_params=params(41),
        cost_estimate=pl.CostEstimate(
            flops=20 * levels * width * rows, bytes_accessed=10 * levels * width * rows * 4, transcendentals=0
        ),
        name="down_to_surface",
    )(tracers, diffusivity, signed, order)


def up_kernel(rim, parts, ratios, arrived, fixed, scale, rims, rim_scale):
    tracers, levels, width, rows = parts.shape
    blocks = levels // ROWS8
    for lanes in lane_parts(rows):

        def block(i, state):
            b = blocks - 1 - i
            start = pl.multiple_of(b * ROWS8, ROWS8)
            scale_now, fixed_now = state[0], list(state[1:])
            for at in reversed(range(ROWS8)):
                l = start + at
                ratio = ratios[l, :, lanes]
                scale_now = ratio * scale_now
                fixed_now = [parts[t, l, :, lanes] + ratio * fixed_now[t] for t in range(tracers)]
                if at == ROWS8 - 1:
                    scale_now = jnp.where(i == 0, 1.0, scale_now)
                    fixed_now = [jnp.where(i == 0, 0.0, value) for value in fixed_now]
                scale[l, :, lanes] = scale_now
                for t in range(tracers):
                    fixed[t, l, :, lanes] = fixed_now[t]
                for c, x in enumerate(rim):
                    rim_scale[c, b, at : at + 1, lanes] = scale_now[x : x + 1]
                    for t in range(tracers):
                        rims[t, c, b, at : at + 1, lanes] = fixed_now[t][x : x + 1]
            return scale_now, *fixed_now

        zero = jnp.zeros((width, lanes.stop - lanes.start), F32)
        lax.fori_loop(0, blocks, block, (zero,) * (1 + tracers))


def speed_kernel(columns, speed, *out):
    out[-1][...] = jnp.zeros_like(out[-1])
    out[-2][speed.shape[0] :, :] = jnp.zeros((out[-2].shape[0] - speed.shape[0], out[-2].shape[1]), F32)
    for l in range(speed.shape[0]):
        for ref, x in zip(out, columns):
            ref[l : l + 1, :] = speed[l, x : x + 1, :]


def speed_columns(speed, columns):
    levels, width, rows = speed.shape
    return pl.pallas_call(
        functools.partial(speed_kernel, columns),
        in_specs=[VMEM],
        out_specs=[VMEM] * (len(columns) + 1),
        out_shape=[shape_of(levels, rows)] * (len(columns) - 1)
        + [shape_of(levels + levels // 2, rows), shape_of(ROWS8, 128)],
        compiler_params=params(20),
        cost_estimate=LITTLE,
        name="speed_columns",
    )(speed)


def up_from_surface(parts, ratios, arrived, rim):
    count, levels, width, rows = parts.shape
    fixed, scale, rims, rim_scale = pl.pallas_call(
        functools.partial(up_kernel, rim),
        in_specs=[VMEM] * 3,
        out_specs=[VMEM] * 4,
        out_shape=[
            shape_of(count, levels, width, rows),
            shape_of(levels, width, rows),
            shape_of(count, len(rim), levels // ROWS8, ROWS8, rows),
            shape_of(len(rim), levels // ROWS8, ROWS8, rows),
        ],
        input_output_aliases={0: 0, 1: 1},
        compiler_params=params(20),
        cost_estimate=LITTLE,
        name="up_from_surface",
    )(parts, ratios, arrived)
    rims, rim_scale = rims.reshape(count, len(rim), levels, rows), rim_scale.reshape(len(rim), levels, rows)
    return fixed, scale, rims, rim_scale


def leaving(u, opening):
    return opening * (jnp.maximum(u, 0.0) + NU), opening * (jnp.minimum(u, 0.0) - NU)


def surface_kernel(
    reach, own, slope, peer, first_pair, second_pair, partner, weight, signed, rims, rim_scale, speed_0, speed_1,
    inflow, surface, open_e, coef_n, *rest,
):
    chunks = chunks_of(rims.shape[2])
    send_1, send_2, wide, opened = rest[: len(chunks)], rest[len(chunks) : 2 * len(chunks)], rest[-2], rest[-1]
    channels, width, rows = own.shape
    tracers = channels - 1
    first = 2 * 8
    even = is_even()

    for c in range(channels):
        wide[c, first : first + width, :] = peer[c]
    opened[:width, :] = jnp.where(signed[...] > 0.0, 1.0, 0.0)
    opened[width:, :] = jnp.zeros((ROWS8, rows), F32)

    def unpack(east, west):
        for c in range(channels):
            part = slice(c * reach, (c + 1) * reach)
            wide[c, first - reach : first, :] = west[part, :]
            wide[c, first + width : first + width + reach, :] = east[part, :]
        at = slice(channels * reach, channels * reach + HALO)
        opened[width : width + HALO, :] = east[at, :]
        opened[width + ROWS8 - HALO :, :] = west[at, :]

    either(even, unpack, first_pair, second_pair)

    start = lax.axis_index("tile") * width
    total = lax.axis_size("tile") * width
    for lanes in lane_parts(rows, 128):
        position = start + lax.broadcasted_iota(jnp.int32, (width, 128), 0)
        own_rest = own[tracers, :, lanes]
        flow = [jnp.zeros((width, 128), F32) for _ in range(tracers)]
        for k in range(partner.shape[0]):
            apart = partner[k, :, lanes] - position
            apart = jnp.where(apart > reach, apart - total, apart)
            apart = jnp.where(apart < -reach, apart + total, apart)
            found = [jnp.zeros((width, 128), F32) for _ in range(channels)]
            for offset in range(-reach, reach + 1):
                hit = apart == offset
                window = slice(first + offset, first + offset + width)
                found = [jnp.where(hit, wide[c, window, lanes], f) for c, f in enumerate(found)]
            factor = weight[k, :, lanes].astype(F32) / (own_rest + found[-1])
            flow = [flow[t] + factor * (own[t, :, lanes] - found[t]) for t in range(tracers)]
        for t in range(tracers):
            into = flow[t] * (-1.0 / QUANT)
            inflow[t, :, lanes] = into
            surface[t, :, lanes] = own[t, :, lanes] + slope[:, lanes] * into

    wide_rows = width + ROWS8
    free = jnp.broadcast_to(lax.axis_index("mp"), (wide_rows, rows)) == 0
    here = jnp.where(free, 1.0, opened[...])
    column = lax.broadcasted_iota(jnp.int32, (wide_rows, rows), 1)
    open_e[...] = here * pltpu.roll(here, wide_rows - 1, 0)
    coef_n[...] = NU * (here * jnp.where(column == rows - 1, 0.0, pltpu.roll(here, rows - 1, 1)))

    for c, (begin, size) in enumerate(chunks):
        part = slice(begin, begin + size)
        faces_w = leaving(speed_0[part, :], open_e[:1, :])
        faces_e = leaving(speed_1[part, :], open_e[width - 2 : width - 1, :])
        for t in range(tracers):
            columns = []
            for i, x in enumerate((0, 1, width - 2, width - 1)):
                columns.append(rims[t, i, part, :] + rim_scale[i, part, :] * surface[t, x : x + 1, :])
            west = columns[0], faces_w[0] * columns[0] + faces_w[1] * columns[1]
            east = columns[3], faces_e[0] * columns[2] + faces_e[1] * columns[3]
            for i in range(2):
                send_1[c][t, i] = jnp.where(even, east[i], west[i])
                send_2[c][t, i] = jnp.where(even, west[i], east[i])


def exchange_surface(
    own, slope, peer, first_pair, second_pair, partner, weight, signed, rims, rim_scale, speeds, reach
):
    channels, width, rows = own.shape
    count, _, levels, _ = rims.shape
    plane = shape_of(width + ROWS8, rows)
    edges = [shape_of(count, 2, size, rows) for _, size in chunks_of(levels)]
    return pl.pallas_call(
        functools.partial(surface_kernel, reach),
        in_specs=[VMEM] * 12,
        out_specs=[VMEM] * (4 + 2 * len(edges)),
        out_shape=[shape_of(count, width, rows)] * 2 + [plane] * 2 + edges * 2,
        scratch_shapes=[pltpu.VMEM((channels, 16 + width + 16, rows), F32), pltpu.VMEM((width + ROWS8, rows), F32)],
        compiler_params=params(20),
        cost_estimate=LITTLE,
        name="exchange_surface",
    )(own, slope, peer, first_pair, second_pair, partner, weight, signed, rims, rim_scale, *speeds)


def along_y(north, value):
    flux = north * (pltpu.roll(value, value.shape[-1] - 1, 1) - value)
    return flux - pltpu.roll(flux, 1, 1)


def inner_steps(q, a, b, north, width, put, keep):
    end = width - 1
    here, flux, once_before, flux_before = q(0), None, None, None
    for x in range(width):
        if x == 0:
            east = q(1)
            flux_e = a(0) * here + b(0) * east
            keep(0, here)
            keep(1, (here - flux_e) + along_y(north(0), here))
            once = None
        elif x == end:
            keep(4, here)
            keep(5, (here + flux) + along_y(north(end), here))
            keep(6, once_before)
            keep(7, (once_before + flux_before) + along_y(north(end - 1), once_before))
            break
        else:
            east = q(x + 1)
            flux_e = a(x) * here + b(x) * east
            once = (here - (flux_e - flux)) + along_y(north(x), here)
        if once_before is not None:
            flux_once = a(x - 1) * once_before + b(x - 1) * once
            second = along_y(north(x - 1), once_before)
            if flux_before is None:
                keep(2, once_before)
                keep(3, (once_before - flux_once) + second)
            else:
                put(x - 1, (once_before - (flux_once - flux_before)) + second)
            flux_before = flux_once
        here, flux, once_before = east, flux_e, once


def rim_steps(kept, west, east, a, b, north, width):
    end = width - 1
    value, behind = west
    flux = a(-1) * value + b(-1) * kept(0)
    outer = (value - (flux - behind)) + along_y(north(-1), value)
    edge = kept(1) + flux
    flux_out = a(-1) * outer + b(-1) * edge
    flux_in = a(0) * edge + b(0) * kept(2)
    new = {0: (edge - (flux_in - flux_out)) + along_y(north(0), edge), 1: kept(3) + flux_in}
    value, behind = east
    flux = a(end) * kept(4) + b(end) * value
    outer = (value - (behind - flux)) + along_y(north(width), value)
    edge = kept(5) - flux
    flux_out = a(end) * edge + b(end) * outer
    flux_in = a(end - 1) * kept(6) + b(end - 1) * edge
    new[end] = (edge - (flux_out - flux_in)) + along_y(north(end), edge)
    new[end - 1] = kept(7) - flux_in
    return new


def tiles_in(turn, value):
    levels, width, _ = value.shape
    for j in range(turn.shape[0]):
        turn[j] = value[:, :, 128 * j : 128 * (j + 1)].reshape(levels * width, 128)


def column(turn, x, width):
    parts = [turn[j, pl.ds(x, ROWS8, stride=width), :] for j in range(turn.shape[0])]
    return jnp.concatenate(parts, axis=1)


def put_column(stage, t, start, x, value):
    parts, tracers, levels, width, lanes = stage.shape
    rows = stage.reshape(parts, tracers, levels * width, lanes)
    for j in range(parts):
        at = pl.ds(start * width + x, ROWS8, stride=width)
        rows[j, t, at, :] = value[:, lanes * j : lanes * (j + 1)]


def ring(x, width):
    return x if x >= 0 else width + ROWS8 + x


def spread_north(coef_n, north_s, width):
    for x in range(1 - HALO, width + HALO - 1):
        row = ring(x, width)
        north_s[x + HALO] = jnp.broadcast_to(coef_n[row : row + 1, :], north_s.shape[1:])


def face(coefs, part, x, u, open_e, width):
    row = ring(x, width)
    coefs[0, x + 1, part, :], coefs[1, x + 1, part, :] = leaving(u, open_e[row : row + 1, :])


def faces(coefs, part):
    return [lambda x, i=i: coefs[i, x + 1, part, :] for i in range(2)]


def first_inner_kernel(
    begin, fixed, scale, surface, speed, open_e, coef_n,
    field, rims, coefs, coef_n_out, north_s, turn, turn_speed,
):
    tracers, levels, width, rows = fixed.shape
    size = field.shape[2]
    spread_north(coef_n, north_s, width)
    north = lambda x: north_s[x + HALO]

    def block(i, _):
        start = pl.multiple_of(i * ROWS8, ROWS8)
        part, whole = pl.ds(start, ROWS8), pl.ds(begin + start, ROWS8)
        tiles_in(turn_speed, speed[whole])
        for x in range(width):
            face(coefs, part, x, column(turn_speed, x, width), open_e, width)

        def tracer(t, _):
            tiles_in(turn, fixed[t, whole] + scale[whole] * surface[t][None])

            def put(x, value):
                field[t, x, part, :] = value

            def keep(i, value):
                rims[t, i, part, :] = value

            q = lambda x: column(turn, x, width)
            inner_steps(q, *faces(coefs, part), north, width, put, keep)
            return 0

        lax.fori_loop(0, tracers, tracer, 0)
        return 0

    lax.fori_loop(0, size // ROWS8, block, 0)


def halo_pair(even, halo_1, halo_2, t, part):
    pairs = [(halo_1[t, i, part, :], halo_2[t, i, part, :]) for i in range(2)]
    west = [jnp.where(even, second, first) for first, second in pairs]
    east = [jnp.where(even, first, second) for first, second in pairs]
    return west, east


def first_rim_kernel(
    begin, rims, speed_w, open_e, halo_1, halo_2, coef_n, field_in, coefs_in,
    field, coefs, send_1, send_2, coef_n_out, north_s,
):
    tracers, width, size, rows = field.shape
    even = is_even()
    spread_north(coef_n, north_s, width)
    north = lambda x: north_s[x + HALO]

    def block(i, _):
        start = pl.multiple_of(i * ROWS8, ROWS8)
        part, whole = pl.ds(start, ROWS8), pl.ds(begin + start, ROWS8)
        face(coefs, part, -1, speed_w[whole, :], open_e, width)
        a, b = faces(coefs, part)

        def tracer(t, _):
            halos = halo_pair(even, halo_1, halo_2, t, part)
            new = rim_steps(lambda i: rims[t, i, part, :], *halos, a, b, north, width)
            for x, value in new.items():
                field[t, x, part, :] = value
            end = width - 1
            west = new[0], a(0) * new[0] + b(0) * new[1]
            east = new[end], a(end - 1) * new[end - 1] + b(end - 1) * new[end]
            for i in range(2):
                send_1[t, i, part, :] = jnp.where(even, east[i], west[i])
                send_2[t, i, part, :] = jnp.where(even, west[i], east[i])
            return 0

        lax.fori_loop(0, tracers, tracer, 0)
        return 0

    lax.fori_loop(0, size // ROWS8, block, 0)


def last_inner_kernel(field, coefs, coef_n, stage, rims, coef_n_out, north_s):
    tracers, width, size, rows = field.shape
    spread_north(coef_n, north_s, width)
    north = lambda x: north_s[x + HALO]

    def block(i, _):
        start = pl.multiple_of(i * ROWS8, ROWS8)
        part = pl.ds(start, ROWS8)

        def tracer(t, _):
            q = lambda x: field[t, x, part, :]
            put = lambda x, value: put_column(stage, t, start, x, value)

            def keep(i, value):
                rims[t, i, part, :] = value

            inner_steps(q, *faces(coefs, part), north, width, put, keep)
            return 0

        lax.fori_loop(0, tracers, tracer, 0)
        return 0

    lax.fori_loop(0, size // ROWS8, block, 0)


def last_rim_kernel(begin, rims, coefs, halo_1, halo_2, coef_n, stage_in, *refs):
    out, stage, coef_n_out, north_s, sems = refs[-5:]
    _, tracers, size, width, _ = stage.shape
    even = is_even()
    spread_north(coef_n, north_s, width)
    north = lambda x: north_s[x + HALO]

    def copies_of(i):
        start = pl.multiple_of(i * ROWS8, ROWS8)
        part, to = pl.ds(start, ROWS8), pl.ds(begin + start, ROWS8)
        return [
            pltpu.make_async_copy(stage.at[j, :, part], out.at[:, to, :, pl.ds(128 * j, 128)], sems.at[i, j])
            for j in range(stage.shape[0])
        ]

    def block(i, _):
        start = pl.multiple_of(i * ROWS8, ROWS8)
        part = pl.ds(start, ROWS8)

        def tracer(t, _):
            halos = halo_pair(even, halo_1, halo_2, t, part)
            new = rim_steps(lambda i: rims[t, i, part, :], *halos, *faces(coefs, part), north, width)
            for x, value in new.items():
                put_column(stage, t, start, x, value)
            return 0

        lax.fori_loop(0, tracers, tracer, 0)
        for copy in copies_of(i):
            copy.start()
        return 0

    def finish(i, _):
        for copy in copies_of(i):
            copy.wait()
        return 0

    lax.fori_loop(0, size // ROWS8, block, 0)
    lax.fori_loop(0, size // ROWS8, finish, 0)


def transport_call(kernel, name, args, out_shape, aliases, scratch, cells, hbm=(), out_hbm=()):
    return pl.pallas_call(
        kernel,
        in_specs=[HBM if i in hbm else VMEM for i in range(len(args))],
        out_specs=[HBM if i in out_hbm else VMEM for i in range(len(out_shape))],
        out_shape=out_shape,
        scratch_shapes=scratch,
        input_output_aliases=aliases,
        compiler_params=params(16),
        cost_estimate=LITTLE,
        name=name,
    )(*args)


def north_scratch(width, rows):
    return pltpu.VMEM((width + 2 * HALO, ROWS8, rows), F32)


def first_inner(chunk, fixed, scale, surface, speed, open_e, coef_n):
    count, levels, width, rows = fixed.shape
    begin, size = chunk
    args = [fixed, scale, surface, speed, open_e, coef_n]
    out_shape = [
        shape_of(count, width, size, rows),
        shape_of(count, 8, size, rows),
        shape_of(2, width + 1, size, rows),
        shape_of(*coef_n.shape),
    ]
    turn = pltpu.VMEM((rows // 128, ROWS8 * width, 128), F32)
    return transport_call(
        functools.partial(first_inner_kernel, begin), "first_inner", args, out_shape, {len(args) - 1: 3},
        [north_scratch(width, rows), turn, turn], count * size * width * rows,
    )


def first_rim(chunk, field, rims, coefs, speed_w, open_e, halos, coef_n):
    count, width, size, rows = field.shape
    args = [rims, speed_w, open_e, *halos, coef_n, field, coefs]
    edge = shape_of(count, 2, size, rows)
    out_shape = [shape_of(*field.shape), shape_of(*coefs.shape), edge, edge, shape_of(*coef_n.shape)]
    field, coefs, send_1, send_2, coef_n = transport_call(
        functools.partial(first_rim_kernel, chunk[0]), "first_rim", args, out_shape, {5: 4, 6: 0, 7: 1},
        [north_scratch(width, rows)], count * size * 4 * rows,
    )
    return field, coefs, (send_1, send_2), coef_n


def last_inner(field, coefs, coef_n):
    count, width, size, rows = field.shape
    out_shape = [
        shape_of(rows // 128, count, size, width, 128),
        shape_of(count, 8, size, rows),
        shape_of(*coef_n.shape),
    ]
    return transport_call(
        last_inner_kernel, "last_inner", [field, coefs, coef_n], out_shape, {2: 2},
        [north_scratch(width, rows)], count * size * width * rows,
    )


def last_rim(chunk, levels, rims, coefs, halos, stage, coef_n, result):
    lane_tiles, count, size, width, lanes = stage.shape
    rows = lane_tiles * lanes
    args = [rims, coefs, *halos, coef_n, stage]
    aliases = {4: 2, 5: 1}
    if result is not None:
        aliases[6] = 0
        args.append(result)
    out_shape = [shape_of(count, levels, width, rows), shape_of(*stage.shape), shape_of(*coef_n.shape)]
    result, _, coef_n = transport_call(
        functools.partial(last_rim_kernel, chunk[0]), "last_rim", args, out_shape, aliases,
        [north_scratch(width, rows), pltpu.SemaphoreType.DMA((size // ROWS8, rows // 128))],
        count * size * 4 * rows, hbm=(6,), out_hbm=(0,),
    )
    return result, coef_n


def per_device(tracers, diffusivity, conductance, face_velocity, partner, weight, sea_mask):
    tiles = lax.axis_size("tile")
    tracers, diffusivity, conductance = tracers[0], diffusivity[0], conductance[0]
    speed, partner, weight = face_velocity[0], partner[0], weight[0]
    width = tracers.shape[2]
    reach = width // 2 + 1

    def move(value, target_of, swap=False):
        pairs = []
        for m in range(2):
            for t in range(tiles):
                target = (1 - m if swap else m) * tiles + target_of(t) % tiles
                pairs.append((m * tiles + t, target))
        return lax.ppermute(value, ("mp", "tile"), pairs)

    one = lambda t: t + 1 - 2 * (t % 2)
    two = lambda t: t - 1 + 2 * (t % 2)

    *speeds, to_east, order = speed_columns(speed, (0, width - 2, width - 1))
    speed_w = move(to_east, lambda t: t + 1)
    signed = jnp.where(sea_mask > 0, conductance, -conductance)
    parts, ratios, slope, own, terms_1, terms_2 = down_to_surface(tracers, diffusivity, signed, order, reach)
    terms_1 = move(terms_1, one, swap=True)
    terms_2 = move(terms_2, two, swap=True)
    peer = move(own, lambda t: t, swap=True)
    rim = (0, 1, width - 2, width - 1)
    fixed, scale, rims, rim_scale = up_from_surface(parts, ratios, speed_w, rim)

    inflow, surface, open_e, coef_n, *sends = exchange_surface(
        own, slope, peer, terms_1, terms_2, partner, weight, signed, rims, rim_scale, speeds, reach
    )
    levels = fixed.shape[1]
    chunks = chunks_of(levels)
    every = range(len(chunks))
    exchange = lambda pair: (move(pair[0], one), move(pair[1], two))
    halos = [exchange((sends[c], sends[len(chunks) + c])) for c in every]
    fields, rims, coefs, stages = [[None] * len(chunks) for _ in range(4)]
    for c in every:
        fields[c], rims[c], coefs[c], coef_n = first_inner(chunks[c], fixed, scale, surface, speed, open_e, coef_n)
    for c in every:
        fields[c], coefs[c], pair, coef_n = first_rim(
            chunks[c], fields[c], rims[c], coefs[c], speed_w, open_e, halos[c], coef_n
        )
        halos[c] = exchange(pair)
    for c in every:
        stages[c], rims[c], coef_n = last_inner(fields[c], coefs[c], coef_n)
    result = None
    for c in every:
        result, coef_n = last_rim(chunks[c], levels, rims[c], coefs[c], halos[c], stages[c], coef_n, result)
    return result[None], inflow[None]


def solution(mesh):
    in_specs = (
        P("mp", None, None, "tile", None),
        P("mp", None, "tile", None),
        P("mp", "tile", None),
        P("mp", None, "tile", None),
        P("mp", None, "tile", None),
        P("mp", None, "tile", None),
        P("tile", None),
    )
    out_specs = (P("mp", None, None, "tile", None), P("mp", None, "tile", None))
    return jax.shard_map(
        per_device, mesh=mesh, in_specs=in_specs, out_specs=out_specs, check_vma=False
    )
```

```python
import functools

import jax
import jax.numpy as jnp
from jax import lax
from jax.experimental import pallas as pl
from jax.experimental.pallas import tpu as pltpu
from jax.sharding import PartitionSpec as P

STEPS = 4
QUANT = 16
NU = 0.12
ROWS8 = 8
PARTS = (1, 1)
HALO = 2
F32 = jnp.float32
LITTLE = pl.CostEstimate(flops=1, bytes_accessed=1024, transcendentals=0)
VMEM = pl.BlockSpec(memory_space=pltpu.VMEM)
HBM = pl.BlockSpec(memory_space=pltpu.HBM)


def shape_of(*shape):
    return jax.ShapeDtypeStruct(shape, F32)


def params(mib):
    return pltpu.CompilerParams(vmem_limit_bytes=mib * 2**20)


def is_even():
    return lax.rem(lax.axis_index("tile"), 2) == 0


def either(even, call, first, second):
    @pl.when(even)
    def _():
        call(first, second)

    @pl.when(jnp.logical_not(even))
    def _():
        call(second, first)


def chunks_of(levels):
    sizes = [part * levels // sum(PARTS) for part in PARTS]
    return [(sum(sizes[:c]), size) for c, size in enumerate(sizes)]


def lane_parts(total, size=256):
    size = min(size, total)
    return [slice(start, start + size) for start in range(0, total, size)]


def down_kernel(reach, source, coupling, signed, order, parts, ratios, slope, terms, half_1, half_2, first_pair, second_pair, state, part_s, sems):
    tracers, levels, width, rows = source.shape
    blocks = levels // ROWS8

    def copy_of(b):
        part = pl.ds(b * ROWS8, ROWS8)
        return pltpu.make_async_copy(source.at[:, part], parts.at[:, part], sems.at[b])

    couplings = pltpu.make_async_copy(coupling, ratios.at[pl.ds(0, levels - 1)], sems.at[blocks])
    couplings.start()
    for b in range(blocks):
        copy_of(b).start()
    state[...] = jnp.zeros_like(state)
    part_s[...] = jnp.zeros_like(part_s)
    couplings.wait()

    def block(b, _):
        copy_of(b).wait()
        for lanes in lane_parts(rows):
            before, ratio, inverse = [state[i, :, lanes] for i in range(3)]
            part = [part_s[t, :, lanes] for t in range(tracers)]
            for at in range(ROWS8):
                l = b * ROWS8 + at
                now = ratios[l, :, lanes]
                if at == ROWS8 - 1:
                    now = jnp.where(b == blocks - 1, 0.0, now)
                inverse = 1.0 / (1.0 + before + now - before * ratio)
                part = [(parts[t, l, :, lanes] + before * part[t]) * inverse for t in range(tracers)]
                ratio = now * inverse
                before = now
                ratios[l, :, lanes] = ratio
                for t in range(tracers):
                    parts[t, l, :, lanes] = part[t]
            for i, value in enumerate((before, ratio, inverse)):
                state[i, :, lanes] = value
            for t in range(tracers):
                part_s[t, :, lanes] = part[t]
        return 0

    lax.fori_loop(0, blocks, block, 0)
    for t in range(tracers):
        terms[t] = part_s[t]
    slope[...] = state[2]
    terms[tracers] = 1.0 / jnp.abs(signed[...]) + state[2]
    half_1[...] = terms[:, : width // 2, :]
    half_2[...] = terms[:, width // 2 :, :]
    mask = jnp.where(signed[...] > 0.0, 1.0, 0.0)

    def pack(east, west):
        for c in range(tracers + 1):
            east[c * reach : (c + 1) * reach, :] = terms[c, width - reach :, :]
            west[c * reach : (c + 1) * reach, :] = terms[c, :reach, :]
        at = (tracers + 1) * reach
        east[at : at + HALO, :] = mask[width - HALO :]
        west[at : at + HALO, :] = mask[:HALO]

    either(is_even(), pack, first_pair, second_pair)


def down_to_surface(tracers, diffusivity, signed, order, reach):
    count, levels, width, rows = tracers.shape
    packed = (count + 1) * reach + HALO
    packed = -(-packed // 8) * 8
    return pl.pallas_call(
        functools.partial(down_kernel, reach),
        in_specs=[HBM, HBM, VMEM, VMEM],
        out_specs=[VMEM] * 8,
        out_shape=[
            shape_of(count, levels, width, rows),
            shape_of(levels, width, rows),
            shape_of(width, rows),
            shape_of(count + 1, width, rows),
            shape_of(count + 1, width // 2, rows),
            shape_of(count + 1, width // 2, rows),
            shape_of(packed, rows),
            shape_of(packed, rows),
        ],
        scratch_shapes=[
            pltpu.VMEM((3, width, rows), F32),
            pltpu.VMEM((count, width, rows), F32),
            pltpu.SemaphoreType.DMA((levels // ROWS8 + 1,)),
        ],
        compiler_params=params(41),
        cost_estimate=pl.CostEstimate(
            flops=20 * levels * width * rows, bytes_accessed=10 * levels * width * rows * 4, transcendentals=0
        ),
        name="down_to_surface",
    )(tracers, diffusivity, signed, order)


def up_kernel(rim, parts, ratios, arrived, fixed, scale, rims, rim_scale):
    tracers, levels, width, rows = parts.shape
    blocks = levels // ROWS8
    for lanes in lane_parts(rows):

        def block(i, state):
            b = blocks - 1 - i
            start = pl.multiple_of(b * ROWS8, ROWS8)
            scale_now, fixed_now = state[0], list(state[1:])
            for at in reversed(range(ROWS8)):
                l = start + at
                ratio = ratios[l, :, lanes]
                scale_now = ratio * scale_now
                fixed_now = [parts[t, l, :, lanes] + ratio * fixed_now[t] for t in range(tracers)]
                if at == ROWS8 - 1:
                    scale_now = jnp.where(i == 0, 1.0, scale_now)
                    fixed_now = [jnp.where(i == 0, 0.0, value) for value in fixed_now]
                scale[l, :, lanes] = scale_now
                for t in range(tracers):
                    fixed[t, l, :, lanes] = fixed_now[t]
                for c, x in enumerate(rim):
                    rim_scale[c, b, at : at + 1, lanes] = scale_now[x : x + 1]
                    for t in range(tracers):
                        rims[t, c, b, at : at + 1, lanes] = fixed_now[t][x : x + 1]
            return scale_now, *fixed_now

        zero = jnp.zeros((width, lanes.stop - lanes.start), F32)
        lax.fori_loop(0, blocks, block, (zero,) * (1 + tracers))


def speed_kernel(columns, speed, *out):
    out[-1][...] = jnp.zeros_like(out[-1])
    for l in range(speed.shape[0]):
        for ref, x in zip(out, columns):
            ref[l : l + 1, :] = speed[l, x : x + 1, :]


def speed_columns(speed, columns):
    levels, width, rows = speed.shape
    return pl.pallas_call(
        functools.partial(speed_kernel, columns),
        in_specs=[VMEM],
        out_specs=[VMEM] * (len(columns) + 1),
        out_shape=[shape_of(levels, rows)] * len(columns) + [shape_of(ROWS8, 128)],
        compiler_params=params(20),
        cost_estimate=LITTLE,
        name="speed_columns",
    )(speed)


def up_from_surface(parts, ratios, arrived, rim):
    count, levels, width, rows = parts.shape
    fixed, scale, rims, rim_scale = pl.pallas_call(
        functools.partial(up_kernel, rim),
        in_specs=[VMEM] * 3,
        out_specs=[VMEM] * 4,
        out_shape=[
            shape_of(count, levels, width, rows),
            shape_of(levels, width, rows),
            shape_of(count, len(rim), levels // ROWS8, ROWS8, rows),
            shape_of(len(rim), levels // ROWS8, ROWS8, rows),
        ],
        input_output_aliases={0: 0, 1: 1},
        compiler_params=params(20),
        cost_estimate=LITTLE,
        name="up_from_surface",
    )(parts, ratios, arrived)
    rims, rim_scale = rims.reshape(count, len(rim), levels, rows), rim_scale.reshape(len(rim), levels, rows)
    return fixed, scale, rims, rim_scale


def leaving(u, opening):
    return opening * (jnp.maximum(u, 0.0) + NU), opening * (jnp.minimum(u, 0.0) - NU)


def surface_kernel(
    reach, own, slope, peer_1, peer_2, first_pair, second_pair, partner, weight, signed, rims, rim_scale, speed_0, speed_1,
    inflow, surface, open_e, coef_n, *rest,
):
    chunks = chunks_of(rims.shape[2])
    send_1, send_2, wide, opened = rest[: len(chunks)], rest[len(chunks) : 2 * len(chunks)], rest[-2], rest[-1]
    channels, width, rows = own.shape
    tracers = channels - 1
    first = 2 * 8
    even = is_even()

    for c in range(channels):
        wide[c, first : first + width // 2, :] = peer_1[c]
        wide[c, first + width // 2 : first + width, :] = peer_2[c]
    opened[:width, :] = jnp.where(signed[...] > 0.0, 1.0, 0.0)
    opened[width:, :] = jnp.zeros((ROWS8, rows), F32)

    def unpack(east, west):
        for c in range(channels):
            part = slice(c * reach, (c + 1) * reach)
            wide[c, first - reach : first, :] = west[part, :]
            wide[c, first + width : first + width + reach, :] = east[part, :]
        at = slice(channels * reach, channels * reach + HALO)
        opened[width : width + HALO, :] = east[at, :]
        opened[width + ROWS8 - HALO :, :] = west[at, :]

    either(even, unpack, first_pair, second_pair)

    start = lax.axis_index("tile") * width
    total = lax.axis_size("tile") * width
    for lanes in lane_parts(rows, 128):
        position = start + lax.broadcasted_iota(jnp.int32, (width, 128), 0)
        own_rest = own[tracers, :, lanes]
        flow = [jnp.zeros((width, 128), F32) for _ in range(tracers)]
        for k in range(partner.shape[0]):
            apart = partner[k, :, lanes] - position
            apart = jnp.where(apart > reach, apart - total, apart)
            apart = jnp.where(apart < -reach, apart + total, apart)
            found = [jnp.zeros((width, 128), F32) for _ in range(channels)]
            for offset in range(-reach, reach + 1):
                hit = apart == offset
                window = slice(first + offset, first + offset + width)
                found = [jnp.where(hit, wide[c, window, lanes], f) for c, f in enumerate(found)]
            factor = weight[k, :, lanes].astype(F32) / (own_rest + found[-1])
            flow = [flow[t] + factor * (own[t, :, lanes] - found[t]) for t in range(tracers)]
        for t in range(tracers):
            into = flow[t] * (-1.0 / QUANT)
            inflow[t, :, lanes] = into
            surface[t, :, lanes] = own[t, :, lanes] + slope[:, lanes] * into

    wide_rows = width + ROWS8
    free = jnp.broadcast_to(lax.axis_index("mp"), (wide_rows, rows)) == 0
    here = jnp.where(free, 1.0, opened[...])
    column = lax.broadcasted_iota(jnp.int32, (wide_rows, rows), 1)
    open_e[...] = here * pltpu.roll(here, wide_rows - 1, 0)
    coef_n[...] = NU * (here * jnp.where(column == rows - 1, 0.0, pltpu.roll(here, rows - 1, 1)))

    for c, (begin, size) in enumerate(chunks):
        part = slice(begin, begin + size)
        faces_w = leaving(speed_0[part, :], open_e[:1, :])
        faces_e = leaving(speed_1[part, :], open_e[width - 2 : width - 1, :])
        for t in range(tracers):
            columns = []
            for i, x in enumerate((0, 1, width - 2, width - 1)):
                columns.append(rims[t, i, part, :] + rim_scale[i, part, :] * surface[t, x : x + 1, :])
            west = columns[0], faces_w[0] * columns[0] + faces_w[1] * columns[1]
            east = columns[3], faces_e[0] * columns[2] + faces_e[1] * columns[3]
            for i in range(2):
                send_1[c][t, i] = jnp.where(even, east[i], west[i])
                send_2[c][t, i] = jnp.where(even, west[i], east[i])


def exchange_surface(
    own, slope, peers, first_pair, second_pair, partner, weight, signed, rims, rim_scale, speeds, reach
):
    channels, width, rows = own.shape
    count, _, levels, _ = rims.shape
    plane = shape_of(width + ROWS8, rows)
    edges = [shape_of(count, 2, size, rows) for _, size in chunks_of(levels)]
    return pl.pallas_call(
        functools.partial(surface_kernel, reach),
        in_specs=[VMEM] * 13,
        out_specs=[VMEM] * (4 + 2 * len(edges)),
        out_shape=[shape_of(count, width, rows)] * 2 + [plane] * 2 + edges * 2,
        scratch_shapes=[pltpu.VMEM((channels, 16 + width + 16, rows), F32), pltpu.VMEM((width + ROWS8, rows), F32)],
        compiler_params=params(20),
        cost_estimate=LITTLE,
        name="exchange_surface",
    )(own, slope, *peers, first_pair, second_pair, partner, weight, signed, rims, rim_scale, *speeds)


def along_y(north, value):
    flux = north * (pltpu.roll(value, value.shape[-1] - 1, 1) - value)
    return flux - pltpu.roll(flux, 1, 1)


def inner_steps(q, a, b, north, width, put, keep):
    end = width - 1
    here, flux, once_before, flux_before = q(0), None, None, None
    for x in range(width):
        if x == 0:
            east = q(1)
            flux_e = a(0) * here + b(0) * east
            keep(0, here)
            keep(1, (here - flux_e) + along_y(north(0), here))
            once = None
        elif x == end:
            keep(4, here)
            keep(5, (here + flux) + along_y(north(end), here))
            keep(6, once_before)
            keep(7, (once_before + flux_before) + along_y(north(end - 1), once_before))
            break
        else:
            east = q(x + 1)
            flux_e = a(x) * here + b(x) * east
            once = (here - (flux_e - flux)) + along_y(north(x), here)
        if once_before is not None:
            flux_once = a(x - 1) * once_before + b(x - 1) * once
            second = along_y(north(x - 1), once_before)
            if flux_before is None:
                keep(2, once_before)
                keep(3, (once_before - flux_once) + second)
            else:
                put(x - 1, (once_before - (flux_once - flux_before)) + second)
            flux_before = flux_once
        here, flux, once_before = east, flux_e, once


def rim_steps(kept, west, east, a, b, north, width):
    end = width - 1
    value, behind = west
    flux = a(-1) * value + b(-1) * kept(0)
    outer = (value - (flux - behind)) + along_y(north(-1), value)
    edge = kept(1) + flux
    flux_out = a(-1) * outer + b(-1) * edge
    flux_in = a(0) * edge + b(0) * kept(2)
    new = {0: (edge - (flux_in - flux_out)) + along_y(north(0), edge), 1: kept(3) + flux_in}
    value, behind = east
    flux = a(end) * kept(4) + b(end) * value
    outer = (value - (behind - flux)) + along_y(north(width), value)
    edge = kept(5) - flux
    flux_out = a(end) * edge + b(end) * outer
    flux_in = a(end - 1) * kept(6) + b(end - 1) * edge
    new[end] = (edge - (flux_out - flux_in)) + along_y(north(end), edge)
    new[end - 1] = kept(7) - flux_in
    return new


def tiles_in(turn, value):
    levels, width, _ = value.shape
    for j in range(turn.shape[0]):
        turn[j] = value[:, :, 128 * j : 128 * (j + 1)].reshape(levels * width, 128)


def column(turn, x, width):
    parts = [turn[j, pl.ds(x, ROWS8, stride=width), :] for j in range(turn.shape[0])]
    return jnp.concatenate(parts, axis=1)


def put_column(stage, t, start, x, value):
    parts, tracers, levels, width, lanes = stage.shape
    rows = stage.reshape(parts, tracers, levels * width, lanes)
    for j in range(parts):
        at = pl.ds(start * width + x, ROWS8, stride=width)
        rows[j, t, at, :] = value[:, lanes * j : lanes * (j + 1)]


def ring(x, width):
    return x if x >= 0 else width + ROWS8 + x


def spread_north(coef_n, north_s, width):
    for x in range(1 - HALO, width + HALO - 1):
        row = ring(x, width)
        north_s[x + HALO] = jnp.broadcast_to(coef_n[row : row + 1, :], north_s.shape[1:])


def face(coefs, part, x, u, open_e, width):
    row = ring(x, width)
    coefs[0, x + 1, part, :], coefs[1, x + 1, part, :] = leaving(u, open_e[row : row + 1, :])


def faces(coefs, part):
    return [lambda x, i=i: coefs[i, x + 1, part, :] for i in range(2)]


def first_inner_kernel(
    begin, fixed, scale, surface, speed, open_e, coef_n,
    field, rims, coefs, coef_n_out, north_s, turn, turn_speed,
):
    tracers, levels, width, rows = fixed.shape
    size = field.shape[2]
    spread_north(coef_n, north_s, width)
    north = lambda x: north_s[x + HALO]

    def block(i, _):
        start = pl.multiple_of(i * ROWS8, ROWS8)
        part, whole = pl.ds(start, ROWS8), pl.ds(begin + start, ROWS8)
        tiles_in(turn_speed, speed[whole])
        for x in range(width):
            face(coefs, part, x, column(turn_speed, x, width), open_e, width)

        def tracer(t, _):
            tiles_in(turn, fixed[t, whole] + scale[whole] * surface[t][None])

            def put(x, value):
                field[t, x, part, :] = value

            def keep(i, value):
                rims[t, i, part, :] = value

            q = lambda x: column(turn, x, width)
            inner_steps(q, *faces(coefs, part), north, width, put, keep)
            return 0

        lax.fori_loop(0, tracers, tracer, 0)
        return 0

    lax.fori_loop(0, size // ROWS8, block, 0)


def halo_pair(even, halo_1, halo_2, t, part):
    pairs = [(halo_1[t, i, part, :], halo_2[t, i, part, :]) for i in range(2)]
    west = [jnp.where(even, second, first) for first, second in pairs]
    east = [jnp.where(even, first, second) for first, second in pairs]
    return west, east


def first_rim_kernel(
    begin, rims, speed_w, open_e, halo_1, halo_2, coef_n, field_in, coefs_in,
    field, coefs, send_1, send_2, coef_n_out, north_s,
):
    tracers, width, size, rows = field.shape
    even = is_even()
    spread_north(coef_n, north_s, width)
    north = lambda x: north_s[x + HALO]

    def block(i, _):
        start = pl.multiple_of(i * ROWS8, ROWS8)
        part, whole = pl.ds(start, ROWS8), pl.ds(begin + start, ROWS8)
        face(coefs, part, -1, speed_w[whole, :], open_e, width)
        a, b = faces(coefs, part)

        def tracer(t, _):
            halos = halo_pair(even, halo_1, halo_2, t, part)
            new = rim_steps(lambda i: rims[t, i, part, :], *halos, a, b, north, width)
            for x, value in new.items():
                field[t, x, part, :] = value
            end = width - 1
            west = new[0], a(0) * new[0] + b(0) * new[1]
            east = new[end], a(end - 1) * new[end - 1] + b(end - 1) * new[end]
            for i in range(2):
                send_1[t, i, part, :] = jnp.where(even, east[i], west[i])
                send_2[t, i, part, :] = jnp.where(even, west[i], east[i])
            return 0

        lax.fori_loop(0, tracers, tracer, 0)
        return 0

    lax.fori_loop(0, size // ROWS8, block, 0)


def last_inner_kernel(field, coefs, coef_n, stage, rims, coef_n_out, north_s):
    tracers, width, size, rows = field.shape
    spread_north(coef_n, north_s, width)
    north = lambda x: north_s[x + HALO]

    def block(i, _):
        start = pl.multiple_of(i * ROWS8, ROWS8)
        part = pl.ds(start, ROWS8)

        def tracer(t, _):
            q = lambda x: field[t, x, part, :]
            put = lambda x, value: put_column(stage, t, start, x, value)

            def keep(i, value):
                rims[t, i, part, :] = value

            inner_steps(q, *faces(coefs, part), north, width, put, keep)
            return 0

        lax.fori_loop(0, tracers, tracer, 0)
        return 0

    lax.fori_loop(0, size // ROWS8, block, 0)


def last_rim_kernel(begin, rims, coefs, halo_1, halo_2, coef_n, stage_in, *refs):
    out, stage, coef_n_out, north_s, sems = refs[-5:]
    _, tracers, size, width, _ = stage.shape
    even = is_even()
    spread_north(coef_n, north_s, width)
    north = lambda x: north_s[x + HALO]

    def copies_of(i):
        start = pl.multiple_of(i * ROWS8, ROWS8)
        part, to = pl.ds(start, ROWS8), pl.ds(begin + start, ROWS8)
        return [
            pltpu.make_async_copy(stage.at[j, :, part], out.at[:, to, :, pl.ds(128 * j, 128)], sems.at[i, j])
            for j in range(stage.shape[0])
        ]

    def block(i, _):
        start = pl.multiple_of(i * ROWS8, ROWS8)
        part = pl.ds(start, ROWS8)

        def tracer(t, _):
            halos = halo_pair(even, halo_1, halo_2, t, part)
            new = rim_steps(lambda i: rims[t, i, part, :], *halos, *faces(coefs, part), north, width)
            for x, value in new.items():
                put_column(stage, t, start, x, value)
            return 0

        lax.fori_loop(0, tracers, tracer, 0)
        for copy in copies_of(i):
            copy.start()
        return 0

    def finish(i, _):
        for copy in copies_of(i):
            copy.wait()
        return 0

    lax.fori_loop(0, size // ROWS8, block, 0)
    lax.fori_loop(0, size // ROWS8, finish, 0)


def transport_call(kernel, name, args, out_shape, aliases, scratch, cells, hbm=(), out_hbm=()):
    return pl.pallas_call(
        kernel,
        in_specs=[HBM if i in hbm else VMEM for i in range(len(args))],
        out_specs=[HBM if i in out_hbm else VMEM for i in range(len(out_shape))],
        out_shape=out_shape,
        scratch_shapes=scratch,
        input_output_aliases=aliases,
        compiler_params=params(16),
        cost_estimate=LITTLE,
        name=name,
    )(*args)


def north_scratch(width, rows):
    return pltpu.VMEM((width + 2 * HALO, ROWS8, rows), F32)


def first_inner(chunk, fixed, scale, surface, speed, open_e, coef_n):
    count, levels, width, rows = fixed.shape
    begin, size = chunk
    args = [fixed, scale, surface, speed, open_e, coef_n]
    out_shape = [
        shape_of(count, width, size, rows),
        shape_of(count, 8, size, rows),
        shape_of(2, width + 1, size, rows),
        shape_of(*coef_n.shape),
    ]
    turn = pltpu.VMEM((rows // 128, ROWS8 * width, 128), F32)
    return transport_call(
        functools.partial(first_inner_kernel, begin), "first_inner", args, out_shape, {len(args) - 1: 3},
        [north_scratch(width, rows), turn, turn], count * size * width * rows,
    )


def first_rim(chunk, field, rims, coefs, speed_w, open_e, halos, coef_n):
    count, width, size, rows = field.shape
    args = [rims, speed_w, open_e, *halos, coef_n, field, coefs]
    edge = shape_of(count, 2, size, rows)
    out_shape = [shape_of(*field.shape), shape_of(*coefs.shape), edge, edge, shape_of(*coef_n.shape)]
    field, coefs, send_1, send_2, coef_n = transport_call(
        functools.partial(first_rim_kernel, chunk[0]), "first_rim", args, out_shape, {5: 4, 6: 0, 7: 1},
        [north_scratch(width, rows)], count * size * 4 * rows,
    )
    return field, coefs, (send_1, send_2), coef_n


def last_inner(field, coefs, coef_n):
    count, width, size, rows = field.shape
    out_shape = [
        shape_of(rows // 128, count, size, width, 128),
        shape_of(count, 8, size, rows),
        shape_of(*coef_n.shape),
    ]
    return transport_call(
        last_inner_kernel, "last_inner", [field, coefs, coef_n], out_shape, {2: 2},
        [north_scratch(width, rows)], count * size * width * rows,
    )


def last_rim(chunk, levels, rims, coefs, halos, stage, coef_n, result):
    lane_tiles, count, size, width, lanes = stage.shape
    rows = lane_tiles * lanes
    args = [rims, coefs, *halos, coef_n, stage]
    aliases = {4: 2, 5: 1}
    if result is not None:
        aliases[6] = 0
        args.append(result)
    out_shape = [shape_of(count, levels, width, rows), shape_of(*stage.shape), shape_of(*coef_n.shape)]
    result, _, coef_n = transport_call(
        functools.partial(last_rim_kernel, chunk[0]), "last_rim", args, out_shape, aliases,
        [north_scratch(width, rows), pltpu.SemaphoreType.DMA((size // ROWS8, rows // 128))],
        count * size * 4 * rows, hbm=(6,), out_hbm=(0,),
    )
    return result, coef_n


def per_device(tracers, diffusivity, conductance, face_velocity, partner, weight, sea_mask):
    tiles = lax.axis_size("tile")
    tracers, diffusivity, conductance = tracers[0], diffusivity[0], conductance[0]
    speed, partner, weight = face_velocity[0], partner[0], weight[0]
    width = tracers.shape[2]
    reach = width // 2 + 1

    def move(value, target_of, swap=False):
        pairs = []
        for m in range(2):
            for t in range(tiles):
                target = (1 - m if swap else m) * tiles + target_of(t) % tiles
                pairs.append((m * tiles + t, target))
        return lax.ppermute(value, ("mp", "tile"), pairs)

    one = lambda t: t + 1 - 2 * (t % 2)
    two = lambda t: t - 1 + 2 * (t % 2)

    *speeds, to_east, order = speed_columns(speed, (0, width - 2, width - 1))
    speed_w = move(to_east, lambda t: t + 1)
    signed = jnp.where(sea_mask > 0, conductance, -conductance)
    parts, ratios, slope, own, *halves, terms_1, terms_2 = down_to_surface(tracers, diffusivity, signed, order, reach)
    terms_1 = move(terms_1, one, swap=True)
    terms_2 = move(terms_2, two, swap=True)
    peers = [move(half, lambda t: t, swap=True) for half in halves]
    rim = (0, 1, width - 2, width - 1)
    fixed, scale, rims, rim_scale = up_from_surface(parts, ratios, speed_w, rim)

    inflow, surface, open_e, coef_n, *sends = exchange_surface(
        own, slope, peers, terms_1, terms_2, partner, weight, signed, rims, rim_scale, speeds, reach
    )
    levels = fixed.shape[1]
    chunks = chunks_of(levels)
    every = range(len(chunks))
    exchange = lambda pair: (move(pair[0], one), move(pair[1], two))
    halos = [exchange((sends[c], sends[len(chunks) + c])) for c in every]
    fields, rims, coefs, stages = [[None] * len(chunks) for _ in range(4)]
    for c in every:
        fields[c], rims[c], coefs[c], coef_n = first_inner(chunks[c], fixed, scale, surface, speed, open_e, coef_n)
    for c in every:
        fields[c], coefs[c], pair, coef_n = first_rim(
            chunks[c], fields[c], rims[c], coefs[c], speed_w, open_e, halos[c], coef_n
        )
        halos[c] = exchange(pair)
    for c in every:
        stages[c], rims[c], coef_n = last_inner(fields[c], coefs[c], coef_n)
    result = None
    for c in every:
        result, coef_n = last_rim(chunks[c], levels, rims[c], coefs[c], halos[c], stages[c], coef_n, result)
    return result[None], inflow[None]


def solution(mesh):
    in_specs = (
        P("mp", None, None, "tile", None),
        P("mp", None, "tile", None),
        P("mp", "tile", None),
        P("mp", None, "tile", None),
        P("mp", None, "tile", None),
        P("mp", None, "tile", None),
        P("tile", None),
    )
    out_specs = (P("mp", None, None, "tile", None), P("mp", None, "tile", None))
    return jax.shard_map(
        per_device, mesh=mesh, in_specs=in_specs, out_specs=out_specs, check_vma=False
    )
```

```python
import functools

import jax
import jax.numpy as jnp
from jax import lax
from jax.experimental import pallas as pl
from jax.experimental.pallas import tpu as pltpu
from jax.sharding import PartitionSpec as P

STEPS = 4
QUANT = 16
NU = 0.12
ROWS8 = 8
PARTS = (1, 1)
HALO = 2
F32 = jnp.float32
LITTLE = pl.CostEstimate(flops=1, bytes_accessed=1024, transcendentals=0)
VMEM = pl.BlockSpec(memory_space=pltpu.VMEM)
HBM = pl.BlockSpec(memory_space=pltpu.HBM)


def shape_of(*shape):
    return jax.ShapeDtypeStruct(shape, F32)


def params(mib):
    return pltpu.CompilerParams(vmem_limit_bytes=mib * 2**20)


def is_even():
    return lax.rem(lax.axis_index("tile"), 2) == 0


def either(even, call, first, second):
    @pl.when(even)
    def _():
        call(first, second)

    @pl.when(jnp.logical_not(even))
    def _():
        call(second, first)


def chunks_of(levels):
    sizes = [part * levels // sum(PARTS) for part in PARTS]
    return [(sum(sizes[:c]), size) for c, size in enumerate(sizes)]


def lane_parts(total, size=256):
    size = min(size, total)
    return [slice(start, start + size) for start in range(0, total, size)]


def down_kernel(reach, source, coupling, signed, order, parts, ratios, slope, terms, half_1, half_2, first_pair, second_pair, state, part_s, sems):
    tracers, levels, width, rows = source.shape
    blocks = levels // ROWS8

    def copies_of(b):
        part = pl.ds(b * ROWS8, ROWS8)
        return [pltpu.make_async_copy(source.at[t, part], parts.at[t, part], sems.at[b, t]) for t in range(tracers)]

    for b in range(blocks):
        for copy in copies_of(b):
            copy.start()
    state[...] = jnp.zeros_like(state)
    part_s[...] = jnp.zeros_like(part_s)

    def block(b, _):
        for copy in copies_of(b):
            copy.wait()
        for lanes in lane_parts(rows):
            before, ratio, inverse = [state[i, :, lanes] for i in range(3)]
            part = [part_s[t, :, lanes] for t in range(tracers)]
            for at in range(ROWS8):
                l = b * ROWS8 + at
                if at == ROWS8 - 1:
                    now = jnp.where(b == blocks - 1, 0.0, coupling[jnp.minimum(l, levels - 2), :, lanes])
                else:
                    now = coupling[l, :, lanes]
                inverse = 1.0 / (1.0 + before + now - before * ratio)
                part = [(parts[t, l, :, lanes] + before * part[t]) * inverse for t in range(tracers)]
                ratio = now * inverse
                before = now
                ratios[l, :, lanes] = ratio
                for t in range(tracers):
                    parts[t, l, :, lanes] = part[t]
            for i, value in enumerate((before, ratio, inverse)):
                state[i, :, lanes] = value
            for t in range(tracers):
                part_s[t, :, lanes] = part[t]
        return 0

    lax.fori_loop(0, blocks, block, 0)
    for t in range(tracers):
        terms[t] = part_s[t]
    slope[...] = state[2]
    terms[tracers] = 1.0 / jnp.abs(signed[...]) + state[2]
    half_1[...] = terms[:, : width // 2, :]
    half_2[...] = terms[:, width // 2 :, :]
    mask = jnp.where(signed[...] > 0.0, 1.0, 0.0)

    def pack(east, west):
        for c in range(tracers + 1):
            east[c * reach : (c + 1) * reach, :] = terms[c, width - reach :, :]
            west[c * reach : (c + 1) * reach, :] = terms[c, :reach, :]
        at = (tracers + 1) * reach
        east[at : at + HALO, :] = mask[width - HALO :]
        west[at : at + HALO, :] = mask[:HALO]

    either(is_even(), pack, first_pair, second_pair)


def down_to_surface(tracers, diffusivity, signed, order, reach):
    count, levels, width, rows = tracers.shape
    packed = (count + 1) * reach + HALO
    packed = -(-packed // 8) * 8
    return pl.pallas_call(
        functools.partial(down_kernel, reach),
        in_specs=[HBM, VMEM, VMEM, VMEM],
        out_specs=[VMEM] * 8,
        out_shape=[
            shape_of(count, levels, width, rows),
            shape_of(levels, width, rows),
            shape_of(width, rows),
            shape_of(count + 1, width, rows),
            shape_of(count + 1, width // 2, rows),
            shape_of(count + 1, width // 2, rows),
            shape_of(packed, rows),
            shape_of(packed, rows),
        ],
        scratch_shapes=[
            pltpu.VMEM((3, width, rows), F32),
            pltpu.VMEM((count, width, rows), F32),
            pltpu.SemaphoreType.DMA((levels // ROWS8, count)),
        ],
        compiler_params=params(41),
        cost_estimate=pl.CostEstimate(
            flops=20 * levels * width * rows, bytes_accessed=10 * levels * width * rows * 4, transcendentals=0
        ),
        name="down_to_surface",
    )(tracers, diffusivity, signed, order)


def up_kernel(rim, parts, ratios, arrived, fixed, scale, rims, rim_scale):
    tracers, levels, width, rows = parts.shape
    blocks = levels // ROWS8
    for lanes in lane_parts(rows):

        def block(i, state):
            b = blocks - 1 - i
            start = pl.multiple_of(b * ROWS8, ROWS8)
            scale_now, fixed_now = state[0], list(state[1:])
            for at in reversed(range(ROWS8)):
                l = start + at
                ratio = ratios[l, :, lanes]
                scale_now = ratio * scale_now
                fixed_now = [parts[t, l, :, lanes] + ratio * fixed_now[t] for t in range(tracers)]
                if at == ROWS8 - 1:
                    scale_now = jnp.where(i == 0, 1.0, scale_now)
                    fixed_now = [jnp.where(i == 0, 0.0, value) for value in fixed_now]
                scale[l, :, lanes] = scale_now
                for t in range(tracers):
                    fixed[t, l, :, lanes] = fixed_now[t]
                for c, x in enumerate(rim):
                    rim_scale[c, b, at : at + 1, lanes] = scale_now[x : x + 1]
                    for t in range(tracers):
                        rims[t, c, b, at : at + 1, lanes] = fixed_now[t][x : x + 1]
            return scale_now, *fixed_now

        zero = jnp.zeros((width, lanes.stop - lanes.start), F32)
        lax.fori_loop(0, blocks, block, (zero,) * (1 + tracers))


def speed_kernel(columns, speed, *out):
    out[-1][...] = jnp.zeros_like(out[-1])
    for l in range(speed.shape[0]):
        for ref, x in zip(out, columns):
            ref[l : l + 1, :] = speed[l, x : x + 1, :]


def speed_columns(speed, columns):
    levels, width, rows = speed.shape
    return pl.pallas_call(
        functools.partial(speed_kernel, columns),
        in_specs=[VMEM],
        out_specs=[VMEM] * (len(columns) + 1),
        out_shape=[shape_of(levels, rows)] * len(columns) + [shape_of(ROWS8, 128)],
        compiler_params=params(20),
        cost_estimate=LITTLE,
        name="speed_columns",
    )(speed)


def up_from_surface(parts, ratios, arrived, rim):
    count, levels, width, rows = parts.shape
    fixed, scale, rims, rim_scale = pl.pallas_call(
        functools.partial(up_kernel, rim),
        in_specs=[VMEM] * 3,
        out_specs=[VMEM] * 4,
        out_shape=[
            shape_of(count, levels, width, rows),
            shape_of(levels, width, rows),
            shape_of(count, len(rim), levels // ROWS8, ROWS8, rows),
            shape_of(len(rim), levels // ROWS8, ROWS8, rows),
        ],
        input_output_aliases={0: 0, 1: 1},
        compiler_params=params(20),
        cost_estimate=LITTLE,
        name="up_from_surface",
    )(parts, ratios, arrived)
    rims, rim_scale = rims.reshape(count, len(rim), levels, rows), rim_scale.reshape(len(rim), levels, rows)
    return fixed, scale, rims, rim_scale


def leaving(u, opening):
    return opening * (jnp.maximum(u, 0.0) + NU), opening * (jnp.minimum(u, 0.0) - NU)


def surface_kernel(
    reach, own, slope, peer_1, peer_2, first_pair, second_pair, partner, weight, signed, rims, rim_scale, speed_0, speed_1,
    inflow, surface, open_e, coef_n, *rest,
):
    chunks = chunks_of(rims.shape[2])
    send_1, send_2, wide, opened = rest[: len(chunks)], rest[len(chunks) : 2 * len(chunks)], rest[-2], rest[-1]
    channels, width, rows = own.shape
    tracers = channels - 1
    first = 2 * 8
    even = is_even()

    for c in range(channels):
        wide[c, first : first + width // 2, :] = peer_1[c]
        wide[c, first + width // 2 : first + width, :] = peer_2[c]
    opened[:width, :] = jnp.where(signed[...] > 0.0, 1.0, 0.0)
    opened[width:, :] = jnp.zeros((ROWS8, rows), F32)

    def unpack(east, west):
        for c in range(channels):
            part = slice(c * reach, (c + 1) * reach)
            wide[c, first - reach : first, :] = west[part, :]
            wide[c, first + width : first + width + reach, :] = east[part, :]
        at = slice(channels * reach, channels * reach + HALO)
        opened[width : width + HALO, :] = east[at, :]
        opened[width + ROWS8 - HALO :, :] = west[at, :]

    either(even, unpack, first_pair, second_pair)

    start = lax.axis_index("tile") * width
    total = lax.axis_size("tile") * width
    for lanes in lane_parts(rows, 128):
        position = start + lax.broadcasted_iota(jnp.int32, (width, 128), 0)
        own_rest = own[tracers, :, lanes]
        flow = [jnp.zeros((width, 128), F32) for _ in range(tracers)]
        for k in range(partner.shape[0]):
            apart = partner[k, :, lanes] - position
            apart = jnp.where(apart > reach, apart - total, apart)
            apart = jnp.where(apart < -reach, apart + total, apart)
            found = [jnp.zeros((width, 128), F32) for _ in range(channels)]
            for offset in range(-reach, reach + 1):
                hit = apart == offset
                window = slice(first + offset, first + offset + width)
                found = [jnp.where(hit, wide[c, window, lanes], f) for c, f in enumerate(found)]
            factor = weight[k, :, lanes].astype(F32) / (own_rest + found[-1])
            flow = [flow[t] + factor * (own[t, :, lanes] - found[t]) for t in range(tracers)]
        for t in range(tracers):
            into = flow[t] * (-1.0 / QUANT)
            inflow[t, :, lanes] = into
            surface[t, :, lanes] = own[t, :, lanes] + slope[:, lanes] * into

    wide_rows = width + ROWS8
    free = jnp.broadcast_to(lax.axis_index("mp"), (wide_rows, rows)) == 0
    here = jnp.where(free, 1.0, opened[...])
    column = lax.broadcasted_iota(jnp.int32, (wide_rows, rows), 1)
    open_e[...] = here * pltpu.roll(here, wide_rows - 1, 0)
    coef_n[...] = NU * (here * jnp.where(column == rows - 1, 0.0, pltpu.roll(here, rows - 1, 1)))

    for c, (begin, size) in enumerate(chunks):
        part = slice(begin, begin + size)
        faces_w = leaving(speed_0[part, :], open_e[:1, :])
        faces_e = leaving(speed_1[part, :], open_e[width - 2 : width - 1, :])
        for t in range(tracers):
            columns = []
            for i, x in enumerate((0, 1, width - 2, width - 1)):
                columns.append(rims[t, i, part, :] + rim_scale[i, part, :] * surface[t, x : x + 1, :])
            west = columns[0], faces_w[0] * columns[0] + faces_w[1] * columns[1]
            east = columns[3], faces_e[0] * columns[2] + faces_e[1] * columns[3]
            for i in range(2):
                send_1[c][t, i] = jnp.where(even, east[i], west[i])
                send_2[c][t, i] = jnp.where(even, west[i], east[i])


def exchange_surface(
    own, slope, peers, first_pair, second_pair, partner, weight, signed, rims, rim_scale, speeds, reach
):
    channels, width, rows = own.shape
    count, _, levels, _ = rims.shape
    plane = shape_of(width + ROWS8, rows)
    edges = [shape_of(count, 2, size, rows) for _, size in chunks_of(levels)]
    return pl.pallas_call(
        functools.partial(surface_kernel, reach),
        in_specs=[VMEM] * 13,
        out_specs=[VMEM] * (4 + 2 * len(edges)),
        out_shape=[shape_of(count, width, rows)] * 2 + [plane] * 2 + edges * 2,
        scratch_shapes=[pltpu.VMEM((channels, 16 + width + 16, rows), F32), pltpu.VMEM((width + ROWS8, rows), F32)],
        compiler_params=params(20),
        cost_estimate=LITTLE,
        name="exchange_surface",
    )(own, slope, *peers, first_pair, second_pair, partner, weight, signed, rims, rim_scale, *speeds)


def along_y(north, value):
    flux = north * (pltpu.roll(value, value.shape[-1] - 1, 1) - value)
    return flux - pltpu.roll(flux, 1, 1)


def inner_steps(q, a, b, north, width, put, keep):
    end = width - 1
    here, flux, once_before, flux_before = q(0), None, None, None
    for x in range(width):
        if x == 0:
            east = q(1)
            flux_e = a(0) * here + b(0) * east
            keep(0, here)
            keep(1, (here - flux_e) + along_y(north(0), here))
            once = None
        elif x == end:
            keep(4, here)
            keep(5, (here + flux) + along_y(north(end), here))
            keep(6, once_before)
            keep(7, (once_before + flux_before) + along_y(north(end - 1), once_before))
            break
        else:
            east = q(x + 1)
            flux_e = a(x) * here + b(x) * east
            once = (here - (flux_e - flux)) + along_y(north(x), here)
        if once_before is not None:
            flux_once = a(x - 1) * once_before + b(x - 1) * once
            second = along_y(north(x - 1), once_before)
            if flux_before is None:
                keep(2, once_before)
                keep(3, (once_before - flux_once) + second)
            else:
                put(x - 1, (once_before - (flux_once - flux_before)) + second)
            flux_before = flux_once
        here, flux, once_before = east, flux_e, once


def rim_steps(kept, west, east, a, b, north, width):
    end = width - 1
    value, behind = west
    flux = a(-1) * value + b(-1) * kept(0)
    outer = (value - (flux - behind)) + along_y(north(-1), value)
    edge = kept(1) + flux
    flux_out = a(-1) * outer + b(-1) * edge
    flux_in = a(0) * edge + b(0) * kept(2)
    new = {0: (edge - (flux_in - flux_out)) + along_y(north(0), edge), 1: kept(3) + flux_in}
    value, behind = east
    flux = a(end) * kept(4) + b(end) * value
    outer = (value - (behind - flux)) + along_y(north(width), value)
    edge = kept(5) - flux
    flux_out = a(end) * edge + b(end) * outer
    flux_in = a(end - 1) * kept(6) + b(end - 1) * edge
    new[end] = (edge - (flux_out - flux_in)) + along_y(north(end), edge)
    new[end - 1] = kept(7) - flux_in
    return new


def tiles_in(turn, value):
    levels, width, _ = value.shape
    for j in range(turn.shape[0]):
        turn[j] = value[:, :, 128 * j : 128 * (j + 1)].reshape(levels * width, 128)


def column(turn, x, width):
    parts = [turn[j, pl.ds(x, ROWS8, stride=width), :] for j in range(turn.shape[0])]
    return jnp.concatenate(parts, axis=1)


def put_column(stage, t, start, x, value):
    parts, tracers, levels, width, lanes = stage.shape
    rows = stage.reshape(parts, tracers, levels * width, lanes)
    for j in range(parts):
        at = pl.ds(start * width + x, ROWS8, stride=width)
        rows[j, t, at, :] = value[:, lanes * j : lanes * (j + 1)]


def ring(x, width):
    return x if x >= 0 else width + ROWS8 + x


def spread_north(coef_n, north_s, width):
    for x in range(1 - HALO, width + HALO - 1):
        row = ring(x, width)
        north_s[x + HALO] = jnp.broadcast_to(coef_n[row : row + 1, :], north_s.shape[1:])


def face(coefs, part, x, u, open_e, width):
    row = ring(x, width)
    coefs[0, x + 1, part, :], coefs[1, x + 1, part, :] = leaving(u, open_e[row : row + 1, :])


def faces(coefs, part):
    return [lambda x, i=i: coefs[i, x + 1, part, :] for i in range(2)]


def first_inner_kernel(
    begin, fixed, scale, surface, speed, open_e, coef_n,
    field, rims, coefs, coef_n_out, north_s, turn, turn_speed,
):
    tracers, levels, width, rows = fixed.shape
    size = field.shape[2]
    spread_north(coef_n, north_s, width)
    north = lambda x: north_s[x + HALO]

    def block(i, _):
        start = pl.multiple_of(i * ROWS8, ROWS8)
        part, whole = pl.ds(start, ROWS8), pl.ds(begin + start, ROWS8)
        tiles_in(turn_speed, speed[whole])
        for x in range(width):
            face(coefs, part, x, column(turn_speed, x, width), open_e, width)

        def tracer(t, _):
            tiles_in(turn, fixed[t, whole] + scale[whole] * surface[t][None])

            def put(x, value):
                field[t, x, part, :] = value

            def keep(i, value):
                rims[t, i, part, :] = value

            q = lambda x: column(turn, x, width)
            inner_steps(q, *faces(coefs, part), north, width, put, keep)
            return 0

        lax.fori_loop(0, tracers, tracer, 0)
        return 0

    lax.fori_loop(0, size // ROWS8, block, 0)


def halo_pair(even, halo_1, halo_2, t, part):
    pairs = [(halo_1[t, i, part, :], halo_2[t, i, part, :]) for i in range(2)]
    west = [jnp.where(even, second, first) for first, second in pairs]
    east = [jnp.where(even, first, second) for first, second in pairs]
    return west, east


def first_rim_kernel(
    begin, rims, speed_w, open_e, halo_1, halo_2, coef_n, field_in, coefs_in,
    field, coefs, send_1, send_2, coef_n_out, north_s,
):
    tracers, width, size, rows = field.shape
    even = is_even()
    spread_north(coef_n, north_s, width)
    north = lambda x: north_s[x + HALO]

    def block(i, _):
        start = pl.multiple_of(i * ROWS8, ROWS8)
        part, whole = pl.ds(start, ROWS8), pl.ds(begin + start, ROWS8)
        face(coefs, part, -1, speed_w[whole, :], open_e, width)
        a, b = faces(coefs, part)

        def tracer(t, _):
            halos = halo_pair(even, halo_1, halo_2, t, part)
            new = rim_steps(lambda i: rims[t, i, part, :], *halos, a, b, north, width)
            for x, value in new.items():
                field[t, x, part, :] = value
            end = width - 1
            west = new[0], a(0) * new[0] + b(0) * new[1]
            east = new[end], a(end - 1) * new[end - 1] + b(end - 1) * new[end]
            for i in range(2):
                send_1[t, i, part, :] = jnp.where(even, east[i], west[i])
                send_2[t, i, part, :] = jnp.where(even, west[i], east[i])
            return 0

        lax.fori_loop(0, tracers, tracer, 0)
        return 0

    lax.fori_loop(0, size // ROWS8, block, 0)


def last_inner_kernel(field, coefs, coef_n, stage, rims, coef_n_out, north_s):
    tracers, width, size, rows = field.shape
    spread_north(coef_n, north_s, width)
    north = lambda x: north_s[x + HALO]

    def block(i, _):
        start = pl.multiple_of(i * ROWS8, ROWS8)
        part = pl.ds(start, ROWS8)

        def tracer(t, _):
            q = lambda x: field[t, x, part, :]
            put = lambda x, value: put_column(stage, t, start, x, value)

            def keep(i, value):
                rims[t, i, part, :] = value

            inner_steps(q, *faces(coefs, part), north, width, put, keep)
            return 0

        lax.fori_loop(0, tracers, tracer, 0)
        return 0

    lax.fori_loop(0, size // ROWS8, block, 0)


def last_rim_kernel(begin, rims, coefs, halo_1, halo_2, coef_n, stage_in, *refs):
    out, stage, coef_n_out, north_s, sems = refs[-5:]
    _, tracers, size, width, _ = stage.shape
    even = is_even()
    spread_north(coef_n, north_s, width)
    north = lambda x: north_s[x + HALO]

    def copies_of(i):
        start = pl.multiple_of(i * ROWS8, ROWS8)
        part, to = pl.ds(start, ROWS8), pl.ds(begin + start, ROWS8)
        return [
            pltpu.make_async_copy(stage.at[j, :, part], out.at[:, to, :, pl.ds(128 * j, 128)], sems.at[i, j])
            for j in range(stage.shape[0])
        ]

    def block(i, _):
        start = pl.multiple_of(i * ROWS8, ROWS8)
        part = pl.ds(start, ROWS8)

        def tracer(t, _):
            halos = halo_pair(even, halo_1, halo_2, t, part)
            new = rim_steps(lambda i: rims[t, i, part, :], *halos, *faces(coefs, part), north, width)
            for x, value in new.items():
                put_column(stage, t, start, x, value)
            return 0

        lax.fori_loop(0, tracers, tracer, 0)
        for copy in copies_of(i):
            copy.start()
        return 0

    def finish(i, _):
        for copy in copies_of(i):
            copy.wait()
        return 0

    lax.fori_loop(0, size // ROWS8, block, 0)
    lax.fori_loop(0, size // ROWS8, finish, 0)


def transport_call(kernel, name, args, out_shape, aliases, scratch, cells, hbm=(), out_hbm=()):
    return pl.pallas_call(
        kernel,
        in_specs=[HBM if i in hbm else VMEM for i in range(len(args))],
        out_specs=[HBM if i in out_hbm else VMEM for i in range(len(out_shape))],
        out_shape=out_shape,
        scratch_shapes=scratch,
        input_output_aliases=aliases,
        compiler_params=params(16),
        cost_estimate=LITTLE,
        name=name,
    )(*args)


def north_scratch(width, rows):
    return pltpu.VMEM((width + 2 * HALO, ROWS8, rows), F32)


def first_inner(chunk, fixed, scale, surface, speed, open_e, coef_n):
    count, levels, width, rows = fixed.shape
    begin, size = chunk
    args = [fixed, scale, surface, speed, open_e, coef_n]
    out_shape = [
        shape_of(count, width, size, rows),
        shape_of(count, 8, size, rows),
        shape_of(2, width + 1, size, rows),
        shape_of(*coef_n.shape),
    ]
    turn = pltpu.VMEM((rows // 128, ROWS8 * width, 128), F32)
    return transport_call(
        functools.partial(first_inner_kernel, begin), "first_inner", args, out_shape, {len(args) - 1: 3},
        [north_scratch(width, rows), turn, turn], count * size * width * rows,
    )


def first_rim(chunk, field, rims, coefs, speed_w, open_e, halos, coef_n):
    count, width, size, rows = field.shape
    args = [rims, speed_w, open_e, *halos, coef_n, field, coefs]
    edge = shape_of(count, 2, size, rows)
    out_shape = [shape_of(*field.shape), shape_of(*coefs.shape), edge, edge, shape_of(*coef_n.shape)]
    field, coefs, send_1, send_2, coef_n = transport_call(
        functools.partial(first_rim_kernel, chunk[0]), "first_rim", args, out_shape, {5: 4, 6: 0, 7: 1},
        [north_scratch(width, rows)], count * size * 4 * rows,
    )
    return field, coefs, (send_1, send_2), coef_n


def last_inner(field, coefs, coef_n):
    count, width, size, rows = field.shape
    out_shape = [
        shape_of(rows // 128, count, size, width, 128),
        shape_of(count, 8, size, rows),
        shape_of(*coef_n.shape),
    ]
    return transport_call(
        last_inner_kernel, "last_inner", [field, coefs, coef_n], out_shape, {2: 2},
        [north_scratch(width, rows)], count * size * width * rows,
    )


def last_rim(chunk, levels, rims, coefs, halos, stage, coef_n, result):
    lane_tiles, count, size, width, lanes = stage.shape
    rows = lane_tiles * lanes
    args = [rims, coefs, *halos, coef_n, stage]
    aliases = {4: 2, 5: 1}
    if result is not None:
        aliases[6] = 0
        args.append(result)
    out_shape = [shape_of(count, levels, width, rows), shape_of(*stage.shape), shape_of(*coef_n.shape)]
    result, _, coef_n = transport_call(
        functools.partial(last_rim_kernel, chunk[0]), "last_rim", args, out_shape, aliases,
        [north_scratch(width, rows), pltpu.SemaphoreType.DMA((size // ROWS8, rows // 128))],
        count * size * 4 * rows, hbm=(6,), out_hbm=(0,),
    )
    return result, coef_n


def per_device(tracers, diffusivity, conductance, face_velocity, partner, weight, sea_mask):
    tiles = lax.axis_size("tile")
    tracers, diffusivity, conductance = tracers[0], diffusivity[0], conductance[0]
    speed, partner, weight = face_velocity[0], partner[0], weight[0]
    width = tracers.shape[2]
    reach = width // 2 + 1

    def move(value, target_of, swap=False):
        pairs = []
        for m in range(2):
            for t in range(tiles):
                target = (1 - m if swap else m) * tiles + target_of(t) % tiles
                pairs.append((m * tiles + t, target))
        return lax.ppermute(value, ("mp", "tile"), pairs)

    one = lambda t: t + 1 - 2 * (t % 2)
    two = lambda t: t - 1 + 2 * (t % 2)

    *speeds, to_east, order = speed_columns(speed, (0, width - 2, width - 1))
    speed_w = move(to_east, lambda t: t + 1)
    signed = jnp.where(sea_mask > 0, conductance, -conductance)
    parts, ratios, slope, own, *halves, terms_1, terms_2 = down_to_surface(tracers, diffusivity, signed, order, reach)
    terms_1 = move(terms_1, one, swap=True)
    terms_2 = move(terms_2, two, swap=True)
    peers = [move(half, lambda t: t, swap=True) for half in halves]
    rim = (0, 1, width - 2, width - 1)
    fixed, scale, rims, rim_scale = up_from_surface(parts, ratios, speed_w, rim)

    inflow, surface, open_e, coef_n, *sends = exchange_surface(
        own, slope, peers, terms_1, terms_2, partner, weight, signed, rims, rim_scale, speeds, reach
    )
    levels = fixed.shape[1]
    chunks = chunks_of(levels)
    every = range(len(chunks))
    exchange = lambda pair: (move(pair[0], one), move(pair[1], two))
    halos = [exchange((sends[c], sends[len(chunks) + c])) for c in every]
    fields, rims, coefs, stages = [[None] * len(chunks) for _ in range(4)]
    for c in every:
        fields[c], rims[c], coefs[c], coef_n = first_inner(chunks[c], fixed, scale, surface, speed, open_e, coef_n)
    for c in every:
        fields[c], coefs[c], pair, coef_n = first_rim(
            chunks[c], fields[c], rims[c], coefs[c], speed_w, open_e, halos[c], coef_n
        )
        halos[c] = exchange(pair)
    for c in every:
        stages[c], rims[c], coef_n = last_inner(fields[c], coefs[c], coef_n)
    result = None
    for c in every:
        result, coef_n = last_rim(chunks[c], levels, rims[c], coefs[c], halos[c], stages[c], coef_n, result)
    return result[None], inflow[None]


def solution(mesh):
    in_specs = (
        P("mp", None, None, "tile", None),
        P("mp", None, "tile", None),
        P("mp", "tile", None),
        P("mp", None, "tile", None),
        P("mp", None, "tile", None),
        P("mp", None, "tile", None),
        P("tile", None),
    )
    out_specs = (P("mp", None, None, "tile", None), P("mp", None, "tile", None))
    return jax.shard_map(
        per_device, mesh=mesh, in_specs=in_specs, out_specs=out_specs, check_vma=False
    )
```

```python
import functools

import jax
import jax.numpy as jnp
from jax import lax
from jax.experimental import pallas as pl
from jax.experimental.pallas import tpu as pltpu
from jax.sharding import PartitionSpec as P

STEPS = 4
QUANT = 16
NU = 0.12
ROWS8 = 8
PARTS = (1, 1)
HALO = 2
F32 = jnp.float32
LITTLE = pl.CostEstimate(flops=1, bytes_accessed=1024, transcendentals=0)
VMEM = pl.BlockSpec(memory_space=pltpu.VMEM)
HBM = pl.BlockSpec(memory_space=pltpu.HBM)


def shape_of(*shape):
    return jax.ShapeDtypeStruct(shape, F32)


def params(mib):
    return pltpu.CompilerParams(vmem_limit_bytes=mib * 2**20)


def is_even():
    return lax.rem(lax.axis_index("tile"), 2) == 0


def either(even, call, first, second):
    @pl.when(even)
    def _():
        call(first, second)

    @pl.when(jnp.logical_not(even))
    def _():
        call(second, first)


def chunks_of(levels):
    sizes = [part * levels // sum(PARTS) for part in PARTS]
    return [(sum(sizes[:c]), size) for c, size in enumerate(sizes)]


def lane_parts(total, size=256):
    size = min(size, total)
    return [slice(start, start + size) for start in range(0, total, size)]


def down_kernel(reach, source, coupling, signed, order, parts, ratios, slope, terms, half_1, half_2, first_pair, second_pair, state, part_s, sems):
    tracers, levels, width, rows = source.shape
    blocks = levels // ROWS8

    def copies_of(b):
        part = pl.ds(b * ROWS8, ROWS8)
        return [pltpu.make_async_copy(source.at[t, part], parts.at[t, part], sems.at[b, t]) for t in range(tracers)]

    for b in range(blocks):
        for copy in copies_of(b):
            copy.start()
    state[...] = jnp.zeros_like(state)
    part_s[...] = jnp.zeros_like(part_s)

    def block(b, _):
        for copy in copies_of(b):
            copy.wait()
        for lanes in lane_parts(rows):
            before, ratio, inverse = [state[i, :, lanes] for i in range(3)]
            part = [part_s[t, :, lanes] for t in range(tracers)]
            for at in range(ROWS8):
                l = b * ROWS8 + at
                if at == ROWS8 - 1:
                    now = jnp.where(b == blocks - 1, 0.0, coupling[jnp.minimum(l, levels - 2), :, lanes])
                else:
                    now = coupling[l, :, lanes]
                inverse = 1.0 / (1.0 + before + now - before * ratio)
                part = [(parts[t, l, :, lanes] + before * part[t]) * inverse for t in range(tracers)]
                ratio = now * inverse
                before = now
                ratios[l, :, lanes] = ratio
                for t in range(tracers):
                    parts[t, l, :, lanes] = part[t]
            for i, value in enumerate((before, ratio, inverse)):
                state[i, :, lanes] = value
            for t in range(tracers):
                part_s[t, :, lanes] = part[t]
        return 0

    lax.fori_loop(0, blocks, block, 0)
    for t in range(tracers):
        terms[t] = part_s[t]
    slope[...] = state[2]
    terms[tracers] = 1.0 / jnp.abs(signed[...]) + state[2]
    half_1[...] = terms[:, : width // 2, :]
    half_2[...] = terms[:, width // 2 :, :]
    mask = jnp.where(signed[...] > 0.0, 1.0, 0.0)

    def pack(east, west):
        for c in range(tracers + 1):
            east[c * reach : (c + 1) * reach, :] = terms[c, width - reach :, :]
            west[c * reach : (c + 1) * reach, :] = terms[c, :reach, :]
        at = (tracers + 1) * reach
        east[at : at + HALO, :] = mask[width - HALO :]
        west[at : at + HALO, :] = mask[:HALO]

    either(is_even(), pack, first_pair, second_pair)


def down_to_surface(tracers, diffusivity, signed, order, reach):
    count, levels, width, rows = tracers.shape
    packed = (count + 1) * reach + HALO
    packed = -(-packed // 8) * 8
    return pl.pallas_call(
        functools.partial(down_kernel, reach),
        in_specs=[HBM, VMEM, VMEM, VMEM],
        out_specs=[VMEM] * 8,
        out_shape=[
            shape_of(count, levels, width, rows),
            shape_of(levels, width, rows),
            shape_of(width, rows),
            shape_of(count + 1, width, rows),
            shape_of(count + 1, width // 2, rows),
            shape_of(count + 1, width // 2, rows),
            shape_of(packed, rows),
            shape_of(packed, rows),
        ],
        scratch_shapes=[
            pltpu.VMEM((3, width, rows), F32),
            pltpu.VMEM((count, width, rows), F32),
            pltpu.SemaphoreType.DMA((levels // ROWS8, count)),
        ],
        compiler_params=params(41),
        cost_estimate=pl.CostEstimate(
            flops=20 * levels * width * rows, bytes_accessed=10 * levels * width * rows * 4, transcendentals=0
        ),
        name="down_to_surface",
    )(tracers, diffusivity, signed, order)


def up_kernel(rim, parts, ratios, arrived, fixed, scale, rims, rim_scale):
    tracers, levels, width, rows = parts.shape
    blocks = levels // ROWS8
    for lanes in lane_parts(rows):

        def block(i, state):
            b = blocks - 1 - i
            start = pl.multiple_of(b * ROWS8, ROWS8)
            scale_now, fixed_now = state[0], list(state[1:])
            for at in reversed(range(ROWS8)):
                l = start + at
                ratio = ratios[l, :, lanes]
                scale_now = ratio * scale_now
                fixed_now = [parts[t, l, :, lanes] + ratio * fixed_now[t] for t in range(tracers)]
                if at == ROWS8 - 1:
                    scale_now = jnp.where(i == 0, 1.0, scale_now)
                    fixed_now = [jnp.where(i == 0, 0.0, value) for value in fixed_now]
                scale[l, :, lanes] = scale_now
                for t in range(tracers):
                    fixed[t, l, :, lanes] = fixed_now[t]
                for c, x in enumerate(rim):
                    rim_scale[c, b, at : at + 1, lanes] = scale_now[x : x + 1]
                    for t in range(tracers):
                        rims[t, c, b, at : at + 1, lanes] = fixed_now[t][x : x + 1]
            return scale_now, *fixed_now

        zero = jnp.zeros((width, lanes.stop - lanes.start), F32)
        lax.fori_loop(0, blocks, block, (zero,) * (1 + tracers))


def speed_kernel(columns, speed, *out):
    out[-1][...] = jnp.zeros_like(out[-1])
    for l in range(speed.shape[0]):
        for ref, x in zip(out, columns):
            ref[l : l + 1, :] = speed[l, x : x + 1, :]


def speed_columns(speed, columns):
    levels, width, rows = speed.shape
    return pl.pallas_call(
        functools.partial(speed_kernel, columns),
        in_specs=[VMEM],
        out_specs=[VMEM] * (len(columns) + 1),
        out_shape=[shape_of(levels, rows)] * len(columns) + [shape_of(ROWS8, 128)],
        compiler_params=params(20),
        cost_estimate=LITTLE,
        name="speed_columns",
    )(speed)


def up_from_surface(parts, ratios, arrived, rim):
    count, levels, width, rows = parts.shape
    fixed, scale, rims, rim_scale = pl.pallas_call(
        functools.partial(up_kernel, rim),
        in_specs=[VMEM] * 3,
        out_specs=[VMEM] * 4,
        out_shape=[
            shape_of(count, levels, width, rows),
            shape_of(levels, width, rows),
            shape_of(count, len(rim), levels // ROWS8, ROWS8, rows),
            shape_of(len(rim), levels // ROWS8, ROWS8, rows),
        ],
        input_output_aliases={0: 0, 1: 1},
        compiler_params=params(20),
        cost_estimate=LITTLE,
        name="up_from_surface",
    )(parts, ratios, arrived)
    rims, rim_scale = rims.reshape(count, len(rim), levels, rows), rim_scale.reshape(len(rim), levels, rows)
    return fixed, scale, rims, rim_scale


def leaving(u, opening):
    return opening * (jnp.maximum(u, 0.0) + NU), opening * (jnp.minimum(u, 0.0) - NU)


def surface_kernel(
    reach, own, slope, peer_1, peer_2, first_pair, second_pair, partner, weight, signed, rims, rim_scale, speed_0, speed_1,
    inflow, surface, open_e, coef_n, *rest,
):
    chunks = chunks_of(rims.shape[2])
    send_1, send_2, wide, opened = rest[: len(chunks)], rest[len(chunks) : 2 * len(chunks)], rest[-2], rest[-1]
    channels, width, rows = own.shape
    tracers = channels - 1
    first = 2 * 8
    even = is_even()

    for c in range(channels):
        wide[c, first : first + width // 2, :] = peer_1[c]
        wide[c, first + width // 2 : first + width, :] = peer_2[c]
    opened[:width, :] = jnp.where(signed[...] > 0.0, 1.0, 0.0)
    opened[width:, :] = jnp.zeros((ROWS8, rows), F32)

    def unpack(east, west):
        for c in range(channels):
            part = slice(c * reach, (c + 1) * reach)
            wide[c, first - reach : first, :] = west[part, :]
            wide[c, first + width : first + width + reach, :] = east[part, :]
        at = slice(channels * reach, channels * reach + HALO)
        opened[width : width + HALO, :] = east[at, :]
        opened[width + ROWS8 - HALO :, :] = west[at, :]

    either(even, unpack, first_pair, second_pair)

    start = lax.axis_index("tile") * width
    total = lax.axis_size("tile") * width
    for lanes in lane_parts(rows, 128):
        position = start + lax.broadcasted_iota(jnp.int32, (width, 128), 0)
        own_rest = own[tracers, :, lanes]
        flow = [jnp.zeros((width, 128), F32) for _ in range(tracers)]
        for k in range(partner.shape[0]):
            apart = partner[k, :, lanes] - position
            apart = jnp.where(apart > reach, apart - total, apart)
            apart = jnp.where(apart < -reach, apart + total, apart)
            found = [jnp.zeros((width, 128), F32) for _ in range(channels)]
            for offset in range(-reach, reach + 1):
                hit = apart == offset
                window = slice(first + offset, first + offset + width)
                found = [jnp.where(hit, wide[c, window, lanes], f) for c, f in enumerate(found)]
            factor = weight[k, :, lanes].astype(F32) / (own_rest + found[-1])
            flow = [flow[t] + factor * (own[t, :, lanes] - found[t]) for t in range(tracers)]
        for t in range(tracers):
            into = flow[t] * (-1.0 / QUANT)
            inflow[t, :, lanes] = into
            surface[t, :, lanes] = own[t, :, lanes] + slope[:, lanes] * into

    wide_rows = width + ROWS8
    free = jnp.broadcast_to(lax.axis_index("mp"), (wide_rows, rows)) == 0
    here = jnp.where(free, 1.0, opened[...])
    column = lax.broadcasted_iota(jnp.int32, (wide_rows, rows), 1)
    open_e[...] = here * pltpu.roll(here, wide_rows - 1, 0)
    coef_n[...] = NU * (here * jnp.where(column == rows - 1, 0.0, pltpu.roll(here, rows - 1, 1)))

    for c, (begin, size) in enumerate(chunks):
        part = slice(begin, begin + size)
        faces_w = leaving(speed_0[part, :], open_e[:1, :])
        faces_e = leaving(speed_1[part, :], open_e[width - 2 : width - 1, :])
        for t in range(tracers):
            columns = []
            for i, x in enumerate((0, 1, width - 2, width - 1)):
                columns.append(rims[t, i, part, :] + rim_scale[i, part, :] * surface[t, x : x + 1, :])
            west = columns[0], faces_w[0] * columns[0] + faces_w[1] * columns[1]
            east = columns[3], faces_e[0] * columns[2] + faces_e[1] * columns[3]
            for i in range(2):
                send_1[c][t, i] = jnp.where(even, east[i], west[i])
                send_2[c][t, i] = jnp.where(even, west[i], east[i])


def exchange_surface(
    own, slope, peers, first_pair, second_pair, partner, weight, signed, rims, rim_scale, speeds, reach
):
    channels, width, rows = own.shape
    count, _, levels, _ = rims.shape
    plane = shape_of(width + ROWS8, rows)
    edges = [shape_of(count, 2, size, rows) for _, size in chunks_of(levels)]
    return pl.pallas_call(
        functools.partial(surface_kernel, reach),
        in_specs=[VMEM] * 13,
        out_specs=[VMEM] * (4 + 2 * len(edges)),
        out_shape=[shape_of(count, width, rows)] * 2 + [plane] * 2 + edges * 2,
        scratch_shapes=[pltpu.VMEM((channels, 16 + width + 16, rows), F32), pltpu.VMEM((width + ROWS8, rows), F32)],
        compiler_params=params(20),
        cost_estimate=LITTLE,
        name="exchange_surface",
    )(own, slope, *peers, first_pair, second_pair, partner, weight, signed, rims, rim_scale, *speeds)


def along_y(north, value):
    flux = north * (pltpu.roll(value, value.shape[-1] - 1, 1) - value)
    return flux - pltpu.roll(flux, 1, 1)


def inner_steps(q, a, b, north, width, put, keep):
    end = width - 1
    here, flux, once_before, flux_before = q(0), None, None, None
    for x in range(width):
        if x == 0:
            east = q(1)
            flux_e = a(0) * here + b(0) * east
            keep(0, here)
            keep(1, (here - flux_e) + along_y(north(0), here))
            once = None
        elif x == end:
            keep(4, here)
            keep(5, (here + flux) + along_y(north(end), here))
            keep(6, once_before)
            keep(7, (once_before + flux_before) + along_y(north(end - 1), once_before))
            break
        else:
            east = q(x + 1)
            flux_e = a(x) * here + b(x) * east
            once = (here - (flux_e - flux)) + along_y(north(x), here)
        if once_before is not None:
            flux_once = a(x - 1) * once_before + b(x - 1) * once
            second = along_y(north(x - 1), once_before)
            if flux_before is None:
                keep(2, once_before)
                keep(3, (once_before - flux_once) + second)
            else:
                put(x - 1, (once_before - (flux_once - flux_before)) + second)
            flux_before = flux_once
        here, flux, once_before = east, flux_e, once


def rim_steps(kept, west, east, a, b, north, width):
    end = width - 1
    value, behind = west
    flux = a(-1) * value + b(-1) * kept(0)
    outer = (value - (flux - behind)) + along_y(north(-1), value)
    edge = kept(1) + flux
    flux_out = a(-1) * outer + b(-1) * edge
    flux_in = a(0) * edge + b(0) * kept(2)
    new = {0: (edge - (flux_in - flux_out)) + along_y(north(0), edge), 1: kept(3) + flux_in}
    value, behind = east
    flux = a(end) * kept(4) + b(end) * value
    outer = (value - (behind - flux)) + along_y(north(width), value)
    edge = kept(5) - flux
    flux_out = a(end) * edge + b(end) * outer
    flux_in = a(end - 1) * kept(6) + b(end - 1) * edge
    new[end] = (edge - (flux_out - flux_in)) + along_y(north(end), edge)
    new[end - 1] = kept(7) - flux_in
    return new


def tiles_in(turn, value):
    levels, width, _ = value.shape
    for j in range(turn.shape[0]):
        turn[j, : levels * width, :] = value[:, :, 128 * j : 128 * (j + 1)].reshape(levels * width, 128)


def column(turn, x, width):
    parts = [turn[j, pl.ds(x, ROWS8, stride=width), :] for j in range(turn.shape[0])]
    return jnp.concatenate(parts, axis=1)


def put_column(stage, t, start, x, value):
    parts, tracers, levels, width, lanes = stage.shape
    rows = stage.reshape(parts, tracers, levels * width, lanes)
    for j in range(parts):
        at = pl.ds(start * width + x, ROWS8, stride=width)
        rows[j, t, at, :] = value[:, lanes * j : lanes * (j + 1)]


def ring(x, width):
    return x if x >= 0 else width + ROWS8 + x


def spread_north(coef_n, north_s, width):
    for x in range(1 - HALO, width + HALO - 1):
        row = ring(x, width)
        north_s[x + HALO] = jnp.broadcast_to(coef_n[row : row + 1, :], north_s.shape[1:])


def face(coefs, part, x, u, open_e, width):
    row = ring(x, width)
    coefs[0, x + 1, part, :], coefs[1, x + 1, part, :] = leaving(u, open_e[row : row + 1, :])


def faces(coefs, part):
    return [lambda x, i=i: coefs[i, x + 1, part, :] for i in range(2)]


def first_inner_kernel(
    begin, fixed, scale, surface, speed, open_e, coef_n,
    field, rims, coefs, coef_n_out, north_s, turn, turn_speed,
):
    tracers, levels, width, rows = fixed.shape
    size = field.shape[2]
    spread_north(coef_n, north_s, width)
    north = lambda x: north_s[x + HALO]

    def block(i, _):
        start = pl.multiple_of(i * ROWS8, ROWS8)
        part, whole = pl.ds(start, ROWS8), pl.ds(begin + start, ROWS8)
        tiles_in(turn_speed, speed[whole])
        for x in range(width):
            face(coefs, part, x, column(turn_speed, x, width), open_e, width)

        def tracer(t, _):
            tiles_in(turn, fixed[t, whole] + scale[whole] * surface[t][None])

            def put(x, value):
                field[t, x, part, :] = value

            def keep(i, value):
                rims[t, i, part, :] = value

            q = lambda x: column(turn, x, width)
            inner_steps(q, *faces(coefs, part), north, width, put, keep)
            return 0

        lax.fori_loop(0, tracers, tracer, 0)
        return 0

    lax.fori_loop(0, size // ROWS8, block, 0)


def halo_pair(even, halo_1, halo_2, t, part):
    pairs = [(halo_1[t, i, part, :], halo_2[t, i, part, :]) for i in range(2)]
    west = [jnp.where(even, second, first) for first, second in pairs]
    east = [jnp.where(even, first, second) for first, second in pairs]
    return west, east


def first_rim_kernel(
    begin, rims, speed_w, open_e, halo_1, halo_2, coef_n, field_in, coefs_in,
    field, coefs, send_1, send_2, coef_n_out, north_s,
):
    tracers, width, size, rows = field.shape
    even = is_even()
    spread_north(coef_n, north_s, width)
    north = lambda x: north_s[x + HALO]

    def block(i, _):
        start = pl.multiple_of(i * ROWS8, ROWS8)
        part, whole = pl.ds(start, ROWS8), pl.ds(begin + start, ROWS8)
        face(coefs, part, -1, speed_w[whole, :], open_e, width)
        a, b = faces(coefs, part)

        def tracer(t, _):
            halos = halo_pair(even, halo_1, halo_2, t, part)
            new = rim_steps(lambda i: rims[t, i, part, :], *halos, a, b, north, width)
            for x, value in new.items():
                field[t, x, part, :] = value
            end = width - 1
            west = new[0], a(0) * new[0] + b(0) * new[1]
            east = new[end], a(end - 1) * new[end - 1] + b(end - 1) * new[end]
            for i in range(2):
                send_1[t, i, part, :] = jnp.where(even, east[i], west[i])
                send_2[t, i, part, :] = jnp.where(even, west[i], east[i])
            return 0

        lax.fori_loop(0, tracers, tracer, 0)
        return 0

    lax.fori_loop(0, size // ROWS8, block, 0)


def last_inner_kernel(field, coefs, coef_n, stage, rims, coef_n_out, north_s):
    tracers, width, size, rows = field.shape
    spread_north(coef_n, north_s, width)
    north = lambda x: north_s[x + HALO]

    def block(i, _):
        start = pl.multiple_of(i * ROWS8, ROWS8)
        part = pl.ds(start, ROWS8)

        def tracer(t, _):
            q = lambda x: field[t, x, part, :]
            put = lambda x, value: put_column(stage, t, start, x, value)

            def keep(i, value):
                rims[t, i, part, :] = value

            inner_steps(q, *faces(coefs, part), north, width, put, keep)
            return 0

        lax.fori_loop(0, tracers, tracer, 0)
        return 0

    lax.fori_loop(0, size // ROWS8, block, 0)


def last_rim_kernel(begin, rims, coefs, halo_1, halo_2, coef_n, stage_in, *refs):
    out, stage, coef_n_out, north_s, sems = refs[-5:]
    tracers, size, width = rims.shape[0], rims.shape[2], stage.shape[3]
    even = is_even()
    spread_north(coef_n, north_s, width)
    north = lambda x: north_s[x + HALO]

    def copies_of(i):
        start = pl.multiple_of(i * ROWS8, ROWS8)
        part, to = pl.ds(start, ROWS8), pl.ds(begin + start, ROWS8)
        return [
            pltpu.make_async_copy(stage.at[j, :, part], out.at[:, to, :, pl.ds(128 * j, 128)], sems.at[i, j])
            for j in range(stage.shape[0])
        ]

    def block(i, _):
        start = pl.multiple_of(i * ROWS8, ROWS8)
        part = pl.ds(start, ROWS8)

        def tracer(t, _):
            halos = halo_pair(even, halo_1, halo_2, t, part)
            new = rim_steps(lambda i: rims[t, i, part, :], *halos, *faces(coefs, part), north, width)
            for x, value in new.items():
                put_column(stage, t, start, x, value)
            return 0

        lax.fori_loop(0, tracers, tracer, 0)
        for copy in copies_of(i):
            copy.start()
        return 0

    def finish(i, _):
        for copy in copies_of(i):
            copy.wait()
        return 0

    lax.fori_loop(0, size // ROWS8, block, 0)
    lax.fori_loop(0, size // ROWS8, finish, 0)


def transport_call(kernel, name, args, out_shape, aliases, scratch, cells, hbm=(), out_hbm=()):
    return pl.pallas_call(
        kernel,
        in_specs=[HBM if i in hbm else VMEM for i in range(len(args))],
        out_specs=[HBM if i in out_hbm else VMEM for i in range(len(out_shape))],
        out_shape=out_shape,
        scratch_shapes=scratch,
        input_output_aliases=aliases,
        compiler_params=params(16),
        cost_estimate=LITTLE,
        name=name,
    )(*args)


def north_scratch(width, rows):
    return pltpu.VMEM((width + 2 * HALO, ROWS8, rows), F32)


def first_inner(chunk, fixed, scale, surface, speed, open_e, coef_n):
    count, levels, width, rows = fixed.shape
    begin, size = chunk
    args = [fixed, scale, surface, speed, open_e, coef_n]
    out_shape = [
        shape_of(count, width, size, rows),
        shape_of(count, 8, size, rows),
        shape_of(2, width + 1, size, rows),
        shape_of(*coef_n.shape),
    ]
    turn = pltpu.VMEM((rows // 128, (ROWS8 + 1) * width, 128), F32)
    return transport_call(
        functools.partial(first_inner_kernel, begin), "first_inner", args, out_shape, {len(args) - 1: 3},
        [north_scratch(width, rows), turn, turn], count * size * width * rows,
    )


def first_rim(chunk, field, rims, coefs, speed_w, open_e, halos, coef_n):
    count, width, size, rows = field.shape
    args = [rims, speed_w, open_e, *halos, coef_n, field, coefs]
    edge = shape_of(count, 2, size, rows)
    out_shape = [shape_of(*field.shape), shape_of(*coefs.shape), edge, edge, shape_of(*coef_n.shape)]
    field, coefs, send_1, send_2, coef_n = transport_call(
        functools.partial(first_rim_kernel, chunk[0]), "first_rim", args, out_shape, {5: 4, 6: 0, 7: 1},
        [north_scratch(width, rows)], count * size * 4 * rows,
    )
    return field, coefs, (send_1, send_2), coef_n


def last_inner(field, coefs, coef_n):
    count, width, size, rows = field.shape
    out_shape = [
        shape_of(rows // 128, count, size + 1, width, 128),
        shape_of(count, 8, size, rows),
        shape_of(*coef_n.shape),
    ]
    return transport_call(
        last_inner_kernel, "last_inner", [field, coefs, coef_n], out_shape, {2: 2},
        [north_scratch(width, rows)], count * size * width * rows,
    )


def last_rim(chunk, levels, rims, coefs, halos, stage, coef_n, result):
    count, _, size, rows = rims.shape
    width = stage.shape[3]
    args = [rims, coefs, *halos, coef_n, stage]
    aliases = {4: 2, 5: 1}
    if result is not None:
        aliases[6] = 0
        args.append(result)
    out_shape = [shape_of(count, levels, width, rows), shape_of(*stage.shape), shape_of(*coef_n.shape)]
    result, _, coef_n = transport_call(
        functools.partial(last_rim_kernel, chunk[0]), "last_rim", args, out_shape, aliases,
        [north_scratch(width, rows), pltpu.SemaphoreType.DMA((size // ROWS8, rows // 128))],
        count * size * 4 * rows, hbm=(6,), out_hbm=(0,),
    )
    return result, coef_n


def per_device(tracers, diffusivity, conductance, face_velocity, partner, weight, sea_mask):
    tiles = lax.axis_size("tile")
    tracers, diffusivity, conductance = tracers[0], diffusivity[0], conductance[0]
    speed, partner, weight = face_velocity[0], partner[0], weight[0]
    width = tracers.shape[2]
    reach = width // 2 + 1

    def move(value, target_of, swap=False):
        pairs = []
        for m in range(2):
            for t in range(tiles):
                target = (1 - m if swap else m) * tiles + target_of(t) % tiles
                pairs.append((m * tiles + t, target))
        return lax.ppermute(value, ("mp", "tile"), pairs)

    one = lambda t: t + 1 - 2 * (t % 2)
    two = lambda t: t - 1 + 2 * (t % 2)

    *speeds, to_east, order = speed_columns(speed, (0, width - 2, width - 1))
    speed_w = move(to_east, lambda t: t + 1)
    signed = jnp.where(sea_mask > 0, conductance, -conductance)
    parts, ratios, slope, own, *halves, terms_1, terms_2 = down_to_surface(tracers, diffusivity, signed, order, reach)
    terms_1 = move(terms_1, one, swap=True)
    terms_2 = move(terms_2, two, swap=True)
    peers = [move(half, lambda t: t, swap=True) for half in halves]
    rim = (0, 1, width - 2, width - 1)
    fixed, scale, rims, rim_scale = up_from_surface(parts, ratios, speed_w, rim)

    inflow, surface, open_e, coef_n, *sends = exchange_surface(
        own, slope, peers, terms_1, terms_2, partner, weight, signed, rims, rim_scale, speeds, reach
    )
    levels = fixed.shape[1]
    chunks = chunks_of(levels)
    every = range(len(chunks))
    exchange = lambda pair: (move(pair[0], one), move(pair[1], two))
    halos = [exchange((sends[c], sends[len(chunks) + c])) for c in every]
    fields, rims, coefs, stages = [[None] * len(chunks) for _ in range(4)]
    for c in every:
        fields[c], rims[c], coefs[c], coef_n = first_inner(chunks[c], fixed, scale, surface, speed, open_e, coef_n)
    for c in every:
        fields[c], coefs[c], pair, coef_n = first_rim(
            chunks[c], fields[c], rims[c], coefs[c], speed_w, open_e, halos[c], coef_n
        )
        halos[c] = exchange(pair)
    for c in every:
        stages[c], rims[c], coef_n = last_inner(fields[c], coefs[c], coef_n)
    result = None
    for c in every:
        result, coef_n = last_rim(chunks[c], levels, rims[c], coefs[c], halos[c], stages[c], coef_n, result)
    return result[None], inflow[None]


def solution(mesh):
    in_specs = (
        P("mp", None, None, "tile", None),
        P("mp", None, "tile", None),
        P("mp", "tile", None),
        P("mp", None, "tile", None),
        P("mp", None, "tile", None),
        P("mp", None, "tile", None),
        P("tile", None),
    )
    out_specs = (P("mp", None, None, "tile", None), P("mp", None, "tile", None))
    return jax.shard_map(
        per_device, mesh=mesh, in_specs=in_specs, out_specs=out_specs, check_vma=False
    )
```

```python
import functools

import jax
import jax.numpy as jnp
from jax import lax
from jax.experimental import pallas as pl
from jax.experimental.pallas import tpu as pltpu
from jax.sharding import PartitionSpec as P

STEPS = 4
QUANT = 16
NU = 0.12
ROWS8 = 8
PARTS = (1, 1)
HALO = 2
F32 = jnp.float32
LITTLE = pl.CostEstimate(flops=1, bytes_accessed=1024, transcendentals=0)
VMEM = pl.BlockSpec(memory_space=pltpu.VMEM)
HBM = pl.BlockSpec(memory_space=pltpu.HBM)


def shape_of(*shape):
    return jax.ShapeDtypeStruct(shape, F32)


def params(mib):
    return pltpu.CompilerParams(vmem_limit_bytes=mib * 2**20)


def is_even():
    return lax.rem(lax.axis_index("tile"), 2) == 0


def either(even, call, first, second):
    @pl.when(even)
    def _():
        call(first, second)

    @pl.when(jnp.logical_not(even))
    def _():
        call(second, first)


def chunks_of(levels):
    sizes = [part * levels // sum(PARTS) for part in PARTS]
    return [(sum(sizes[:c]), size) for c, size in enumerate(sizes)]


def lane_parts(total, size=256):
    size = min(size, total)
    return [slice(start, start + size) for start in range(0, total, size)]


def down_kernel(reach, source, coupling, signed, order, parts, ratios, slope, terms, half_1, half_2, first_pair, second_pair, state, part_s, sems):
    tracers, levels, width, rows = source.shape
    blocks = levels // ROWS8

    def copies_of(b):
        part = pl.ds(b * ROWS8, ROWS8)
        return [pltpu.make_async_copy(source.at[t, part], parts.at[t, part], sems.at[b, t]) for t in range(tracers)]

    for b in range(blocks):
        for copy in copies_of(b):
            copy.start()
    state[...] = jnp.zeros_like(state)
    part_s[...] = jnp.zeros_like(part_s)

    def block(b, _):
        for copy in copies_of(b):
            copy.wait()
        for lanes in lane_parts(rows):
            before, ratio, inverse = [state[i, :, lanes] for i in range(3)]
            part = [part_s[t, :, lanes] for t in range(tracers)]
            for at in range(ROWS8):
                l = b * ROWS8 + at
                if at == ROWS8 - 1:
                    now = jnp.where(b == blocks - 1, 0.0, coupling[jnp.minimum(l, levels - 2), :, lanes])
                else:
                    now = coupling[l, :, lanes]
                inverse = 1.0 / (1.0 + before + now - before * ratio)
                part = [(parts[t, l, :, lanes] + before * part[t]) * inverse for t in range(tracers)]
                ratio = now * inverse
                before = now
                ratios[l, :, lanes] = ratio
                for t in range(tracers):
                    parts[t, l, :, lanes] = part[t]
            for i, value in enumerate((before, ratio, inverse)):
                state[i, :, lanes] = value
            for t in range(tracers):
                part_s[t, :, lanes] = part[t]
        return 0

    lax.fori_loop(0, blocks, block, 0)
    for t in range(tracers):
        terms[t] = part_s[t]
    slope[...] = state[2]
    terms[tracers] = 1.0 / jnp.abs(signed[...]) + state[2]
    half_1[...] = terms[:, : width // 2, :]
    half_2[...] = terms[:, width // 2 :, :]
    mask = jnp.where(signed[...] > 0.0, 1.0, 0.0)

    def pack(east, west):
        for c in range(tracers + 1):
            east[c * reach : (c + 1) * reach, :] = terms[c, width - reach :, :]
            west[c * reach : (c + 1) * reach, :] = terms[c, :reach, :]
        at = (tracers + 1) * reach
        east[at : at + HALO, :] = mask[width - HALO :]
        west[at : at + HALO, :] = mask[:HALO]

    either(is_even(), pack, first_pair, second_pair)


def down_to_surface(tracers, diffusivity, signed, order, reach):
    count, levels, width, rows = tracers.shape
    packed = (count + 1) * reach + HALO
    packed = -(-packed // 8) * 8
    return pl.pallas_call(
        functools.partial(down_kernel, reach),
        in_specs=[HBM, VMEM, VMEM, VMEM],
        out_specs=[VMEM] * 8,
        out_shape=[
            shape_of(count, levels, width, rows),
            shape_of(levels, width, rows),
            shape_of(width, rows),
            shape_of(count + 1, width, rows),
            shape_of(count + 1, width // 2, rows),
            shape_of(count + 1, width // 2, rows),
            shape_of(packed, rows),
            shape_of(packed, rows),
        ],
        scratch_shapes=[
            pltpu.VMEM((3, width, rows), F32),
            pltpu.VMEM((count, width, rows), F32),
            pltpu.SemaphoreType.DMA((levels // ROWS8, count)),
        ],
        compiler_params=params(41),
        cost_estimate=pl.CostEstimate(
            flops=20 * levels * width * rows, bytes_accessed=10 * levels * width * rows * 4, transcendentals=0
        ),
        name="down_to_surface",
    )(tracers, diffusivity, signed, order)


def up_kernel(rim, parts, ratios, arrived, fixed, scale, rims, rim_scale):
    tracers, levels, width, rows = parts.shape
    blocks = levels // ROWS8
    for lanes in lane_parts(rows):

        def block(i, state):
            b = blocks - 1 - i
            start = pl.multiple_of(b * ROWS8, ROWS8)
            scale_now, fixed_now = state[0], list(state[1:])
            for at in reversed(range(ROWS8)):
                l = start + at
                ratio = ratios[l, :, lanes]
                scale_now = ratio * scale_now
                fixed_now = [parts[t, l, :, lanes] + ratio * fixed_now[t] for t in range(tracers)]
                if at == ROWS8 - 1:
                    scale_now = jnp.where(i == 0, 1.0, scale_now)
                    fixed_now = [jnp.where(i == 0, 0.0, value) for value in fixed_now]
                scale[l, :, lanes] = scale_now
                for t in range(tracers):
                    fixed[t, l, :, lanes] = fixed_now[t]
                for c, x in enumerate(rim):
                    rim_scale[c, b, at : at + 1, lanes] = scale_now[x : x + 1]
                    for t in range(tracers):
                        rims[t, c, b, at : at + 1, lanes] = fixed_now[t][x : x + 1]
            return scale_now, *fixed_now

        zero = jnp.zeros((width, lanes.stop - lanes.start), F32)
        lax.fori_loop(0, blocks, block, (zero,) * (1 + tracers))


def speed_kernel(columns, speed, *out):
    out[-1][...] = jnp.zeros_like(out[-1])
    for l in range(speed.shape[0]):
        for ref, x in zip(out, columns):
            ref[l : l + 1, :] = speed[l, x : x + 1, :]


def speed_columns(speed, columns):
    levels, width, rows = speed.shape
    return pl.pallas_call(
        functools.partial(speed_kernel, columns),
        in_specs=[VMEM],
        out_specs=[VMEM] * (len(columns) + 1),
        out_shape=[shape_of(levels, rows)] * len(columns) + [shape_of(ROWS8, 128)],
        compiler_params=params(20),
        cost_estimate=LITTLE,
        name="speed_columns",
    )(speed)


def up_from_surface(parts, ratios, arrived, rim):
    count, levels, width, rows = parts.shape
    fixed, scale, rims, rim_scale = pl.pallas_call(
        functools.partial(up_kernel, rim),
        in_specs=[VMEM] * 3,
        out_specs=[VMEM] * 4,
        out_shape=[
            shape_of(count, levels, width, rows),
            shape_of(levels, width, rows),
            shape_of(count, len(rim), levels // ROWS8, ROWS8, rows),
            shape_of(len(rim), levels // ROWS8, ROWS8, rows),
        ],
        input_output_aliases={0: 0, 1: 1},
        compiler_params=params(20),
        cost_estimate=LITTLE,
        name="up_from_surface",
    )(parts, ratios, arrived)
    rims, rim_scale = rims.reshape(count, len(rim), levels, rows), rim_scale.reshape(len(rim), levels, rows)
    return fixed, scale, rims, rim_scale


def leaving(u, opening):
    return opening * (jnp.maximum(u, 0.0) + NU), opening * (jnp.minimum(u, 0.0) - NU)


def surface_kernel(
    reach, own, slope, peer_1, peer_2, first_pair, second_pair, partner, weight, signed, rims, rim_scale, speed_0, speed_1,
    inflow, surface, open_e, coef_n, *rest,
):
    chunks = chunks_of(rims.shape[2])
    send_1, send_2, wide, opened = rest[: len(chunks)], rest[len(chunks) : 2 * len(chunks)], rest[-2], rest[-1]
    channels, width, rows = own.shape
    tracers = channels - 1
    first = 2 * 8
    even = is_even()

    for c in range(channels):
        wide[c, first : first + width // 2, :] = peer_1[c]
        wide[c, first + width // 2 : first + width, :] = peer_2[c]
    opened[:width, :] = jnp.where(signed[...] > 0.0, 1.0, 0.0)
    opened[width:, :] = jnp.zeros((ROWS8, rows), F32)

    def unpack(east, west):
        for c in range(channels):
            part = slice(c * reach, (c + 1) * reach)
            wide[c, first - reach : first, :] = west[part, :]
            wide[c, first + width : first + width + reach, :] = east[part, :]
        at = slice(channels * reach, channels * reach + HALO)
        opened[width : width + HALO, :] = east[at, :]
        opened[width + ROWS8 - HALO :, :] = west[at, :]

    either(even, unpack, first_pair, second_pair)

    start = lax.axis_index("tile") * width
    total = lax.axis_size("tile") * width
    for lanes in lane_parts(rows, 128):
        position = start + lax.broadcasted_iota(jnp.int32, (width, 128), 0)
        own_rest = own[tracers, :, lanes]
        flow = [jnp.zeros((width, 128), F32) for _ in range(tracers)]
        for k in range(partner.shape[0]):
            apart = partner[k, :, lanes] - position
            apart = jnp.where(apart > reach, apart - total, apart)
            apart = jnp.where(apart < -reach, apart + total, apart)
            found = [jnp.zeros((width, 128), F32) for _ in range(channels)]
            for offset in range(-reach, reach + 1):
                hit = apart == offset
                window = slice(first + offset, first + offset + width)
                found = [jnp.where(hit, wide[c, window, lanes], f) for c, f in enumerate(found)]
            factor = weight[k, :, lanes].astype(F32) / (own_rest + found[-1])
            flow = [flow[t] + factor * (own[t, :, lanes] - found[t]) for t in range(tracers)]
        for t in range(tracers):
            into = flow[t] * (-1.0 / QUANT)
            inflow[t, :, lanes] = into
            surface[t, :, lanes] = own[t, :, lanes] + slope[:, lanes] * into

    wide_rows = width + ROWS8
    free = jnp.broadcast_to(lax.axis_index("mp"), (wide_rows, rows)) == 0
    here = jnp.where(free, 1.0, opened[...])
    column = lax.broadcasted_iota(jnp.int32, (wide_rows, rows), 1)
    open_e[...] = here * pltpu.roll(here, wide_rows - 1, 0)
    coef_n[...] = NU * (here * jnp.where(column == rows - 1, 0.0, pltpu.roll(here, rows - 1, 1)))

    for c, (begin, size) in enumerate(chunks):
        part = slice(begin, begin + size)
        faces_w = leaving(speed_0[part, :], open_e[:1, :])
        faces_e = leaving(speed_1[part, :], open_e[width - 2 : width - 1, :])
        for t in range(tracers):
            columns = []
            for i, x in enumerate((0, 1, width - 2, width - 1)):
                columns.append(rims[t, i, part, :] + rim_scale[i, part, :] * surface[t, x : x + 1, :])
            west = columns[0], faces_w[0] * columns[0] + faces_w[1] * columns[1]
            east = columns[3], faces_e[0] * columns[2] + faces_e[1] * columns[3]
            for i in range(2):
                send_1[c][t, i] = jnp.where(even, east[i], west[i])
                send_2[c][t, i] = jnp.where(even, west[i], east[i])


def exchange_surface(
    own, slope, peers, first_pair, second_pair, partner, weight, signed, rims, rim_scale, speeds, reach
):
    channels, width, rows = own.shape
    count, _, levels, _ = rims.shape
    plane = shape_of(width + ROWS8, rows)
    edges = [shape_of(count, 2, size, rows) for _, size in chunks_of(levels)]
    return pl.pallas_call(
        functools.partial(surface_kernel, reach),
        in_specs=[VMEM] * 13,
        out_specs=[VMEM] * (4 + 2 * len(edges)),
        out_shape=[shape_of(count, width, rows)] * 2 + [plane] * 2 + edges * 2,
        scratch_shapes=[pltpu.VMEM((channels, 16 + width + 16, rows), F32), pltpu.VMEM((width + ROWS8, rows), F32)],
        compiler_params=params(20),
        cost_estimate=LITTLE,
        name="exchange_surface",
    )(own, slope, *peers, first_pair, second_pair, partner, weight, signed, rims, rim_scale, *speeds)


def along_y(north, value):
    flux = north * (pltpu.roll(value, value.shape[-1] - 1, 1) - value)
    return flux - pltpu.roll(flux, 1, 1)


def inner_steps(q, a, b, north, width, put, keep):
    end = width - 1
    here, flux, once_before, flux_before = q(0), None, None, None
    for x in range(width):
        if x == 0:
            east = q(1)
            flux_e = a(0) * here + b(0) * east
            keep(0, here)
            keep(1, (here - flux_e) + along_y(north(0), here))
            once = None
        elif x == end:
            keep(4, here)
            keep(5, (here + flux) + along_y(north(end), here))
            keep(6, once_before)
            keep(7, (once_before + flux_before) + along_y(north(end - 1), once_before))
            break
        else:
            east = q(x + 1)
            flux_e = a(x) * here + b(x) * east
            once = (here - (flux_e - flux)) + along_y(north(x), here)
        if once_before is not None:
            flux_once = a(x - 1) * once_before + b(x - 1) * once
            second = along_y(north(x - 1), once_before)
            if flux_before is None:
                keep(2, once_before)
                keep(3, (once_before - flux_once) + second)
            else:
                put(x - 1, (once_before - (flux_once - flux_before)) + second)
            flux_before = flux_once
        here, flux, once_before = east, flux_e, once


def rim_steps(kept, west, east, a, b, north, width):
    end = width - 1
    value, behind = west
    flux = a(-1) * value + b(-1) * kept(0)
    outer = (value - (flux - behind)) + along_y(north(-1), value)
    edge = kept(1) + flux
    flux_out = a(-1) * outer + b(-1) * edge
    flux_in = a(0) * edge + b(0) * kept(2)
    new = {0: (edge - (flux_in - flux_out)) + along_y(north(0), edge), 1: kept(3) + flux_in}
    value, behind = east
    flux = a(end) * kept(4) + b(end) * value
    outer = (value - (behind - flux)) + along_y(north(width), value)
    edge = kept(5) - flux
    flux_out = a(end) * edge + b(end) * outer
    flux_in = a(end - 1) * kept(6) + b(end - 1) * edge
    new[end] = (edge - (flux_out - flux_in)) + along_y(north(end), edge)
    new[end - 1] = kept(7) - flux_in
    return new


def tiles_in(turn, value):
    levels, width, _ = value.shape
    for j in range(turn.shape[0]):
        turn[j, : levels * width, :] = value[:, :, 128 * j : 128 * (j + 1)].reshape(levels * width, 128)


def column(turn, x, width):
    parts = [turn[j, pl.ds(x, ROWS8, stride=width), :] for j in range(turn.shape[0])]
    return jnp.concatenate(parts, axis=1)


def put_column(stage, t, start, x, value):
    parts, tracers, levels, width, lanes = stage.shape
    rows = stage.reshape(parts, tracers, levels * width, lanes)
    for j in range(parts):
        at = pl.ds(start * width + x, ROWS8, stride=width)
        rows[j, t, at, :] = value[:, lanes * j : lanes * (j + 1)]


def ring(x, width):
    return x if x >= 0 else width + ROWS8 + x


def spread_north(coef_n, north_s, width):
    for x in range(1 - HALO, width + HALO - 1):
        row = ring(x, width)
        north_s[x + HALO] = jnp.broadcast_to(coef_n[row : row + 1, :], north_s.shape[1:])


def face(coefs, part, x, u, open_e, width):
    row = ring(x, width)
    coefs[0, x + 1, part, :], coefs[1, x + 1, part, :] = leaving(u, open_e[row : row + 1, :])


def faces(coefs, part):
    return [lambda x, i=i: coefs[i, x + 1, part, :] for i in range(2)]


def first_inner_kernel(
    begin, fixed, scale, surface, speed, open_e, coef_n,
    field, rims, coefs, coef_n_out, north_s, turn, turn_speed,
):
    tracers, levels, width, rows = fixed.shape
    size = field.shape[2]
    spread_north(coef_n, north_s, width)
    north = lambda x: north_s[x + HALO]

    def block(i, _):
        start = pl.multiple_of(i * ROWS8, ROWS8)
        part, whole = pl.ds(start, ROWS8), pl.ds(begin + start, ROWS8)
        tiles_in(turn_speed, speed[whole])
        for x in range(width):
            face(coefs, part, x, column(turn_speed, x, width), open_e, width)

        def tracer(t, _):
            tiles_in(turn, fixed[t, whole] + scale[whole] * surface[t][None])

            def put(x, value):
                field[t, x, part, :] = value

            def keep(i, value):
                rims[t, i, part, :] = value

            q = lambda x: column(turn, x, width)
            inner_steps(q, *faces(coefs, part), north, width, put, keep)
            return 0

        lax.fori_loop(0, tracers, tracer, 0)
        return 0

    lax.fori_loop(0, size // ROWS8, block, 0)


def halo_pair(even, halo_1, halo_2, t, part):
    pairs = [(halo_1[t, i, part, :], halo_2[t, i, part, :]) for i in range(2)]
    west = [jnp.where(even, second, first) for first, second in pairs]
    east = [jnp.where(even, first, second) for first, second in pairs]
    return west, east


def first_rim_kernel(
    begin, rims, speed_w, open_e, halo_1, halo_2, coef_n, field_in, coefs_in,
    field, coefs, send_1, send_2, coef_n_out, north_s,
):
    tracers, width, size, rows = field.shape
    even = is_even()
    spread_north(coef_n, north_s, width)
    north = lambda x: north_s[x + HALO]

    def block(i, _):
        start = pl.multiple_of(i * ROWS8, ROWS8)
        part, whole = pl.ds(start, ROWS8), pl.ds(begin + start, ROWS8)
        face(coefs, part, -1, speed_w[whole, :], open_e, width)
        a, b = faces(coefs, part)

        def tracer(t, _):
            halos = halo_pair(even, halo_1, halo_2, t, part)
            new = rim_steps(lambda i: rims[t, i, part, :], *halos, a, b, north, width)
            for x, value in new.items():
                field[t, x, part, :] = value
            end = width - 1
            west = new[0], a(0) * new[0] + b(0) * new[1]
            east = new[end], a(end - 1) * new[end - 1] + b(end - 1) * new[end]
            for i in range(2):
                send_1[t, i, part, :] = jnp.where(even, east[i], west[i])
                send_2[t, i, part, :] = jnp.where(even, west[i], east[i])
            return 0

        lax.fori_loop(0, tracers, tracer, 0)
        return 0

    lax.fori_loop(0, size // ROWS8, block, 0)


def last_inner_kernel(field, coefs, coef_n, stage, rims, coef_n_out, north_s):
    tracers, width, size, rows = field.shape
    spread_north(coef_n, north_s, width)
    north = lambda x: north_s[x + HALO]

    def block(i, _):
        start = pl.multiple_of(i * ROWS8, ROWS8)
        part = pl.ds(start, ROWS8)

        def tracer(t, _):
            q = lambda x: field[t, x, part, :]
            put = lambda x, value: put_column(stage, t, start, x, value)

            def keep(i, value):
                rims[t, i, part, :] = value

            inner_steps(q, *faces(coefs, part), north, width, put, keep)
            return 0

        lax.fori_loop(0, tracers, tracer, 0)
        return 0

    lax.fori_loop(0, size // ROWS8, block, 0)


def last_rim_kernel(begin, rims, coefs, halo_2, halo_1, coef_n, stage_in, *refs):
    out, stage, coef_n_out, north_s, sems = refs[-5:]
    tracers, size, width = rims.shape[0], rims.shape[2], stage.shape[3]
    even = is_even()
    spread_north(coef_n, north_s, width)
    north = lambda x: north_s[x + HALO]

    def copies_of(i):
        start = pl.multiple_of(i * ROWS8, ROWS8)
        part, to = pl.ds(start, ROWS8), pl.ds(begin + start, ROWS8)
        return [
            pltpu.make_async_copy(stage.at[j, :, part], out.at[:, to, :, pl.ds(128 * j, 128)], sems.at[i, j])
            for j in range(stage.shape[0])
        ]

    def block(i, _):
        start = pl.multiple_of(i * ROWS8, ROWS8)
        part = pl.ds(start, ROWS8)

        def tracer(t, _):
            halos = halo_pair(even, halo_1, halo_2, t, part)
            new = rim_steps(lambda i: rims[t, i, part, :], *halos, *faces(coefs, part), north, width)
            for x, value in new.items():
                put_column(stage, t, start, x, value)
            return 0

        lax.fori_loop(0, tracers, tracer, 0)
        for copy in copies_of(i):
            copy.start()
        return 0

    def finish(i, _):
        for copy in copies_of(i):
            copy.wait()
        return 0

    lax.fori_loop(0, size // ROWS8, block, 0)
    lax.fori_loop(0, size // ROWS8, finish, 0)


def transport_call(kernel, name, args, out_shape, aliases, scratch, cells, hbm=(), out_hbm=()):
    return pl.pallas_call(
        kernel,
        in_specs=[HBM if i in hbm else VMEM for i in range(len(args))],
        out_specs=[HBM if i in out_hbm else VMEM for i in range(len(out_shape))],
        out_shape=out_shape,
        scratch_shapes=scratch,
        input_output_aliases=aliases,
        compiler_params=params(16),
        cost_estimate=LITTLE,
        name=name,
    )(*args)


def north_scratch(width, rows):
    return pltpu.VMEM((width + 2 * HALO, ROWS8, rows), F32)


def first_inner(chunk, fixed, scale, surface, speed, open_e, coef_n):
    count, levels, width, rows = fixed.shape
    begin, size = chunk
    args = [fixed, scale, surface, speed, open_e, coef_n]
    out_shape = [
        shape_of(count, width, size, rows),
        shape_of(count, 8, size, rows),
        shape_of(2, width + 1, size, rows),
        shape_of(*coef_n.shape),
    ]
    turn = pltpu.VMEM((rows // 128, (ROWS8 + 1) * width, 128), F32)
    return transport_call(
        functools.partial(first_inner_kernel, begin), "first_inner", args, out_shape, {len(args) - 1: 3},
        [north_scratch(width, rows), turn, turn], count * size * width * rows,
    )


def first_rim(chunk, field, rims, coefs, speed_w, open_e, halos, coef_n):
    count, width, size, rows = field.shape
    args = [rims, speed_w, open_e, *halos, coef_n, field, coefs]
    edge = shape_of(count, 2, size, rows)
    out_shape = [shape_of(*field.shape), shape_of(*coefs.shape), edge, edge, shape_of(*coef_n.shape)]
    field, coefs, send_1, send_2, coef_n = transport_call(
        functools.partial(first_rim_kernel, chunk[0]), "first_rim", args, out_shape, {5: 4, 6: 0, 7: 1},
        [north_scratch(width, rows)], count * size * 4 * rows,
    )
    return field, coefs, (send_1, send_2), coef_n


def last_inner(field, coefs, coef_n):
    count, width, size, rows = field.shape
    out_shape = [
        shape_of(rows // 128, count, size + 1, width, 128),
        shape_of(count, 8, size, rows),
        shape_of(*coef_n.shape),
    ]
    return transport_call(
        last_inner_kernel, "last_inner", [field, coefs, coef_n], out_shape, {2: 2},
        [north_scratch(width, rows)], count * size * width * rows,
    )


def last_rim(chunk, levels, rims, coefs, halos, stage, coef_n, result):
    count, _, size, rows = rims.shape
    width = stage.shape[3]
    args = [rims, coefs, *reversed(halos), coef_n, stage]
    aliases = {4: 2, 5: 1}
    if result is not None:
        aliases[6] = 0
        args.append(result)
    out_shape = [shape_of(count, levels, width, rows), shape_of(*stage.shape), shape_of(*coef_n.shape)]
    result, _, coef_n = transport_call(
        functools.partial(last_rim_kernel, chunk[0]), "last_rim", args, out_shape, aliases,
        [north_scratch(width, rows), pltpu.SemaphoreType.DMA((size // ROWS8, rows // 128))],
        count * size * 4 * rows, hbm=(6,), out_hbm=(0,),
    )
    return result, coef_n


def per_device(tracers, diffusivity, conductance, face_velocity, partner, weight, sea_mask):
    tiles = lax.axis_size("tile")
    tracers, diffusivity, conductance = tracers[0], diffusivity[0], conductance[0]
    speed, partner, weight = face_velocity[0], partner[0], weight[0]
    width = tracers.shape[2]
    reach = width // 2 + 1

    def move(value, target_of, swap=False):
        pairs = []
        for m in range(2):
            for t in range(tiles):
                target = (1 - m if swap else m) * tiles + target_of(t) % tiles
                pairs.append((m * tiles + t, target))
        return lax.ppermute(value, ("mp", "tile"), pairs)

    one = lambda t: t + 1 - 2 * (t % 2)
    two = lambda t: t - 1 + 2 * (t % 2)

    *speeds, to_east, order = speed_columns(speed, (0, width - 2, width - 1))
    speed_w = move(to_east, lambda t: t + 1)
    signed = jnp.where(sea_mask > 0, conductance, -conductance)
    parts, ratios, slope, own, *halves, terms_1, terms_2 = down_to_surface(tracers, diffusivity, signed, order, reach)
    terms_1 = move(terms_1, one, swap=True)
    terms_2 = move(terms_2, two, swap=True)
    peers = [move(half, lambda t: t, swap=True) for half in halves]
    rim = (0, 1, width - 2, width - 1)
    fixed, scale, rims, rim_scale = up_from_surface(parts, ratios, speed_w, rim)

    inflow, surface, open_e, coef_n, *sends = exchange_surface(
        own, slope, peers, terms_1, terms_2, partner, weight, signed, rims, rim_scale, speeds, reach
    )
    levels = fixed.shape[1]
    chunks = chunks_of(levels)
    every = range(len(chunks))
    exchange = lambda pair: (move(pair[0], one), move(pair[1], two))
    exchange_far_first = lambda pair: tuple(reversed((move(pair[1], two), move(pair[0], one))))
    halos = [exchange((sends[c], sends[len(chunks) + c])) for c in every]
    fields, rims, coefs, stages = [[None] * len(chunks) for _ in range(4)]
    for c in every:
        fields[c], rims[c], coefs[c], coef_n = first_inner(chunks[c], fixed, scale, surface, speed, open_e, coef_n)
    for c in every:
        fields[c], coefs[c], pair, coef_n = first_rim(
            chunks[c], fields[c], rims[c], coefs[c], speed_w, open_e, halos[c], coef_n
        )
        halos[c] = exchange_far_first(pair)
    for c in every:
        stages[c], rims[c], coef_n = last_inner(fields[c], coefs[c], coef_n)
    result = None
    for c in every:
        result, coef_n = last_rim(chunks[c], levels, rims[c], coefs[c], halos[c], stages[c], coef_n, result)
    return result[None], inflow[None]


def solution(mesh):
    in_specs = (
        P("mp", None, None, "tile", None),
        P("mp", None, "tile", None),
        P("mp", "tile", None),
        P("mp", None, "tile", None),
        P("mp", None, "tile", None),
        P("mp", None, "tile", None),
        P("tile", None),
    )
    out_specs = (P("mp", None, None, "tile", None), P("mp", None, "tile", None))
    return jax.shard_map(
        per_device, mesh=mesh, in_specs=in_specs, out_specs=out_specs, check_vma=False
    )
```

```python
import functools

import jax
import jax.numpy as jnp
from jax import lax
from jax.experimental import pallas as pl
from jax.experimental.pallas import tpu as pltpu
from jax.sharding import PartitionSpec as P

STEPS = 4
QUANT = 16
NU = 0.12
ROWS8 = 8
PARTS = (1, 1)
HALO = 2
F32 = jnp.float32
LITTLE = pl.CostEstimate(flops=1, bytes_accessed=1024, transcendentals=0)
VMEM = pl.BlockSpec(memory_space=pltpu.VMEM)
HBM = pl.BlockSpec(memory_space=pltpu.HBM)


def shape_of(*shape):
    return jax.ShapeDtypeStruct(shape, F32)


def params(mib):
    return pltpu.CompilerParams(vmem_limit_bytes=mib * 2**20)


def is_even():
    return lax.rem(lax.axis_index("tile"), 2) == 0


def either(even, call, first, second):
    @pl.when(even)
    def _():
        call(first, second)

    @pl.when(jnp.logical_not(even))
    def _():
        call(second, first)


def chunks_of(levels):
    sizes = [part * levels // sum(PARTS) for part in PARTS]
    return [(sum(sizes[:c]), size) for c, size in enumerate(sizes)]


def lane_parts(total, size=256):
    size = min(size, total)
    return [slice(start, start + size) for start in range(0, total, size)]


def down_kernel(reach, source, coupling, signed, order, parts, ratios, slope, terms, half_1, half_2, first_pair, second_pair, state, part_s, sems):
    tracers, levels, width, rows = source.shape
    blocks = levels // ROWS8

    def copies_of(b):
        part = pl.ds(b * ROWS8, ROWS8)
        return [pltpu.make_async_copy(source.at[t, part], parts.at[t, part], sems.at[b, t]) for t in range(tracers)]

    for b in range(blocks):
        for copy in copies_of(b):
            copy.start()
    state[...] = jnp.zeros_like(state)
    part_s[...] = jnp.zeros_like(part_s)

    def block(b, _):
        for copy in copies_of(b):
            copy.wait()
        for lanes in lane_parts(rows):
            before, ratio, inverse = [state[i, :, lanes] for i in range(3)]
            part = [part_s[t, :, lanes] for t in range(tracers)]
            for at in range(ROWS8):
                l = b * ROWS8 + at
                if at == ROWS8 - 1:
                    now = jnp.where(b == blocks - 1, 0.0, coupling[jnp.minimum(l, levels - 2), :, lanes])
                else:
                    now = coupling[l, :, lanes]
                inverse = 1.0 / (1.0 + before + now - before * ratio)
                part = [(parts[t, l, :, lanes] + before * part[t]) * inverse for t in range(tracers)]
                ratio = now * inverse
                before = now
                ratios[l, :, lanes] = ratio
                for t in range(tracers):
                    parts[t, l, :, lanes] = part[t]
            for i, value in enumerate((before, ratio, inverse)):
                state[i, :, lanes] = value
            for t in range(tracers):
                part_s[t, :, lanes] = part[t]
        return 0

    lax.fori_loop(0, blocks, block, 0)
    for t in range(tracers):
        terms[t] = part_s[t]
    slope[...] = state[2]
    terms[tracers] = 1.0 / jnp.abs(signed[...]) + state[2]
    half_1[...] = terms[:, : width // 2, :]
    half_2[...] = terms[:, width // 2 :, :]
    mask = jnp.where(signed[...] > 0.0, 1.0, 0.0)

    def pack(east, west):
        for c in range(tracers + 1):
            east[c * reach : (c + 1) * reach, :] = terms[c, width - reach :, :]
            west[c * reach : (c + 1) * reach, :] = terms[c, :reach, :]
        at = (tracers + 1) * reach
        east[at : at + HALO, :] = mask[width - HALO :]
        west[at : at + HALO, :] = mask[:HALO]

    either(is_even(), pack, first_pair, second_pair)


def down_to_surface(tracers, diffusivity, signed, order, reach):
    count, levels, width, rows = tracers.shape
    packed = (count + 1) * reach + HALO
    packed = -(-packed // 8) * 8
    return pl.pallas_call(
        functools.partial(down_kernel, reach),
        in_specs=[HBM, VMEM, VMEM, VMEM],
        out_specs=[VMEM] * 8,
        out_shape=[
            shape_of(count, levels, width, rows),
            shape_of(levels, width, rows),
            shape_of(width, rows),
            shape_of(count + 1, width, rows),
            shape_of(count + 1, width // 2, rows),
            shape_of(count + 1, width // 2, rows),
            shape_of(packed, rows),
            shape_of(packed, rows),
        ],
        scratch_shapes=[
            pltpu.VMEM((3, width, rows), F32),
            pltpu.VMEM((count, width, rows), F32),
            pltpu.SemaphoreType.DMA((levels // ROWS8, count)),
        ],
        compiler_params=params(41),
        cost_estimate=pl.CostEstimate(
            flops=20 * levels * width * rows, bytes_accessed=10 * levels * width * rows * 4, transcendentals=0
        ),
        name="down_to_surface",
    )(tracers, diffusivity, signed, order)


def up_kernel(rim, parts, ratios, arrived, fixed, scale, rims, rim_scale):
    tracers, levels, width, rows = parts.shape
    blocks = levels // ROWS8
    for lanes in lane_parts(rows):

        def block(i, state):
            b = blocks - 1 - i
            start = pl.multiple_of(b * ROWS8, ROWS8)
            scale_now, fixed_now = state[0], list(state[1:])
            for at in reversed(range(ROWS8)):
                l = start + at
                ratio = ratios[l, :, lanes]
                scale_now = ratio * scale_now
                fixed_now = [parts[t, l, :, lanes] + ratio * fixed_now[t] for t in range(tracers)]
                if at == ROWS8 - 1:
                    scale_now = jnp.where(i == 0, 1.0, scale_now)
                    fixed_now = [jnp.where(i == 0, 0.0, value) for value in fixed_now]
                scale[l, :, lanes] = scale_now
                for t in range(tracers):
                    fixed[t, l, :, lanes] = fixed_now[t]
                for c, x in enumerate(rim):
                    rim_scale[c, b, at : at + 1, lanes] = scale_now[x : x + 1]
                    for t in range(tracers):
                        rims[t, c, b, at : at + 1, lanes] = fixed_now[t][x : x + 1]
            return scale_now, *fixed_now

        zero = jnp.zeros((width, lanes.stop - lanes.start), F32)
        lax.fori_loop(0, blocks, block, (zero,) * (1 + tracers))


def speed_kernel(columns, speed, *out):
    out[-1][...] = jnp.zeros_like(out[-1])
    for l in range(speed.shape[0]):
        for ref, x in zip(out, columns):
            ref[l : l + 1, :] = speed[l, x : x + 1, :]


def speed_columns(speed, columns):
    levels, width, rows = speed.shape
    return pl.pallas_call(
        functools.partial(speed_kernel, columns),
        in_specs=[VMEM],
        out_specs=[VMEM] * (len(columns) + 1),
        out_shape=[shape_of(levels, rows)] * len(columns) + [shape_of(ROWS8, 128)],
        compiler_params=params(20),
        cost_estimate=LITTLE,
        name="speed_columns",
    )(speed)


def up_from_surface(parts, ratios, arrived, rim):
    count, levels, width, rows = parts.shape
    fixed, scale, rims, rim_scale = pl.pallas_call(
        functools.partial(up_kernel, rim),
        in_specs=[VMEM] * 3,
        out_specs=[VMEM] * 4,
        out_shape=[
            shape_of(count, levels, width, rows),
            shape_of(levels, width, rows),
            shape_of(count, len(rim), levels // ROWS8, ROWS8, rows),
            shape_of(len(rim), levels // ROWS8, ROWS8, rows),
        ],
        input_output_aliases={0: 0, 1: 1},
        compiler_params=params(20),
        cost_estimate=LITTLE,
        name="up_from_surface",
    )(parts, ratios, arrived)
    rims, rim_scale = rims.reshape(count, len(rim), levels, rows), rim_scale.reshape(len(rim), levels, rows)
    return fixed, scale, rims, rim_scale


def leaving(u, opening):
    return opening * (jnp.maximum(u, 0.0) + NU), opening * (jnp.minimum(u, 0.0) - NU)


def surface_kernel(
    reach, own, slope, peer_1, peer_2, first_pair, second_pair, partner, weight, signed, rims, rim_scale, speed_0, speed_1,
    inflow, surface, open_e, coef_n, *rest,
):
    chunks = chunks_of(rims.shape[2])
    send_1, send_2, wide, opened = rest[: len(chunks)], rest[len(chunks) : 2 * len(chunks)], rest[-2], rest[-1]
    channels, width, rows = own.shape
    tracers = channels - 1
    first = 2 * 8
    even = is_even()

    for c in range(channels):
        wide[c, first : first + width // 2, :] = peer_1[c]
        wide[c, first + width // 2 : first + width, :] = peer_2[c]
    opened[:width, :] = jnp.where(signed[...] > 0.0, 1.0, 0.0)
    opened[width:, :] = jnp.zeros((ROWS8, rows), F32)

    def unpack(east, west):
        for c in range(channels):
            part = slice(c * reach, (c + 1) * reach)
            wide[c, first - reach : first, :] = west[part, :]
            wide[c, first + width : first + width + reach, :] = east[part, :]
        at = slice(channels * reach, channels * reach + HALO)
        opened[width : width + HALO, :] = east[at, :]
        opened[width + ROWS8 - HALO :, :] = west[at, :]

    either(even, unpack, first_pair, second_pair)

    start = lax.axis_index("tile") * width
    total = lax.axis_size("tile") * width
    for lanes in lane_parts(rows, 128):
        position = start + lax.broadcasted_iota(jnp.int32, (width, 128), 0)
        own_rest = own[tracers, :, lanes]
        flow = [jnp.zeros((width, 128), F32) for _ in range(tracers)]
        for k in range(partner.shape[0]):
            apart = partner[k, :, lanes] - position
            apart = jnp.where(apart > reach, apart - total, apart)
            apart = jnp.where(apart < -reach, apart + total, apart)
            found = [jnp.zeros((width, 128), F32) for _ in range(channels)]
            for offset in range(-reach, reach + 1):
                hit = apart == offset
                window = slice(first + offset, first + offset + width)
                found = [jnp.where(hit, wide[c, window, lanes], f) for c, f in enumerate(found)]
            factor = weight[k, :, lanes].astype(F32) / (own_rest + found[-1])
            flow = [flow[t] + factor * (own[t, :, lanes] - found[t]) for t in range(tracers)]
        for t in range(tracers):
            into = flow[t] * (-1.0 / QUANT)
            inflow[t, :, lanes] = into
            surface[t, :, lanes] = own[t, :, lanes] + slope[:, lanes] * into

    wide_rows = width + ROWS8
    free = jnp.broadcast_to(lax.axis_index("mp"), (wide_rows, rows)) == 0
    here = jnp.where(free, 1.0, opened[...])
    column = lax.broadcasted_iota(jnp.int32, (wide_rows, rows), 1)
    open_e[...] = here * pltpu.roll(here, wide_rows - 1, 0)
    coef_n[...] = NU * (here * jnp.where(column == rows - 1, 0.0, pltpu.roll(here, rows - 1, 1)))

    for c, (begin, size) in enumerate(chunks):
        part = slice(begin, begin + size)
        faces_w = leaving(speed_0[part, :], open_e[:1, :])
        faces_e = leaving(speed_1[part, :], open_e[width - 2 : width - 1, :])
        for t in range(tracers):
            columns = []
            for i, x in enumerate((0, 1, width - 2, width - 1)):
                columns.append(rims[t, i, part, :] + rim_scale[i, part, :] * surface[t, x : x + 1, :])
            west = columns[0], faces_w[0] * columns[0] + faces_w[1] * columns[1]
            east = columns[3], faces_e[0] * columns[2] + faces_e[1] * columns[3]
            for i in range(2):
                send_1[c][t, i] = jnp.where(even, east[i], west[i])
                send_2[c][t, i] = jnp.where(even, west[i], east[i])


def exchange_surface(
    own, slope, peers, first_pair, second_pair, partner, weight, signed, rims, rim_scale, speeds, reach
):
    channels, width, rows = own.shape
    count, _, levels, _ = rims.shape
    plane = shape_of(width + ROWS8, rows)
    edges = [shape_of(count, 2, size, rows) for _, size in chunks_of(levels)]
    return pl.pallas_call(
        functools.partial(surface_kernel, reach),
        in_specs=[VMEM] * 13,
        out_specs=[VMEM] * (4 + 2 * len(edges)),
        out_shape=[shape_of(count, width, rows)] * 2 + [plane] * 2 + edges * 2,
        scratch_shapes=[pltpu.VMEM((channels, 16 + width + 16, rows), F32), pltpu.VMEM((width + ROWS8, rows), F32)],
        compiler_params=params(20),
        cost_estimate=LITTLE,
        name="exchange_surface",
    )(own, slope, *peers, first_pair, second_pair, partner, weight, signed, rims, rim_scale, *speeds)


def along_y(north, value):
    flux = north * (pltpu.roll(value, value.shape[-1] - 1, 1) - value)
    return flux - pltpu.roll(flux, 1, 1)


def inner_steps(q, a, b, north, width, put, keep):
    end = width - 1
    here, flux, once_before, flux_before = q(0), None, None, None
    for x in range(width):
        if x == 0:
            east = q(1)
            flux_e = a(0) * here + b(0) * east
            keep(0, here)
            keep(1, (here - flux_e) + along_y(north(0), here))
            once = None
        elif x == end:
            keep(4, here)
            keep(5, (here + flux) + along_y(north(end), here))
            keep(6, once_before)
            keep(7, (once_before + flux_before) + along_y(north(end - 1), once_before))
            break
        else:
            east = q(x + 1)
            flux_e = a(x) * here + b(x) * east
            once = (here - (flux_e - flux)) + along_y(north(x), here)
        if once_before is not None:
            flux_once = a(x - 1) * once_before + b(x - 1) * once
            second = along_y(north(x - 1), once_before)
            if flux_before is None:
                keep(2, once_before)
                keep(3, (once_before - flux_once) + second)
            else:
                put(x - 1, (once_before - (flux_once - flux_before)) + second)
            flux_before = flux_once
        here, flux, once_before = east, flux_e, once


def rim_steps(kept, west, east, a, b, north, width):
    end = width - 1
    value, behind = west
    flux = a(-1) * value + b(-1) * kept(0)
    outer = (value - (flux - behind)) + along_y(north(-1), value)
    edge = kept(1) + flux
    flux_out = a(-1) * outer + b(-1) * edge
    flux_in = a(0) * edge + b(0) * kept(2)
    new = {0: (edge - (flux_in - flux_out)) + along_y(north(0), edge), 1: kept(3) + flux_in}
    value, behind = east
    flux = a(end) * kept(4) + b(end) * value
    outer = (value - (behind - flux)) + along_y(north(width), value)
    edge = kept(5) - flux
    flux_out = a(end) * edge + b(end) * outer
    flux_in = a(end - 1) * kept(6) + b(end - 1) * edge
    new[end] = (edge - (flux_out - flux_in)) + along_y(north(end), edge)
    new[end - 1] = kept(7) - flux_in
    return new


def tiles_in(turn, value):
    levels, width, _ = value.shape
    for j in range(turn.shape[0]):
        turn[j, : levels * width, :] = value[:, :, 128 * j : 128 * (j + 1)].reshape(levels * width, 128)


def column(turn, x, width):
    parts = [turn[j, pl.ds(x, ROWS8, stride=width), :] for j in range(turn.shape[0])]
    return jnp.concatenate(parts, axis=1)


def put_column(stage, t, start, x, value):
    parts, tracers, levels, width, lanes = stage.shape
    rows = stage.reshape(parts, tracers, levels * width, lanes)
    for j in range(parts):
        at = pl.ds(start * width + x, ROWS8, stride=width)
        rows[j, t, at, :] = value[:, lanes * j : lanes * (j + 1)]


def ring(x, width):
    return x if x >= 0 else width + ROWS8 + x


def spread_north(coef_n, north_s, width, columns=None):
    for x in columns or range(width):
        row = ring(x, width)
        north_s[x + HALO] = jnp.broadcast_to(coef_n[row : row + 1, :], north_s.shape[1:])


def face(coefs, part, x, u, open_e, width):
    row = ring(x, width)
    coefs[0, x + 1, part, :], coefs[1, x + 1, part, :] = leaving(u, open_e[row : row + 1, :])


def faces(coefs, part):
    return [lambda x, i=i: coefs[i, x + 1, part, :] for i in range(2)]


def first_inner_kernel(
    begin, fixed, scale, surface, speed, open_e, coef_n,
    field, rims, coefs, coef_n_out, north_s, turn, turn_speed,
):
    tracers, levels, width, rows = fixed.shape
    size = field.shape[2]
    spread_north(coef_n, north_s, width)
    north = lambda x: north_s[x + HALO]

    def block(i, _):
        start = pl.multiple_of(i * ROWS8, ROWS8)
        part, whole = pl.ds(start, ROWS8), pl.ds(begin + start, ROWS8)
        tiles_in(turn_speed, speed[whole])
        for x in range(width):
            face(coefs, part, x, column(turn_speed, x, width), open_e, width)

        def tracer(t, _):
            tiles_in(turn, fixed[t, whole] + scale[whole] * surface[t][None])

            def put(x, value):
                field[t, x, part, :] = value

            def keep(i, value):
                rims[t, i, part, :] = value

            q = lambda x: column(turn, x, width)
            inner_steps(q, *faces(coefs, part), north, width, put, keep)
            return 0

        lax.fori_loop(0, tracers, tracer, 0)
        return 0

    lax.fori_loop(0, size // ROWS8, block, 0)


def halo_pair(even, halo_1, halo_2, t, part):
    pairs = [(halo_1[t, i, part, :], halo_2[t, i, part, :]) for i in range(2)]
    west = [jnp.where(even, second, first) for first, second in pairs]
    east = [jnp.where(even, first, second) for first, second in pairs]
    return west, east


def first_rim_kernel(
    begin, rims, speed_w, open_e, halo_1, halo_2, coef_n, field_in, coefs_in,
    field, coefs, send_1, send_2, coef_n_out, north_s,
):
    tracers, width, size, rows = field.shape
    even = is_even()
    spread_north(coef_n, north_s, width, (-1, 0, width - 1, width))
    north = lambda x: north_s[x + HALO]

    def block(i, _):
        start = pl.multiple_of(i * ROWS8, ROWS8)
        part, whole = pl.ds(start, ROWS8), pl.ds(begin + start, ROWS8)
        face(coefs, part, -1, speed_w[whole, :], open_e, width)
        a, b = faces(coefs, part)

        def tracer(t, _):
            halos = halo_pair(even, halo_1, halo_2, t, part)
            new = rim_steps(lambda i: rims[t, i, part, :], *halos, a, b, north, width)
            for x, value in new.items():
                field[t, x, part, :] = value
            end = width - 1
            west = new[0], a(0) * new[0] + b(0) * new[1]
            east = new[end], a(end - 1) * new[end - 1] + b(end - 1) * new[end]
            for i in range(2):
                send_1[t, i, part, :] = jnp.where(even, east[i], west[i])
                send_2[t, i, part, :] = jnp.where(even, west[i], east[i])
            return 0

        lax.fori_loop(0, tracers, tracer, 0)
        return 0

    lax.fori_loop(0, size // ROWS8, block, 0)


def last_inner_kernel(field, coefs, coef_n, stage, rims, coef_n_out, north_s):
    tracers, width, size, rows = field.shape
    spread_north(coef_n, north_s, width)
    north = lambda x: north_s[x + HALO]

    def block(i, _):
        start = pl.multiple_of(i * ROWS8, ROWS8)
        part = pl.ds(start, ROWS8)

        def tracer(t, _):
            q = lambda x: field[t, x, part, :]
            put = lambda x, value: put_column(stage, t, start, x, value)

            def keep(i, value):
                rims[t, i, part, :] = value

            inner_steps(q, *faces(coefs, part), north, width, put, keep)
            return 0

        lax.fori_loop(0, tracers, tracer, 0)
        return 0

    lax.fori_loop(0, size // ROWS8, block, 0)


def last_rim_kernel(begin, rims, coefs, halo_1, halo_2, coef_n, stage_in, *refs):
    out, stage, coef_n_out, north_s, sems = refs[-5:]
    tracers, size, width = rims.shape[0], rims.shape[2], stage.shape[3]
    even = is_even()
    spread_north(coef_n, north_s, width, (-1, 0, width - 1, width))
    north = lambda x: north_s[x + HALO]

    def copies_of(i, t):
        start = pl.multiple_of(i * ROWS8, ROWS8)
        part, to = pl.ds(start, ROWS8), pl.ds(begin + start, ROWS8)
        return [
            pltpu.make_async_copy(stage.at[j, t, part], out.at[t, to, :, pl.ds(128 * j, 128)], sems.at[i, t, j])
            for j in range(stage.shape[0])
        ]

    def block(i, _):
        start = pl.multiple_of(i * ROWS8, ROWS8)
        part = pl.ds(start, ROWS8)

        def tracer(t, _):
            halos = halo_pair(even, halo_1, halo_2, t, part)
            new = rim_steps(lambda i: rims[t, i, part, :], *halos, *faces(coefs, part), north, width)
            for x, value in new.items():
                put_column(stage, t, start, x, value)
            for copy in copies_of(i, t):
                copy.start()
            return 0

        lax.fori_loop(0, tracers, tracer, 0)
        return 0

    def finish(i, _):
        for t in range(tracers):
            for copy in copies_of(i, t):
                copy.wait()
        return 0

    lax.fori_loop(0, size // ROWS8, block, 0)
    lax.fori_loop(0, size // ROWS8, finish, 0)


def transport_call(kernel, name, args, out_shape, aliases, scratch, cells, hbm=(), out_hbm=()):
    return pl.pallas_call(
        kernel,
        in_specs=[HBM if i in hbm else VMEM for i in range(len(args))],
        out_specs=[HBM if i in out_hbm else VMEM for i in range(len(out_shape))],
        out_shape=out_shape,
        scratch_shapes=scratch,
        input_output_aliases=aliases,
        compiler_params=params(16),
        cost_estimate=LITTLE,
        name=name,
    )(*args)


def north_scratch(width, rows):
    return pltpu.VMEM((width + 2 * HALO, ROWS8, rows), F32)


def first_inner(chunk, fixed, scale, surface, speed, open_e, coef_n):
    count, levels, width, rows = fixed.shape
    begin, size = chunk
    args = [fixed, scale, surface, speed, open_e, coef_n]
    out_shape = [
        shape_of(count, width, size, rows),
        shape_of(count, 8, size, rows),
        shape_of(2, width + 1, size, rows),
        shape_of(*coef_n.shape),
    ]
    turn = pltpu.VMEM((rows // 128, (ROWS8 + 1) * width, 128), F32)
    return transport_call(
        functools.partial(first_inner_kernel, begin), "first_inner", args, out_shape, {len(args) - 1: 3},
        [north_scratch(width, rows), turn, turn], count * size * width * rows,
    )


def first_rim(chunk, field, rims, coefs, speed_w, open_e, halos, coef_n):
    count, width, size, rows = field.shape
    args = [rims, speed_w, open_e, *halos, coef_n, field, coefs]
    edge = shape_of(count, 2, size, rows)
    out_shape = [shape_of(*field.shape), shape_of(*coefs.shape), edge, edge, shape_of(*coef_n.shape)]
    field, coefs, send_1, send_2, coef_n = transport_call(
        functools.partial(first_rim_kernel, chunk[0]), "first_rim", args, out_shape, {5: 4, 6: 0, 7: 1},
        [north_scratch(width, rows)], count * size * 4 * rows,
    )
    return field, coefs, (send_1, send_2), coef_n


def last_inner(field, coefs, coef_n):
    count, width, size, rows = field.shape
    out_shape = [
        shape_of(rows // 128, count, size + 1, width, 128),
        shape_of(count, 8, size, rows),
        shape_of(*coef_n.shape),
    ]
    return transport_call(
        last_inner_kernel, "last_inner", [field, coefs, coef_n], out_shape, {2: 2},
        [north_scratch(width, rows)], count * size * width * rows,
    )


def last_rim(chunk, levels, rims, coefs, halos, stage, coef_n, result):
    count, _, size, rows = rims.shape
    width = stage.shape[3]
    args = [rims, coefs, *halos, coef_n, stage]
    aliases = {4: 2, 5: 1}
    if result is not None:
        aliases[6] = 0
        args.append(result)
    out_shape = [shape_of(count, levels, width, rows), shape_of(*stage.shape), shape_of(*coef_n.shape)]
    result, _, coef_n = transport_call(
        functools.partial(last_rim_kernel, chunk[0]), "last_rim", args, out_shape, aliases,
        [north_scratch(width, rows), pltpu.SemaphoreType.DMA((size // ROWS8, count, rows // 128))],
        count * size * 4 * rows, hbm=(6,), out_hbm=(0,),
    )
    return result, coef_n


def per_device(tracers, diffusivity, conductance, face_velocity, partner, weight, sea_mask):
    tiles = lax.axis_size("tile")
    tracers, diffusivity, conductance = tracers[0], diffusivity[0], conductance[0]
    speed, partner, weight = face_velocity[0], partner[0], weight[0]
    width = tracers.shape[2]
    reach = width // 2 + 1

    def move(value, target_of, swap=False):
        pairs = []
        for m in range(2):
            for t in range(tiles):
                target = (1 - m if swap else m) * tiles + target_of(t) % tiles
                pairs.append((m * tiles + t, target))
        return lax.ppermute(value, ("mp", "tile"), pairs)

    one = lambda t: t + 1 - 2 * (t % 2)
    two = lambda t: t - 1 + 2 * (t % 2)

    *speeds, to_east, order = speed_columns(speed, (0, width - 2, width - 1))
    speed_w = move(to_east, lambda t: t + 1)
    signed = jnp.where(sea_mask > 0, conductance, -conductance)
    parts, ratios, slope, own, *halves, terms_1, terms_2 = down_to_surface(tracers, diffusivity, signed, order, reach)
    terms_1 = move(terms_1, one, swap=True)
    terms_2 = move(terms_2, two, swap=True)
    peers = [move(half, lambda t: t, swap=True) for half in halves]
    rim = (0, 1, width - 2, width - 1)
    fixed, scale, rims, rim_scale = up_from_surface(parts, ratios, speed_w, rim)

    inflow, surface, open_e, coef_n, *sends = exchange_surface(
        own, slope, peers, terms_1, terms_2, partner, weight, signed, rims, rim_scale, speeds, reach
    )
    levels = fixed.shape[1]
    chunks = chunks_of(levels)
    every = range(len(chunks))
    exchange = lambda pair: (move(pair[0], one), move(pair[1], two))
    halos = [exchange((sends[c], sends[len(chunks) + c])) for c in every]
    fields, rims, coefs, stages = [[None] * len(chunks) for _ in range(4)]
    for c in every:
        fields[c], rims[c], coefs[c], coef_n = first_inner(chunks[c], fixed, scale, surface, speed, open_e, coef_n)
    for c in every:
        fields[c], coefs[c], pair, coef_n = first_rim(
            chunks[c], fields[c], rims[c], coefs[c], speed_w, open_e, halos[c], coef_n
        )
        halos[c] = exchange(pair)
    for c in every:
        stages[c], rims[c], coef_n = last_inner(fields[c], coefs[c], coef_n)
    result = None
    for c in every:
        result, coef_n = last_rim(chunks[c], levels, rims[c], coefs[c], halos[c], stages[c], coef_n, result)
    return result[None], inflow[None]


def solution(mesh):
    in_specs = (
        P("mp", None, None, "tile", None),
        P("mp", None, "tile", None),
        P("mp", "tile", None),
        P("mp", None, "tile", None),
        P("mp", None, "tile", None),
        P("mp", None, "tile", None),
        P("tile", None),
    )
    out_specs = (P("mp", None, None, "tile", None), P("mp", None, "tile", None))
    return jax.shard_map(
        per_device, mesh=mesh, in_specs=in_specs, out_specs=out_specs, check_vma=False
    )
```
